32 devices in a mesh: dp: 8 (over y, x, core), tensor: 4 (over z).
Axes of the slice: x: 2, y: 2, z: 4, core: 2. Of those that a mesh axis runs over, the one named last changes fastest.
Arguments:
- tokens: bfloat16 [8192, 1536], P(('dp', 'tensor')), may hold values from -6 to 6
- first_gain: float32 [1536], replicated, may hold values from 0.25 to 1.75
- query_weight: bfloat16 [1536, 768], P(None, 'tensor'), may hold values from -0.0625 to 0.0625
- key_weight: bfloat16 [1536, 768], P(None, 'tensor'), may hold values from -0.0625 to 0.0625
- value_weight: bfloat16 [1536, 768], P(None, 'tensor'), may hold values from -0.15625 to 0.15625
- out_weight: bfloat16 [1536, 768], P(None, 'tensor'), may hold values from -0.875 to 0.875
- bucket_table: float32 [32, 12], P(None, 'tensor'), may hold values from -3 to 3
- second_gain: float32 [1536], replicated, may hold values from 0.25 to 1.75
- gate_weight: bfloat16 [1536, 3968], P(None, 'tensor'), may hold values from -0.15625 to 0.15625
- up_weight: bfloat16 [1536, 3968], P(None, 'tensor'), may hold values from -0.15625 to 0.15625
- down_weight: bfloat16 [1536, 3968], P(None, 'tensor'), may hold values from -0.09375 to 0.09375
- piece_start: int32 [8, 2], P('dp'), may hold values from 0 to 768, as said below
- bucket_index: int32 [2047], replicated, may hold values from 0 to 31, as said below
- cotangent: bfloat16 [8192, 1536], P(('dp', 'tensor')), may hold values from -6 to 6
Outputs:
- layer_out: bfloat16 [8192, 1536], P(('dp', 'tensor'))
- input_grad: bfloat16 [8192, 1536], P(('dp', 'tensor'))
- first_gain_grad: float32 [1536], replicated
- query_grad: float32 [1536, 768], P('dp', 'tensor')
- key_grad: float32 [1536, 768], P('dp', 'tensor')
- value_grad: float32 [1536, 768], P('dp', 'tensor')
- out_grad: float32 [1536, 768], P('dp', 'tensor')
- table_grad: float32 [32, 12], P(None, 'tensor')
- second_gain_grad: float32 [1536], replicated
- gate_grad: float32 [1536, 3968], P('dp', 'tensor')
- up_grad: float32 [1536, 3968], P('dp', 'tensor')
- down_grad: float32 [1536, 3968], P('dp', 'tensor')
The draws below stay inside these ranges and needn't reach their ends.
Inputs may be any that keep to these rules, and one draw needn't show every extreme that they name: `piece_start`: piece p of a sequence lies within positions p * 512 to (p + 1) * 512 - 1, so pieces never intersect. bucket_index[d + 1023] is the bucket of key minus query position d: for d <= 0 it lies below 16 and equals |d| when |d| < 8; for d > 0 it is 16 plus the bucket that -d has, so it equals |d| + 32 // 2 when |d| < 8; it never falls as |d| grows on either side.
All inputs are finite; a program needn't handle non-finite values.
Results may differ from the reference program's by a relative error of at most 0.02.
Values may be sent and summed in bfloat16 or wider, within the bound.
A program may use at most 192 MiB of HBM per device.

```python
import jax
import jax.numpy as jnp
from jax import lax

D = 1536
H = 12
DK = 64
FF = 3968
NB = 32
LEN = 1024
PIECE = 256
NPIECE = 2
SEQ_GRP = 1
INNER = 768
SEQS = 8
TOKENS = 8192
N_DP = 8


def draw_piece_start(key, part):
    region = LEN // NPIECE
    offsets = jax.random.randint(key, (SEQS, NPIECE), 0, region - PIECE + 1)
    bases = jnp.arange(NPIECE, dtype=jnp.int32) * region
    return (offsets + bases[None, :]).astype(jnp.int32)


def draw_bucket_index(key, part):
    half = NB // 2
    exact = half // 2
    cut_count = half - exact - 1
    pool = LEN // 2 - exact - 1
    cuts = jnp.sort(jax.random.permutation(key, pool)[:cut_count]) + exact + 1
    distance = jnp.arange(2 * LEN - 1, dtype=jnp.int32) - (LEN - 1)
    magnitude = jnp.abs(distance)
    beyond = jnp.sum((magnitude[:, None] >= cuts[None, :]).astype(jnp.int32), axis=1)
    within = jnp.where(magnitude < exact, magnitude, exact + beyond)
    return (within + half * (distance > 0).astype(jnp.int32)).astype(jnp.int32)


def spiked(entries, own_key, source, target, shards_of, factor):
    def block_of(dim):
        return (jnp.arange(entries.shape[dim]) // (entries.shape[dim] // shards_of)).reshape((-1,) + (1,) * (entries.ndim - 1 - dim))

    first = jax.random.permutation(own_key, shards_of)[block_of(target)]
    far = (block_of(target) + shards_of // 2) % shards_of
    return jnp.where((block_of(source) == first) | (block_of(source) == far), factor * entries, entries)


def steps_of(rng, dims, split, least, top_value):
    def one(dim, shards_of):
        heights = jax.random.uniform(jax.random.fold_in(jax.random.fold_in(rng, 6), dim), (shards_of,), jnp.float32, least / len(split), top_value / len(split))
        return jnp.repeat(jnp.exp(heights), dims[dim] // shards_of).reshape((-1,) + (1,) * (len(dims) - dim - 1))

    loudness = one(*split[0])
    for cut in split[1:]:
        loudness = loudness * one(*cut)
    return loudness


def scatter_about(key, shape, scale, most, pieces=(), kind=jnp.bfloat16):
    level = steps_of(key, shape, pieces, -0.22, 0.18) if pieces else 1.0
    drawn = jax.random.normal(key, shape, jnp.float32) * scale * level
    return jnp.minimum(jnp.maximum(drawn, -most), most).astype(kind)


def heavy_noise(own_key, dims, scale, most, split, heavy, held_as=jnp.bfloat16):
    entries = scale * jax.random.normal(own_key, dims, jnp.float32)
    if split:
        entries = entries * steps_of(own_key, dims, split, -0.22, 0.18)
    return jnp.clip(spiked(entries, jax.random.fold_in(own_key, 3), *heavy), -most, most).astype(held_as)


def setup_inputs(seed: int = 0) -> dict:
    keys = jax.random.split(jax.random.key(seed), 15)
    tokens = heavy_noise(keys[0], (TOKENS, D), 1.0, 6.0, ((0, 32),), (0, 1, 32, 2.75))
    first_gain = jnp.clip(1.0 + 0.15 * jax.random.normal(keys[1], (D,), jnp.float32), 0.25, 1.75)
    query_weight = scatter_about(keys[2], (D, INNER), (5 * D) ** -0.5, 0.0625, ((1, 4),))
    key_weight = scatter_about(keys[3], (D, INNER), (5 * D) ** -0.5, 0.0625, ((1, 4),))
    value_weight = scatter_about(keys[4], (D, INNER), D ** -0.5, 0.15625, ((1, 4),))
    out_weight = scatter_about(keys[5], (D, INNER), (INNER // 16) ** -0.5, 0.875, ((1, 4),))
    bucket_table = scatter_about(keys[6], (NB, H), 0.5, 3.0, ((1, 4),), jnp.float32)
    second_gain = jnp.clip(1.0 + 0.15 * jax.random.normal(keys[7], (D,), jnp.float32), 0.25, 1.75)
    gate_weight = scatter_about(keys[8], (D, FF), D ** -0.5, 0.15625, ((1, 4),))
    up_weight = scatter_about(keys[9], (D, FF), D ** -0.5, 0.15625, ((1, 4),))
    down_weight = scatter_about(keys[10], (D, FF), FF ** -0.5, 0.09375, ((1, 4),))
    piece_start = draw_piece_start(jax.random.fold_in(keys[14], 71), 0)
    bucket_index = draw_bucket_index(jax.random.fold_in(keys[14], 71), 0)
    cotangent = heavy_noise(keys[13], (TOKENS, D), 1.0, 6.0, ((0, 32),), (0, 1, 32, 2.75))
    return {"tokens": tokens, "first_gain": first_gain, "query_weight": query_weight, "key_weight": key_weight, "value_weight": value_weight, "out_weight": out_weight, "bucket_table": bucket_table, "second_gain": second_gain, "gate_weight": gate_weight, "up_weight": up_weight, "down_weight": down_weight, "piece_start": piece_start, "bucket_index": bucket_index, "cotangent": cotangent}


@jax.custom_vjp
def low(v):
    return lax.optimization_barrier(v.astype(jnp.bfloat16)).astype(jnp.float32)

@jax.custom_vjp
def low_back(v):
    return v

def low_keep(v):
    return (low(v), None)

def low_pass(kept, grad):
    return (grad,)

def back_keep(v):
    return (v, None)

def back_low(kept, grad):
    return (low(grad),)
low.defvjp(low_keep, low_pass)
low_back.defvjp(back_keep, back_low)
EPSILON = 1e-06
MASKED = -1000000000.0
HIGHEST = lax.Precision.HIGHEST

def normed(row_block, gain_vec):
    inv_rms = lax.rsqrt(lax.optimization_barrier(jnp.mean(row_block * row_block, axis=-1, keepdims=True)) + EPSILON)
    return row_block * inv_rms * gain_vec

def piece_labels(starts_row, position):
    inside = (position[None, :] >= starts_row[:, None]) & (position[None, :] < starts_row[:, None] + PIECE)
    labels = jnp.arange(1, NPIECE + 1, dtype=jnp.int32)
    return lax.optimization_barrier(jnp.sum(inside.astype(jnp.int32) * labels[:, None], axis=0)) - 1

def allowed_mask(starts_row):
    position = jnp.arange(LEN, dtype=jnp.int32)
    labels = piece_labels(starts_row, position)
    causal = position[None, :] <= position[:, None]
    shared = (labels[:, None] == labels[None, :]) & (labels[:, None] >= 0)
    return causal | shared

def attend_sequence(queries, key_rows, value_rows, bias_full, allowed):
    raw_scores = jnp.einsum('qhd,khd->hqk', queries, key_rows, precision=HIGHEST) + bias_full
    scores = jnp.where(allowed[None], low_back(raw_scores), MASKED)
    peak = lax.optimization_barrier(jnp.max(scores, axis=-1, keepdims=True))
    powered = jnp.exp(scores - peak)
    softmax_rows = powered / lax.optimization_barrier(jnp.sum(powered, axis=-1, keepdims=True))
    return jnp.einsum('hqk,khd->qhd', low(softmax_rows), value_rows, precision=HIGHEST)

def layer(parameters, input_rows, starts_group, lookup):
    first_gain, query_weight, key_weight, value_weight, out_weight, bucket_table, second_gain, gate_weight, up_weight, down_weight = parameters
    norm_first = low(normed(input_rows, first_gain))

    def project(weight):
        return low(low_back(jnp.dot(norm_first, weight, precision=HIGHEST)))

    def to_heads(matrix):
        return matrix.reshape(SEQ_GRP, LEN, H, DK)
    bias_full = jnp.transpose(jnp.take(bucket_table, lookup, axis=0), (2, 0, 1))
    checked = jax.checkpoint(attend_sequence)

    def attend_one(inputs_seq):
        queries, key_rows, value_rows, starts_row = inputs_seq
        return checked(queries, key_rows, value_rows, bias_full, allowed_mask(starts_row))
    attended = lax.map(attend_one, (to_heads(project(query_weight)), to_heads(project(key_weight)), to_heads(project(value_weight)), starts_group))
    attended = low(low_back(attended.reshape(SEQ_GRP * LEN, H * DK)))
    middle = input_rows + low_back(jnp.dot(attended, out_weight.T, precision=HIGHEST))
    norm_second = low(normed(middle, second_gain))
    gate_pre = low_back(jnp.dot(norm_second, gate_weight, precision=HIGHEST))
    up_proj = low_back(jnp.dot(norm_second, up_weight, precision=HIGHEST))
    hidden = low(jax.nn.gelu(gate_pre, approximate=True) * up_proj)
    return middle + low_back(jnp.dot(hidden, down_weight.T, precision=HIGHEST))

def reference(tokens, first_gain, query_weight, key_weight, value_weight, out_weight, bucket_table, second_gain, gate_weight, up_weight, down_weight, piece_start, bucket_index, cotangent):
    position = jnp.arange(LEN, dtype=jnp.int32)
    lookup = bucket_index[(position[None, :] - position[:, None] + (LEN - 1)).astype(jnp.int32)]
    parameters = tuple((member.astype(jnp.float32) for member in (first_gain, query_weight, key_weight, value_weight, out_weight, bucket_table, second_gain, gate_weight, up_weight, down_weight)))
    input_all = tokens.astype(jnp.float32).reshape(N_DP, SEQ_GRP * LEN, D)
    cot_all = cotangent.astype(jnp.float32).reshape(N_DP, SEQ_GRP * LEN, D)
    starts_all = piece_start.reshape(N_DP, SEQ_GRP, NPIECE)

    def scan_step(running, inputs_group):
        input_rows, cot_rows, starts_group = inputs_group

        def forward(parameters_in, rows_in):
            return layer(parameters_in, rows_in, starts_group, lookup)
        layer_rows, pull_back = jax.vjp(forward, parameters, input_rows)
        param_grads, input_grads = pull_back(cot_rows)
        running = jax.tree.map(jnp.add, running, param_grads)
        return (running, (layer_rows.astype(jnp.bfloat16), input_grads.astype(jnp.bfloat16)))
    zero_grads = jax.tree.map(jnp.zeros_like, parameters)
    summed, (layer_rows, input_grads) = lax.scan(scan_step, zero_grads, (input_all, cot_all, starts_all))
    return (layer_rows.reshape(TOKENS, D), input_grads.reshape(TOKENS, D), summed[0], summed[1], summed[2], summed[3], summed[4], summed[5], summed[6], summed[7], summed[8], summed[9])
```

```python
import functools

import jax
import jax.numpy as jnp
from jax import lax
from jax.experimental import pallas as pl
from jax.experimental.pallas import tpu as pltpu
from jax.sharding import PartitionSpec as P

NB = 32
LEN = 1024
QB = 256
PIECE = 256
NPIECE = 2
HALF = LEN // NPIECE
SPAN = 5 * QB
DIST = 2 * LEN

EPSILON = 1e-06
MASKED = -1000000000.0
VMEM_LIMIT = 60 * 1024 * 1024


def normed(row_block, gain_vec):
    inv_rms = lax.rsqrt(jnp.mean(row_block * row_block, axis=-1, keepdims=True) + EPSILON)
    return row_block * inv_rms * gain_vec


def gelu_tanh(values):
    return jax.nn.gelu(values, approximate=True)


def dot(a, b, dims):
    return lax.dot_general(a, b, (dims, ((), ())), preferred_element_type=jnp.float32)


def key_count(block):
    return HALF if (block + 1) * QB <= HALF else LEN


def toeplitz(bucket_row, table_ref, head):
    row = jnp.zeros(bucket_row.shape, jnp.float32)
    for bucket in range(NB):
        row = jnp.where(bucket_row == bucket, table_ref[bucket, head], row)
    rows = jnp.broadcast_to(row, (QB, DIST))
    return pltpu.roll(rows, DIST - (QB - 1), 1, stride=1, stride_axis=0)[:, :SPAN]


def label_of(position, starts):
    label = jnp.zeros(position.shape, jnp.int32)
    for piece, start in enumerate(starts):
        inside = (position >= start) & (position < start + PIECE)
        label = jnp.where(inside, piece + 1, label)
    return label


def allowed_block(block, starts):
    keys = key_count(block)
    query = block * QB + lax.broadcasted_iota(jnp.int32, (QB, 1), 0)
    key = lax.broadcasted_iota(jnp.int32, (1, keys), 1)
    query_label = label_of(query, starts)
    key_label = label_of(key, starts)
    return (key <= query) | ((query_label == key_label) & (query_label > 0))


def attend_kernel(heads, head_dim, q_ref, k_ref, v_ref, bucket_ref, table_ref, start_ref, att_ref, low_ref, high_ref, bias_ref):
    starts = [start_ref[0, piece] for piece in range(NPIECE)]
    for head in range(heads):
        bias_ref[head] = toeplitz(bucket_ref[...], table_ref, head)
    for block in range(LEN // QB):
        keys = key_count(block)
        allowed = allowed_block(block, starts)
        first = LEN - QB - block * QB
        rows = pl.ds(block * QB, QB)
        outs = []
        for head in range(heads):
            cols = pl.ds(head * head_dim, head_dim)
            raw = dot(q_ref[rows, cols], k_ref[pl.ds(0, keys), cols], ((1,), (1,)))
            scores = jnp.where(allowed, raw + bias_ref[head, :, pl.ds(first, keys)], MASKED)
            peak = jnp.max(scores, axis=-1, keepdims=True)
            powered = jnp.exp(scores - peak)
            total = jnp.sum(powered, axis=-1, keepdims=True)
            probs = (powered * (1.0 / total)).astype(jnp.bfloat16)
            if keys == HALF:
                low_ref[head, rows, :] = probs
            else:
                high_ref[head, pl.ds(block * QB - HALF, QB), :] = probs
            outs.append(dot(probs, v_ref[pl.ds(0, keys), cols], ((1,), (0,))))
        att_ref[rows, :] = jnp.concatenate(outs, axis=1).astype(jnp.bfloat16)


def fold_diagonals(grid):
    rows = QB // 2
    width = grid.shape[1]
    while rows >= 1:
        grid = grid[:rows] + pltpu.roll(grid[rows : 2 * rows], width - rows, 1)
        rows //= 2
    return grid


def attend_back_kernel(heads, head_dim, q_ref, k_ref, v_ref, do_ref, low_ref, high_ref, dq_ref, dk_ref, dv_ref, dist_ref, diag_ref, dk_acc, dv_acc):
    blocks = LEN // QB
    for head in range(heads):
        cols = pl.ds(head * head_dim, head_dim)
        diag_ref[...] = jnp.zeros_like(diag_ref)
        for block in reversed(range(blocks)):
            keys = key_count(block)
            rows = pl.ds(block * QB, QB)
            first = LEN - block * QB
            if keys == HALF:
                probs_low = low_ref[head, rows, :]
            else:
                probs_low = high_ref[head, pl.ds(block * QB - HALF, QB), :]
            probs = probs_low.astype(jnp.float32)
            do = do_ref[rows, cols]
            grad_probs = dot(do, v_ref[pl.ds(0, keys), cols], ((1,), (1,)))
            weighted = jnp.sum(probs * grad_probs, axis=-1, keepdims=True)
            grad_low = (probs * (grad_probs - weighted)).astype(jnp.bfloat16)
            span = pl.ds(first, keys)
            diag_ref[:, span] = diag_ref[:, span] + grad_low.astype(jnp.float32)
            dq_ref[rows, cols] = dot(grad_low, k_ref[pl.ds(0, keys), cols], ((1,), (0,))).astype(
                jnp.bfloat16
            )
            key_part = dot(grad_low, q_ref[rows, cols], ((0,), (0,)))
            value_part = dot(probs_low, do, ((0,), (0,)))
            if block == blocks - 1:
                dk_acc[...] = key_part
                dv_acc[...] = value_part
            else:
                dk_acc[pl.ds(0, keys), :] += key_part
                dv_acc[pl.ds(0, keys), :] += value_part
        dk_ref[:, cols] = dk_acc[...].astype(jnp.bfloat16)
        dv_ref[:, cols] = dv_acc[...].astype(jnp.bfloat16)
        dist_ref[pl.ds(head, 1), :] = fold_diagonals(diag_ref[...])


def whole_vmem(count):
    return [pl.BlockSpec(memory_space=pltpu.VMEM)] * count


def attend(query, key, value, bucket_row, table, starts):
    heads = table.shape[1]
    inner = query.shape[1]
    smem = pl.BlockSpec(memory_space=pltpu.SMEM)
    return pl.pallas_call(
        functools.partial(attend_kernel, heads, inner // heads),
        out_shape=(
            jax.ShapeDtypeStruct(query.shape, jnp.bfloat16),
            jax.ShapeDtypeStruct((heads, HALF, HALF), jnp.bfloat16),
            jax.ShapeDtypeStruct((heads, HALF, LEN), jnp.bfloat16),
        ),
        in_specs=whole_vmem(4) + [smem, smem],
        out_specs=tuple(whole_vmem(3)),
        scratch_shapes=[pltpu.VMEM((heads, QB, SPAN), jnp.float32)],
        compiler_params=pltpu.CompilerParams(vmem_limit_bytes=VMEM_LIMIT),
        name="attend",
    )(query, key, value, bucket_row, table, starts)


def attend_back(query, key, value, grad_attended, low, high):
    heads = low.shape[0]
    inner = query.shape[1]
    shape = jax.ShapeDtypeStruct(query.shape, jnp.bfloat16)
    return pl.pallas_call(
        functools.partial(attend_back_kernel, heads, inner // heads),
        out_shape=(shape, shape, shape, jax.ShapeDtypeStruct((heads, SPAN + QB), jnp.float32)),
        in_specs=whole_vmem(6),
        out_specs=tuple(whole_vmem(4)),
        scratch_shapes=[
            pltpu.VMEM((QB, SPAN + QB), jnp.float32),
            pltpu.VMEM((LEN, inner // heads), jnp.float32),
            pltpu.VMEM((LEN, inner // heads), jnp.float32),
        ],
        compiler_params=pltpu.CompilerParams(vmem_limit_bytes=VMEM_LIMIT),
        name="attend_back",
    )(query, key, value, grad_attended, low, high)


def per_device(
    tokens,
    first_gain,
    query_weight,
    key_weight,
    value_weight,
    out_weight,
    bucket_table,
    second_gain,
    gate_weight,
    up_weight,
    down_weight,
    piece_start,
    bucket_index,
    cotangent,
):
    own_rows = tokens.shape[0]
    contract_cols = (((1,), (1,)), ((), ()))
    contract_rows = (((0,), (0,)), ((), ()))
    bucket_row = jnp.pad(bucket_index, (0, 1))[None, :]
    inputs = tokens.astype(jnp.float32)
    norm_first = normed(inputs, first_gain).astype(jnp.bfloat16)
    first_all = lax.all_gather(norm_first, "tensor", axis=0, tiled=True)
    query_low = jnp.dot(first_all, query_weight, preferred_element_type=jnp.float32).astype(
        jnp.bfloat16
    )
    key_low = jnp.dot(first_all, key_weight, preferred_element_type=jnp.float32).astype(
        jnp.bfloat16
    )
    value_low = jnp.dot(first_all, value_weight, preferred_element_type=jnp.float32).astype(
        jnp.bfloat16
    )
    attended_low, probs_low, probs_high = attend(
        query_low, key_low, value_low, bucket_row, bucket_table, piece_start
    )
    picked = attended_low
    middle = inputs + lax.psum_scatter(
        lax.dot_general(
            picked, out_weight, contract_cols, preferred_element_type=jnp.float32
        ).astype(jnp.bfloat16),
        "tensor",
        scatter_dimension=0,
        tiled=True,
    ).astype(jnp.float32)
    norm_second = normed(middle, second_gain).astype(jnp.bfloat16)
    second_all = lax.all_gather(norm_second, "tensor", axis=0, tiled=True)
    gate_pre = jnp.dot(second_all, gate_weight, preferred_element_type=jnp.float32)
    up_proj = jnp.dot(second_all, up_weight, preferred_element_type=jnp.float32)
    activated, gelu_back = jax.vjp(gelu_tanh, gate_pre)
    hidden_low = (activated * up_proj).astype(jnp.bfloat16)
    picked = hidden_low
    layer_out = middle + lax.psum_scatter(
        lax.dot_general(
            picked, down_weight, contract_cols, preferred_element_type=jnp.float32
        ).astype(jnp.bfloat16),
        "tensor",
        scatter_dimension=0,
        tiled=True,
    ).astype(jnp.float32)
    grad_all = lax.all_gather(cotangent, "tensor", axis=0, tiled=True)
    down_grad = lax.dot_general(
        grad_all, hidden_low, contract_rows, preferred_element_type=jnp.float32
    )
    grad_hidden = jnp.dot(grad_all, down_weight, preferred_element_type=jnp.float32)
    (grad_act,) = gelu_back(grad_hidden * up_proj)
    grad_gate_low = grad_act.astype(jnp.bfloat16)
    grad_up_low = (grad_hidden * activated).astype(jnp.bfloat16)
    gate_grad = lax.dot_general(
        second_all, grad_gate_low, contract_rows, preferred_element_type=jnp.float32
    )
    up_grad = lax.dot_general(
        second_all, grad_up_low, contract_rows, preferred_element_type=jnp.float32
    )
    summed_rows = lax.dot_general(
        grad_gate_low, gate_weight, contract_cols, preferred_element_type=jnp.float32
    )
    grad_second = lax.psum_scatter(
        (
            summed_rows
            + lax.dot_general(
                grad_up_low, up_weight, contract_cols, preferred_element_type=jnp.float32
            )
        ).astype(jnp.bfloat16),
        "tensor",
        scatter_dimension=0,
        tiled=True,
    ).astype(jnp.float32)
    _, second_back = jax.vjp(normed, middle, second_gain)
    middle_part, second_gain_grad = second_back(grad_second)
    grad_middle = cotangent.astype(jnp.float32) + middle_part
    middle_all = lax.all_gather(grad_middle.astype(jnp.bfloat16), "tensor", axis=0, tiled=True)
    out_grad = lax.dot_general(
        middle_all, attended_low, contract_rows, preferred_element_type=jnp.float32
    )
    grad_attended = jnp.dot(middle_all, out_weight, preferred_element_type=jnp.float32).astype(
        jnp.bfloat16
    )
    grad_query_low, grad_key_low, grad_value_low, distance_sums = attend_back(
        query_low, key_low, value_low, grad_attended, probs_low, probs_high
    )
    width = min(distance_sums.shape[1] - 1, bucket_index.shape[0])
    table_hot = bucket_index[None, :width] == jnp.arange(NB, dtype=jnp.int32)[:, None]
    table_grad = jnp.sum(
        jnp.where(table_hot[:, None, :], distance_sums[None, :, 1 : width + 1], 0.0), axis=2
    )
    query_grad = lax.dot_general(
        first_all, grad_query_low, contract_rows, preferred_element_type=jnp.float32
    )
    key_grad = lax.dot_general(
        first_all, grad_key_low, contract_rows, preferred_element_type=jnp.float32
    )
    value_grad = lax.dot_general(
        first_all, grad_value_low, contract_rows, preferred_element_type=jnp.float32
    )
    summed_rows = jnp.zeros(
        (lax.axis_size("tensor") * own_rows, query_weight.shape[0]), jnp.float32
    )
    for grad_low, weight in (
        (grad_query_low, query_weight),
        (grad_key_low, key_weight),
        (grad_value_low, value_weight),
    ):
        picked = grad_low
        summed_rows = summed_rows + lax.dot_general(
            picked, weight, contract_cols, preferred_element_type=jnp.float32
        )
    grad_first = lax.psum_scatter(
        summed_rows.astype(jnp.bfloat16), "tensor", scatter_dimension=0, tiled=True
    ).astype(jnp.float32)
    _, first_back = jax.vjp(normed, inputs, first_gain)
    input_part, first_gain_grad = first_back(grad_first)
    input_grad = grad_middle + input_part
    grads = (query_grad, key_grad, value_grad, out_grad, gate_grad, up_grad, down_grad)
    joined = jnp.concatenate([grad.astype(jnp.bfloat16) for grad in grads], axis=1)
    summed = lax.psum_scatter(joined, "dp", scatter_dimension=0, tiled=True).astype(jnp.float32)
    edges = []
    for grad in grads[:-1]:
        edges.append((edges[-1] if edges else 0) + grad.shape[1])
    query_grad, key_grad, value_grad, out_grad, gate_grad, up_grad, down_grad = jnp.split(
        summed, edges, axis=1
    )
    table_grad = lax.psum(table_grad, "dp")
    first_gain_grad, second_gain_grad = lax.psum(
        (first_gain_grad, second_gain_grad), ("dp", "tensor")
    )
    return (
        layer_out.astype(jnp.bfloat16),
        input_grad.astype(jnp.bfloat16),
        first_gain_grad,
        query_grad,
        key_grad,
        value_grad,
        out_grad,
        table_grad,
        second_gain_grad,
        gate_grad,
        up_grad,
        down_grad,
    )


def solution(mesh):
    return jax.shard_map(
        per_device,
        mesh=mesh,
        in_specs=(
            P(("dp", "tensor"), None),
            P(),
            P(None, "tensor"),
            P(None, "tensor"),
            P(None, "tensor"),
            P(None, "tensor"),
            P(None, "tensor"),
            P(),
            P(None, "tensor"),
            P(None, "tensor"),
            P(None, "tensor"),
            P("dp", None),
            P(),
            P(("dp", "tensor"), None),
        ),
        out_specs=(
            P(("dp", "tensor"), None),
            P(("dp", "tensor"), None),
            P(),
            P("dp", "tensor"),
            P("dp", "tensor"),
            P("dp", "tensor"),
            P("dp", "tensor"),
            P(None, "tensor"),
            P(),
            P("dp", "tensor"),
            P("dp", "tensor"),
            P("dp", "tensor"),
        ),
        check_vma=False,
    )
```

```python
import functools

import jax
import jax.numpy as jnp
from jax import lax
from jax.experimental import pallas as pl
from jax.experimental.pallas import tpu as pltpu
from jax.sharding import PartitionSpec as P

NB = 32
LEN = 1024
QB = 256
PIECE = 256
NPIECE = 2
HALF = LEN // NPIECE
SPAN = 5 * QB
DIST = 2 * LEN

EPSILON = 1e-06
MASKED = -1000000000.0
VMEM_LIMIT = 60 * 1024 * 1024
MESH = pl.DeviceIdType.MESH


def normed(row_block, gain_vec):
    inv_rms = lax.rsqrt(jnp.mean(row_block * row_block, axis=-1, keepdims=True) + EPSILON)
    return row_block * inv_rms * gain_vec


def gelu_tanh(values):
    return jax.nn.gelu(values, approximate=True)


def dot(a, b, dims):
    return lax.dot_general(a, b, (dims, ((), ())), preferred_element_type=jnp.float32)


def key_count(block):
    return HALF if (block + 1) * QB <= HALF else LEN


def toeplitz(bucket_row, table_ref, head):
    row = jnp.zeros(bucket_row.shape, jnp.float32)
    for bucket in range(NB):
        row = jnp.where(bucket_row == bucket, table_ref[bucket, head], row)
    rows = jnp.broadcast_to(row, (QB, DIST))
    return pltpu.roll(rows, DIST - (QB - 1), 1, stride=1, stride_axis=0)[:, :SPAN]


def label_of(position, starts):
    label = jnp.zeros(position.shape, jnp.int32)
    for piece, start in enumerate(starts):
        inside = (position >= start) & (position < start + PIECE)
        label = jnp.where(inside, piece + 1, label)
    return label


def allowed_block(block, starts):
    keys = key_count(block)
    query = block * QB + lax.broadcasted_iota(jnp.int32, (QB, 1), 0)
    key = lax.broadcasted_iota(jnp.int32, (1, keys), 1)
    query_label = label_of(query, starts)
    key_label = label_of(key, starts)
    return (key <= query) | ((query_label == key_label) & (query_label > 0))


def attend_block(block, head_dim, allowed, qkv_ref, bias_ref, low_ref, high_ref):
    keys = key_count(block)
    first = LEN - QB - block * QB
    rows = pl.ds(block * QB, QB)
    outs = []
    for head in range(bias_ref.shape[0]):
        cols = pl.ds(head * head_dim, head_dim)
        raw = dot(qkv_ref[0, rows, cols], qkv_ref[1, pl.ds(0, keys), cols], ((1,), (1,)))
        scores = jnp.where(allowed, raw + bias_ref[head, :, pl.ds(first, keys)], MASKED)
        peak = jnp.max(scores, axis=-1, keepdims=True)
        powered = jnp.exp(scores - peak)
        total = jnp.sum(powered, axis=-1, keepdims=True)
        probs = (powered * (1.0 / total)).astype(jnp.bfloat16)
        if keys == HALF:
            low_ref[head, rows, :] = probs
        else:
            high_ref[head, pl.ds(block * QB - HALF, QB), :] = probs
        outs.append(dot(probs, qkv_ref[2, pl.ds(0, keys), cols], ((1,), (0,))))
    return jnp.concatenate(outs, axis=1).astype(jnp.bfloat16)


def greet(t, nt):
    barrier = pltpu.get_barrier_semaphore()
    for k in range(1, nt):
        pl.semaphore_signal(
            barrier, inc=1, device_id={"tensor": lax.rem(t + k, nt)}, device_id_type=MESH
        )
    return barrier


def line_copy(t, nt, way, step, buf, piece, pieces, send_sem, recv_sem):
    sign = 1 if way == 0 else -1
    origin = jnp.clip(t - sign * step, 0, nt - 1)
    rows = buf.shape[1] // pieces
    part = buf.at[origin, pl.ds(piece * rows, rows)]
    return pltpu.make_async_remote_copy(
        src_ref=part,
        dst_ref=part,
        send_sem=send_sem,
        recv_sem=recv_sem,
        device_id={"tensor": jnp.clip(t + sign, 0, nt - 1)},
        device_id_type=MESH,
    )


def gather_attend_kernel(
    nt, pieces, heads, head_dim,
    x_ref, cot_ref, gain_ref, wq_ref, wk_ref, wv_ref, bucket_ref, table_ref, start_ref,
    first_out, cot_out, qkv_out, low_out, high_out, own_out, att_out,
    first, qkv, low, high, bias, att,
    send_sem, recv_sem, swap_send, swap_recv, local_sem,
):
    t = lax.axis_index("tensor")
    barrier = greet(t, nt)
    own_cot = pltpu.make_async_copy(cot_ref, cot_out.at[t], local_sem.at[0])
    own_cot.start()
    first[t] = normed(x_ref[...].astype(jnp.float32), gain_ref[...]).astype(jnp.bfloat16)
    pl.semaphore_wait(barrier, nt - 1)

    def copy(way, stage, step, piece):
        buf = first if stage == 0 else cot_out
        return line_copy(
            t, nt, way, step, buf, piece, pieces,
            send_sem.at[way, stage, step, piece], recv_sem.at[way, stage, step, piece],
        )

    def landed(way, stage, step, piece):
        sign = 1 if way == 0 else -1
        buf = first if stage == 0 else cot_out
        rows = buf.shape[1] // pieces
        part = buf.at[jnp.clip(t - sign * step, 0, nt - 1), pl.ds(piece * rows, rows)]
        pltpu.make_async_remote_copy(
            src_ref=part, dst_ref=part,
            send_sem=send_sem.at[way, stage, step - 1, piece],
            recv_sem=recv_sem.at[way, stage, step - 1, piece],
            device_id={"tensor": jnp.clip(t + sign, 0, nt - 1)}, device_id_type=MESH,
        ).wait_recv()

    ways = ((0, t, t < nt - 1), (1, nt - 1 - t, t > 0))

    def tick(k):
        for piece in range(pieces):
            for way, last, onward in ways:
                if k < nt:
                    @pl.when(k <= last)
                    def _():
                        if k > 0:
                            landed(way, 0, k, piece)

                        @pl.when(onward)
                        def _():
                            copy(way, 0, k, piece).start()

                if k > 0:
                    step = k - last - 1

                    @pl.when((step >= 1) & (step <= last))
                    def _():
                        landed(way, 1, step, piece)

                        @pl.when(onward)
                        def _():
                            copy(way, 1, step, piece).start()

                    @pl.when((step == 0) & onward)
                    def _():
                        copy(way, 0, last, piece).wait_send()
                        copy(way, 1, 0, piece).start()

    def project(origin):
        rows = pl.ds(pl.multiple_of(origin * QB, QB), QB)
        for place, weight in enumerate((wq_ref, wk_ref, wv_ref)):
            qkv[place, rows, :] = dot(first[origin], weight[...], ((1,), (0,))).astype(jnp.bfloat16)

    tick(0)
    project(t)
    for head in range(heads):
        bias[head] = toeplitz(bucket_ref[...], table_ref, head)
    own_cot.wait()
    for k in range(1, nt):
        tick(k)

        @pl.when(t - k >= 0)
        def _():
            project(t - k)

        @pl.when(t + k < nt)
        def _():
            project(t + k)

    starts = [start_ref[0, piece] for piece in range(NPIECE)]
    keep = [pltpu.make_async_copy(first, first_out, local_sem.at[1]), pltpu.make_async_copy(qkv, qkv_out, local_sem.at[2])]
    for one in keep:
        one.start()

    def swap(block):
        return pltpu.make_async_remote_copy(
            src_ref=att.at[block], dst_ref=own_out.at[t],
            send_sem=swap_send.at[block], recv_sem=swap_recv.at[t],
            device_id={"tensor": block}, device_id_type=MESH,
        )

    own_att = pltpu.make_async_copy(att.at[t], own_out.at[t], local_sem.at[3])
    for block in range(LEN // QB):
        att[block] = attend_block(block, head_dim, allowed_block(block, starts), qkv, bias, low, high)

        @pl.when(t != block)
        def _():
            swap(block).start()

        @pl.when(t == block)
        def _():
            own_att.start()

    late = [
        pltpu.make_async_copy(low, low_out, local_sem.at[4]),
        pltpu.make_async_copy(high, high_out, local_sem.at[5]),
        pltpu.make_async_copy(att, att_out, local_sem.at[6]),
    ]
    for one in late:
        one.start()
    for k in range(nt, 2 * nt):
        tick(k)
    for block in range(nt):
        @pl.when(t != block)
        def _():
            swap(block).wait_send()
            pltpu.make_async_remote_copy(
                src_ref=att.at[block], dst_ref=own_out.at[block],
                send_sem=swap_send.at[block], recv_sem=swap_recv.at[block],
                device_id={"tensor": block}, device_id_type=MESH,
            ).wait_recv()

    own_att.wait()
    for one in keep + late:
        one.wait()
    for piece in range(pieces):
        for way, last, onward in ways:
            for stage in range(2):
                for step in range(nt):
                    @pl.when(onward & ((step < last) if stage == 0 else (step <= last)))
                    def _():
                        copy(way, stage, step, piece).wait_send()


def gather_attend(nt, tokens, cotangent, gain, weights, bucket_row, table, starts):
    heads = table.shape[1]
    inner = weights[0].shape[1]
    rows, width = tokens.shape
    low = jnp.bfloat16
    pieces = 2
    smem = pl.BlockSpec(memory_space=pltpu.SMEM)
    hbm = pl.BlockSpec(memory_space=pl.ANY)
    vmem = pl.BlockSpec(memory_space=pltpu.VMEM)
    shapes = (
        (nt, rows, width), (nt, rows, width), (3, LEN, inner), (heads, HALF, HALF), (heads, HALF, LEN),
        (nt, rows, inner), (nt, rows, inner),
    )
    dma = pltpu.SemaphoreType.DMA
    return pl.pallas_call(
        functools.partial(gather_attend_kernel, nt, pieces, heads, inner // heads),
        out_shape=tuple(jax.ShapeDtypeStruct(shape, low) for shape in shapes),
        in_specs=[vmem, hbm] + [vmem] * 5 + [smem, smem],
        out_specs=(hbm,) * 7,
        scratch_shapes=[
            pltpu.VMEM((nt, rows, width), low),
            pltpu.VMEM((3, LEN, inner), low),
            pltpu.VMEM((heads, HALF, HALF), low),
            pltpu.VMEM((heads, HALF, LEN), low),
            pltpu.VMEM((heads, QB, SPAN), jnp.float32),
            pltpu.VMEM((nt, rows, inner), low),
            dma((2, 2, nt, pieces)), dma((2, 2, nt, pieces)), dma((nt,)), dma((nt,)), dma((7,)),
        ],
        compiler_params=pltpu.CompilerParams(
            vmem_limit_bytes=VMEM_LIMIT, collective_id=0, has_side_effects=True
        ),
        name="gather_attend",
    )(tokens, cotangent, gain[None, :], *weights, bucket_row, table, starts)


def fold_diagonals(grid):
    rows = QB // 2
    width = grid.shape[1]
    while rows >= 1:
        grid = grid[:rows] + pltpu.roll(grid[rows : 2 * rows], width - rows, 1)
        rows //= 2
    return grid


def attend_back_kernel(heads, head_dim, q_ref, k_ref, v_ref, do_ref, low_ref, high_ref, dq_ref, dk_ref, dv_ref, dist_ref, diag_ref, dk_acc, dv_acc):
    blocks = LEN // QB
    for head in range(heads):
        cols = pl.ds(head * head_dim, head_dim)
        diag_ref[...] = jnp.zeros_like(diag_ref)
        for block in reversed(range(blocks)):
            keys = key_count(block)
            rows = pl.ds(block * QB, QB)
            first = LEN - block * QB
            if keys == HALF:
                probs_low = low_ref[head, rows, :]
            else:
                probs_low = high_ref[head, pl.ds(block * QB - HALF, QB), :]
            probs = probs_low.astype(jnp.float32)
            do = do_ref[rows, cols]
            grad_probs = dot(do, v_ref[pl.ds(0, keys), cols], ((1,), (1,)))
            weighted = jnp.sum(probs * grad_probs, axis=-1, keepdims=True)
            grad_low = (probs * (grad_probs - weighted)).astype(jnp.bfloat16)
            span = pl.ds(first, keys)
            diag_ref[:, span] = diag_ref[:, span] + grad_low.astype(jnp.float32)
            dq_ref[rows, cols] = dot(grad_low, k_ref[pl.ds(0, keys), cols], ((1,), (0,))).astype(
                jnp.bfloat16
            )
            key_part = dot(grad_low, q_ref[rows, cols], ((0,), (0,)))
            value_part = dot(probs_low, do, ((0,), (0,)))
            if block == blocks - 1:
                dk_acc[...] = key_part
                dv_acc[...] = value_part
            else:
                dk_acc[pl.ds(0, keys), :] += key_part
                dv_acc[pl.ds(0, keys), :] += value_part
        dk_ref[:, cols] = dk_acc[...].astype(jnp.bfloat16)
        dv_ref[:, cols] = dv_acc[...].astype(jnp.bfloat16)
        dist_ref[pl.ds(head, 1), :] = fold_diagonals(diag_ref[...])


def whole_vmem(count):
    return [pl.BlockSpec(memory_space=pltpu.VMEM)] * count


def attend_back(query, key, value, grad_attended, low, high):
    heads = low.shape[0]
    inner = query.shape[1]
    shape = jax.ShapeDtypeStruct(query.shape, jnp.bfloat16)
    return pl.pallas_call(
        functools.partial(attend_back_kernel, heads, inner // heads),
        out_shape=(shape, shape, shape, jax.ShapeDtypeStruct((heads, SPAN + QB), jnp.float32)),
        in_specs=whole_vmem(6),
        out_specs=tuple(whole_vmem(4)),
        scratch_shapes=[
            pltpu.VMEM((QB, SPAN + QB), jnp.float32),
            pltpu.VMEM((LEN, inner // heads), jnp.float32),
            pltpu.VMEM((LEN, inner // heads), jnp.float32),
        ],
        compiler_params=pltpu.CompilerParams(vmem_limit_bytes=VMEM_LIMIT),
        name="attend_back",
    )(query, key, value, grad_attended, low, high)


def per_device(
    tokens,
    first_gain,
    query_weight,
    key_weight,
    value_weight,
    out_weight,
    bucket_table,
    second_gain,
    gate_weight,
    up_weight,
    down_weight,
    piece_start,
    bucket_index,
    cotangent,
):
    own_rows = tokens.shape[0]
    contract_cols = (((1,), (1,)), ((), ()))
    contract_rows = (((0,), (0,)), ((), ()))
    bucket_row = jnp.pad(bucket_index, (0, 1))[None, :]
    inputs = tokens.astype(jnp.float32)
    nt = lax.axis_size("tensor")
    first_all, grad_all, qkv, probs_low, probs_high, attended_own, attended_heads = gather_attend(
        nt, tokens, cotangent, first_gain, (query_weight, key_weight, value_weight),
        bucket_row, bucket_table, piece_start,
    )
    first_all = first_all.reshape(-1, tokens.shape[1])
    grad_all = grad_all.reshape(-1, tokens.shape[1])
    attended_low = attended_heads.reshape(-1, query_weight.shape[1])
    query_low, key_low, value_low = qkv[0], qkv[1], qkv[2]
    own_part = out_weight.shape[0] // lax.axis_size("dp")
    out_all = lax.all_gather(
        lax.dynamic_slice_in_dim(out_weight, lax.axis_index("dp") * own_part, own_part, 0),
        ("tensor", "dp"), axis=0, tiled=True,
    ).reshape(nt, *out_weight.shape)
    middle = inputs + jnp.einsum(
        "tri,tdi->rd", attended_own, out_all, preferred_element_type=jnp.float32
    )
    norm_second = normed(middle, second_gain).astype(jnp.bfloat16)
    second_all = lax.all_gather(norm_second, "tensor", axis=0, tiled=True)
    gate_pre = jnp.dot(second_all, gate_weight, preferred_element_type=jnp.float32)
    up_proj = jnp.dot(second_all, up_weight, preferred_element_type=jnp.float32)
    activated, gelu_back = jax.vjp(gelu_tanh, gate_pre)
    hidden_low = (activated * up_proj).astype(jnp.bfloat16)
    picked = hidden_low
    layer_out = middle + lax.psum_scatter(
        lax.dot_general(
            picked, down_weight, contract_cols, preferred_element_type=jnp.float32
        ).astype(jnp.bfloat16),
        "tensor",
        scatter_dimension=0,
        tiled=True,
    ).astype(jnp.float32)
    down_grad = lax.dot_general(
        grad_all, hidden_low, contract_rows, preferred_element_type=jnp.float32
    )
    grad_hidden = jnp.dot(grad_all, down_weight, preferred_element_type=jnp.float32)
    (grad_act,) = gelu_back(grad_hidden * up_proj)
    grad_gate_low = grad_act.astype(jnp.bfloat16)
    grad_up_low = (grad_hidden * activated).astype(jnp.bfloat16)
    gate_grad = lax.dot_general(
        second_all, grad_gate_low, contract_rows, preferred_element_type=jnp.float32
    )
    up_grad = lax.dot_general(
        second_all, grad_up_low, contract_rows, preferred_element_type=jnp.float32
    )
    summed_rows = lax.dot_general(
        grad_gate_low, gate_weight, contract_cols, preferred_element_type=jnp.float32
    )
    grad_second = lax.psum_scatter(
        (
            summed_rows
            + lax.dot_general(
                grad_up_low, up_weight, contract_cols, preferred_element_type=jnp.float32
            )
        ).astype(jnp.bfloat16),
        "tensor",
        scatter_dimension=0,
        tiled=True,
    ).astype(jnp.float32)
    _, second_back = jax.vjp(normed, middle, second_gain)
    middle_part, second_gain_grad = second_back(grad_second)
    grad_middle = cotangent.astype(jnp.float32) + middle_part
    middle_all = lax.all_gather(grad_middle.astype(jnp.bfloat16), "tensor", axis=0, tiled=True)
    out_grad = lax.dot_general(
        middle_all, attended_low, contract_rows, preferred_element_type=jnp.float32
    )
    grad_attended = jnp.dot(middle_all, out_weight, preferred_element_type=jnp.float32).astype(
        jnp.bfloat16
    )
    grad_query_low, grad_key_low, grad_value_low, distance_sums = attend_back(
        query_low, key_low, value_low, grad_attended, probs_low, probs_high
    )
    width = min(distance_sums.shape[1] - 1, bucket_index.shape[0])
    table_hot = bucket_index[None, :width] == jnp.arange(NB, dtype=jnp.int32)[:, None]
    table_grad = jnp.sum(
        jnp.where(table_hot[:, None, :], distance_sums[None, :, 1 : width + 1], 0.0), axis=2
    )
    query_grad = lax.dot_general(
        first_all, grad_query_low, contract_rows, preferred_element_type=jnp.float32
    )
    key_grad = lax.dot_general(
        first_all, grad_key_low, contract_rows, preferred_element_type=jnp.float32
    )
    value_grad = lax.dot_general(
        first_all, grad_value_low, contract_rows, preferred_element_type=jnp.float32
    )
    summed_rows = jnp.zeros(
        (lax.axis_size("tensor") * own_rows, query_weight.shape[0]), jnp.float32
    )
    for grad_low, weight in (
        (grad_query_low, query_weight),
        (grad_key_low, key_weight),
        (grad_value_low, value_weight),
    ):
        picked = grad_low
        summed_rows = summed_rows + lax.dot_general(
            picked, weight, contract_cols, preferred_element_type=jnp.float32
        )
    grad_first = lax.psum_scatter(
        summed_rows.astype(jnp.bfloat16), "tensor", scatter_dimension=0, tiled=True
    ).astype(jnp.float32)
    _, first_back = jax.vjp(normed, inputs, first_gain)
    input_part, first_gain_grad = first_back(grad_first)
    input_grad = grad_middle + input_part
    grads = (query_grad, key_grad, value_grad, out_grad, gate_grad, up_grad, down_grad)
    joined = jnp.concatenate([grad.astype(jnp.bfloat16) for grad in grads], axis=1)
    summed = lax.psum_scatter(joined, "dp", scatter_dimension=0, tiled=True).astype(jnp.float32)
    edges = []
    for grad in grads[:-1]:
        edges.append((edges[-1] if edges else 0) + grad.shape[1])
    query_grad, key_grad, value_grad, out_grad, gate_grad, up_grad, down_grad = jnp.split(
        summed, edges, axis=1
    )
    table_grad = lax.psum(table_grad, "dp")
    first_gain_grad, second_gain_grad = lax.psum(
        (first_gain_grad, second_gain_grad), ("dp", "tensor")
    )
    return (
        layer_out.astype(jnp.bfloat16),
        input_grad.astype(jnp.bfloat16),
        first_gain_grad,
        query_grad,
        key_grad,
        value_grad,
        out_grad,
        table_grad,
        second_gain_grad,
        gate_grad,
        up_grad,
        down_grad,
    )


def solution(mesh):
    return jax.shard_map(
        per_device,
        mesh=mesh,
        in_specs=(
            P(("dp", "tensor"), None),
            P(),
            P(None, "tensor"),
            P(None, "tensor"),
            P(None, "tensor"),
            P(None, "tensor"),
            P(None, "tensor"),
            P(),
            P(None, "tensor"),
            P(None, "tensor"),
            P(None, "tensor"),
            P("dp", None),
            P(),
            P(("dp", "tensor"), None),
        ),
        out_specs=(
            P(("dp", "tensor"), None),
            P(("dp", "tensor"), None),
            P(),
            P("dp", "tensor"),
            P("dp", "tensor"),
            P("dp", "tensor"),
            P("dp", "tensor"),
            P(None, "tensor"),
            P(),
            P("dp", "tensor"),
            P("dp", "tensor"),
            P("dp", "tensor"),
        ),
        check_vma=False,
    )
```

```python
import functools

import jax
import jax.numpy as jnp
from jax import lax
from jax.experimental import pallas as pl
from jax.experimental.pallas import tpu as pltpu
from jax.sharding import PartitionSpec as P

NB = 32
LEN = 1024
QB = 256
PIECE = 256
NPIECE = 2
HALF = LEN // NPIECE
SPAN = 5 * QB
DIST = 2 * LEN

EPSILON = 1e-06
MASKED = -1000000000.0
VMEM_LIMIT = 60 * 1024 * 1024
MESH = pl.DeviceIdType.MESH


def normed(row_block, gain_vec):
    inv_rms = lax.rsqrt(jnp.mean(row_block * row_block, axis=-1, keepdims=True) + EPSILON)
    return row_block * inv_rms * gain_vec


def dot(a, b, dims):
    return lax.dot_general(a, b, (dims, ((), ())), preferred_element_type=jnp.float32)


def key_count(block):
    return HALF if (block + 1) * QB <= HALF else LEN


def toeplitz(bucket_row, table_ref, head):
    row = jnp.zeros(bucket_row.shape, jnp.float32)
    for bucket in range(NB):
        row = jnp.where(bucket_row == bucket, table_ref[bucket, head], row)
    rows = jnp.broadcast_to(row, (QB, DIST))
    return pltpu.roll(rows, DIST - (QB - 1), 1, stride=1, stride_axis=0)[:, :SPAN]


def label_of(position, starts):
    label = jnp.zeros(position.shape, jnp.int32)
    for piece, start in enumerate(starts):
        inside = (position >= start) & (position < start + PIECE)
        label = jnp.where(inside, piece + 1, label)
    return label


def allowed_block(block, starts):
    keys = key_count(block)
    query = block * QB + lax.broadcasted_iota(jnp.int32, (QB, 1), 0)
    key = lax.broadcasted_iota(jnp.int32, (1, keys), 1)
    query_label = label_of(query, starts)
    key_label = label_of(key, starts)
    return (key <= query) | ((query_label == key_label) & (query_label > 0))


def attend_block(block, head_dim, allowed, qkv_ref, bias_ref, low_ref, high_ref):
    keys = key_count(block)
    first = LEN - QB - block * QB
    rows = pl.ds(block * QB, QB)
    outs = []
    for head in range(bias_ref.shape[0]):
        cols = pl.ds(head * head_dim, head_dim)
        raw = dot(qkv_ref[0, rows, cols], qkv_ref[1, pl.ds(0, keys), cols], ((1,), (1,)))
        scores = jnp.where(allowed, raw + bias_ref[head, :, pl.ds(first, keys)], MASKED)
        peak = jnp.max(scores, axis=-1, keepdims=True)
        powered = jnp.exp(scores - peak)
        total = jnp.sum(powered, axis=-1, keepdims=True)
        probs = (powered * (1.0 / total)).astype(jnp.bfloat16)
        if keys == HALF:
            low_ref[head, rows, :] = probs
        else:
            high_ref[head, pl.ds(block * QB - HALF, QB), :] = probs
        outs.append(dot(probs, qkv_ref[2, pl.ds(0, keys), cols], ((1,), (0,))))
    return jnp.concatenate(outs, axis=1).astype(jnp.bfloat16)


def greet(t, nt):
    barrier = pltpu.get_barrier_semaphore()
    for k in range(1, nt):
        pl.semaphore_signal(
            barrier, inc=1, device_id={"tensor": lax.rem(t + k, nt)}, device_id_type=MESH
        )
    return barrier


def line_copy(t, nt, way, step, buf, piece, pieces, send_sem, recv_sem):
    sign = 1 if way == 0 else -1
    origin = jnp.clip(t - sign * step, 0, nt - 1)
    rows = buf.shape[1] // pieces
    part = buf.at[origin, pl.ds(piece * rows, rows)]
    return pltpu.make_async_remote_copy(
        src_ref=part,
        dst_ref=part,
        send_sem=send_sem,
        recv_sem=recv_sem,
        device_id={"tensor": jnp.clip(t + sign, 0, nt - 1)},
        device_id_type=MESH,
    )


def gather_attend_kernel(
    nt, pieces, heads, head_dim,
    x_ref, cot_ref, gain_ref, wq_ref, wk_ref, wv_ref, bucket_ref, table_ref, start_ref,
    first_out, cot_out, qkv_out, low_out, high_out, own_out, att_out,
    first, qkv, low, high, bias, att,
    send_sem, recv_sem, swap_send, swap_recv, local_sem,
):
    t = lax.axis_index("tensor")
    barrier = greet(t, nt)
    own_cot = pltpu.make_async_copy(cot_ref, cot_out.at[t], local_sem.at[0])
    own_cot.start()
    first[t] = normed(x_ref[...].astype(jnp.float32), gain_ref[...]).astype(jnp.bfloat16)
    pl.semaphore_wait(barrier, nt - 1)

    def copy(way, stage, step, piece):
        buf = first if stage == 0 else cot_out
        return line_copy(
            t, nt, way, step, buf, piece, pieces,
            send_sem.at[way, stage, step, piece], recv_sem.at[way, stage, step, piece],
        )

    def landed(way, stage, step, piece):
        sign = 1 if way == 0 else -1
        buf = first if stage == 0 else cot_out
        rows = buf.shape[1] // pieces
        part = buf.at[jnp.clip(t - sign * step, 0, nt - 1), pl.ds(piece * rows, rows)]
        pltpu.make_async_remote_copy(
            src_ref=part, dst_ref=part,
            send_sem=send_sem.at[way, stage, step - 1, piece],
            recv_sem=recv_sem.at[way, stage, step - 1, piece],
            device_id={"tensor": jnp.clip(t + sign, 0, nt - 1)}, device_id_type=MESH,
        ).wait_recv()

    ways = ((0, t, t < nt - 1), (1, nt - 1 - t, t > 0))

    def tick(k):
        for piece in range(pieces):
            for way, last, onward in ways:
                if k < nt:
                    @pl.when(k <= last)
                    def _():
                        if k > 0:
                            landed(way, 0, k, piece)

                        @pl.when(onward)
                        def _():
                            copy(way, 0, k, piece).start()

                if k > 0:
                    step = k - last - 1

                    @pl.when((step >= 1) & (step <= last))
                    def _():
                        landed(way, 1, step, piece)

                        @pl.when(onward)
                        def _():
                            copy(way, 1, step, piece).start()

                    @pl.when((step == 0) & onward)
                    def _():
                        copy(way, 0, last, piece).wait_send()
                        copy(way, 1, 0, piece).start()

    def project(origin):
        rows = pl.ds(pl.multiple_of(origin * QB, QB), QB)
        for place, weight in enumerate((wq_ref, wk_ref, wv_ref)):
            qkv[place, rows, :] = dot(first[origin], weight[...], ((1,), (1,))).astype(jnp.bfloat16)

    tick(0)
    project(t)
    for head in range(heads):
        bias[head] = toeplitz(bucket_ref[...], table_ref, head)
    own_cot.wait()
    for k in range(1, nt):
        tick(k)

        @pl.when(t - k >= 0)
        def _():
            project(t - k)

        @pl.when(t + k < nt)
        def _():
            project(t + k)

    starts = [start_ref[0, piece] for piece in range(NPIECE)]
    keep = [pltpu.make_async_copy(first, first_out, local_sem.at[1]), pltpu.make_async_copy(qkv, qkv_out, local_sem.at[2])]
    for one in keep:
        one.start()

    def swap(block):
        return pltpu.make_async_remote_copy(
            src_ref=att.at[block], dst_ref=own_out.at[t],
            send_sem=swap_send.at[block], recv_sem=swap_recv.at[t],
            device_id={"tensor": block}, device_id_type=MESH,
        )

    own_att = pltpu.make_async_copy(att.at[t], own_out.at[t], local_sem.at[3])
    for block in range(LEN // QB):
        att[block] = attend_block(block, head_dim, allowed_block(block, starts), qkv, bias, low, high)

        @pl.when(t != block)
        def _():
            swap(block).start()

        @pl.when(t == block)
        def _():
            own_att.start()

    late = [
        pltpu.make_async_copy(low, low_out, local_sem.at[4]),
        pltpu.make_async_copy(high, high_out, local_sem.at[5]),
        pltpu.make_async_copy(att, att_out, local_sem.at[6]),
    ]
    for one in late:
        one.start()
    for k in range(nt, 2 * nt):
        tick(k)
    for block in range(nt):
        @pl.when(t != block)
        def _():
            swap(block).wait_send()
            pltpu.make_async_remote_copy(
                src_ref=att.at[block], dst_ref=own_out.at[block],
                send_sem=swap_send.at[block], recv_sem=swap_recv.at[block],
                device_id={"tensor": block}, device_id_type=MESH,
            ).wait_recv()

    own_att.wait()
    for one in keep + late:
        one.wait()
    for piece in range(pieces):
        for way, last, onward in ways:
            for stage in range(2):
                for step in range(nt):
                    @pl.when(onward & ((step < last) if stage == 0 else (step <= last)))
                    def _():
                        copy(way, stage, step, piece).wait_send()


def gather_attend(nt, tokens, cotangent, gain, weights, bucket_row, table, starts):
    heads = table.shape[1]
    inner = weights[0].shape[0]
    rows, width = tokens.shape
    low = jnp.bfloat16
    pieces = 2
    smem = pl.BlockSpec(memory_space=pltpu.SMEM)
    hbm = pl.BlockSpec(memory_space=pl.ANY)
    vmem = pl.BlockSpec(memory_space=pltpu.VMEM)
    shapes = (
        (nt, rows, width), (nt, rows, width), (3, LEN, inner), (heads, HALF, HALF), (heads, HALF, LEN),
        (nt, rows, inner), (nt, rows, inner),
    )
    dma = pltpu.SemaphoreType.DMA
    return pl.pallas_call(
        functools.partial(gather_attend_kernel, nt, pieces, heads, inner // heads),
        out_shape=tuple(jax.ShapeDtypeStruct(shape, low) for shape in shapes),
        in_specs=[vmem, hbm] + [vmem] * 5 + [smem, smem],
        out_specs=(hbm,) * 7,
        scratch_shapes=[
            pltpu.VMEM((nt, rows, width), low),
            pltpu.VMEM((3, LEN, inner), low),
            pltpu.VMEM((heads, HALF, HALF), low),
            pltpu.VMEM((heads, HALF, LEN), low),
            pltpu.VMEM((heads, QB, SPAN), jnp.float32),
            pltpu.VMEM((nt, rows, inner), low),
            dma((2, 2, nt, pieces)), dma((2, 2, nt, pieces)), dma((nt,)), dma((nt,)), dma((7,)),
        ],
        compiler_params=pltpu.CompilerParams(
            vmem_limit_bytes=VMEM_LIMIT, collective_id=0, has_side_effects=True
        ),
        name="gather_attend",
    )(tokens, cotangent, gain[None, :], *weights, bucket_row, table, starts)


def fold_diagonals(grid):
    rows = QB // 2
    width = grid.shape[1]
    while rows >= 1:
        grid = grid[:rows] + pltpu.roll(grid[rows : 2 * rows], width - rows, 1)
        rows //= 2
    return grid


def gelu_parts(v):
    root, cubic = 0.7978845608028654, 0.044715
    square = v * v
    bend = jnp.tanh(root * v * (1.0 + cubic * square))
    half = 0.5 * (1.0 + bend)
    slope = half + 0.5 * v * (1.0 - bend * bend) * root * (1.0 + 3.0 * cubic * square)
    return v * half, slope


def feed_kernel(
    nt, pieces,
    x_ref, own_ref, wo_ref, gain_ref, cot_own_ref, cot_hbm, wg_hbm, wu_hbm, wd_hbm,
    middle_out, gm_out, gain_out, ga_out, lo_out, grads_out,
    buf, cot, wg, wu, wd, hid, gg, gu, gs, lo, mate_in, acc_in, far_in, middle, grads,
    send_sem, recv_sem, rs_send, rs_recv, local_sem,
):
    t = lax.axis_index("tensor")
    barrier = greet(t, nt)
    loads = [
        pltpu.make_async_copy(a, b, local_sem.at[i])
        for i, (a, b) in enumerate(((wg_hbm, wg), (wu_hbm, wu), (wd_hbm, wd), (cot_hbm, cot)))
    ]
    for one in loads:
        one.start()
    row_count = x_ref.shape[0]
    size = row_count // pieces
    total = x_ref[...].astype(jnp.float32)
    for j in range(nt):
        total = total + dot(own_ref[j], wo_ref[j], ((1,), (0,)))
    middle[...] = total
    buf[t] = normed(total, gain_ref[...]).astype(jnp.bfloat16)
    keep = [pltpu.make_async_copy(middle, middle_out, local_sem.at[4])]
    keep[0].start()
    pl.semaphore_wait(barrier, nt - 1)
    mate = t + 1 - 2 * lax.rem(t, 2)
    is_end = (t == 0) | (t == nt - 1)
    ways = ((0, t, t < nt - 1), (1, nt - 1 - t, t > 0))

    def copy(way, step, piece):
        return line_copy(
            t, nt, way, step, buf, piece, pieces,
            send_sem.at[way, step, piece], recv_sem.at[way, step, piece],
        )

    def landed(way, step, piece):
        sign = 1 if way == 0 else -1
        part = buf.at[jnp.clip(t - sign * step, 0, nt - 1), pl.ds(piece * size, size)]
        pltpu.make_async_remote_copy(
            src_ref=part, dst_ref=part,
            send_sem=send_sem.at[way, step - 1, piece], recv_sem=recv_sem.at[way, step - 1, piece],
            device_id={"tensor": jnp.clip(t + sign, 0, nt - 1)}, device_id_type=MESH,
        ).wait_recv()

    def remote(src, dst, target, send, recv):
        return pltpu.make_async_remote_copy(
            src_ref=src, dst_ref=dst, send_sem=send, recv_sem=recv,
            device_id={"tensor": target}, device_id_type=MESH,
        )

    def to_mate(piece):
        rows = pl.ds(piece * size, size)
        return remote(gs.at[mate, rows], mate_in.at[rows], mate, rs_send.at[0, piece], rs_recv.at[0, piece])

    def to_acc(origin, piece):
        rows = pl.ds(piece * size, size)
        j = lax.rem(origin, 2)
        return remote(
            gs.at[origin, rows], acc_in.at[j, rows], mate, rs_send.at[1 + j, piece], rs_recv.at[1 + j, piece]
        )

    def to_far(origin, piece):
        rows = pl.ds(piece * size, size)
        j = lax.rem(origin, 2)
        return remote(
            gs.at[origin, rows], far_in.at[rows], origin, rs_send.at[3 + j, piece], rs_recv.at[3, piece]
        )

    def feed(origin, piece):
        rows = pl.ds(pl.multiple_of(piece * size, size), size)
        flat = pl.ds(pl.multiple_of(origin * row_count + piece * size, size), size)
        normal = buf[origin, rows]
        gate = dot(normal, wg[...], ((1,), (1,)))
        up = dot(normal, wu[...], ((1,), (1,)))
        grad_hidden = dot(cot[origin, rows], wd[...], ((1,), (1,)))
        act, slope = gelu_parts(gate)
        hid[flat, :] = (act * up).astype(jnp.bfloat16)
        grad_gate = (grad_hidden * up * slope).astype(jnp.bfloat16)
        grad_up = (grad_hidden * act).astype(jnp.bfloat16)
        gg[flat, :] = grad_gate
        gu[flat, :] = grad_up
        gs[origin, rows] = (
            dot(grad_gate, wg[...], ((1,), (0,))) + dot(grad_up, wu[...], ((1,), (0,)))
        ).astype(jnp.bfloat16)

    for piece in range(pieces):
        for way, last, onward in ways:
            @pl.when(onward)
            def _():
                copy(way, 0, piece).start()

    for one in loads:
        one.wait()

    def unit(u, carry):
        step = u // pieces
        piece = lax.rem(u, pieces)

        @pl.when(step > 0)
        def _():
            for way, last, onward in ways:
                @pl.when(step <= last)
                def _():
                    landed(way, step, piece)

                    @pl.when(onward)
                    def _():
                        copy(way, step, piece).start()

        def side(way, carry):
            origin = t - (1 - 2 * way) * step
            there = (origin >= 0) & (origin < nt) & ((step > 0) | (way == 0))

            @pl.when(there)
            def _():
                feed(origin, piece)

                @pl.when(origin == mate)
                def _():
                    to_mate(piece).start()

                @pl.when((origin != mate) & (origin != t) & is_end)
                def _():
                    to_acc(origin, piece).start()

            return carry

        return lax.fori_loop(0, 2, side, carry)

    lax.fori_loop(0, nt * pieces, unit, 0)

    near = jnp.where(t < nt // 2, nt // 2, nt // 2 - 1)
    far = jnp.where(t < nt // 2, nt - 1, 0)

    def pass_on(origin, piece):
        @pl.when(jnp.logical_not(is_end))
        def _():
            to_acc(origin, piece).wait_recv()
            rows = pl.ds(piece * size, size)
            j = lax.rem(origin, 2)
            gs[origin, rows] = (
                gs[origin, rows].astype(jnp.float32) + acc_in[j, rows].astype(jnp.float32)
            ).astype(jnp.bfloat16)
            to_far(origin, piece).start()

    span = 256
    flat_rows = nt * row_count
    spans = buf.shape[2] // span

    def columns(ref, i):
        cols = pl.ds(pl.multiple_of(i * span, span), span)
        return ref[:, :, cols].reshape(flat_rows, span)

    def down_cols(i, carry):
        rows = pl.ds(pl.multiple_of(i * span, span), span)
        grads[2, rows, :] = dot(columns(cot, i), hid[...], ((0,), (0,))).astype(jnp.bfloat16)
        return carry

    def gate_up_cols(i, carry):
        rows = pl.ds(pl.multiple_of(i * span, span), span)
        left = columns(buf, i)
        grads[0, rows, :] = dot(left, gg[...], ((0,), (0,))).astype(jnp.bfloat16)
        grads[1, rows, :] = dot(left, gu[...], ((0,), (0,))).astype(jnp.bfloat16)
        return carry

    def down_rows(i, carry):
        rows = pl.ds(pl.multiple_of(i * row_count, row_count), row_count)
        lo[i] = dot(hid[rows, :], wd[...], ((1,), (0,))).astype(jnp.bfloat16)
        return carry

    pass_on(near, 0)
    lax.fori_loop(0, spans, down_cols, 0)
    pass_on(near, 1)
    lax.fori_loop(0, nt, down_rows, 0)
    keep.append(pltpu.make_async_copy(lo, lo_out, local_sem.at[5]))
    keep[-1].start()
    pass_on(far, 0)
    lax.fori_loop(0, spans // 2, gate_up_cols, 0)
    pass_on(far, 1)
    lax.fori_loop(spans // 2, spans, gate_up_cols, 0)
    keep.append(pltpu.make_async_copy(grads, grads_out, local_sem.at[6]))
    keep[-1].start()

    for piece in range(pieces):
        rows = pl.ds(piece * size, size)
        to_mate(piece).wait_recv()
        remote(gs.at[t, rows], far_in.at[rows], mate, rs_send.at[3, piece], rs_recv.at[3, piece]).wait_recv()
        grad_second = (
            gs[t, rows].astype(jnp.float32)
            + mate_in[rows].astype(jnp.float32)
            + far_in[rows].astype(jnp.float32)
        )
        mid = middle[rows]
        inv = lax.rsqrt(jnp.mean(mid * mid, axis=-1, keepdims=True) + EPSILON)
        scaled = gain_ref[...] * grad_second
        along = jnp.mean(scaled * mid, axis=-1, keepdims=True)
        grad_middle = cot_own_ref[rows].astype(jnp.float32) + inv * scaled - mid * (inv * inv * inv * along)
        gm_out[rows] = grad_middle
        part = jnp.sum(grad_second * mid * inv, axis=0, keepdims=True)
        if piece == 0:
            gain_out[...] = part
        else:
            gain_out[...] += part
        grad_low = grad_middle.astype(jnp.bfloat16)
        for j in range(nt):
            ga_out[j, rows] = dot(grad_low, wo_ref[j], ((1,), (1,))).astype(jnp.bfloat16)

    for one in keep:
        one.wait()
    for piece in range(pieces):
        for way, last, onward in ways:
            for step in range(nt):
                @pl.when(onward & (step <= last))
                def _():
                    copy(way, step, piece).wait_send()

        to_mate(piece).wait_send()
        for origin in (near, far):
            @pl.when(is_end)
            def _():
                to_acc(origin, piece).wait_send()

            @pl.when(jnp.logical_not(is_end))
            def _():
                to_far(origin, piece).wait_send()


def feed(nt, tokens, attended, out_all, gain, cotangent, cot_all, gate_weight, up_weight, down_weight):
    rows, width = tokens.shape
    hidden = gate_weight.shape[0]
    low, full = jnp.bfloat16, jnp.float32
    pieces = 2
    hbm = pl.BlockSpec(memory_space=pl.ANY)
    vmem = pl.BlockSpec(memory_space=pltpu.VMEM)
    inner = attended.shape[2]
    dma = pltpu.SemaphoreType.DMA
    shape = jax.ShapeDtypeStruct
    return pl.pallas_call(
        functools.partial(feed_kernel, nt, pieces),
        out_shape=(
            shape((rows, width), full), shape((rows, width), full), shape((1, width), full),
            shape((nt, rows, inner), low), shape((nt, rows, width), low), shape((3, width, hidden), low),
        ),
        in_specs=[vmem] * 5 + [hbm] * 4,
        out_specs=(hbm, vmem, vmem, vmem, hbm, hbm),
        scratch_shapes=[
            pltpu.VMEM((nt, rows, width), low), pltpu.VMEM((nt, rows, width), low),
            pltpu.VMEM((hidden, width), low), pltpu.VMEM((hidden, width), low), pltpu.VMEM((hidden, width), low),
            pltpu.VMEM((nt * rows, hidden), low), pltpu.VMEM((nt * rows, hidden), low), pltpu.VMEM((nt * rows, hidden), low),
            pltpu.VMEM((nt, rows, width), low), pltpu.VMEM((nt, rows, width), low),
            pltpu.VMEM((rows, width), low), pltpu.VMEM((2, rows, width), low), pltpu.VMEM((rows, width), low),
            pltpu.VMEM((rows, width), full), pltpu.VMEM((3, width, hidden), low),
            dma((2, nt, pieces)), dma((2, nt, pieces)), dma((5, pieces)), dma((4, pieces)), dma((7,)),
        ],
        compiler_params=pltpu.CompilerParams(
            vmem_limit_bytes=VMEM_LIMIT, collective_id=1, has_side_effects=True
        ),
        name="feed",
    )(tokens, attended, out_all, gain[None, :], cotangent, cot_all, gate_weight, up_weight, down_weight)


def attend_back_kernel(heads, head_dim, q_ref, k_ref, v_ref, do_ref, low_ref, high_ref, dq_ref, dk_ref, dv_ref, dist_ref, diag_ref, dk_acc, dv_acc):
    blocks = LEN // QB
    for head in range(heads):
        cols = pl.ds(head * head_dim, head_dim)
        diag_ref[...] = jnp.zeros_like(diag_ref)
        for block in reversed(range(blocks)):
            keys = key_count(block)
            rows = pl.ds(block * QB, QB)
            first = LEN - block * QB
            if keys == HALF:
                probs_low = low_ref[head, rows, :]
            else:
                probs_low = high_ref[head, pl.ds(block * QB - HALF, QB), :]
            probs = probs_low.astype(jnp.float32)
            do = do_ref[rows, cols]
            grad_probs = dot(do, v_ref[pl.ds(0, keys), cols], ((1,), (1,)))
            weighted = jnp.sum(probs * grad_probs, axis=-1, keepdims=True)
            grad_low = (probs * (grad_probs - weighted)).astype(jnp.bfloat16)
            span = pl.ds(first, keys)
            diag_ref[:, span] = diag_ref[:, span] + grad_low.astype(jnp.float32)
            dq_ref[rows, cols] = dot(grad_low, k_ref[pl.ds(0, keys), cols], ((1,), (0,))).astype(
                jnp.bfloat16
            )
            key_part = dot(grad_low, q_ref[rows, cols], ((0,), (0,)))
            value_part = dot(probs_low, do, ((0,), (0,)))
            if block == blocks - 1:
                dk_acc[...] = key_part
                dv_acc[...] = value_part
            else:
                dk_acc[pl.ds(0, keys), :] += key_part
                dv_acc[pl.ds(0, keys), :] += value_part
        dk_ref[:, cols] = dk_acc[...].astype(jnp.bfloat16)
        dv_ref[:, cols] = dv_acc[...].astype(jnp.bfloat16)
        dist_ref[pl.ds(head, 1), :] = fold_diagonals(diag_ref[...])


def whole_vmem(count):
    return [pl.BlockSpec(memory_space=pltpu.VMEM)] * count


def attend_back(query, key, value, grad_attended, low, high):
    heads = low.shape[0]
    inner = query.shape[1]
    shape = jax.ShapeDtypeStruct(query.shape, jnp.bfloat16)
    return pl.pallas_call(
        functools.partial(attend_back_kernel, heads, inner // heads),
        out_shape=(shape, shape, shape, jax.ShapeDtypeStruct((heads, SPAN + QB), jnp.float32)),
        in_specs=whole_vmem(6),
        out_specs=tuple(whole_vmem(4)),
        scratch_shapes=[
            pltpu.VMEM((QB, SPAN + QB), jnp.float32),
            pltpu.VMEM((LEN, inner // heads), jnp.float32),
            pltpu.VMEM((LEN, inner // heads), jnp.float32),
        ],
        compiler_params=pltpu.CompilerParams(vmem_limit_bytes=VMEM_LIMIT),
        name="attend_back",
    )(query, key, value, grad_attended, low, high)


def per_device(
    tokens,
    first_gain,
    query_weight,
    key_weight,
    value_weight,
    out_weight,
    bucket_table,
    second_gain,
    gate_weight,
    up_weight,
    down_weight,
    piece_start,
    bucket_index,
    cotangent,
):
    own_rows = tokens.shape[0]
    contract_cols = (((1,), (1,)), ((), ()))
    contract_rows = (((0,), (0,)), ((), ()))
    bucket_row = jnp.pad(bucket_index, (0, 1))[None, :]
    inputs = tokens.astype(jnp.float32)
    nt = lax.axis_size("tensor")
    first_all, grad_all, qkv, probs_low, probs_high, attended_own, attended_heads = gather_attend(
        nt, tokens, cotangent, first_gain, (query_weight.T, key_weight.T, value_weight.T),
        bucket_row, bucket_table, piece_start,
    )
    first_all = first_all.reshape(-1, tokens.shape[1])
    attended_low = attended_heads.reshape(-1, query_weight.shape[1])
    query_low, key_low, value_low = qkv[0], qkv[1], qkv[2]
    out_cols = out_weight.T
    own_part = out_cols.shape[0] // lax.axis_size("dp")
    out_all = lax.all_gather(
        lax.dynamic_slice_in_dim(out_cols, lax.axis_index("dp") * own_part, own_part, 0),
        ("tensor", "dp"), axis=0, tiled=True,
    ).reshape(nt, *out_cols.shape)
    middle, grad_middle, second_gain_grad, grad_attended_own, layer_parts, feed_grads = feed(
        nt, tokens, attended_own, out_all, second_gain, cotangent, grad_all,
        gate_weight.T, up_weight.T, down_weight.T,
    )
    second_gain_grad = second_gain_grad[0]
    layer_out = middle + lax.psum_scatter(
        layer_parts.reshape(-1, tokens.shape[1]), "tensor", scatter_dimension=0, tiled=True
    ).astype(jnp.float32)
    gate_grad, up_grad, down_grad = feed_grads[0], feed_grads[1], feed_grads[2]
    middle_all = lax.all_gather(grad_middle.astype(jnp.bfloat16), "tensor", axis=0, tiled=True)
    out_grad = lax.dot_general(
        middle_all, attended_low, contract_rows, preferred_element_type=jnp.float32
    )
    grad_attended = lax.all_to_all(
        grad_attended_own, "tensor", split_axis=0, concat_axis=0, tiled=True
    ).reshape(-1, query_weight.shape[1])
    grad_query_low, grad_key_low, grad_value_low, distance_sums = attend_back(
        query_low, key_low, value_low, grad_attended, probs_low, probs_high
    )
    width = min(distance_sums.shape[1] - 1, bucket_index.shape[0])
    table_hot = bucket_index[None, :width] == jnp.arange(NB, dtype=jnp.int32)[:, None]
    table_grad = jnp.sum(
        jnp.where(table_hot[:, None, :], distance_sums[None, :, 1 : width + 1], 0.0), axis=2
    )
    query_grad = lax.dot_general(
        first_all, grad_query_low, contract_rows, preferred_element_type=jnp.float32
    )
    key_grad = lax.dot_general(
        first_all, grad_key_low, contract_rows, preferred_element_type=jnp.float32
    )
    value_grad = lax.dot_general(
        first_all, grad_value_low, contract_rows, preferred_element_type=jnp.float32
    )
    summed_rows = jnp.zeros(
        (lax.axis_size("tensor") * own_rows, query_weight.shape[0]), jnp.float32
    )
    for grad_low, weight in (
        (grad_query_low, query_weight),
        (grad_key_low, key_weight),
        (grad_value_low, value_weight),
    ):
        picked = grad_low
        summed_rows = summed_rows + lax.dot_general(
            picked, weight, contract_cols, preferred_element_type=jnp.float32
        )
    grad_first = lax.psum_scatter(
        summed_rows.astype(jnp.bfloat16), "tensor", scatter_dimension=0, tiled=True
    ).astype(jnp.float32)
    _, first_back = jax.vjp(normed, inputs, first_gain)
    input_part, first_gain_grad = first_back(grad_first)
    input_grad = grad_middle + input_part
    grads = (query_grad, key_grad, value_grad, out_grad, gate_grad, up_grad, down_grad)
    joined = jnp.concatenate([grad.astype(jnp.bfloat16) for grad in grads], axis=1)
    summed = lax.psum_scatter(joined, "dp", scatter_dimension=0, tiled=True).astype(jnp.float32)
    edges = []
    for grad in grads[:-1]:
        edges.append((edges[-1] if edges else 0) + grad.shape[1])
    query_grad, key_grad, value_grad, out_grad, gate_grad, up_grad, down_grad = jnp.split(
        summed, edges, axis=1
    )
    table_grad = lax.psum(table_grad, "dp")
    first_gain_grad, second_gain_grad = lax.psum(
        (first_gain_grad, second_gain_grad), ("dp", "tensor")
    )
    return (
        layer_out.astype(jnp.bfloat16),
        input_grad.astype(jnp.bfloat16),
        first_gain_grad,
        query_grad,
        key_grad,
        value_grad,
        out_grad,
        table_grad,
        second_gain_grad,
        gate_grad,
        up_grad,
        down_grad,
    )


def solution(mesh):
    return jax.shard_map(
        per_device,
        mesh=mesh,
        in_specs=(
            P(("dp", "tensor"), None),
            P(),
            P(None, "tensor"),
            P(None, "tensor"),
            P(None, "tensor"),
            P(None, "tensor"),
            P(None, "tensor"),
            P(),
            P(None, "tensor"),
            P(None, "tensor"),
            P(None, "tensor"),
            P("dp", None),
            P(),
            P(("dp", "tensor"), None),
        ),
        out_specs=(
            P(("dp", "tensor"), None),
            P(("dp", "tensor"), None),
            P(),
            P("dp", "tensor"),
            P("dp", "tensor"),
            P("dp", "tensor"),
            P("dp", "tensor"),
            P(None, "tensor"),
            P(),
            P("dp", "tensor"),
            P("dp", "tensor"),
            P("dp", "tensor"),
        ),
        check_vma=False,
    )
```

```python
import functools

import jax
import jax.numpy as jnp
from jax import lax
from jax.experimental import pallas as pl
from jax.experimental.pallas import tpu as pltpu
from jax.sharding import PartitionSpec as P

NB = 32
LEN = 1024
QB = 256
PIECE = 256
NPIECE = 2
HALF = LEN // NPIECE
SPAN = 5 * QB
DIST = 2 * LEN

EPSILON = 1e-06
MASKED = -1000000000.0
HIGHEST = lax.Precision.HIGHEST
VMEM_LIMIT = 60 * 1024 * 1024
MESH = pl.DeviceIdType.MESH


def normed(row_block, gain_vec):
    inv_rms = lax.rsqrt(jnp.mean(row_block * row_block, axis=-1, keepdims=True) + EPSILON)
    return row_block * inv_rms * gain_vec


def dot(a, b, dims):
    return lax.dot_general(a, b, (dims, ((), ())), preferred_element_type=jnp.float32)


def key_count(block):
    return HALF if (block + 1) * QB <= HALF else LEN


def toeplitz(bucket_row, table_ref, head):
    row = jnp.zeros(bucket_row.shape, jnp.float32)
    for bucket in range(NB):
        row = jnp.where(bucket_row == bucket, table_ref[bucket, head], row)
    rows = jnp.broadcast_to(row, (QB, DIST))
    return pltpu.roll(rows, DIST - (QB - 1), 1, stride=1, stride_axis=0)[:, :SPAN]


def label_of(position, starts):
    label = jnp.zeros(position.shape, jnp.int32)
    for piece, start in enumerate(starts):
        inside = (position >= start) & (position < start + PIECE)
        label = jnp.where(inside, piece + 1, label)
    return label


def allowed_block(block, starts):
    keys = key_count(block)
    query = block * QB + lax.broadcasted_iota(jnp.int32, (QB, 1), 0)
    key = lax.broadcasted_iota(jnp.int32, (1, keys), 1)
    query_label = label_of(query, starts)
    key_label = label_of(key, starts)
    return (key <= query) | ((query_label == key_label) & (query_label > 0))


def attend_block(block, head_dim, allowed, qkv_ref, bias_ref, low_ref, high_ref):
    keys = key_count(block)
    first = LEN - QB - block * QB
    rows = pl.ds(block * QB, QB)
    outs = []
    for head in range(bias_ref.shape[0]):
        cols = pl.ds(head * head_dim, head_dim)
        raw = dot(qkv_ref[0, rows, cols], qkv_ref[1, pl.ds(0, keys), cols], ((1,), (1,)))
        scores = jnp.where(allowed, raw + bias_ref[head, :, pl.ds(first, keys)], MASKED)
        peak = jnp.max(scores, axis=-1, keepdims=True)
        powered = jnp.exp(scores - peak)
        total = jnp.sum(powered, axis=-1, keepdims=True)
        probs = (powered * (1.0 / total)).astype(jnp.bfloat16)
        if keys == HALF:
            low_ref[head, rows, :] = probs
        else:
            high_ref[head, pl.ds(block * QB - HALF, QB), :] = probs
        outs.append(dot(probs, qkv_ref[2, pl.ds(0, keys), cols], ((1,), (0,))))
    return jnp.concatenate(outs, axis=1).astype(jnp.bfloat16)


def greet(t, nt):
    barrier = pltpu.get_barrier_semaphore()
    for k in range(1, nt):
        pl.semaphore_signal(
            barrier, inc=1, device_id={"tensor": lax.rem(t + k, nt)}, device_id_type=MESH
        )
    return barrier


def line_copy(t, nt, way, step, buf, piece, pieces, send_sem, recv_sem):
    sign = 1 if way == 0 else -1
    origin = jnp.clip(t - sign * step, 0, nt - 1)
    rows = buf.shape[1] // pieces
    part = buf.at[origin, pl.ds(piece * rows, rows)]
    return pltpu.make_async_remote_copy(
        src_ref=part,
        dst_ref=part,
        send_sem=send_sem,
        recv_sem=recv_sem,
        device_id={"tensor": jnp.clip(t + sign, 0, nt - 1)},
        device_id_type=MESH,
    )


def gather_attend_kernel(
    nt, pieces, heads, head_dim,
    x_ref, cot_ref, gain_ref, wq_ref, wk_ref, wv_ref, bucket_ref, table_ref, start_ref,
    first_out, cot_out, qkv_out, low_out, high_out, own_out,
    first, qkv, low, high, bias, att,
    send_sem, recv_sem, swap_send, swap_recv, local_sem,
):
    t = lax.axis_index("tensor")
    barrier = greet(t, nt)
    own_cot = pltpu.make_async_copy(cot_ref, cot_out.at[t], local_sem.at[0])
    own_cot.start()
    first[t] = normed(x_ref[...].astype(jnp.float32), gain_ref[...]).astype(jnp.bfloat16)
    pl.semaphore_wait(barrier, nt - 1)

    def copy(way, stage, step, piece):
        buf = first if stage == 0 else cot_out
        return line_copy(
            t, nt, way, step, buf, piece, pieces,
            send_sem.at[way, stage, step, piece], recv_sem.at[way, stage, step, piece],
        )

    def landed(way, stage, step, piece):
        sign = 1 if way == 0 else -1
        buf = first if stage == 0 else cot_out
        rows = buf.shape[1] // pieces
        part = buf.at[jnp.clip(t - sign * step, 0, nt - 1), pl.ds(piece * rows, rows)]
        pltpu.make_async_remote_copy(
            src_ref=part, dst_ref=part,
            send_sem=send_sem.at[way, stage, step - 1, piece],
            recv_sem=recv_sem.at[way, stage, step - 1, piece],
            device_id={"tensor": jnp.clip(t + sign, 0, nt - 1)}, device_id_type=MESH,
        ).wait_recv()

    ways = ((0, t, t < nt - 1), (1, nt - 1 - t, t > 0))

    def tick(k):
        for piece in range(pieces):
            for way, last, onward in ways:
                if k < nt:
                    @pl.when(k <= last)
                    def _():
                        if k > 0:
                            landed(way, 0, k, piece)

                        @pl.when(onward)
                        def _():
                            copy(way, 0, k, piece).start()

                if k > 0:
                    step = k - last - 1

                    @pl.when((step >= 1) & (step <= last))
                    def _():
                        landed(way, 1, step, piece)

                        @pl.when(onward)
                        def _():
                            copy(way, 1, step, piece).start()

                    @pl.when((step == 0) & onward)
                    def _():
                        copy(way, 0, last, piece).wait_send()
                        copy(way, 1, 0, piece).start()

    def project(origin):
        rows = pl.ds(pl.multiple_of(origin * QB, QB), QB)
        for place, weight in enumerate((wq_ref, wk_ref, wv_ref)):
            qkv[place, rows, :] = dot(first[origin], weight[...], ((1,), (1,))).astype(jnp.bfloat16)

    tick(0)
    project(t)
    for head in range(heads):
        bias[head] = toeplitz(bucket_ref[...], table_ref, head)
    own_cot.wait()
    for k in range(1, nt):
        tick(k)

        @pl.when(t - k >= 0)
        def _():
            project(t - k)

        @pl.when(t + k < nt)
        def _():
            project(t + k)

    starts = [start_ref[0, piece] for piece in range(NPIECE)]
    keep = [pltpu.make_async_copy(first, first_out, local_sem.at[1]), pltpu.make_async_copy(qkv, qkv_out, local_sem.at[2])]
    for one in keep:
        one.start()

    def swap(block):
        return pltpu.make_async_remote_copy(
            src_ref=att.at[block], dst_ref=own_out.at[t],
            send_sem=swap_send.at[block], recv_sem=swap_recv.at[t],
            device_id={"tensor": block}, device_id_type=MESH,
        )

    own_att = pltpu.make_async_copy(att.at[t], own_out.at[t], local_sem.at[3])
    for block in range(LEN // QB):
        att[block] = attend_block(block, head_dim, allowed_block(block, starts), qkv, bias, low, high)

        @pl.when(t != block)
        def _():
            swap(block).start()

        @pl.when(t == block)
        def _():
            own_att.start()

    late = [
        pltpu.make_async_copy(low, low_out, local_sem.at[4]),
        pltpu.make_async_copy(high, high_out, local_sem.at[5]),
    ]
    for one in late:
        one.start()
    for k in range(nt, 2 * nt):
        tick(k)
    for block in range(nt):
        @pl.when(t != block)
        def _():
            swap(block).wait_send()
            pltpu.make_async_remote_copy(
                src_ref=att.at[block], dst_ref=own_out.at[block],
                send_sem=swap_send.at[block], recv_sem=swap_recv.at[block],
                device_id={"tensor": block}, device_id_type=MESH,
            ).wait_recv()

    own_att.wait()
    for one in keep + late:
        one.wait()
    for piece in range(pieces):
        for way, last, onward in ways:
            for stage in range(2):
                for step in range(nt):
                    @pl.when(onward & ((step < last) if stage == 0 else (step <= last)))
                    def _():
                        copy(way, stage, step, piece).wait_send()


def gather_attend(nt, tokens, cotangent, gain, weights, bucket_row, table, starts):
    heads = table.shape[1]
    inner = weights[0].shape[0]
    rows, width = tokens.shape
    low = jnp.bfloat16
    pieces = 2
    smem = pl.BlockSpec(memory_space=pltpu.SMEM)
    hbm = pl.BlockSpec(memory_space=pl.ANY)
    vmem = pl.BlockSpec(memory_space=pltpu.VMEM)
    shapes = (
        (nt, rows, width), (nt, rows, width), (3, LEN, inner), (heads, HALF, HALF), (heads, HALF, LEN),
        (nt, rows, inner),
    )
    dma = pltpu.SemaphoreType.DMA
    return pl.pallas_call(
        functools.partial(gather_attend_kernel, nt, pieces, heads, inner // heads),
        out_shape=tuple(jax.ShapeDtypeStruct(shape, low) for shape in shapes),
        in_specs=[vmem, hbm] + [vmem] * 5 + [smem, smem],
        out_specs=(hbm,) * 6,
        scratch_shapes=[
            pltpu.VMEM((nt, rows, width), low),
            pltpu.VMEM((3, LEN, inner), low),
            pltpu.VMEM((heads, HALF, HALF), low),
            pltpu.VMEM((heads, HALF, LEN), low),
            pltpu.VMEM((heads, QB, SPAN), jnp.float32),
            pltpu.VMEM((nt, rows, inner), low),
            dma((2, 2, nt, pieces)), dma((2, 2, nt, pieces)), dma((nt,)), dma((nt,)), dma((6,)),
        ],
        compiler_params=pltpu.CompilerParams(
            vmem_limit_bytes=VMEM_LIMIT, collective_id=0, has_side_effects=True
        ),
        name="gather_attend",
    )(tokens, cotangent, gain[None, :], *weights, bucket_row, table, starts)


def fold_diagonals(grid):
    rows = QB // 2
    width = grid.shape[1]
    while rows >= 1:
        grid = grid[:rows] + pltpu.roll(grid[rows : 2 * rows], width - rows, 1)
        rows //= 2
    return grid


def gelu_parts(v):
    root, cubic = 0.7978845608028654, 0.044715
    square = v * v
    bend = jnp.tanh(root * v * (1.0 + cubic * square))
    half = 0.5 * (1.0 + bend)
    slope = half + 0.5 * v * (1.0 - bend * bend) * root * (1.0 + 3.0 * cubic * square)
    return v * half, slope


def feed_kernel(
    nt, pieces,
    x_ref, own_ref, wo_ref, gain_ref, cot_own_ref, cot_hbm, wg_hbm, wu_hbm, wd_hbm,
    base_out, gm_out, gain_out, ga_out, lo_out, grads_out,
    buf, cot, wg, wu, wd, hid, gg, gu, gs, lo, mate_in, acc_in, far_in, middle, grads, mate_lo,
    send_sem, recv_sem, rs_send, rs_recv, lo_sem, local_sem,
):
    t = lax.axis_index("tensor")
    barrier = greet(t, nt)
    loads = [
        pltpu.make_async_copy(a, b, local_sem.at[i])
        for i, (a, b) in enumerate(((wg_hbm, wg), (wu_hbm, wu), (wd_hbm, wd), (cot_hbm, cot)))
    ]
    for one in loads:
        one.start()
    row_count = x_ref.shape[0]
    size = row_count // pieces
    total = x_ref[...].astype(jnp.float32)
    for j in range(nt):
        total = total + dot(own_ref[j], wo_ref[j], ((1,), (0,)))
    middle[...] = total
    buf[t] = normed(total, gain_ref[...]).astype(jnp.bfloat16)
    keep = []
    pl.semaphore_wait(barrier, nt - 1)
    mate = t + 1 - 2 * lax.rem(t, 2)
    is_end = (t == 0) | (t == nt - 1)
    ways = ((0, t, t < nt - 1), (1, nt - 1 - t, t > 0))

    def copy(way, step, piece):
        return line_copy(
            t, nt, way, step, buf, piece, pieces,
            send_sem.at[way, step, piece], recv_sem.at[way, step, piece],
        )

    def landed(way, step, piece):
        sign = 1 if way == 0 else -1
        part = buf.at[jnp.clip(t - sign * step, 0, nt - 1), pl.ds(piece * size, size)]
        pltpu.make_async_remote_copy(
            src_ref=part, dst_ref=part,
            send_sem=send_sem.at[way, step - 1, piece], recv_sem=recv_sem.at[way, step - 1, piece],
            device_id={"tensor": jnp.clip(t + sign, 0, nt - 1)}, device_id_type=MESH,
        ).wait_recv()

    def remote(src, dst, target, send, recv):
        return pltpu.make_async_remote_copy(
            src_ref=src, dst_ref=dst, send_sem=send, recv_sem=recv,
            device_id={"tensor": target}, device_id_type=MESH,
        )

    def to_mate(piece):
        rows = pl.ds(piece * size, size)
        return remote(gs.at[mate, rows], mate_in.at[rows], mate, rs_send.at[0, piece], rs_recv.at[0, piece])

    def to_acc(origin, piece):
        rows = pl.ds(piece * size, size)
        j = lax.rem(origin, 2)
        return remote(
            gs.at[origin, rows], acc_in.at[j, rows], mate, rs_send.at[1 + j, piece], rs_recv.at[1 + j, piece]
        )

    def to_far(origin, piece):
        rows = pl.ds(piece * size, size)
        j = lax.rem(origin, 2)
        return remote(
            gs.at[origin, rows], far_in.at[rows], origin, rs_send.at[3 + j, piece], rs_recv.at[3, piece]
        )

    def feed(origin, piece):
        rows = pl.ds(pl.multiple_of(piece * size, size), size)
        flat = pl.ds(pl.multiple_of(origin * row_count + piece * size, size), size)
        normal = buf[origin, rows]
        gate = dot(normal, wg[...], ((1,), (1,)))
        up = dot(normal, wu[...], ((1,), (1,)))
        grad_hidden = dot(cot[origin, rows], wd[...], ((1,), (1,)))
        act, slope = gelu_parts(gate)
        hid[flat, :] = (act * up).astype(jnp.bfloat16)
        grad_gate = (grad_hidden * up * slope).astype(jnp.bfloat16)
        grad_up = (grad_hidden * act).astype(jnp.bfloat16)
        gg[flat, :] = grad_gate
        gu[flat, :] = grad_up
        gs[origin, rows] = (
            dot(grad_gate, wg[...], ((1,), (0,))) + dot(grad_up, wu[...], ((1,), (0,)))
        ).astype(jnp.bfloat16)

    for piece in range(pieces):
        for way, last, onward in ways:
            @pl.when(onward)
            def _():
                copy(way, 0, piece).start()

    for one in loads:
        one.wait()

    def unit(u, carry):
        step = u // pieces
        piece = lax.rem(u, pieces)

        @pl.when(step > 0)
        def _():
            for way, last, onward in ways:
                @pl.when(step <= last)
                def _():
                    landed(way, step, piece)

                    @pl.when(onward)
                    def _():
                        copy(way, step, piece).start()

        def side(way, carry):
            origin = t - (1 - 2 * way) * step
            there = (origin >= 0) & (origin < nt) & ((step > 0) | (way == 0))

            @pl.when(there)
            def _():
                feed(origin, piece)

                @pl.when(origin == mate)
                def _():
                    to_mate(piece).start()

                @pl.when((origin != mate) & (origin != t) & is_end)
                def _():
                    to_acc(origin, piece).start()

            return carry

        return lax.fori_loop(0, 2, side, carry)

    lax.fori_loop(0, nt * pieces, unit, 0)

    near = jnp.where(t < nt // 2, nt // 2, nt // 2 - 1)
    far = jnp.where(t < nt // 2, nt - 1, 0)

    def pass_on(origin, piece):
        @pl.when(jnp.logical_not(is_end))
        def _():
            to_acc(origin, piece).wait_recv()
            rows = pl.ds(piece * size, size)
            j = lax.rem(origin, 2)
            gs[origin, rows] = (
                gs[origin, rows].astype(jnp.float32) + acc_in[j, rows].astype(jnp.float32)
            ).astype(jnp.bfloat16)
            to_far(origin, piece).start()

    span = 256
    flat_rows = nt * row_count
    spans = buf.shape[2] // span

    def columns(ref, i):
        cols = pl.ds(pl.multiple_of(i * span, span), span)
        return ref[:, :, cols].reshape(flat_rows, span)

    def down_cols(i, carry):
        rows = pl.ds(pl.multiple_of(i * span, span), span)
        grads[2, rows, :] = dot(columns(cot, i), hid[...], ((0,), (0,))).astype(jnp.bfloat16)
        return carry

    def gate_up_cols(i, carry):
        rows = pl.ds(pl.multiple_of(i * span, span), span)
        left = columns(buf, i)
        grads[0, rows, :] = dot(left, gg[...], ((0,), (0,))).astype(jnp.bfloat16)
        grads[1, rows, :] = dot(left, gu[...], ((0,), (0,))).astype(jnp.bfloat16)
        return carry

    def down_rows(i, carry):
        rows = pl.ds(pl.multiple_of(i * row_count, row_count), row_count)
        lo[i] = dot(hid[rows, :], wd[...], ((1,), (0,))).astype(jnp.bfloat16)
        return carry

    pass_on(near, 0)
    lax.fori_loop(0, spans, down_cols, 0)
    pass_on(near, 1)
    lax.fori_loop(0, nt, down_rows, 0)
    keep.append(pltpu.make_async_copy(lo, lo_out, local_sem.at[5]))
    keep[-1].start()
    lo_swap = remote(lo.at[mate], mate_lo, mate, lo_sem.at[0], lo_sem.at[1])
    lo_swap.start()
    pass_on(far, 0)
    lax.fori_loop(0, spans // 2, gate_up_cols, 0)
    pass_on(far, 1)
    lax.fori_loop(spans // 2, spans, gate_up_cols, 0)
    keep.append(pltpu.make_async_copy(grads, grads_out, local_sem.at[6]))
    keep[-1].start()

    for piece in range(pieces):
        rows = pl.ds(piece * size, size)
        to_mate(piece).wait_recv()
        remote(gs.at[t, rows], far_in.at[rows], mate, rs_send.at[3, piece], rs_recv.at[3, piece]).wait_recv()
        grad_second = (
            gs[t, rows].astype(jnp.float32)
            + mate_in[rows].astype(jnp.float32)
            + far_in[rows].astype(jnp.float32)
        )
        mid = middle[rows]
        inv = lax.rsqrt(jnp.mean(mid * mid, axis=-1, keepdims=True) + EPSILON)
        scaled = gain_ref[...] * grad_second
        along = jnp.mean(scaled * mid, axis=-1, keepdims=True)
        grad_middle = cot_own_ref[rows].astype(jnp.float32) + inv * scaled - mid * (inv * inv * inv * along)
        gm_out[rows] = grad_middle
        part = jnp.sum(grad_second * mid * inv, axis=0, keepdims=True)
        if piece == 0:
            gain_out[...] = part
        else:
            gain_out[...] += part
        grad_low = grad_middle.astype(jnp.bfloat16)
        for j in range(nt):
            ga_out[j, rows] = dot(grad_low, wo_ref[j], ((1,), (1,))).astype(jnp.bfloat16)

    lo_swap.wait()
    base_out[...] = middle[...] + lo[t].astype(jnp.float32) + mate_lo[...].astype(jnp.float32)
    for one in keep:
        one.wait()
    for piece in range(pieces):
        for way, last, onward in ways:
            for step in range(nt):
                @pl.when(onward & (step <= last))
                def _():
                    copy(way, step, piece).wait_send()

        to_mate(piece).wait_send()
        for origin in (near, far):
            @pl.when(is_end)
            def _():
                to_acc(origin, piece).wait_send()

            @pl.when(jnp.logical_not(is_end))
            def _():
                to_far(origin, piece).wait_send()


def feed(nt, tokens, attended, out_all, gain, cotangent, cot_all, gate_weight, up_weight, down_weight):
    rows, width = tokens.shape
    hidden = gate_weight.shape[0]
    low, full = jnp.bfloat16, jnp.float32
    pieces = 2
    hbm = pl.BlockSpec(memory_space=pl.ANY)
    vmem = pl.BlockSpec(memory_space=pltpu.VMEM)
    inner = attended.shape[2]
    dma = pltpu.SemaphoreType.DMA
    shape = jax.ShapeDtypeStruct
    return pl.pallas_call(
        functools.partial(feed_kernel, nt, pieces),
        out_shape=(
            shape((rows, width), full), shape((rows, width), full), shape((1, width), full),
            shape((nt, rows, inner), low), shape((nt, rows, width), low), shape((3, width, hidden), low),
        ),
        in_specs=[vmem] * 5 + [hbm] * 4,
        out_specs=(vmem, vmem, vmem, vmem, hbm, hbm),
        scratch_shapes=[
            pltpu.VMEM((nt, rows, width), low), pltpu.VMEM((nt, rows, width), low),
            pltpu.VMEM((hidden, width), low), pltpu.VMEM((hidden, width), low), pltpu.VMEM((hidden, width), low),
            pltpu.VMEM((nt * rows, hidden), low), pltpu.VMEM((nt * rows, hidden), low), pltpu.VMEM((nt * rows, hidden), low),
            pltpu.VMEM((nt, rows, width), low), pltpu.VMEM((nt, rows, width), low),
            pltpu.VMEM((rows, width), low), pltpu.VMEM((2, rows, width), low), pltpu.VMEM((rows, width), low),
            pltpu.VMEM((rows, width), full), pltpu.VMEM((3, width, hidden), low), pltpu.VMEM((rows, width), low),
            dma((2, nt, pieces)), dma((2, nt, pieces)), dma((5, pieces)), dma((4, pieces)), dma((2,)), dma((7,)),
        ],
        compiler_params=pltpu.CompilerParams(
            vmem_limit_bytes=VMEM_LIMIT, collective_id=1, has_side_effects=True
        ),
        name="feed",
    )(tokens, attended, out_all, gain[None, :], cotangent, cot_all, gate_weight, up_weight, down_weight)


def back_kernel(
    nt, ndp, pieces, heads, head_dim, grad_type,
    ga_ref, gm_ref, base_ref, x_ref, gain_ref, gain2_ref, own_ref, bucket_ref,
    qkv_hbm, low_hbm, high_hbm, first_hbm, weight_hbm, lo_hbm,
    layer_out, input_out, gain_out, gain2_out, table_out, q_out, k_out, v_out, o_out,
    ga_in, qkv, low, high, first, weight, lo, acc_in, far_in,
    gq, gq_in, diag, dk_acc, dv_acc,
    og, og_sum, og_chip, og_line, og_line_in, pg, pg_sum, pg_chip,
    gains_line, gains_in, dist_in,
    swap_send, swap_recv, back_send, back_recv, lo_send, lo_recv,
    pair_send, pair_recv, chip_send, chip_recv, line_send, line_recv,
    gl_send, gl_recv, gd_send, gd_recv, dist_send, dist_recv, local_sem,
):
    t = lax.axis_index("tensor")
    d = lax.axis_index("dp")
    core = lax.rem(d, 2)
    chip = d // 2
    chips = ndp // 2
    barrier = greet(t, nt)
    for k in range(1, ndp):
        pl.semaphore_signal(
            barrier, inc=1, device_id={"dp": lax.rem(d + k, ndp)}, device_id_type=MESH
        )
    mate = t + 1 - 2 * lax.rem(t, 2)
    is_end = (t == 0) | (t == nt - 1)
    near = jnp.where(t < nt // 2, nt // 2, nt // 2 - 1)
    far = jnp.where(t < nt // 2, nt - 1, 0)
    loads = [
        pltpu.make_async_copy(a, b, local_sem.at[i])
        for i, (a, b) in enumerate(
            ((qkv_hbm, qkv), (low_hbm, low), (high_hbm, high), (first_hbm, first), (weight_hbm, weight),
             (lo_hbm.at[near], lo.at[lax.rem(near, 2)]), (lo_hbm.at[far], lo.at[lax.rem(far, 2)]))
        )
    ]
    for one in loads:
        one.start()
    others = (far, near, mate)
    row_count, width = x_ref.shape
    inner = heads * head_dim
    size = row_count // pieces
    share = width // ndp
    full = jnp.float32

    def remote(src, dst, send, recv, **target):
        return pltpu.make_async_remote_copy(
            src_ref=src, dst_ref=dst, send_sem=send, recv_sem=recv,
            device_id=target, device_id_type=MESH,
        )

    def swap(peer):
        return remote(ga_ref.at[peer], ga_in.at[t], swap_send.at[peer], swap_recv.at[t], tensor=peer)

    def swap_in(peer):
        return remote(ga_ref.at[peer], ga_in.at[peer], swap_send.at[peer], swap_recv.at[peer], tensor=peer)

    def lo_acc(origin, piece):
        rows = pl.ds(piece * size, size)
        j = lax.rem(origin, 2)
        return remote(
            lo.at[j, rows], acc_in.at[j, rows], lo_send.at[j, piece], lo_recv.at[j, piece], tensor=mate
        )

    def lo_far(origin, piece):
        rows = pl.ds(piece * size, size)
        j = lax.rem(origin, 2)
        return remote(
            lo.at[j, rows], far_in.at[rows], lo_send.at[j, piece], lo_recv.at[2, piece], tensor=origin
        )

    def pass_on(origin, piece):
        @pl.when(jnp.logical_not(is_end))
        def _():
            lo_acc(origin, piece).wait_recv()
            rows = pl.ds(piece * size, size)
            j = lax.rem(origin, 2)
            lo[j, rows] = (lo[j, rows].astype(full) + acc_in[j, rows].astype(full)).astype(jnp.bfloat16)
            lo_far(origin, piece).start()

    pl.semaphore_wait(barrier, nt - 1 + ndp - 1)
    for peer in others:
        swap(peer).start()
    ga_in[t] = ga_ref[t]
    loads[5].wait()
    loads[6].wait()

    @pl.when(is_end)
    def _():
        for origin in (far, near):
            for piece in range(pieces):
                lo_acc(origin, piece).start()

    def block_rows(index):
        return pl.ds(pl.multiple_of(index * share, share), share)

    def pair(kind, c):
        grads, landing = ((og, og_sum), (pg, pg_sum))[kind]
        return remote(
            grads.at[block_rows(2 * c + 1 - core)], landing.at[c],
            pair_send.at[kind, c], pair_recv.at[kind, c], dp=d + 1 - 2 * core,
        )

    def chip_copy(kind, k):
        sums, landing = ((og_sum, og_chip), (pg_sum, pg_chip))[kind]
        to = lax.rem(chip + k, chips)
        return remote(
            sums.at[to], landing.at[k - 1], chip_send.at[kind, k - 1], chip_recv.at[kind, k - 1], dp=2 * to + core
        )

    def pair_sum(kind):
        grads, sums = ((og, og_sum), (pg, pg_sum))[kind]
        for c in range(chips):
            pair(kind, c).wait_recv()
            sums[c] = (grads[block_rows(2 * c + core)].astype(full) + sums[c].astype(full)).astype(grad_type)
        for k in range(1, chips):
            chip_copy(kind, k).start()

    def chip_sum(kind):
        sums, landing = ((og_sum, og_chip), (pg_sum, pg_chip))[kind]
        total = sums[chip].astype(full)
        for k in range(1, chips):
            chip_copy(kind, k).wait_recv()
            total = total + landing[k - 1].astype(full)
        return total

    span = 256
    spans = width // span
    own = jnp.concatenate([own_ref[j] for j in range(nt)], axis=1)
    for i in range(spans):
        left = gm_ref[:, pl.ds(i * span, span)].astype(jnp.bfloat16)
        og[pl.ds(i * span, span), :] = dot(left, own, ((0,), (0,))).astype(grad_type)
    for c in range(chips):
        pair(0, c).start()

    for i in range(3):
        loads[i].wait()
    blocks = LEN // QB
    diag[...] = jnp.zeros_like(diag)
    for block in reversed(range(blocks)):
        keys = key_count(block)
        rows = pl.ds(block * QB, QB)
        first_col = LEN - block * QB

        @pl.when(t != block)
        def _():
            swap_in(block).wait_recv()

        parts = []
        for head in range(heads):
            cols = pl.ds(head * head_dim, head_dim)
            if keys == HALF:
                probs_low = low[head, rows, :]
            else:
                probs_low = high[head, pl.ds(block * QB - HALF, QB), :]
            probs = probs_low.astype(full)
            do = ga_in[block, :, cols]
            grad_probs = dot(do, qkv[2, pl.ds(0, keys), cols], ((1,), (1,)))
            weighted = jnp.sum(probs * grad_probs, axis=-1, keepdims=True)
            grad_low = (probs * (grad_probs - weighted)).astype(jnp.bfloat16)
            reach = pl.ds(first_col, keys)
            diag[head, :, reach] = diag[head, :, reach] + grad_low.astype(full)
            parts.append(dot(grad_low, qkv[1, pl.ds(0, keys), cols], ((1,), (0,))))
            key_part = dot(grad_low, qkv[0, rows, cols], ((0,), (0,)))
            value_part = dot(probs_low, do, ((0,), (0,)))
            if block == blocks - 1:
                dk_acc[head] = key_part
                dv_acc[head] = value_part
            else:
                dk_acc[head, pl.ds(0, keys), :] += key_part
                dv_acc[head, pl.ds(0, keys), :] += value_part
        gq[rows, pl.ds(0, inner)] = jnp.concatenate(parts, axis=1).astype(jnp.bfloat16)
        if block == 1:
            pair_sum(0)
    for block in range(blocks):
        rows = pl.ds(block * QB, QB)
        sides = [acc[head, rows, :] for acc in (dk_acc, dv_acc) for head in range(heads)]
        gq[rows, pl.ds(inner, 2 * inner)] = jnp.concatenate(sides, axis=1).astype(jnp.bfloat16)

    def token_rows(peer):
        return pl.ds(pl.multiple_of(peer * row_count, row_count), row_count)

    def give(peer):
        return remote(
            gq.at[token_rows(peer)], gq_in.at[t], back_send.at[peer], back_recv.at[t], tensor=peer
        )

    def taken(peer):
        return remote(
            gq.at[token_rows(peer)], gq_in.at[peer], back_send.at[peer], back_recv.at[peer], tensor=peer
        )

    for peer in others:
        give(peer).start()
    for head in range(heads):
        dist_in[d, pl.ds(head, 1), :] = fold_diagonals(diag[head])

    def dist_copy(k):
        return remote(
            dist_in.at[d], dist_in.at[d], dist_send.at[k - 1], dist_recv.at[d], dp=lax.rem(d + k, ndp)
        )

    for k in range(1, ndp):
        dist_copy(k).start()
    pass_on(far, 0)
    loads[3].wait()
    for i in range(spans):
        cols = pl.ds(i * span, span)
        left = first[:, :, cols].reshape(nt * row_count, span)
        pg[cols, :] = dot(left, gq[...], ((0,), (0,))).astype(grad_type)
    for c in range(chips):
        pair(1, c).start()
    pass_on(far, 1)
    total = chip_sum(0)
    for j in range(nt):
        og_line[j] = total[:, j * inner : (j + 1) * inner].astype(grad_type)

    def line_copy_out(peer):
        return remote(og_line.at[peer], og_line_in.at[t], line_send.at[peer], line_recv.at[t], tensor=peer)

    def line_in(peer):
        return remote(og_line.at[peer], og_line_in.at[peer], line_send.at[peer], line_recv.at[peer], tensor=peer)

    for peer in others:
        line_copy_out(peer).start()
    pair_sum(1)
    pass_on(near, 0)
    pass_on(near, 1)
    loads[4].wait()
    inputs = x_ref[...].astype(full)
    inv = lax.rsqrt(jnp.mean(inputs * inputs, axis=-1, keepdims=True) + EPSILON)
    grad_first = dot(gq[token_rows(t)], weight[t], ((1,), (0,)))
    for peer in (mate, near, far):
        taken(peer).wait_recv()
        grad_first = grad_first + dot(gq_in[peer], weight[peer], ((1,), (0,)))
    scaled = gain_ref[...] * grad_first
    along = jnp.mean(scaled * inputs, axis=-1, keepdims=True)
    gains_line[t, pl.ds(0, 1), :] = jnp.sum(grad_first * inputs * inv, axis=0, keepdims=True)
    gains_line[t, pl.ds(1, 1), :] = gain2_ref[...]

    def gain_copy(peer):
        return remote(gains_line.at[t], gains_line.at[t], gl_send.at[peer], gl_recv.at[t], tensor=peer)

    def gain_landed(peer):
        return remote(gains_line.at[peer], gains_line.at[peer], gl_send.at[peer], gl_recv.at[peer], tensor=peer)

    for peer in others:
        gain_copy(peer).start()
    input_out[...] = (gm_ref[...] + inv * scaled - inputs * (inv * inv * inv * along)).astype(jnp.bfloat16)
    for peer in others:
        gain_landed(peer).wait_recv()
    gains_in[d] = gains_line[0] + gains_line[1] + gains_line[2] + gains_line[3]

    def gains_copy(k):
        return remote(
            gains_in.at[d], gains_in.at[d], gd_send.at[k - 1], gd_recv.at[d], dp=lax.rem(d + k, ndp)
        )

    for k in range(1, ndp):
        gains_copy(k).start()
    total = chip_sum(1)
    q_out[...] = total[:, :inner]
    k_out[...] = total[:, inner : 2 * inner]
    v_out[...] = total[:, 2 * inner :]
    total = og_line[t].astype(full)
    for peer in others:
        line_in(peer).wait_recv()
        total = total + og_line_in[peer].astype(full)
    o_out[...] = total

    def others_of(landing, send, recv):
        for k in range(1, ndp):
            peer = lax.rem(d + k, ndp)
            remote(landing.at[peer], landing.at[peer], send.at[k - 1], recv.at[peer], dp=peer).wait_recv()

    others_of(dist_in, dist_send, dist_recv)
    dist = dist_in[0]
    for k in range(1, ndp):
        dist = dist + dist_in[k]
    reach = dist.shape[1]
    bucket = pltpu.roll(bucket_ref[...], 1, 1)[:, :reach]
    hot = (lax.broadcasted_iota(jnp.int32, (NB, reach), 0) == bucket).astype(full)
    table_out[...] = lax.dot_general(
        dist, hot, (((1,), (1,)), ((), ())), precision=HIGHEST, preferred_element_type=full
    )
    for piece in range(pieces):
        rows = pl.ds(piece * size, size)
        remote(lo.at[0, rows], far_in.at[rows], lo_send.at[0, piece], lo_recv.at[2, piece], tensor=mate).wait_recv()
        layer_out[rows] = (base_ref[rows] + far_in[rows].astype(full)).astype(jnp.bfloat16)
    others_of(gains_in, gd_send, gd_recv)
    total = gains_in[0]
    for k in range(1, ndp):
        total = total + gains_in[k]
    gain_out[...] = total[0:1]
    gain2_out[...] = total[1:2]

    for peer in others:
        swap(peer).wait_send()
        give(peer).wait_send()
        line_copy_out(peer).wait_send()
        gain_copy(peer).wait_send()
    for origin in (near, far):
        for piece in range(pieces):
            lo_acc(origin, piece).wait_send()
    for kind in range(2):
        for c in range(chips):
            pair(kind, c).wait_send()
        for k in range(1, chips):
            chip_copy(kind, k).wait_send()
    for k in range(1, ndp):
        dist_copy(k).wait_send()
        gains_copy(k).wait_send()


def back(nt, ndp, grad_attended, grad_middle, base, tokens, gain, gain2_part, attended, bucket_row, qkv, probs_low, probs_high, first_all, weights, layer_parts):
    rows, width = tokens.shape
    heads = probs_low.shape[0]
    inner = qkv.shape[2]
    head_dim = inner // heads
    low, full = jnp.bfloat16, jnp.float32
    pieces = 2
    share, chips = width // ndp, ndp // 2
    grad_type = low if share % 16 == 0 else full
    hbm = pl.BlockSpec(memory_space=pl.ANY)
    vmem = pl.BlockSpec(memory_space=pltpu.VMEM)
    dma = pltpu.SemaphoreType.DMA
    shape = jax.ShapeDtypeStruct
    reach = SPAN + QB
    scratch = lambda *dims, kind=low: pltpu.VMEM(dims, kind)
    part = shape((share, inner), full)
    return pl.pallas_call(
        functools.partial(back_kernel, nt, ndp, pieces, heads, head_dim, grad_type),
        out_shape=(
            shape((rows, width), low), shape((rows, width), low), shape((1, width), full), shape((1, width), full),
            shape((heads, NB), full), part, part, part, part,
        ),
        in_specs=[vmem] * 8 + [hbm] * 6,
        out_specs=(vmem,) * 9,
        scratch_shapes=[
            scratch(nt, rows, inner), scratch(3, LEN, inner), scratch(heads, HALF, HALF), scratch(heads, HALF, LEN),
            scratch(nt, rows, width), scratch(nt, 3 * inner, width), scratch(2, rows, width),
            scratch(2, rows, width), scratch(rows, width),
            scratch(nt * rows, 3 * inner), scratch(nt, rows, 3 * inner), scratch(heads, QB, reach, kind=full),
            scratch(heads, LEN, head_dim, kind=full), scratch(heads, LEN, head_dim, kind=full),
            scratch(width, nt * inner, kind=grad_type), scratch(chips, share, nt * inner, kind=grad_type), scratch(chips - 1, share, nt * inner, kind=grad_type),
            scratch(nt, share, inner, kind=grad_type), scratch(nt, share, inner, kind=grad_type),
            scratch(width, 3 * inner, kind=grad_type), scratch(chips, share, 3 * inner, kind=grad_type), scratch(chips - 1, share, 3 * inner, kind=grad_type),
            scratch(nt, 2, width, kind=full), scratch(ndp, 2, width, kind=full),
            scratch(ndp, heads, reach, kind=full),
            dma((nt,)), dma((nt,)), dma((nt,)), dma((nt,)), dma((2, pieces)), dma((3, pieces)),
            dma((2, chips)), dma((2, chips)), dma((2, chips - 1)), dma((2, chips - 1)), dma((nt,)), dma((nt,)),
            dma((nt,)), dma((nt,)), dma((ndp - 1,)), dma((ndp,)), dma((ndp - 1,)), dma((ndp,)), dma((7,)),
        ],
        compiler_params=pltpu.CompilerParams(
            vmem_limit_bytes=VMEM_LIMIT, collective_id=2, has_side_effects=True
        ),
        cost_estimate=pl.CostEstimate(flops=60 * 10**9, bytes_accessed=200 * 10**6, transcendentals=0),
        name="back",
    )(
        grad_attended, grad_middle, base, tokens, gain[None, :], gain2_part, attended, bucket_row,
        qkv, probs_low, probs_high, first_all, weights, layer_parts,
    )


def per_device(
    tokens,
    first_gain,
    query_weight,
    key_weight,
    value_weight,
    out_weight,
    bucket_table,
    second_gain,
    gate_weight,
    up_weight,
    down_weight,
    piece_start,
    bucket_index,
    cotangent,
):
    nt, ndp = lax.axis_size("tensor"), lax.axis_size("dp")
    bucket_row = jnp.pad(bucket_index, (0, 1))[None, :]
    first_weights = (query_weight.T, key_weight.T, value_weight.T)

    def whole(rows):
        part = rows.shape[0] // ndp
        mine = lax.dynamic_slice_in_dim(rows, lax.axis_index("dp") * part, part, 0)
        return lax.all_gather(mine, ("tensor", "dp"), axis=0, tiled=True).reshape(nt, *rows.shape)

    out_all = whole(out_weight.T)
    first_all, cot_all, qkv, probs_low, probs_high, attended = gather_attend(
        nt, tokens, cotangent, first_gain, first_weights, bucket_row, bucket_table, piece_start
    )
    joined, attended = lax.optimization_barrier((jnp.concatenate(first_weights, axis=0), attended))
    weights_all = whole(joined)
    base, grad_middle, second_part, grad_attended, layer_parts, feed_grads = feed(
        nt, tokens, attended, out_all, second_gain, cotangent, cot_all,
        gate_weight.T, up_weight.T, down_weight.T,
    )
    feed_sums = lax.psum_scatter(feed_grads, "dp", scatter_dimension=1, tiled=True).astype(jnp.float32)
    (
        layer_out, input_grad, first_gain_grad, second_gain_grad, table_grad,
        query_grad, key_grad, value_grad, out_grad,
    ) = back(
        nt, ndp, grad_attended, grad_middle, base, tokens, first_gain, second_part, attended, bucket_row,
        qkv, probs_low, probs_high, first_all, weights_all, layer_parts,
    )
    return (
        layer_out,
        input_grad,
        first_gain_grad[0],
        query_grad,
        key_grad,
        value_grad,
        out_grad,
        table_grad.T,
        second_gain_grad[0],
        feed_sums[0],
        feed_sums[1],
        feed_sums[2],
    )


def solution(mesh):
    return jax.shard_map(
        per_device,
        mesh=mesh,
        in_specs=(
            P(("dp", "tensor"), None),
            P(),
            P(None, "tensor"),
            P(None, "tensor"),
            P(None, "tensor"),
            P(None, "tensor"),
            P(None, "tensor"),
            P(),
            P(None, "tensor"),
            P(None, "tensor"),
            P(None, "tensor"),
            P("dp", None),
            P(),
            P(("dp", "tensor"), None),
        ),
        out_specs=(
            P(("dp", "tensor"), None),
            P(("dp", "tensor"), None),
            P(),
            P("dp", "tensor"),
            P("dp", "tensor"),
            P("dp", "tensor"),
            P("dp", "tensor"),
            P(None, "tensor"),
            P(),
            P("dp", "tensor"),
            P("dp", "tensor"),
            P("dp", "tensor"),
        ),
        check_vma=False,
    )
```

```python
import functools

import jax
import jax.numpy as jnp
from jax import lax
from jax.experimental import pallas as pl
from jax.experimental.pallas import tpu as pltpu
from jax.sharding import PartitionSpec as P

NB = 32
LEN = 1024
QB = 256
PIECE = 256
NPIECE = 2
HALF = LEN // NPIECE
SPAN = 5 * QB
DIST = 2 * LEN

EPSILON = 1e-06
MASKED = -1000000000.0
HIGHEST = lax.Precision.HIGHEST
VMEM_LIMIT = 60 * 1024 * 1024
MESH = pl.DeviceIdType.MESH


def normed(row_block, gain_vec):
    inv_rms = lax.rsqrt(jnp.mean(row_block * row_block, axis=-1, keepdims=True) + EPSILON)
    return row_block * inv_rms * gain_vec


def dot(a, b, dims):
    return lax.dot_general(a, b, (dims, ((), ())), preferred_element_type=jnp.float32)


def key_count(block):
    return HALF if (block + 1) * QB <= HALF else LEN


def toeplitz(bucket_row, table_ref, head):
    row = jnp.zeros(bucket_row.shape, jnp.float32)
    for bucket in range(NB):
        row = jnp.where(bucket_row == bucket, table_ref[head, bucket], row)
    rows = jnp.broadcast_to(row, (QB, DIST))
    return pltpu.roll(rows, DIST - (QB - 1), 1, stride=1, stride_axis=0)[:, :SPAN]


def label_of(position, starts):
    label = jnp.zeros(position.shape, jnp.int32)
    for piece, start in enumerate(starts):
        inside = (position >= start) & (position < start + PIECE)
        label = jnp.where(inside, piece + 1, label)
    return label


def allowed_block(block, starts):
    keys = key_count(block)
    query = block * QB + lax.broadcasted_iota(jnp.int32, (QB, 1), 0)
    key = lax.broadcasted_iota(jnp.int32, (1, keys), 1)
    query_label = label_of(query, starts)
    key_label = label_of(key, starts)
    return (key <= query) | ((query_label == key_label) & (query_label > 0))


def attend_block(block, head_dim, allowed, qkv_ref, bias_ref, low_ref, high_ref):
    keys = key_count(block)
    first = LEN - QB - block * QB
    rows = pl.ds(block * QB, QB)
    outs = []
    for head in range(bias_ref.shape[0]):
        cols = pl.ds(head * head_dim, head_dim)
        raw = dot(qkv_ref[0, rows, cols], qkv_ref[1, pl.ds(0, keys), cols], ((1,), (1,)))
        scores = jnp.where(allowed, raw + bias_ref[head, :, pl.ds(first, keys)], MASKED)
        peak = jnp.max(scores, axis=-1, keepdims=True)
        powered = jnp.exp(scores - peak)
        total = jnp.sum(powered, axis=-1, keepdims=True)
        probs = (powered * (1.0 / total)).astype(jnp.bfloat16)
        if keys == HALF:
            low_ref[head, rows, :] = probs
        else:
            high_ref[head, pl.ds(block * QB - HALF, QB), :] = probs
        outs.append(dot(probs, qkv_ref[2, pl.ds(0, keys), cols], ((1,), (0,))))
    return jnp.concatenate(outs, axis=1).astype(jnp.bfloat16)


def greet(t, nt):
    barrier = pltpu.get_barrier_semaphore()
    for k in range(1, nt):
        pl.semaphore_signal(
            barrier, inc=1, device_id={"tensor": lax.rem(t + k, nt)}, device_id_type=MESH
        )
    return barrier


def line_copy(t, nt, way, step, buf, piece, pieces, send_sem, recv_sem):
    sign = 1 if way == 0 else -1
    origin = jnp.clip(t - sign * step, 0, nt - 1)
    rows = buf.shape[1] // pieces
    part = buf.at[origin, pl.ds(piece * rows, rows)]
    return pltpu.make_async_remote_copy(
        src_ref=part,
        dst_ref=part,
        send_sem=send_sem,
        recv_sem=recv_sem,
        device_id={"tensor": jnp.clip(t + sign, 0, nt - 1)},
        device_id_type=MESH,
    )


def gather_attend_kernel(
    nt, ndp, pieces, heads, head_dim, exchange,
    x_ref, cot_ref, gain_ref, gain2_ref, bucket_ref, table_ref, start_ref, *rest,
):
    weight_refs, rest = rest[: 4 if exchange else 1], rest[4 if exchange else 1 :]
    (
        first_out, cot_out, qkv_out, low_out, high_out, own_out, whole_out, middle_out, second_out,
        first, qkv, low, high, bias, att, own, whole,
        send_sem, recv_sem, swap_send, swap_recv, line_send, line_recv, chip_send, chip_recv, core_send, core_recv,
        local_sem,
    ) = rest
    t = lax.axis_index("tensor")
    d = lax.axis_index("dp")
    core = lax.rem(d, 2)
    chip = d // 2
    chips = ndp // 2
    barrier = greet(t, nt)
    greeted = nt - 1
    if exchange:
        for k in range(chips):
            peer = 2 * lax.rem(chip + k, chips) + core if k else d + 1 - 2 * core
            pl.semaphore_signal(barrier, inc=1, device_id={"dp": peer}, device_id_type=MESH)
        greeted += chips
    inner = heads * head_dim
    share = whole.shape[1] // ndp
    own_cot = pltpu.make_async_copy(cot_ref, cot_out.at[t], local_sem.at[0])
    own_cot.start()
    if exchange:
        loads = [
            pltpu.make_async_copy(weight, whole.at[t, pl.ds(i * inner, inner)], local_sem.at[1 + i])
            for i, weight in enumerate(weight_refs)
        ]
    else:
        loads = [pltpu.make_async_copy(weight_refs[0], whole, local_sem.at[1])]
    for one in loads:
        one.start()

    def slices(index, plane):
        return whole.at[plane, pl.ds(pl.multiple_of(index * share, share), share)]

    def remote(src, dst, send, recv, **target):
        return pltpu.make_async_remote_copy(
            src_ref=src, dst_ref=dst, send_sem=send, recv_sem=recv, device_id=target, device_id_type=MESH
        )

    def plane_at(q):
        return lax.rem(t + q, nt)

    def to_plane(q):
        return remote(slices(d, t), slices(d, t), line_send.at[q - 1], line_recv.at[t], tensor=plane_at(q))

    def from_plane(q):
        p = plane_at(q)
        return remote(slices(d, p), slices(d, p), line_send.at[q - 1], line_recv.at[p], tensor=p)

    def to_chip(k, q):
        part = slices(d, plane_at(q))
        return remote(
            part, part, chip_send.at[k - 1, q - 1], chip_recv.at[k - 1, q - 1], dp=2 * lax.rem(chip + k, chips) + core
        )

    def from_chip(k, q):
        peer = 2 * lax.rem(chip - k + chips, chips) + core
        part = slices(peer, plane_at(q))
        return remote(part, part, chip_send.at[k - 1, q - 1], chip_recv.at[k - 1, q - 1], dp=peer)

    def to_core(k, q):
        part = slices(2 * lax.rem(chip - k + chips, chips) + core, plane_at(q))
        return remote(part, part, core_send.at[k, q - 1], core_recv.at[k, q - 1], dp=d + 1 - 2 * core)

    def from_core(k, q):
        part = slices(2 * lax.rem(chip - k + chips, chips) + 1 - core, plane_at(q))
        return remote(part, part, core_send.at[k, q - 1], core_recv.at[k, q - 1], dp=d + 1 - 2 * core)

    first[t] = normed(x_ref[...].astype(jnp.float32), gain_ref[...]).astype(jnp.bfloat16)
    pl.semaphore_wait(barrier, greeted)

    def copy(way, stage, step, piece):
        buf = first if stage == 0 else cot_out
        return line_copy(
            t, nt, way, step, buf, piece, pieces,
            send_sem.at[way, stage, step, piece], recv_sem.at[way, stage, step, piece],
        )

    def landed(way, stage, step, piece):
        sign = 1 if way == 0 else -1
        buf = first if stage == 0 else cot_out
        rows = buf.shape[1] // pieces
        part = buf.at[jnp.clip(t - sign * step, 0, nt - 1), pl.ds(piece * rows, rows)]
        remote(
            part, part, send_sem.at[way, stage, step - 1, piece], recv_sem.at[way, stage, step - 1, piece],
            tensor=jnp.clip(t + sign, 0, nt - 1),
        ).wait_recv()

    ways = ((0, t, t < nt - 1), (1, nt - 1 - t, t > 0))

    def tick(k):
        for piece in range(pieces):
            for way, last, onward in ways:
                if k < nt:
                    @pl.when(k <= last)
                    def _():
                        if k > 0:
                            landed(way, 0, k, piece)

                        @pl.when(onward)
                        def _():
                            copy(way, 0, k, piece).start()

                if k > 0:
                    step = k - last - 1

                    @pl.when((step >= 1) & (step <= last))
                    def _():
                        landed(way, 1, step, piece)

                        @pl.when(onward)
                        def _():
                            copy(way, 1, step, piece).start()

                    @pl.when((step == 0) & onward)
                    def _():
                        copy(way, 0, last, piece).wait_send()
                        copy(way, 1, 0, piece).start()

    def project(origin):
        rows = pl.ds(pl.multiple_of(origin * QB, QB), QB)
        for place in range(3):
            weight = whole[t, pl.ds(place * inner, inner), :]
            qkv[place, rows, :] = dot(first[origin], weight, ((1,), (1,))).astype(jnp.bfloat16)

    tick(0)
    for one in loads:
        one.wait()
    if exchange:
        for q in range(1, nt):
            to_plane(q).start()
    project(t)
    for head in range(heads):
        bias[head] = toeplitz(bucket_ref[...], table_ref, head)
    own_cot.wait()
    for k in range(1, nt):
        tick(k)

        @pl.when(t - k >= 0)
        def _():
            project(t - k)

        @pl.when(t + k < nt)
        def _():
            project(t + k)

        if exchange and k == 2:
            for q in range(1, nt):
                from_plane(q).wait_recv()
                for j in range(1, chips):
                    to_chip(j, q).start()
                to_core(0, q).start()

    starts = [start_ref[0, piece] for piece in range(NPIECE)]
    keep = [
        pltpu.make_async_copy(first, first_out, local_sem.at[5]),
        pltpu.make_async_copy(qkv, qkv_out, local_sem.at[6]),
    ]
    for one in keep:
        one.start()

    def swap(block):
        return remote(att.at[block], own.at[t], swap_send.at[block], swap_recv.at[t], tensor=block)

    for block in range(LEN // QB):
        att[block] = attend_block(block, head_dim, allowed_block(block, starts), qkv, bias, low, high)

        @pl.when(t != block)
        def _():
            swap(block).start()

        @pl.when(t == block)
        def _():
            own[t] = att[block]

    late = [
        pltpu.make_async_copy(low, low_out, local_sem.at[7]),
        pltpu.make_async_copy(high, high_out, local_sem.at[8]),
    ]
    for one in late:
        one.start()
    tick(nt)
    if exchange:
        for k in range(1, chips):
            for q in range(1, nt):
                from_chip(k, q).wait_recv()
                to_core(k, q).start()
    tick(nt + 1)
    for block in range(nt):
        @pl.when(t != block)
        def _():
            remote(att.at[block], own.at[block], swap_send.at[block], swap_recv.at[block], tensor=block).wait_recv()

    if exchange:
        for k in range(chips):
            for q in range(1, nt):
                from_core(k, q).wait_recv()
    late += [
        pltpu.make_async_copy(own, own_out, local_sem.at[9]),
        pltpu.make_async_copy(whole, whole_out, local_sem.at[10]),
    ]
    for one in late[2:]:
        one.start()
    total = x_ref[...].astype(jnp.float32)
    for j in range(nt):
        total = total + dot(own[j], whole[j, pl.ds(3 * inner, inner), :], ((1,), (0,)))
    middle_out[...] = total
    second_out[...] = normed(total, gain2_ref[...]).astype(jnp.bfloat16)
    for k in range(nt + 2, 2 * nt):
        tick(k)
    for block in range(nt):
        @pl.when(t != block)
        def _():
            swap(block).wait_send()

    for one in keep + late:
        one.wait()
    if exchange:
        for q in range(1, nt):
            to_plane(q).wait_send()
            for k in range(1, chips):
                to_chip(k, q).wait_send()
            for k in range(chips):
                to_core(k, q).wait_send()
    for piece in range(pieces):
        for way, last, onward in ways:
            for stage in range(2):
                for step in range(nt):
                    @pl.when(onward & ((step < last) if stage == 0 else (step <= last)))
                    def _():
                        copy(way, stage, step, piece).wait_send()


def gather_attend(nt, ndp, tokens, cotangent, gain, gain2, weights, bucket_row, table, starts):
    heads = table.shape[0]
    rows, width = tokens.shape
    inner = weights[0].shape[0]
    low, full = jnp.bfloat16, jnp.float32
    pieces = 2
    exchange = (4 * inner // ndp) % 16 == 0
    if not exchange:
        joined = jnp.concatenate(weights, axis=0)
        part = joined.shape[0] // ndp
        mine = lax.dynamic_slice_in_dim(joined, lax.axis_index("dp") * part, part, 0)
        weights = (lax.all_gather(mine, ("tensor", "dp"), axis=0, tiled=True).reshape(nt, *joined.shape),)
    chips = ndp // 2
    smem = pl.BlockSpec(memory_space=pltpu.SMEM)
    hbm = pl.BlockSpec(memory_space=pl.ANY)
    vmem = pl.BlockSpec(memory_space=pltpu.VMEM)
    shapes = (
        (nt, rows, width), (nt, rows, width), (3, LEN, inner), (heads, HALF, HALF), (heads, HALF, LEN),
        (nt, rows, inner), (nt, 4 * inner, width),
    )
    dma = pltpu.SemaphoreType.DMA
    return pl.pallas_call(
        functools.partial(gather_attend_kernel, nt, ndp, pieces, heads, inner // heads, exchange),
        out_shape=tuple(jax.ShapeDtypeStruct(shape, low) for shape in shapes)
        + (jax.ShapeDtypeStruct((rows, width), full), jax.ShapeDtypeStruct((rows, width), low)),
        in_specs=[vmem, hbm, vmem, vmem, vmem, smem, smem] + [hbm] * len(weights),
        out_specs=(hbm,) * 7 + (vmem, vmem),
        scratch_shapes=[
            pltpu.VMEM((nt, rows, width), low),
            pltpu.VMEM((3, LEN, inner), low),
            pltpu.VMEM((heads, HALF, HALF), low),
            pltpu.VMEM((heads, HALF, LEN), low),
            pltpu.VMEM((heads, QB, SPAN), full),
            pltpu.VMEM((nt, rows, inner), low),
            pltpu.VMEM((nt, rows, inner), low),
            pltpu.VMEM((nt, 4 * inner, width), low),
            dma((2, 2, nt, pieces)), dma((2, 2, nt, pieces)), dma((nt,)), dma((nt,)),
            dma((nt - 1,)), dma((nt,)), dma((chips - 1, nt - 1)), dma((chips - 1, nt - 1)),
            dma((chips, nt - 1)), dma((chips, nt - 1)), dma((11,)),
        ],
        compiler_params=pltpu.CompilerParams(
            vmem_limit_bytes=VMEM_LIMIT, collective_id=0, has_side_effects=True
        ),
        name="gather_attend",
    )(tokens, cotangent, gain[None, :], gain2[None, :], bucket_row, table, starts, *weights)


def fold_diagonals(grid):
    rows = QB // 2
    width = grid.shape[1]
    while rows >= 1:
        grid = grid[:rows] + pltpu.roll(grid[rows : 2 * rows], width - rows, 1)
        rows //= 2
    return grid


def gelu_parts(v):
    root, cubic = 0.7978845608028654, 0.044715
    square = v * v
    bend = jnp.tanh(root * v * (1.0 + cubic * square))
    half = 0.5 * (1.0 + bend)
    slope = half + 0.5 * v * (1.0 - bend * bend) * root * (1.0 + 3.0 * cubic * square)
    return v * half, slope


def feed_kernel(
    nt, pieces,
    middle, second_ref, gain_ref, cot_own_ref, whole_hbm, cot_hbm, wg_hbm, wu_hbm, wd_hbm,
    base_out, gm_out, gain_out, ga_out, lo_out, grads_out,
    buf, cot, wg, wu, wd, hid, gg, gu, gs, lo, wo, mate_in, acc_in, far_in, grads, mate_lo,
    send_sem, recv_sem, rs_send, rs_recv, lo_sem, local_sem,
):
    t = lax.axis_index("tensor")
    barrier = greet(t, nt)
    loads = [
        pltpu.make_async_copy(a, b, local_sem.at[i])
        for i, (a, b) in enumerate(((wg_hbm, wg), (wu_hbm, wu), (wd_hbm, wd), (cot_hbm, cot)))
    ]
    for one in loads:
        one.start()
    row_count = middle.shape[0]
    size = row_count // pieces
    inner = wo.shape[1]
    wo_load = pltpu.make_async_copy(whole_hbm.at[:, pl.ds(3 * inner, inner)], wo, local_sem.at[4])
    wo_load.start()
    buf[t] = second_ref[...]
    keep = []
    pl.semaphore_wait(barrier, nt - 1)
    mate = t + 1 - 2 * lax.rem(t, 2)
    is_end = (t == 0) | (t == nt - 1)
    ways = ((0, t, t < nt - 1), (1, nt - 1 - t, t > 0))

    def copy(way, step, piece):
        return line_copy(
            t, nt, way, step, buf, piece, pieces,
            send_sem.at[way, step, piece], recv_sem.at[way, step, piece],
        )

    def landed(way, step, piece):
        sign = 1 if way == 0 else -1
        part = buf.at[jnp.clip(t - sign * step, 0, nt - 1), pl.ds(piece * size, size)]
        pltpu.make_async_remote_copy(
            src_ref=part, dst_ref=part,
            send_sem=send_sem.at[way, step - 1, piece], recv_sem=recv_sem.at[way, step - 1, piece],
            device_id={"tensor": jnp.clip(t + sign, 0, nt - 1)}, device_id_type=MESH,
        ).wait_recv()

    def remote(src, dst, target, send, recv):
        return pltpu.make_async_remote_copy(
            src_ref=src, dst_ref=dst, send_sem=send, recv_sem=recv,
            device_id={"tensor": target}, device_id_type=MESH,
        )

    def to_mate(piece):
        rows = pl.ds(piece * size, size)
        return remote(gs.at[mate, rows], mate_in.at[rows], mate, rs_send.at[0, piece], rs_recv.at[0, piece])

    def to_acc(origin, piece):
        rows = pl.ds(piece * size, size)
        j = lax.rem(origin, 2)
        return remote(
            gs.at[origin, rows], acc_in.at[j, rows], mate, rs_send.at[1 + j, piece], rs_recv.at[1 + j, piece]
        )

    def to_far(origin, piece):
        rows = pl.ds(piece * size, size)
        j = lax.rem(origin, 2)
        return remote(
            gs.at[origin, rows], far_in.at[rows], origin, rs_send.at[3 + j, piece], rs_recv.at[3, piece]
        )

    def feed(origin, piece):
        rows = pl.ds(pl.multiple_of(piece * size, size), size)
        flat = pl.ds(pl.multiple_of(origin * row_count + piece * size, size), size)
        normal = buf[origin, rows]
        gate = dot(normal, wg[...], ((1,), (1,)))
        up = dot(normal, wu[...], ((1,), (1,)))
        grad_hidden = dot(cot[origin, rows], wd[...], ((1,), (1,)))
        act, slope = gelu_parts(gate)
        hid[flat, :] = (act * up).astype(jnp.bfloat16)
        grad_gate = (grad_hidden * up * slope).astype(jnp.bfloat16)
        grad_up = (grad_hidden * act).astype(jnp.bfloat16)
        gg[flat, :] = grad_gate
        gu[flat, :] = grad_up
        gs[origin, rows] = (
            dot(grad_gate, wg[...], ((1,), (0,))) + dot(grad_up, wu[...], ((1,), (0,)))
        ).astype(jnp.bfloat16)

    for piece in range(pieces):
        for way, last, onward in ways:
            @pl.when(onward)
            def _():
                copy(way, 0, piece).start()

    for one in loads:
        one.wait()

    def unit(u, carry):
        step = u // pieces
        piece = lax.rem(u, pieces)

        @pl.when(step > 0)
        def _():
            for way, last, onward in ways:
                @pl.when(step <= last)
                def _():
                    landed(way, step, piece)

                    @pl.when(onward)
                    def _():
                        copy(way, step, piece).start()

        def side(way, carry):
            origin = t - (1 - 2 * way) * step
            there = (origin >= 0) & (origin < nt) & ((step > 0) | (way == 0))

            @pl.when(there)
            def _():
                feed(origin, piece)

                @pl.when(origin == mate)
                def _():
                    to_mate(piece).start()

                @pl.when((origin != mate) & (origin != t) & is_end)
                def _():
                    to_acc(origin, piece).start()

            return carry

        return lax.fori_loop(0, 2, side, carry)

    lax.fori_loop(0, nt * pieces, unit, 0)

    near = jnp.where(t < nt // 2, nt // 2, nt // 2 - 1)
    far = jnp.where(t < nt // 2, nt - 1, 0)

    def pass_on(origin, piece):
        @pl.when(jnp.logical_not(is_end))
        def _():
            to_acc(origin, piece).wait_recv()
            rows = pl.ds(piece * size, size)
            j = lax.rem(origin, 2)
            gs[origin, rows] = (
                gs[origin, rows].astype(jnp.float32) + acc_in[j, rows].astype(jnp.float32)
            ).astype(jnp.bfloat16)
            to_far(origin, piece).start()

    span = 256
    flat_rows = nt * row_count
    spans = buf.shape[2] // span

    def columns(ref, i):
        cols = pl.ds(pl.multiple_of(i * span, span), span)
        return ref[:, :, cols].reshape(flat_rows, span)

    def down_cols(i, carry):
        rows = pl.ds(pl.multiple_of(i * span, span), span)
        grads[2, rows, :] = dot(columns(cot, i), hid[...], ((0,), (0,))).astype(jnp.bfloat16)
        return carry

    def gate_up_cols(i, carry):
        rows = pl.ds(pl.multiple_of(i * span, span), span)
        left = columns(buf, i)
        grads[0, rows, :] = dot(left, gg[...], ((0,), (0,))).astype(jnp.bfloat16)
        grads[1, rows, :] = dot(left, gu[...], ((0,), (0,))).astype(jnp.bfloat16)
        return carry

    def down_rows(i, carry):
        rows = pl.ds(pl.multiple_of(i * row_count, row_count), row_count)
        lo[i] = dot(hid[rows, :], wd[...], ((1,), (0,))).astype(jnp.bfloat16)
        return carry

    pass_on(near, 0)
    lax.fori_loop(0, spans, down_cols, 0)
    pass_on(near, 1)
    lax.fori_loop(0, nt, down_rows, 0)
    keep.append(pltpu.make_async_copy(lo, lo_out, local_sem.at[5]))
    keep[-1].start()
    lo_swap = remote(lo.at[mate], mate_lo, mate, lo_sem.at[0], lo_sem.at[1])
    lo_swap.start()
    pass_on(far, 0)
    lax.fori_loop(0, spans // 2, gate_up_cols, 0)
    pass_on(far, 1)
    lax.fori_loop(spans // 2, spans, gate_up_cols, 0)
    keep.append(pltpu.make_async_copy(grads, grads_out, local_sem.at[6]))
    keep[-1].start()

    wo_load.wait()
    for piece in range(pieces):
        rows = pl.ds(piece * size, size)
        to_mate(piece).wait_recv()
        remote(gs.at[t, rows], far_in.at[rows], mate, rs_send.at[3, piece], rs_recv.at[3, piece]).wait_recv()
        grad_second = (
            gs[t, rows].astype(jnp.float32)
            + mate_in[rows].astype(jnp.float32)
            + far_in[rows].astype(jnp.float32)
        )
        mid = middle[rows]
        inv = lax.rsqrt(jnp.mean(mid * mid, axis=-1, keepdims=True) + EPSILON)
        scaled = gain_ref[...] * grad_second
        along = jnp.mean(scaled * mid, axis=-1, keepdims=True)
        grad_middle = cot_own_ref[rows].astype(jnp.float32) + inv * scaled - mid * (inv * inv * inv * along)
        gm_out[rows] = grad_middle
        part = jnp.sum(grad_second * mid * inv, axis=0, keepdims=True)
        if piece == 0:
            gain_out[...] = part
        else:
            gain_out[...] += part
        grad_low = grad_middle.astype(jnp.bfloat16)
        for j in range(nt):
            ga_out[j, rows] = dot(grad_low, wo[j], ((1,), (1,))).astype(jnp.bfloat16)

    lo_swap.wait()
    base_out[...] = middle[...] + lo[t].astype(jnp.float32) + mate_lo[...].astype(jnp.float32)
    for one in keep:
        one.wait()
    for piece in range(pieces):
        for way, last, onward in ways:
            for step in range(nt):
                @pl.when(onward & (step <= last))
                def _():
                    copy(way, step, piece).wait_send()

        to_mate(piece).wait_send()
        for origin in (near, far):
            @pl.when(is_end)
            def _():
                to_acc(origin, piece).wait_send()

            @pl.when(jnp.logical_not(is_end))
            def _():
                to_far(origin, piece).wait_send()


def feed(nt, middle, second, gain, cotangent, whole, cot_all, gate_weight, up_weight, down_weight):
    rows, width = middle.shape
    hidden = gate_weight.shape[0]
    low, full = jnp.bfloat16, jnp.float32
    pieces = 2
    hbm = pl.BlockSpec(memory_space=pl.ANY)
    vmem = pl.BlockSpec(memory_space=pltpu.VMEM)
    inner = whole.shape[1] // 4
    dma = pltpu.SemaphoreType.DMA
    shape = jax.ShapeDtypeStruct
    return pl.pallas_call(
        functools.partial(feed_kernel, nt, pieces),
        out_shape=(
            shape((rows, width), full), shape((rows, width), full), shape((1, width), full),
            shape((nt, rows, inner), low), shape((nt, rows, width), low), shape((3, width, hidden), low),
        ),
        in_specs=[vmem] * 4 + [hbm] * 5,
        out_specs=(vmem, vmem, vmem, vmem, hbm, hbm),
        scratch_shapes=[
            pltpu.VMEM((nt, rows, width), low), pltpu.VMEM((nt, rows, width), low),
            pltpu.VMEM((hidden, width), low), pltpu.VMEM((hidden, width), low), pltpu.VMEM((hidden, width), low),
            pltpu.VMEM((nt * rows, hidden), low), pltpu.VMEM((nt * rows, hidden), low), pltpu.VMEM((nt * rows, hidden), low),
            pltpu.VMEM((nt, rows, width), low), pltpu.VMEM((nt, rows, width), low),
            pltpu.VMEM((nt, inner, width), low),
            pltpu.VMEM((rows, width), low), pltpu.VMEM((2, rows, width), low), pltpu.VMEM((rows, width), low),
            pltpu.VMEM((3, width, hidden), low), pltpu.VMEM((rows, width), low),
            dma((2, nt, pieces)), dma((2, nt, pieces)), dma((5, pieces)), dma((4, pieces)), dma((2,)), dma((7,)),
        ],
        compiler_params=pltpu.CompilerParams(
            vmem_limit_bytes=VMEM_LIMIT, collective_id=1, has_side_effects=True
        ),
        name="feed",
    )(middle, second, gain[None, :], cotangent, whole, cot_all, gate_weight, up_weight, down_weight)


def back_kernel(
    nt, ndp, pieces, heads, head_dim, grad_type,
    ga_ref, gm_ref, base_ref, x_ref, gain_ref, gain2_ref, own_ref, bucket_ref,
    qkv_hbm, low_hbm, high_hbm, first_hbm, weight_hbm, lo_hbm,
    layer_out, input_out, gain_out, gain2_out, table_out, q_out, k_out, v_out, o_out,
    ga_in, qkv, low, high, first, weight, lo, acc_in, far_in,
    gq, gq_in, diag, dk_acc, dv_acc,
    og, og_sum, og_chip, og_line, og_line_in, pg, pg_sum, pg_chip,
    gains_line, gains_in, dist_in,
    swap_send, swap_recv, back_send, back_recv, lo_send, lo_recv,
    pair_send, pair_recv, chip_send, chip_recv, line_send, line_recv,
    gl_send, gl_recv, gd_send, gd_recv, dist_send, dist_recv, local_sem,
):
    t = lax.axis_index("tensor")
    d = lax.axis_index("dp")
    core = lax.rem(d, 2)
    chip = d // 2
    chips = ndp // 2
    barrier = greet(t, nt)
    for k in range(1, ndp):
        pl.semaphore_signal(
            barrier, inc=1, device_id={"dp": lax.rem(d + k, ndp)}, device_id_type=MESH
        )
    mate = t + 1 - 2 * lax.rem(t, 2)
    is_end = (t == 0) | (t == nt - 1)
    near = jnp.where(t < nt // 2, nt // 2, nt // 2 - 1)
    far = jnp.where(t < nt // 2, nt - 1, 0)
    loads = [
        pltpu.make_async_copy(a, b, local_sem.at[i])
        for i, (a, b) in enumerate(
            ((qkv_hbm, qkv), (low_hbm, low), (high_hbm, high), (first_hbm, first),
             (weight_hbm.at[:, pl.ds(0, weight.shape[1])], weight),
             (lo_hbm.at[near], lo.at[lax.rem(near, 2)]), (lo_hbm.at[far], lo.at[lax.rem(far, 2)]))
        )
    ]
    for one in loads:
        one.start()
    others = (far, near, mate)
    row_count, width = x_ref.shape
    inner = heads * head_dim
    size = row_count // pieces
    share = width // ndp
    full = jnp.float32

    def remote(src, dst, send, recv, **target):
        return pltpu.make_async_remote_copy(
            src_ref=src, dst_ref=dst, send_sem=send, recv_sem=recv,
            device_id=target, device_id_type=MESH,
        )

    def swap(peer):
        return remote(ga_ref.at[peer], ga_in.at[t], swap_send.at[peer], swap_recv.at[t], tensor=peer)

    def swap_in(peer):
        return remote(ga_ref.at[peer], ga_in.at[peer], swap_send.at[peer], swap_recv.at[peer], tensor=peer)

    def lo_acc(origin, piece):
        rows = pl.ds(piece * size, size)
        j = lax.rem(origin, 2)
        return remote(
            lo.at[j, rows], acc_in.at[j, rows], lo_send.at[j, piece], lo_recv.at[j, piece], tensor=mate
        )

    def lo_far(origin, piece):
        rows = pl.ds(piece * size, size)
        j = lax.rem(origin, 2)
        return remote(
            lo.at[j, rows], far_in.at[rows], lo_send.at[j, piece], lo_recv.at[2, piece], tensor=origin
        )

    def pass_on(origin, piece):
        @pl.when(jnp.logical_not(is_end))
        def _():
            lo_acc(origin, piece).wait_recv()
            rows = pl.ds(piece * size, size)
            j = lax.rem(origin, 2)
            lo[j, rows] = (lo[j, rows].astype(full) + acc_in[j, rows].astype(full)).astype(jnp.bfloat16)
            lo_far(origin, piece).start()

    pl.semaphore_wait(barrier, nt - 1 + ndp - 1)
    for peer in others:
        swap(peer).start()
    ga_in[t] = ga_ref[t]
    loads[5].wait()
    loads[6].wait()

    @pl.when(is_end)
    def _():
        for origin in (far, near):
            for piece in range(pieces):
                lo_acc(origin, piece).start()

    def block_rows(index):
        return pl.ds(pl.multiple_of(index * share, share), share)

    def pair(kind, c):
        grads, landing = ((og, og_sum), (pg, pg_sum))[kind]
        return remote(
            grads.at[block_rows(2 * c + 1 - core)], landing.at[c],
            pair_send.at[kind, c], pair_recv.at[kind, c], dp=d + 1 - 2 * core,
        )

    def chip_copy(kind, k):
        sums, landing = ((og_sum, og_chip), (pg_sum, pg_chip))[kind]
        to = lax.rem(chip + k, chips)
        return remote(
            sums.at[to], landing.at[k - 1], chip_send.at[kind, k - 1], chip_recv.at[kind, k - 1], dp=2 * to + core
        )

    def pair_sum(kind):
        grads, sums = ((og, og_sum), (pg, pg_sum))[kind]
        for c in range(chips):
            pair(kind, c).wait_recv()
            sums[c] = (grads[block_rows(2 * c + core)].astype(full) + sums[c].astype(full)).astype(grad_type)
        for k in range(1, chips):
            chip_copy(kind, k).start()

    def chip_sum(kind):
        sums, landing = ((og_sum, og_chip), (pg_sum, pg_chip))[kind]
        total = sums[chip].astype(full)
        for k in range(1, chips):
            chip_copy(kind, k).wait_recv()
            total = total + landing[k - 1].astype(full)
        return total

    span = 256
    spans = width // span
    own = jnp.concatenate([own_ref[j] for j in range(nt)], axis=1)
    for i in range(spans):
        left = gm_ref[:, pl.ds(i * span, span)].astype(jnp.bfloat16)
        og[pl.ds(i * span, span), :] = dot(left, own, ((0,), (0,))).astype(grad_type)
    for c in range(chips):
        pair(0, c).start()

    for i in range(3):
        loads[i].wait()
    blocks = LEN // QB
    diag[...] = jnp.zeros_like(diag)
    for block in reversed(range(blocks)):
        keys = key_count(block)
        rows = pl.ds(block * QB, QB)
        first_col = LEN - block * QB

        @pl.when(t != block)
        def _():
            swap_in(block).wait_recv()

        parts = []
        for head in range(heads):
            cols = pl.ds(head * head_dim, head_dim)
            if keys == HALF:
                probs_low = low[head, rows, :]
            else:
                probs_low = high[head, pl.ds(block * QB - HALF, QB), :]
            probs = probs_low.astype(full)
            do = ga_in[block, :, cols]
            grad_probs = dot(do, qkv[2, pl.ds(0, keys), cols], ((1,), (1,)))
            weighted = jnp.sum(probs * grad_probs, axis=-1, keepdims=True)
            grad_low = (probs * (grad_probs - weighted)).astype(jnp.bfloat16)
            reach = pl.ds(first_col, keys)
            diag[head, :, reach] = diag[head, :, reach] + grad_low.astype(full)
            parts.append(dot(grad_low, qkv[1, pl.ds(0, keys), cols], ((1,), (0,))))
            key_part = dot(grad_low, qkv[0, rows, cols], ((0,), (0,)))
            value_part = dot(probs_low, do, ((0,), (0,)))
            if block == blocks - 1:
                dk_acc[head] = key_part
                dv_acc[head] = value_part
            else:
                dk_acc[head, pl.ds(0, keys), :] += key_part
                dv_acc[head, pl.ds(0, keys), :] += value_part
        gq[rows, pl.ds(0, inner)] = jnp.concatenate(parts, axis=1).astype(jnp.bfloat16)
        if block == 1:
            pair_sum(0)
    for block in range(blocks):
        rows = pl.ds(block * QB, QB)
        sides = [acc[head, rows, :] for acc in (dk_acc, dv_acc) for head in range(heads)]
        gq[rows, pl.ds(inner, 2 * inner)] = jnp.concatenate(sides, axis=1).astype(jnp.bfloat16)

    def token_rows(peer):
        return pl.ds(pl.multiple_of(peer * row_count, row_count), row_count)

    def give(peer):
        return remote(
            gq.at[token_rows(peer)], gq_in.at[t], back_send.at[peer], back_recv.at[t], tensor=peer
        )

    def taken(peer):
        return remote(
            gq.at[token_rows(peer)], gq_in.at[peer], back_send.at[peer], back_recv.at[peer], tensor=peer
        )

    for peer in others:
        give(peer).start()
    for head in range(heads):
        dist_in[d, pl.ds(head, 1), :] = fold_diagonals(diag[head])

    def dist_copy(k):
        return remote(
            dist_in.at[d], dist_in.at[d], dist_send.at[k - 1], dist_recv.at[d], dp=lax.rem(d + k, ndp)
        )

    for k in range(1, ndp):
        dist_copy(k).start()
    pass_on(far, 0)
    loads[3].wait()
    for i in range(spans):
        cols = pl.ds(i * span, span)
        left = first[:, :, cols].reshape(nt * row_count, span)
        pg[cols, :] = dot(left, gq[...], ((0,), (0,))).astype(grad_type)
    for c in range(chips):
        pair(1, c).start()
    pass_on(far, 1)
    total = chip_sum(0)
    for j in range(nt):
        og_line[j] = total[:, j * inner : (j + 1) * inner].astype(grad_type)

    def line_copy_out(peer):
        return remote(og_line.at[peer], og_line_in.at[t], line_send.at[peer], line_recv.at[t], tensor=peer)

    def line_in(peer):
        return remote(og_line.at[peer], og_line_in.at[peer], line_send.at[peer], line_recv.at[peer], tensor=peer)

    for peer in others:
        line_copy_out(peer).start()
    pair_sum(1)
    pass_on(near, 0)
    pass_on(near, 1)
    loads[4].wait()
    inputs = x_ref[...].astype(full)
    inv = lax.rsqrt(jnp.mean(inputs * inputs, axis=-1, keepdims=True) + EPSILON)
    grad_first = dot(gq[token_rows(t)], weight[t], ((1,), (0,)))
    for peer in (mate, near, far):
        taken(peer).wait_recv()
        grad_first = grad_first + dot(gq_in[peer], weight[peer], ((1,), (0,)))
    scaled = gain_ref[...] * grad_first
    along = jnp.mean(scaled * inputs, axis=-1, keepdims=True)
    gains_line[t, pl.ds(0, 1), :] = jnp.sum(grad_first * inputs * inv, axis=0, keepdims=True)
    gains_line[t, pl.ds(1, 1), :] = gain2_ref[...]

    def gain_copy(peer):
        return remote(gains_line.at[t], gains_line.at[t], gl_send.at[peer], gl_recv.at[t], tensor=peer)

    def gain_landed(peer):
        return remote(gains_line.at[peer], gains_line.at[peer], gl_send.at[peer], gl_recv.at[peer], tensor=peer)

    for peer in others:
        gain_copy(peer).start()
    input_out[...] = (gm_ref[...] + inv * scaled - inputs * (inv * inv * inv * along)).astype(jnp.bfloat16)
    for peer in others:
        gain_landed(peer).wait_recv()
    gains_in[d] = gains_line[0] + gains_line[1] + gains_line[2] + gains_line[3]

    def gains_copy(k):
        return remote(
            gains_in.at[d], gains_in.at[d], gd_send.at[k - 1], gd_recv.at[d], dp=lax.rem(d + k, ndp)
        )

    for k in range(1, ndp):
        gains_copy(k).start()
    total = chip_sum(1)
    q_out[...] = total[:, :inner]
    k_out[...] = total[:, inner : 2 * inner]
    v_out[...] = total[:, 2 * inner :]
    total = og_line[t].astype(full)
    for peer in others:
        line_in(peer).wait_recv()
        total = total + og_line_in[peer].astype(full)
    o_out[...] = total

    def others_of(landing, send, recv):
        for k in range(1, ndp):
            peer = lax.rem(d + k, ndp)
            remote(landing.at[peer], landing.at[peer], send.at[k - 1], recv.at[peer], dp=peer).wait_recv()

    others_of(dist_in, dist_send, dist_recv)
    dist = dist_in[0]
    for k in range(1, ndp):
        dist = dist + dist_in[k]
    reach = dist.shape[1]
    bucket = pltpu.roll(bucket_ref[...], 1, 1)[:, :reach]
    hot = (lax.broadcasted_iota(jnp.int32, (NB, reach), 0) == bucket).astype(full)
    table_out[...] = lax.dot_general(
        dist, hot, (((1,), (1,)), ((), ())), precision=HIGHEST, preferred_element_type=full
    )
    for piece in range(pieces):
        rows = pl.ds(piece * size, size)
        remote(lo.at[0, rows], far_in.at[rows], lo_send.at[0, piece], lo_recv.at[2, piece], tensor=mate).wait_recv()
        layer_out[rows] = (base_ref[rows] + far_in[rows].astype(full)).astype(jnp.bfloat16)
    others_of(gains_in, gd_send, gd_recv)
    total = gains_in[0]
    for k in range(1, ndp):
        total = total + gains_in[k]
    gain_out[...] = total[0:1]
    gain2_out[...] = total[1:2]

    for peer in others:
        swap(peer).wait_send()
        give(peer).wait_send()
        line_copy_out(peer).wait_send()
        gain_copy(peer).wait_send()
    for origin in (near, far):
        for piece in range(pieces):
            lo_acc(origin, piece).wait_send()
    for kind in range(2):
        for c in range(chips):
            pair(kind, c).wait_send()
        for k in range(1, chips):
            chip_copy(kind, k).wait_send()
    for k in range(1, ndp):
        dist_copy(k).wait_send()
        gains_copy(k).wait_send()


def back(nt, ndp, grad_attended, grad_middle, base, tokens, gain, gain2_part, attended, bucket_row, qkv, probs_low, probs_high, first_all, weights, layer_parts):
    rows, width = tokens.shape
    heads = probs_low.shape[0]
    inner = qkv.shape[2]
    head_dim = inner // heads
    low, full = jnp.bfloat16, jnp.float32
    pieces = 2
    share, chips = width // ndp, ndp // 2
    grad_type = low if share % 16 == 0 else full
    hbm = pl.BlockSpec(memory_space=pl.ANY)
    vmem = pl.BlockSpec(memory_space=pltpu.VMEM)
    dma = pltpu.SemaphoreType.DMA
    shape = jax.ShapeDtypeStruct
    reach = SPAN + QB
    scratch = lambda *dims, kind=low: pltpu.VMEM(dims, kind)
    part = shape((share, inner), full)
    return pl.pallas_call(
        functools.partial(back_kernel, nt, ndp, pieces, heads, head_dim, grad_type),
        out_shape=(
            shape((rows, width), low), shape((rows, width), low), shape((1, width), full), shape((1, width), full),
            shape((heads, NB), full), part, part, part, part,
        ),
        in_specs=[vmem] * 8 + [hbm] * 6,
        out_specs=(vmem,) * 9,
        scratch_shapes=[
            scratch(nt, rows, inner), scratch(3, LEN, inner), scratch(heads, HALF, HALF), scratch(heads, HALF, LEN),
            scratch(nt, rows, width), scratch(nt, 3 * inner, width), scratch(2, rows, width),
            scratch(2, rows, width), scratch(rows, width),
            scratch(nt * rows, 3 * inner), scratch(nt, rows, 3 * inner), scratch(heads, QB, reach, kind=full),
            scratch(heads, LEN, head_dim, kind=full), scratch(heads, LEN, head_dim, kind=full),
            scratch(width, nt * inner, kind=grad_type), scratch(chips, share, nt * inner, kind=grad_type), scratch(chips - 1, share, nt * inner, kind=grad_type),
            scratch(nt, share, inner, kind=grad_type), scratch(nt, share, inner, kind=grad_type),
            scratch(width, 3 * inner, kind=grad_type), scratch(chips, share, 3 * inner, kind=grad_type), scratch(chips - 1, share, 3 * inner, kind=grad_type),
            scratch(nt, 2, width, kind=full), scratch(ndp, 2, width, kind=full),
            scratch(ndp, heads, reach, kind=full),
            dma((nt,)), dma((nt,)), dma((nt,)), dma((nt,)), dma((2, pieces)), dma((3, pieces)),
            dma((2, chips)), dma((2, chips)), dma((2, chips - 1)), dma((2, chips - 1)), dma((nt,)), dma((nt,)),
            dma((nt,)), dma((nt,)), dma((ndp - 1,)), dma((ndp,)), dma((ndp - 1,)), dma((ndp,)), dma((7,)),
        ],
        compiler_params=pltpu.CompilerParams(
            vmem_limit_bytes=VMEM_LIMIT, collective_id=2, has_side_effects=True
        ),
        cost_estimate=pl.CostEstimate(flops=60 * 10**9, bytes_accessed=200 * 10**6, transcendentals=0),
        name="back",
    )(
        grad_attended, grad_middle, base, tokens, gain[None, :], gain2_part, attended, bucket_row,
        qkv, probs_low, probs_high, first_all, weights, layer_parts,
    )


def per_device(
    tokens,
    first_gain,
    query_weight,
    key_weight,
    value_weight,
    out_weight,
    bucket_table,
    second_gain,
    gate_weight,
    up_weight,
    down_weight,
    piece_start,
    bucket_index,
    cotangent,
):
    nt, ndp = lax.axis_size("tensor"), lax.axis_size("dp")
    bucket_row = jnp.pad(bucket_index, (0, 1))[None, :]
    weights = (query_weight.T, key_weight.T, value_weight.T, out_weight.T)
    first_all, cot_all, qkv, probs_low, probs_high, attended, whole, middle, second = gather_attend(
        nt, ndp, tokens, cotangent, first_gain, second_gain, weights, bucket_row, bucket_table.T, piece_start
    )
    base, grad_middle, second_part, grad_attended, layer_parts, feed_grads = feed(
        nt, middle, second, second_gain, cotangent, whole, cot_all, gate_weight.T, up_weight.T, down_weight.T
    )
    feed_sums = lax.psum_scatter(feed_grads, "dp", scatter_dimension=1, tiled=True).astype(jnp.float32)
    (
        layer_out, input_grad, first_gain_grad, second_gain_grad, table_grad,
        query_grad, key_grad, value_grad, out_grad,
    ) = back(
        nt, ndp, grad_attended, grad_middle, base, tokens, first_gain, second_part, attended, bucket_row,
        qkv, probs_low, probs_high, first_all, whole, layer_parts,
    )
    return (
        layer_out,
        input_grad,
        first_gain_grad[0],
        query_grad,
        key_grad,
        value_grad,
        out_grad,
        table_grad.T,
        second_gain_grad[0],
        feed_sums[0],
        feed_sums[1],
        feed_sums[2],
    )


def solution(mesh):
    return jax.shard_map(
        per_device,
        mesh=mesh,
        in_specs=(
            P(("dp", "tensor"), None),
            P(),
            P(None, "tensor"),
            P(None, "tensor"),
            P(None, "tensor"),
            P(None, "tensor"),
            P(None, "tensor"),
            P(),
            P(None, "tensor"),
            P(None, "tensor"),
            P(None, "tensor"),
            P("dp", None),
            P(),
            P(("dp", "tensor"), None),
        ),
        out_specs=(
            P(("dp", "tensor"), None),
            P(("dp", "tensor"), None),
            P(),
            P("dp", "tensor"),
            P("dp", "tensor"),
            P("dp", "tensor"),
            P("dp", "tensor"),
            P(None, "tensor"),
            P(),
            P("dp", "tensor"),
            P("dp", "tensor"),
            P("dp", "tensor"),
        ),
        check_vma=False,
    )
```

```python
import functools

import jax
import jax.numpy as jnp
from jax import lax
from jax.experimental import pallas as pl
from jax.experimental.pallas import tpu as pltpu
from jax.sharding import PartitionSpec as P

NB = 32
LEN = 1024
QB = 256
PIECE = 256
NPIECE = 2
HALF = LEN // NPIECE
SPAN = 5 * QB
DIST = 2 * LEN

EPSILON = 1e-06
MASKED = -1000000000.0
HIGHEST = lax.Precision.HIGHEST
VMEM_LIMIT = 60 * 1024 * 1024
MESH = pl.DeviceIdType.MESH


def normed(row_block, gain_vec):
    inv_rms = lax.rsqrt(jnp.mean(row_block * row_block, axis=-1, keepdims=True) + EPSILON)
    return row_block * inv_rms * gain_vec


def dot(a, b, dims):
    return lax.dot_general(a, b, (dims, ((), ())), preferred_element_type=jnp.float32)


def key_count(block):
    return HALF if (block + 1) * QB <= HALF else LEN


def toeplitz(bucket_ref, table_ref, head):
    bucket_row = jnp.concatenate([row_of(bucket_ref), jnp.zeros((1, 1), jnp.int32)], axis=1)
    row = jnp.zeros(bucket_row.shape, jnp.float32)
    for bucket in range(NB):
        row = jnp.where(bucket_row == bucket, table_ref[head, bucket], row)
    rows = jnp.broadcast_to(row, (QB, DIST))
    return pltpu.roll(rows, DIST - (QB - 1), 1, stride=1, stride_axis=0)[:, :SPAN]


def row_of(ref):
    return ref[...].reshape(1, ref.shape[0])


def label_of(position, starts):
    label = jnp.zeros(position.shape, jnp.int32)
    for piece, start in enumerate(starts):
        inside = (position >= start) & (position < start + PIECE)
        label = jnp.where(inside, piece + 1, label)
    return label


def allowed_block(block, starts):
    keys = key_count(block)
    query = block * QB + lax.broadcasted_iota(jnp.int32, (QB, 1), 0)
    key = lax.broadcasted_iota(jnp.int32, (1, keys), 1)
    query_label = label_of(query, starts)
    key_label = label_of(key, starts)
    return (key <= query) | ((query_label == key_label) & (query_label > 0))


def attend_block(block, head_dim, allowed, qkv_ref, bias_ref, low_ref, high_ref):
    keys = key_count(block)
    first = LEN - QB - block * QB
    rows = pl.ds(block * QB, QB)
    outs = []
    for head in range(bias_ref.shape[0]):
        cols = pl.ds(head * head_dim, head_dim)
        raw = dot(qkv_ref[0, rows, cols], qkv_ref[1, pl.ds(0, keys), cols], ((1,), (1,)))
        scores = jnp.where(allowed, raw + bias_ref[head, :, pl.ds(first, keys)], MASKED)
        peak = jnp.max(scores, axis=-1, keepdims=True)
        powered = jnp.exp(scores - peak)
        total = jnp.sum(powered, axis=-1, keepdims=True)
        probs = (powered * (1.0 / total)).astype(jnp.bfloat16)
        if keys == HALF:
            low_ref[head, rows, :] = probs
        else:
            high_ref[head, pl.ds(block * QB - HALF, QB), :] = probs
        outs.append(dot(probs, qkv_ref[2, pl.ds(0, keys), cols], ((1,), (0,))))
    return jnp.concatenate(outs, axis=1).astype(jnp.bfloat16)


def greet(t, nt):
    barrier = pltpu.get_barrier_semaphore()
    for k in range(1, nt):
        pl.semaphore_signal(
            barrier, inc=1, device_id={"tensor": lax.rem(t + k, nt)}, device_id_type=MESH
        )
    return barrier


def line_copy(t, nt, way, step, buf, piece, pieces, send_sem, recv_sem):
    sign = 1 if way == 0 else -1
    origin = jnp.clip(t - sign * step, 0, nt - 1)
    rows = buf.shape[1] // pieces
    part = buf.at[origin, pl.ds(piece * rows, rows)]
    return pltpu.make_async_remote_copy(
        src_ref=part,
        dst_ref=part,
        send_sem=send_sem,
        recv_sem=recv_sem,
        device_id={"tensor": jnp.clip(t + sign, 0, nt - 1)},
        device_id_type=MESH,
    )


def gather_attend_kernel(
    nt, ndp, pieces, heads, head_dim, exchange,
    x_ref, cot_ref, gain_ref, gain2_ref, bucket_ref, table_ref, start_ref, *rest,
):
    weight_refs, rest = rest[: 4 if exchange else 1], rest[4 if exchange else 1 :]
    (
        first_out, cot_out, qkv_out, low_out, high_out, own_out, whole_out, middle_out, second_out,
        first, qkv, low, high, bias, att, own, whole,
        send_sem, recv_sem, swap_send, swap_recv, line_send, line_recv, chip_send, chip_recv, core_send, core_recv,
        local_sem,
    ) = rest
    t = lax.axis_index("tensor")
    d = lax.axis_index("dp")
    core = lax.rem(d, 2)
    chip = d // 2
    chips = ndp // 2
    barrier = greet(t, nt)
    greeted = nt - 1
    if exchange:
        for k in range(chips):
            peer = 2 * lax.rem(chip + k, chips) + core if k else d + 1 - 2 * core
            pl.semaphore_signal(barrier, inc=1, device_id={"dp": peer}, device_id_type=MESH)
        greeted += chips
    inner = heads * head_dim
    share = whole.shape[1] // ndp
    own_cot = pltpu.make_async_copy(cot_ref, cot_out.at[t], local_sem.at[0])
    own_cot.start()
    if exchange:
        loads = [
            pltpu.make_async_copy(weight, whole.at[t, pl.ds(i * inner, inner)], local_sem.at[1 + i])
            for i, weight in enumerate(weight_refs)
        ]
    else:
        loads = [pltpu.make_async_copy(weight_refs[0], whole, local_sem.at[1])]
    for one in loads:
        one.start()

    def slices(index, plane):
        return whole.at[plane, pl.ds(pl.multiple_of(index * share, share), share)]

    def remote(src, dst, send, recv, **target):
        return pltpu.make_async_remote_copy(
            src_ref=src, dst_ref=dst, send_sem=send, recv_sem=recv, device_id=target, device_id_type=MESH
        )

    def plane_at(q):
        return lax.rem(t + q, nt)

    def to_plane(q):
        return remote(slices(d, t), slices(d, t), line_send.at[q - 1], line_recv.at[t], tensor=plane_at(q))

    def from_plane(q):
        p = plane_at(q)
        return remote(slices(d, p), slices(d, p), line_send.at[q - 1], line_recv.at[p], tensor=p)

    def to_chip(k, q):
        part = slices(d, plane_at(q))
        return remote(
            part, part, chip_send.at[k - 1, q - 1], chip_recv.at[k - 1, q - 1], dp=2 * lax.rem(chip + k, chips) + core
        )

    def from_chip(k, q):
        peer = 2 * lax.rem(chip - k + chips, chips) + core
        part = slices(peer, plane_at(q))
        return remote(part, part, chip_send.at[k - 1, q - 1], chip_recv.at[k - 1, q - 1], dp=peer)

    def to_core(k, q):
        part = slices(2 * lax.rem(chip - k + chips, chips) + core, plane_at(q))
        return remote(part, part, core_send.at[k, q - 1], core_recv.at[k, q - 1], dp=d + 1 - 2 * core)

    def from_core(k, q):
        part = slices(2 * lax.rem(chip - k + chips, chips) + 1 - core, plane_at(q))
        return remote(part, part, core_send.at[k, q - 1], core_recv.at[k, q - 1], dp=d + 1 - 2 * core)

    first[t] = normed(x_ref[...].astype(jnp.float32), row_of(gain_ref)).astype(jnp.bfloat16)
    pl.semaphore_wait(barrier, greeted)

    def copy(way, stage, step, piece):
        buf = first if stage == 0 else cot_out
        return line_copy(
            t, nt, way, step, buf, piece, pieces,
            send_sem.at[way, stage, step, piece], recv_sem.at[way, stage, step, piece],
        )

    def landed(way, stage, step, piece):
        sign = 1 if way == 0 else -1
        buf = first if stage == 0 else cot_out
        rows = buf.shape[1] // pieces
        part = buf.at[jnp.clip(t - sign * step, 0, nt - 1), pl.ds(piece * rows, rows)]
        remote(
            part, part, send_sem.at[way, stage, step - 1, piece], recv_sem.at[way, stage, step - 1, piece],
            tensor=jnp.clip(t + sign, 0, nt - 1),
        ).wait_recv()

    ways = ((0, t, t < nt - 1), (1, nt - 1 - t, t > 0))

    def tick(k):
        for piece in range(pieces):
            for way, last, onward in ways:
                if k < nt:
                    @pl.when(k <= last)
                    def _():
                        if k > 0:
                            landed(way, 0, k, piece)

                        @pl.when(onward)
                        def _():
                            copy(way, 0, k, piece).start()

                if k > 0:
                    step = k - last - 1

                    @pl.when((step >= 1) & (step <= last))
                    def _():
                        landed(way, 1, step, piece)

                        @pl.when(onward)
                        def _():
                            copy(way, 1, step, piece).start()

                    @pl.when((step == 0) & onward)
                    def _():
                        copy(way, 0, last, piece).wait_send()
                        copy(way, 1, 0, piece).start()

    def project(origin):
        rows = pl.ds(pl.multiple_of(origin * QB, QB), QB)
        for place in range(3):
            weight = whole[t, pl.ds(place * inner, inner), :]
            qkv[place, rows, :] = dot(first[origin], weight, ((1,), (1,))).astype(jnp.bfloat16)

    tick(0)
    for one in loads:
        one.wait()
    if exchange:
        for q in range(1, nt):
            to_plane(q).start()
    project(t)
    for head in range(heads):
        bias[head] = toeplitz(bucket_ref, table_ref, head)
    own_cot.wait()
    for k in range(1, nt):
        tick(k)

        @pl.when(t - k >= 0)
        def _():
            project(t - k)

        @pl.when(t + k < nt)
        def _():
            project(t + k)

        if exchange and k == 2:
            for q in range(1, nt):
                from_plane(q).wait_recv()
                for j in range(1, chips):
                    to_chip(j, q).start()
                to_core(0, q).start()

    starts = [start_ref[0, piece] for piece in range(NPIECE)]
    keep = [
        pltpu.make_async_copy(first, first_out, local_sem.at[5]),
        pltpu.make_async_copy(qkv, qkv_out, local_sem.at[6]),
    ]
    for one in keep:
        one.start()

    def swap(block):
        return remote(att.at[block], own.at[t], swap_send.at[block], swap_recv.at[t], tensor=block)

    for block in range(LEN // QB):
        att[block] = attend_block(block, head_dim, allowed_block(block, starts), qkv, bias, low, high)

        @pl.when(t != block)
        def _():
            swap(block).start()

        @pl.when(t == block)
        def _():
            own[t] = att[block]

    late = [
        pltpu.make_async_copy(low, low_out, local_sem.at[7]),
        pltpu.make_async_copy(high, high_out, local_sem.at[8]),
    ]
    for one in late:
        one.start()
    tick(nt)
    if exchange:
        for k in range(1, chips):
            for q in range(1, nt):
                from_chip(k, q).wait_recv()
                to_core(k, q).start()
    tick(nt + 1)
    for block in range(nt):
        @pl.when(t != block)
        def _():
            remote(att.at[block], own.at[block], swap_send.at[block], swap_recv.at[block], tensor=block).wait_recv()

    if exchange:
        for k in range(chips):
            for q in range(1, nt):
                from_core(k, q).wait_recv()
    late += [
        pltpu.make_async_copy(own, own_out, local_sem.at[9]),
        pltpu.make_async_copy(whole, whole_out, local_sem.at[10]),
    ]
    for one in late[2:]:
        one.start()
    total = x_ref[...].astype(jnp.float32)
    for j in range(nt):
        total = total + dot(own[j], whole[j, pl.ds(3 * inner, inner), :], ((1,), (0,)))
    middle_out[...] = total
    second_out[...] = normed(total, row_of(gain2_ref)).astype(jnp.bfloat16)
    for k in range(nt + 2, 2 * nt):
        tick(k)
    for block in range(nt):
        @pl.when(t != block)
        def _():
            swap(block).wait_send()

    for one in keep + late:
        one.wait()
    if exchange:
        for q in range(1, nt):
            to_plane(q).wait_send()
            for k in range(1, chips):
                to_chip(k, q).wait_send()
            for k in range(chips):
                to_core(k, q).wait_send()
    for piece in range(pieces):
        for way, last, onward in ways:
            for stage in range(2):
                for step in range(nt):
                    @pl.when(onward & ((step < last) if stage == 0 else (step <= last)))
                    def _():
                        copy(way, stage, step, piece).wait_send()


def gather_attend(nt, ndp, tokens, cotangent, gain, gain2, weights, buckets, table, starts):
    heads = table.shape[0]
    rows, width = tokens.shape
    inner = weights[0].shape[0]
    low, full = jnp.bfloat16, jnp.float32
    pieces = 2
    exchange = (4 * inner // ndp) % 16 == 0
    if not exchange:
        joined = jnp.concatenate(weights, axis=0)
        part = joined.shape[0] // ndp
        mine = lax.dynamic_slice_in_dim(joined, lax.axis_index("dp") * part, part, 0)
        weights = (lax.all_gather(mine, ("tensor", "dp"), axis=0, tiled=True).reshape(nt, *joined.shape),)
    chips = ndp // 2
    smem = pl.BlockSpec(memory_space=pltpu.SMEM)
    hbm = pl.BlockSpec(memory_space=pl.ANY)
    vmem = pl.BlockSpec(memory_space=pltpu.VMEM)
    shapes = (
        (nt, rows, width), (nt, rows, width), (3, LEN, inner), (heads, HALF, HALF), (heads, HALF, LEN),
        (nt, rows, inner), (nt, 4 * inner, width),
    )
    dma = pltpu.SemaphoreType.DMA
    return pl.pallas_call(
        functools.partial(gather_attend_kernel, nt, ndp, pieces, heads, inner // heads, exchange),
        out_shape=tuple(jax.ShapeDtypeStruct(shape, low) for shape in shapes)
        + (jax.ShapeDtypeStruct((rows, width), full), jax.ShapeDtypeStruct((rows, width), low)),
        in_specs=[vmem, hbm, vmem, vmem, vmem, smem, smem] + [hbm] * len(weights),
        out_specs=(hbm,) * 7 + (vmem, vmem),
        scratch_shapes=[
            pltpu.VMEM((nt, rows, width), low),
            pltpu.VMEM((3, LEN, inner), low),
            pltpu.VMEM((heads, HALF, HALF), low),
            pltpu.VMEM((heads, HALF, LEN), low),
            pltpu.VMEM((heads, QB, SPAN), full),
            pltpu.VMEM((nt, rows, inner), low),
            pltpu.VMEM((nt, rows, inner), low),
            pltpu.VMEM((nt, 4 * inner, width), low),
            dma((2, 2, nt, pieces)), dma((2, 2, nt, pieces)), dma((nt,)), dma((nt,)),
            dma((nt - 1,)), dma((nt,)), dma((chips - 1, nt - 1)), dma((chips - 1, nt - 1)),
            dma((chips, nt - 1)), dma((chips, nt - 1)), dma((11,)),
        ],
        compiler_params=pltpu.CompilerParams(
            vmem_limit_bytes=VMEM_LIMIT, collective_id=0, has_side_effects=True
        ),
        name="gather_attend",
    )(tokens, cotangent, gain, gain2, buckets, table, starts, *weights)


def fold_diagonals(grid):
    rows = QB // 2
    width = grid.shape[1]
    while rows >= 1:
        grid = grid[:rows] + pltpu.roll(grid[rows : 2 * rows], width - rows, 1)
        rows //= 2
    return grid


def gelu_parts(v):
    root, cubic = 0.7978845608028654, 0.044715
    square = v * v
    bend = jnp.tanh(root * v * (1.0 + cubic * square))
    half = 0.5 * (1.0 + bend)
    slope = half + 0.5 * v * (1.0 - bend * bend) * root * (1.0 + 3.0 * cubic * square)
    return v * half, slope


def feed_kernel(
    nt, ndp, pieces, fused,
    gain_ref, middle_hbm, second_hbm, cot_own_hbm, whole_hbm, cot_hbm, wg_hbm, wu_hbm, wd_hbm,
    base_out, gm_out, gain_out, ga_out, lo_out, grads_out, *rest,
):
    if fused:
        down_out, *rest = rest
    (
        middle, cot_own_ref, buf, cot, wg, wu, wd, hid, gg, gu, gs, lo, wo, mate_in, acc_in, far_in, grads, lo_in, *rest,
    ) = rest
    *rest, send_sem, recv_sem, rs_send, rs_recv, lo_send, lo_recv, local_sem = rest
    t = lax.axis_index("tensor")
    d = lax.axis_index("dp")
    core = lax.rem(d, 2)
    chips = ndp // 2
    barrier = greet(t, nt)
    own_load = pltpu.make_async_copy(second_hbm, buf.at[t], local_sem.at[11])
    own_load.start()
    if fused:
        sums, pair_send, pair_recv, chip_send, chip_recv = rest
        chip = d // 2
        for k in range(chips):
            peer = 2 * lax.rem(chip + k, chips) + core if k else d + 1 - 2 * core
            pl.semaphore_signal(barrier, inc=1, device_id={"dp": peer}, device_id_type=MESH)
    loads = [
        pltpu.make_async_copy(a, b, local_sem.at[i])
        for i, (a, b) in enumerate(((wg_hbm, wg), (wu_hbm, wu), (wd_hbm, wd), (cot_hbm, cot)))
    ]
    for one in loads:
        one.start()
    row_count = middle.shape[0]
    size = row_count // pieces
    inner = wo.shape[1]
    wo_load = pltpu.make_async_copy(whole_hbm.at[:, pl.ds(3 * inner, inner)], wo, local_sem.at[4])
    wo_load.start()
    late_loads = [
        pltpu.make_async_copy(middle_hbm, middle, local_sem.at[9]),
        pltpu.make_async_copy(cot_own_hbm, cot_own_ref, local_sem.at[10]),
    ]
    for one in late_loads:
        one.start()
    keep = []
    own_load.wait()
    pl.semaphore_wait(barrier, nt - 1 + chips * fused)
    mate = t + 1 - 2 * lax.rem(t, 2)
    is_end = (t == 0) | (t == nt - 1)
    ways = ((0, t, t < nt - 1), (1, nt - 1 - t, t > 0))

    def copy(way, step, piece):
        return line_copy(
            t, nt, way, step, buf, piece, pieces,
            send_sem.at[way, step, piece], recv_sem.at[way, step, piece],
        )

    def landed(way, step, piece):
        sign = 1 if way == 0 else -1
        part = buf.at[jnp.clip(t - sign * step, 0, nt - 1), pl.ds(piece * size, size)]
        pltpu.make_async_remote_copy(
            src_ref=part, dst_ref=part,
            send_sem=send_sem.at[way, step - 1, piece], recv_sem=recv_sem.at[way, step - 1, piece],
            device_id={"tensor": jnp.clip(t + sign, 0, nt - 1)}, device_id_type=MESH,
        ).wait_recv()

    def remote(src, dst, target, send, recv):
        return pltpu.make_async_remote_copy(
            src_ref=src, dst_ref=dst, send_sem=send, recv_sem=recv,
            device_id={"tensor": target}, device_id_type=MESH,
        )

    def to_mate(piece):
        rows = pl.ds(piece * size, size)
        return remote(gs.at[mate, rows], mate_in.at[rows], mate, rs_send.at[0, piece], rs_recv.at[0, piece])

    def to_acc(origin, piece):
        rows = pl.ds(piece * size, size)
        j = lax.rem(origin, 2)
        return remote(
            gs.at[origin, rows], acc_in.at[j, rows], mate, rs_send.at[1 + j, piece], rs_recv.at[1 + j, piece]
        )

    def to_far(origin, piece):
        rows = pl.ds(piece * size, size)
        j = lax.rem(origin, 2)
        return remote(
            gs.at[origin, rows], far_in.at[rows], origin, rs_send.at[3 + j, piece], rs_recv.at[3, piece]
        )

    def feed(origin, piece):
        rows = pl.ds(pl.multiple_of(piece * size, size), size)
        flat = pl.ds(pl.multiple_of(origin * row_count + piece * size, size), size)
        normal = buf[origin, rows]
        gate = dot(normal, wg[...], ((1,), (1,)))
        up = dot(normal, wu[...], ((1,), (1,)))
        grad_hidden = dot(cot[origin, rows], wd[...], ((1,), (1,)))
        act, slope = gelu_parts(gate)
        hid[flat, :] = (act * up).astype(jnp.bfloat16)
        grad_gate = (grad_hidden * up * slope).astype(jnp.bfloat16)
        grad_up = (grad_hidden * act).astype(jnp.bfloat16)
        gg[flat, :] = grad_gate
        gu[flat, :] = grad_up
        gs[origin, rows] = (
            dot(grad_gate, wg[...], ((1,), (0,))) + dot(grad_up, wu[...], ((1,), (0,)))
        ).astype(jnp.bfloat16)

    for piece in range(pieces):
        for way, last, onward in ways:
            @pl.when(onward)
            def _():
                copy(way, 0, piece).start()

    for one in loads:
        one.wait()

    def unit(u, carry):
        step = u // pieces
        piece = lax.rem(u, pieces)

        @pl.when(step > 0)
        def _():
            for way, last, onward in ways:
                @pl.when(step <= last)
                def _():
                    landed(way, step, piece)

                    @pl.when(onward)
                    def _():
                        copy(way, step, piece).start()

        def side(way, carry):
            origin = t - (1 - 2 * way) * step
            there = (origin >= 0) & (origin < nt) & ((step > 0) | (way == 0))

            @pl.when(there)
            def _():
                feed(origin, piece)

                @pl.when(origin == mate)
                def _():
                    to_mate(piece).start()

                @pl.when((origin != mate) & (origin != t) & is_end)
                def _():
                    to_acc(origin, piece).start()

            return carry

        return lax.fori_loop(0, 2, side, carry)

    lax.fori_loop(0, nt * pieces, unit, 0)

    near = jnp.where(t < nt // 2, nt // 2, nt // 2 - 1)
    far = jnp.where(t < nt // 2, nt - 1, 0)

    def pass_on(origin, piece):
        @pl.when(jnp.logical_not(is_end))
        def _():
            to_acc(origin, piece).wait_recv()
            rows = pl.ds(piece * size, size)
            j = lax.rem(origin, 2)
            gs[origin, rows] = (
                gs[origin, rows].astype(jnp.float32) + acc_in[j, rows].astype(jnp.float32)
            ).astype(jnp.bfloat16)
            to_far(origin, piece).start()

    span = 256
    flat_rows = nt * row_count
    spans = buf.shape[2] // span

    def columns(ref, i):
        cols = pl.ds(pl.multiple_of(i * span, span), span)
        return ref[:, :, cols].reshape(flat_rows, span)

    share = buf.shape[2] // ndp

    def block_rows(index):
        return pl.ds(pl.multiple_of(index * share, share), share)

    def pair(which, c):
        return pltpu.make_async_remote_copy(
            src_ref=grads.at[which, block_rows(2 * c + 1 - core)], dst_ref=sums.at[which, c],
            send_sem=pair_send.at[which, c], recv_sem=pair_recv.at[which, c],
            device_id={"dp": d + 1 - 2 * core}, device_id_type=MESH,
        )

    def down_copy(k):
        to = lax.rem(chip + k, chips)
        return pltpu.make_async_remote_copy(
            src_ref=sums.at[2, to], dst_ref=down_out.at[k - 1],
            send_sem=chip_send.at[k - 1], recv_sem=chip_recv.at[k - 1],
            device_id={"dp": 2 * to + core}, device_id_type=MESH,
        )

    def pair_start(*which):
        if fused:
            for w in which:
                for c in range(chips):
                    pair(w, c).start()

    def pair_sum(which):
        if fused:
            for c in range(chips):
                pair(which, c).wait_recv()
                sums[which, c] = (
                    grads[which, block_rows(2 * c + core)].astype(jnp.float32) + sums[which, c].astype(jnp.float32)
                ).astype(jnp.bfloat16)
            if which == 2:
                for k in range(1, chips):
                    down_copy(k).start()
            one = pltpu.make_async_copy(sums.at[which], grads_out.at[which], local_sem.at[6 + which])
        else:
            one = pltpu.make_async_copy(grads.at[which], grads_out.at[which], local_sem.at[6 + which])
        one.start()
        keep.append(one)

    def down_cols(i, carry):
        rows = pl.ds(pl.multiple_of(i * span, span), span)
        grads[2, rows, :] = dot(columns(cot, i), hid[...], ((0,), (0,))).astype(jnp.bfloat16)
        return carry

    def gate_up_cols(i, carry):
        rows = pl.ds(pl.multiple_of(i * span, span), span)
        left = columns(buf, i)
        grads[0, rows, :] = dot(left, gg[...], ((0,), (0,))).astype(jnp.bfloat16)
        grads[1, rows, :] = dot(left, gu[...], ((0,), (0,))).astype(jnp.bfloat16)
        return carry

    def down_rows(i, carry):
        rows = pl.ds(pl.multiple_of(i * row_count, row_count), row_count)
        lo[i] = dot(hid[rows, :], wd[...], ((1,), (0,))).astype(jnp.bfloat16)
        return carry

    def lo_acc(piece):
        rows = pl.ds(piece * size, size)
        return remote(lo.at[far, rows], lo_in.at[rows], mate, lo_send.at[piece], lo_recv.at[piece])

    pass_on(near, 0)
    lax.fori_loop(0, nt, down_rows, 0)

    @pl.when(is_end)
    def _():
        for piece in range(pieces):
            lo_acc(piece).start()

    pass_on(near, 1)
    lax.fori_loop(0, spans, down_cols, 0)
    pair_start(2)
    pass_on(far, 0)
    lax.fori_loop(0, spans // 2, gate_up_cols, 0)
    pair_sum(2)
    pass_on(far, 1)
    lax.fori_loop(spans // 2, spans, gate_up_cols, 0)
    pair_start(0, 1)
    for one in late_loads:
        one.wait()

    wo_load.wait()
    for piece in range(pieces):
        rows = pl.ds(piece * size, size)
        to_mate(piece).wait_recv()
        remote(gs.at[t, rows], far_in.at[rows], mate, rs_send.at[3, piece], rs_recv.at[3, piece]).wait_recv()
        grad_second = (
            gs[t, rows].astype(jnp.float32)
            + mate_in[rows].astype(jnp.float32)
            + far_in[rows].astype(jnp.float32)
        )
        mid = middle[rows]
        inv = lax.rsqrt(jnp.mean(mid * mid, axis=-1, keepdims=True) + EPSILON)
        scaled = row_of(gain_ref) * grad_second
        along = jnp.mean(scaled * mid, axis=-1, keepdims=True)
        grad_middle = cot_own_ref[rows].astype(jnp.float32) + inv * scaled - mid * (inv * inv * inv * along)
        gm_out[rows] = grad_middle
        part = jnp.sum(grad_second * mid * inv, axis=0, keepdims=True)
        if piece == 0:
            gain_out[...] = part
        else:
            gain_out[...] += part
        grad_low = grad_middle.astype(jnp.bfloat16)
        for j in range(nt):
            ga_out[j, rows] = dot(grad_low, wo[j], ((1,), (1,))).astype(jnp.bfloat16)

    pair_sum(0)
    pair_sum(1)
    base_out[...] = middle[...] + lo[t].astype(jnp.float32)

    @pl.when(jnp.logical_not(is_end))
    def _():
        for piece in range(pieces):
            lo_acc(piece).wait_recv()
        lo[far] = (lo[far].astype(jnp.float32) + lo_in[...].astype(jnp.float32)).astype(jnp.bfloat16)

    keep.append(pltpu.make_async_copy(lo, lo_out, local_sem.at[5]))
    keep[-1].start()
    for one in keep:
        one.wait()
    for piece in range(pieces):
        for way, last, onward in ways:
            for step in range(nt):
                @pl.when(onward & (step <= last))
                def _():
                    copy(way, step, piece).wait_send()

        @pl.when(is_end)
        def _():
            lo_acc(piece).wait_send()

        to_mate(piece).wait_send()
        for origin in (near, far):
            @pl.when(is_end)
            def _():
                to_acc(origin, piece).wait_send()

            @pl.when(jnp.logical_not(is_end))
            def _():
                to_far(origin, piece).wait_send()

    if fused:
        for which in range(3):
            for c in range(chips):
                pair(which, c).wait_send()
        for k in range(1, chips):
            down_copy(k).wait()


def feed(nt, ndp, middle, second, gain, cotangent, whole, cot_all, gate_weight, up_weight, down_weight):
    rows, width = middle.shape
    hidden = gate_weight.shape[0]
    low, full = jnp.bfloat16, jnp.float32
    pieces = 2
    hbm = pl.BlockSpec(memory_space=pl.ANY)
    vmem = pl.BlockSpec(memory_space=pltpu.VMEM)
    inner = whole.shape[1] // 4
    dma = pltpu.SemaphoreType.DMA
    shape = jax.ShapeDtypeStruct
    share, chips = width // ndp, ndp // 2
    fused = share % 16 == 0
    sums = (3, chips, share, hidden)
    pairs = [
        pltpu.VMEM(sums, low), dma((3, chips)), dma((3, chips)), dma((chips - 1,)), dma((chips - 1,))
    ] if fused else []
    return pl.pallas_call(
        functools.partial(feed_kernel, nt, ndp, pieces, fused),
        out_shape=(
            shape((rows, width), full), shape((rows, width), full), shape((1, width), full),
            shape((nt, rows, inner), low), shape((nt, rows, width), low), shape(sums if fused else (3, width, hidden), low),
        ) + (shape((chips - 1, share, hidden), low),) * fused,
        in_specs=[vmem] + [hbm] * 8,
        out_specs=(vmem, vmem, vmem, vmem, hbm, hbm) + (hbm,) * fused,
        scratch_shapes=[
            pltpu.VMEM((rows, width), full), pltpu.VMEM((rows, width), low),
            pltpu.VMEM((nt, rows, width), low), pltpu.VMEM((nt, rows, width), low),
            pltpu.VMEM((hidden, width), low), pltpu.VMEM((hidden, width), low), pltpu.VMEM((hidden, width), low),
            pltpu.VMEM((nt * rows, hidden), low), pltpu.VMEM((nt * rows, hidden), low), pltpu.VMEM((nt * rows, hidden), low),
            pltpu.VMEM((nt, rows, width), low), pltpu.VMEM((nt, rows, width), low),
            pltpu.VMEM((nt, inner, width), low),
            pltpu.VMEM((rows, width), low), pltpu.VMEM((2, rows, width), low), pltpu.VMEM((rows, width), low),
            pltpu.VMEM((3, width, hidden), low), pltpu.VMEM((rows, width), low), *pairs,
            dma((2, nt, pieces)), dma((2, nt, pieces)), dma((5, pieces)), dma((4, pieces)), dma((pieces,)), dma((pieces,)),
            dma((12,)),
        ],
        compiler_params=pltpu.CompilerParams(
            vmem_limit_bytes=VMEM_LIMIT, collective_id=1, has_side_effects=True
        ),
        name="feed",
    )(gain, middle, second, cotangent, whole, cot_all, gate_weight, up_weight, down_weight)


def back_kernel(
    nt, ndp, pieces, heads, head_dim, grad_type, fused,
    ga_ref, gain_ref, gain2_ref, gm_hbm, x_hbm, own_hbm,
    qkv_hbm, low_hbm, high_hbm, first_hbm, weight_hbm, lo_hbm, *rest,
):
    if fused:
        feed_hbm, *rest = rest
    input_out, q_out, k_out, v_out, o_out, gains_in, dist_in, far_in, mate_in, *rest = rest
    if fused:
        feed_in, *rest = rest
    (
        gm_ref, x_ref, own_ref,
        ga_in, qkv, low, high, first, weight, lo, acc_in,
        gq, gq_in, diag, dk_acc, dv_acc,
        og, og_sum, og_chip, og_line, og_line_in, pg, pg_sum, pg_chip,
        gains_line, gains_own, dist_own,
        swap_send, swap_recv, back_send, back_recv, lo_send, lo_recv,
        pair_send, pair_recv, chip_send, chip_recv, line_send, line_recv,
        gl_send, gl_recv, gd_send, gd_recv, dist_send, dist_recv, local_sem, *rest,
    ) = rest
    if fused:
        feed_send, feed_recv = rest
    t = lax.axis_index("tensor")
    d = lax.axis_index("dp")
    core = lax.rem(d, 2)
    chip = d // 2
    chips = ndp // 2
    barrier = greet(t, nt)
    for k in range(1, ndp):
        pl.semaphore_signal(
            barrier, inc=1, device_id={"dp": lax.rem(d + k, ndp)}, device_id_type=MESH
        )
    mate = t + 1 - 2 * lax.rem(t, 2)
    is_end = (t == 0) | (t == nt - 1)
    near = jnp.where(t < nt // 2, nt // 2, nt // 2 - 1)
    far = jnp.where(t < nt // 2, nt - 1, 0)
    loads = [
        pltpu.make_async_copy(a, b, local_sem.at[i])
        for i, (a, b) in enumerate(
            ((qkv_hbm, qkv), (low_hbm, low), (high_hbm, high), (first_hbm, first),
             (weight_hbm.at[:, pl.ds(0, weight.shape[1])], weight),
             (lo_hbm.at[near], lo.at[0]), (lo_hbm.at[far], lo.at[1]), (lo_hbm.at[mate], lo.at[2]),
             (gm_hbm, gm_ref), (x_hbm, x_ref), (own_hbm, own_ref))
        )
    ]
    for one in loads:
        one.start()
    others = (far, near, mate)
    row_count, width = x_ref.shape
    inner = heads * head_dim
    size = row_count // pieces
    share = width // ndp
    full = jnp.float32

    def remote(src, dst, send, recv, **target):
        return pltpu.make_async_remote_copy(
            src_ref=src, dst_ref=dst, send_sem=send, recv_sem=recv,
            device_id=target, device_id_type=MESH,
        )

    def swap(peer):
        return remote(ga_ref.at[peer], ga_in.at[t], swap_send.at[peer], swap_recv.at[t], tensor=peer)

    def swap_in(peer):
        return remote(ga_ref.at[peer], ga_in.at[peer], swap_send.at[peer], swap_recv.at[peer], tensor=peer)

    def lo_acc(piece):
        rows = pl.ds(piece * size, size)
        return remote(lo.at[0, rows], acc_in.at[rows], lo_send.at[0, piece], lo_recv.at[0, piece], tensor=mate)

    def lo_final(place, origin, piece):
        rows = pl.ds(piece * size, size)
        return remote(
            lo.at[place, rows], far_in.at[rows], lo_send.at[place, piece], lo_recv.at[1, piece], tensor=origin
        )

    def lo_mate(piece):
        rows = pl.ds(piece * size, size)
        return remote(lo.at[2, rows], mate_in.at[rows], lo_send.at[2, piece], lo_recv.at[2, piece], tensor=mate)

    pl.semaphore_wait(barrier, nt - 1 + ndp - 1)
    for peer in others:
        swap(peer).start()
    ga_in[t] = ga_ref[t]
    if fused:
        def feed_copy(which, k):
            to = lax.rem(chip + k, chips)
            return remote(
                feed_hbm.at[which, to], feed_in.at[k - 1, which],
                feed_send.at[k - 1, which], feed_recv.at[k - 1, which], dp=2 * to + core,
            )

        for which in range(2):
            for k in range(1, chips):
                feed_copy(which, k).start()

    def block_rows(index):
        return pl.ds(pl.multiple_of(index * share, share), share)

    def pair(kind, c):
        grads, landing = ((og, og_sum), (pg, pg_sum))[kind]
        return remote(
            grads.at[block_rows(2 * c + 1 - core)], landing.at[c],
            pair_send.at[kind, c], pair_recv.at[kind, c], dp=d + 1 - 2 * core,
        )

    def chip_copy(kind, k):
        sums, landing = ((og_sum, og_chip), (pg_sum, pg_chip))[kind]
        to = lax.rem(chip + k, chips)
        return remote(
            sums.at[to], landing.at[k - 1], chip_send.at[kind, k - 1], chip_recv.at[kind, k - 1], dp=2 * to + core
        )

    def pair_sum(kind):
        grads, sums = ((og, og_sum), (pg, pg_sum))[kind]
        for c in range(chips):
            pair(kind, c).wait_recv()
            sums[c] = (grads[block_rows(2 * c + core)].astype(full) + sums[c].astype(full)).astype(grad_type)
        for k in range(1, chips):
            chip_copy(kind, k).start()

    def chip_sum(kind):
        sums, landing = ((og_sum, og_chip), (pg_sum, pg_chip))[kind]
        total = sums[chip].astype(full)
        for k in range(1, chips):
            chip_copy(kind, k).wait_recv()
            total = total + landing[k - 1].astype(full)
        return total

    for one in loads[5:]:
        one.wait()
    span = 256
    spans = width // span
    own = jnp.concatenate([own_ref[j] for j in range(nt)], axis=1)
    for i in range(spans):
        left = gm_ref[:, pl.ds(i * span, span)].astype(jnp.bfloat16)
        og[pl.ds(i * span, span), :] = dot(left, own, ((0,), (0,))).astype(grad_type)
    for c in range(chips):
        pair(0, c).start()

    for i in range(3):
        loads[i].wait()
    blocks = LEN // QB
    diag[...] = jnp.zeros_like(diag)
    for block in reversed(range(blocks)):
        keys = key_count(block)
        rows = pl.ds(block * QB, QB)
        first_col = LEN - block * QB

        for waited in (1, 0) if block == 1 else () if block == 0 else (block,):
            @pl.when(t != waited)
            def _():
                swap_in(waited).wait_recv()

        if block == 1:
            for piece in range(pieces):
                @pl.when(is_end)
                def _():
                    lo_acc(piece).start()

                @pl.when(jnp.logical_not(is_end))
                def _():
                    lo_final(1, far, piece).start()

        parts = []
        for head in range(heads):
            cols = pl.ds(head * head_dim, head_dim)
            if keys == HALF:
                probs_low = low[head, rows, :]
            else:
                probs_low = high[head, pl.ds(block * QB - HALF, QB), :]
            probs = probs_low.astype(full)
            do = ga_in[block, :, cols]
            grad_probs = dot(do, qkv[2, pl.ds(0, keys), cols], ((1,), (1,)))
            weighted = jnp.sum(probs * grad_probs, axis=-1, keepdims=True)
            grad_low = (probs * (grad_probs - weighted)).astype(jnp.bfloat16)
            reach = pl.ds(first_col, keys)
            diag[head, :, reach] = diag[head, :, reach] + grad_low.astype(full)
            parts.append(dot(grad_low, qkv[1, pl.ds(0, keys), cols], ((1,), (0,))))
            key_part = dot(grad_low, qkv[0, rows, cols], ((0,), (0,)))
            value_part = dot(probs_low, do, ((0,), (0,)))
            if block == blocks - 1:
                dk_acc[head] = key_part
                dv_acc[head] = value_part
            else:
                dk_acc[head, pl.ds(0, keys), :] += key_part
                dv_acc[head, pl.ds(0, keys), :] += value_part
        gq[rows, pl.ds(0, inner)] = jnp.concatenate(parts, axis=1).astype(jnp.bfloat16)
        if block == 1:
            pair_sum(0)
    for block in range(blocks):
        rows = pl.ds(block * QB, QB)
        sides = [acc[head, rows, :] for acc in (dk_acc, dv_acc) for head in range(heads)]
        gq[rows, pl.ds(inner, 2 * inner)] = jnp.concatenate(sides, axis=1).astype(jnp.bfloat16)

    def token_rows(peer):
        return pl.ds(pl.multiple_of(peer * row_count, row_count), row_count)

    def give(peer):
        return remote(
            gq.at[token_rows(peer)], gq_in.at[t], back_send.at[peer], back_recv.at[t], tensor=peer
        )

    def taken(peer):
        return remote(
            gq.at[token_rows(peer)], gq_in.at[peer], back_send.at[peer], back_recv.at[peer], tensor=peer
        )

    for peer in others:
        give(peer).start()
    for head in range(heads):
        dist_own[pl.ds(head, 1), :] = fold_diagonals(diag[head])
    dist_keep = pltpu.make_async_copy(dist_own, dist_in.at[d], local_sem.at[11])
    dist_keep.start()

    def dist_copy(k):
        return remote(
            dist_own, dist_in.at[d], dist_send.at[k - 1], dist_recv.at[d], dp=lax.rem(d + k, ndp)
        )

    for k in range(1, ndp):
        dist_copy(k).start()
    loads[3].wait()
    for i in range(spans):
        cols = pl.ds(i * span, span)
        left = first[:, :, cols].reshape(nt * row_count, span)
        pg[cols, :] = dot(left, gq[...], ((0,), (0,))).astype(grad_type)
    for c in range(chips):
        pair(1, c).start()
    total = chip_sum(0)
    for j in range(nt):
        og_line[j] = total[:, j * inner : (j + 1) * inner].astype(grad_type)

    def line_copy_out(peer):
        return remote(og_line.at[peer], og_line_in.at[t], line_send.at[peer], line_recv.at[t], tensor=peer)

    def line_in(peer):
        return remote(og_line.at[peer], og_line_in.at[peer], line_send.at[peer], line_recv.at[peer], tensor=peer)

    for peer in others:
        line_copy_out(peer).start()
    pair_sum(1)

    @pl.when(jnp.logical_not(is_end))
    def _():
        for piece in range(pieces):
            lo_acc(piece).wait_recv()
        lo[0] = (lo[0].astype(full) + acc_in[...].astype(full)).astype(jnp.bfloat16)

    loads[4].wait()
    inputs = x_ref[...].astype(full)
    inv = lax.rsqrt(jnp.mean(inputs * inputs, axis=-1, keepdims=True) + EPSILON)
    grad_first = dot(gq[token_rows(t)], weight[t], ((1,), (0,)))
    for peer in (mate, near, far):
        taken(peer).wait_recv()
        if peer is far:
            for piece in range(pieces):
                lo_mate(piece).start()

                @pl.when(jnp.logical_not(is_end))
                def _():
                    lo_final(0, near, piece).start()

        grad_first = grad_first + dot(gq_in[peer], weight[peer], ((1,), (0,)))
    scaled = row_of(gain_ref) * grad_first
    along = jnp.mean(scaled * inputs, axis=-1, keepdims=True)
    gains_line[t, pl.ds(0, 1), :] = jnp.sum(grad_first * inputs * inv, axis=0, keepdims=True)
    gains_line[t, pl.ds(1, 1), :] = gain2_ref[...]

    def gain_copy(peer):
        return remote(gains_line.at[t], gains_line.at[t], gl_send.at[peer], gl_recv.at[t], tensor=peer)

    def gain_landed(peer):
        return remote(gains_line.at[peer], gains_line.at[peer], gl_send.at[peer], gl_recv.at[peer], tensor=peer)

    for peer in others:
        gain_copy(peer).start()
    input_out[...] = (gm_ref[...] + inv * scaled - inputs * (inv * inv * inv * along)).astype(jnp.bfloat16)
    for peer in others:
        gain_landed(peer).wait_recv()
    gains_own[...] = gains_line[0] + gains_line[1] + gains_line[2] + gains_line[3]
    gains_keep = pltpu.make_async_copy(gains_own, gains_in.at[d], local_sem.at[12])
    gains_keep.start()

    def gains_copy(k):
        return remote(
            gains_own, gains_in.at[d], gd_send.at[k - 1], gd_recv.at[d], dp=lax.rem(d + k, ndp)
        )

    for k in range(1, ndp):
        gains_copy(k).start()
    total = chip_sum(1)
    q_out[...] = total[:, :inner]
    k_out[...] = total[:, inner : 2 * inner]
    v_out[...] = total[:, 2 * inner :]
    total = og_line[t].astype(full)
    for peer in others:
        line_in(peer).wait_recv()
        total = total + og_line_in[peer].astype(full)
    o_out[...] = total

    def others_of(landing, send, recv):
        for k in range(1, ndp):
            peer = lax.rem(d + k, ndp)
            remote(landing.at[peer], landing.at[peer], send.at[k - 1], recv.at[peer], dp=peer).wait_recv()

    others_of(dist_in, dist_send, dist_recv)
    if fused:
        for which in range(2):
            for k in range(1, chips):
                feed_copy(which, k).wait_recv()
    for piece in range(pieces):
        lo_final(0, near, piece).wait_recv()
        lo_mate(piece).wait_recv()
    others_of(gains_in, gd_send, gd_recv)
    dist_keep.wait()
    gains_keep.wait()

    for peer in others:
        swap(peer).wait_send()
        give(peer).wait_send()
        line_copy_out(peer).wait_send()
        gain_copy(peer).wait_send()
    for piece in range(pieces):
        lo_mate(piece).wait_send()

        @pl.when(is_end)
        def _():
            lo_acc(piece).wait_send()

        @pl.when(jnp.logical_not(is_end))
        def _():
            lo_final(0, near, piece).wait_send()
            lo_final(1, far, piece).wait_send()

    if fused:
        for which in range(2):
            for k in range(1, chips):
                feed_copy(which, k).wait_send()
    for kind in range(2):
        for c in range(chips):
            pair(kind, c).wait_send()
        for k in range(1, chips):
            chip_copy(kind, k).wait_send()
    for k in range(1, ndp):
        dist_copy(k).wait_send()
        gains_copy(k).wait_send()


def back(nt, ndp, grad_attended, grad_middle, tokens, gain, gain2_part, attended, qkv, probs_low, probs_high, first_all, weights, layer_parts, feed_grads):
    rows, width = tokens.shape
    heads = probs_low.shape[0]
    inner = qkv.shape[2]
    head_dim = inner // heads
    low, full = jnp.bfloat16, jnp.float32
    pieces = 2
    share, chips = width // ndp, ndp // 2
    grad_type = low if share % 16 == 0 else full
    hbm = pl.BlockSpec(memory_space=pl.ANY)
    vmem = pl.BlockSpec(memory_space=pltpu.VMEM)
    dma = pltpu.SemaphoreType.DMA
    shape = jax.ShapeDtypeStruct
    reach = SPAN + QB
    scratch = lambda *dims, kind=low: pltpu.VMEM(dims, kind)
    part = shape((share, inner), full)
    fused = feed_grads.ndim == 4
    hidden = feed_grads.shape[-1]
    feeds = [dma((chips - 1, 2)), dma((chips - 1, 2))] if fused else []
    return pl.pallas_call(
        functools.partial(back_kernel, nt, ndp, pieces, heads, head_dim, grad_type, fused),
        out_shape=(
            shape((rows, width), low), part, part, part, part,
            shape((ndp, 2, width), full), shape((ndp, heads, reach), full),
            shape((rows, width), low), shape((rows, width), low),
        ) + (shape((chips - 1, 2, share, hidden), low),) * fused,
        in_specs=[vmem] * 3 + [hbm] * (9 + fused),
        out_specs=(vmem,) * 5 + (hbm,) * (4 + fused),
        scratch_shapes=[
            scratch(rows, width, kind=full), scratch(rows, width), scratch(nt, rows, inner),
            scratch(nt, rows, inner), scratch(3, LEN, inner), scratch(heads, HALF, HALF), scratch(heads, HALF, LEN),
            scratch(nt, rows, width), scratch(nt, 3 * inner, width), scratch(3, rows, width), scratch(rows, width),
            scratch(nt * rows, 3 * inner), scratch(nt, rows, 3 * inner), scratch(heads, QB, reach, kind=full),
            scratch(heads, LEN, head_dim, kind=full), scratch(heads, LEN, head_dim, kind=full),
            scratch(width, nt * inner, kind=grad_type), scratch(chips, share, nt * inner, kind=grad_type),
            scratch(chips - 1, share, nt * inner, kind=grad_type),
            scratch(nt, share, inner, kind=grad_type), scratch(nt, share, inner, kind=grad_type),
            scratch(width, 3 * inner, kind=grad_type), scratch(chips, share, 3 * inner, kind=grad_type),
            scratch(chips - 1, share, 3 * inner, kind=grad_type),
            scratch(nt, 2, width, kind=full), scratch(2, width, kind=full), scratch(heads, reach, kind=full),
            dma((nt,)), dma((nt,)), dma((nt,)), dma((nt,)), dma((3, pieces)), dma((3, pieces)),
            dma((2, chips)), dma((2, chips)), dma((2, chips - 1)), dma((2, chips - 1)), dma((nt,)), dma((nt,)),
            dma((nt,)), dma((nt,)), dma((ndp - 1,)), dma((ndp,)), dma((ndp - 1,)), dma((ndp,)), dma((13,)), *feeds,
        ],
        compiler_params=pltpu.CompilerParams(
            vmem_limit_bytes=VMEM_LIMIT, collective_id=2, has_side_effects=True
        ),
        cost_estimate=pl.CostEstimate(flops=60 * 10**9, bytes_accessed=200 * 10**6, transcendentals=0),
        name="back",
    )(
        grad_attended, gain, gain2_part, grad_middle, tokens, attended,
        qkv, probs_low, probs_high, first_all, weights, layer_parts, *((feed_grads,) if fused else ()),
    )


def finish_kernel(
    chips, fused,
    bucket_ref, base_ref, far_ref, mate_ref, input_ref, q_ref, k_ref, v_ref, o_ref, gains_ref, dist_ref, *rest,
):
    if fused:
        down_ref, feed_ref, feed_hbm, *rest = rest
    layer_out, input_out, gain_out, q_out, k_out, v_out, o_out, table_out, gain2_out, *rest = rest
    full = jnp.float32
    if fused:
        *feed_outs, own, sem = rest
        load = pltpu.make_async_copy(feed_hbm.at[:, lax.axis_index("dp") // 2], own, sem)
        load.start()
    layer_out[...] = (base_ref[...] + far_ref[...].astype(full) + mate_ref[...].astype(full)).astype(jnp.bfloat16)
    input_out[...] = input_ref[...]
    for a, b in ((q_ref, q_out), (k_ref, k_out), (v_ref, v_out), (o_ref, o_out)):
        b[...] = a[...]
    gains, dist = gains_ref[0], dist_ref[0]
    for k in range(1, gains_ref.shape[0]):
        gains = gains + gains_ref[k]
        dist = dist + dist_ref[k]
    gain_out[...] = gains[0:1].reshape(gain_out.shape)
    gain2_out[...] = gains[1:2].reshape(gain2_out.shape)
    reach = dist.shape[1]
    shifted = jnp.concatenate([jnp.zeros((1, 1), jnp.int32), row_of(bucket_ref)], axis=1)[:, :reach]
    hot = (lax.broadcasted_iota(jnp.int32, (NB, reach), 0) == shifted).astype(full)
    table_out[...] = lax.dot_general(
        dist, hot, (((1,), (1,)), ((), ())), precision=HIGHEST, preferred_element_type=full
    )
    if fused:
        load.wait()
        for which in range(3):
            total = own[which].astype(full)
            for k in range(chips - 1):
                total = total + (down_ref[k] if which == 2 else feed_ref[k, which]).astype(full)
            feed_outs[which][...] = total


def finish(ndp, buckets, base, outs, down_in, feed_grads):
    fused = down_in is not None
    input_grad, query_grad, key_grad, value_grad, out_grad, gains, dist, far_in, mate_in = outs[:9]
    rows, width = base.shape
    low, full = jnp.bfloat16, jnp.float32
    shape = jax.ShapeDtypeStruct
    hbm = pl.BlockSpec(memory_space=pl.ANY)
    vmem = pl.BlockSpec(memory_space=pltpu.VMEM)
    part = shape(query_grad.shape, full)
    feeds, extra = (), []
    if fused:
        share, hidden = down_in.shape[1:]
        feeds = (shape((share, hidden), full),) * 3
        extra = [pltpu.VMEM((3, share, hidden), low), pltpu.SemaphoreType.DMA]
    return pl.pallas_call(
        functools.partial(finish_kernel, ndp // 2, fused),
        out_shape=(
            shape((rows, width), low), shape((rows, width), low), shape((width,), full), part, part, part, part,
            shape((dist.shape[1], NB), full), shape((width,), full),
        ) + feeds,
        in_specs=[vmem] * (11 + 2 * fused) + [hbm] * fused,
        out_specs=(vmem,) * (9 + 3 * fused),
        scratch_shapes=extra,
        compiler_params=pltpu.CompilerParams(vmem_limit_bytes=VMEM_LIMIT),
        name="finish",
    )(
        buckets, base, far_in, mate_in, input_grad, query_grad, key_grad, value_grad, out_grad, gains, dist,
        *((down_in, outs[9], feed_grads) if fused else ()),
    )


def per_device(
    tokens,
    first_gain,
    query_weight,
    key_weight,
    value_weight,
    out_weight,
    bucket_table,
    second_gain,
    gate_weight,
    up_weight,
    down_weight,
    piece_start,
    bucket_index,
    cotangent,
):
    nt, ndp = lax.axis_size("tensor"), lax.axis_size("dp")
    weights = (query_weight.T, key_weight.T, value_weight.T, out_weight.T)
    first_all, cot_all, qkv, probs_low, probs_high, attended, whole, middle, second = gather_attend(
        nt, ndp, tokens, cotangent, first_gain, second_gain, weights, bucket_index, bucket_table.T, piece_start
    )
    base, grad_middle, second_part, grad_attended, layer_parts, feed_grads, *down_in = feed(
        nt, ndp, middle, second, second_gain, cotangent, whole, cot_all, gate_weight.T, up_weight.T, down_weight.T
    )
    outs = back(
        nt, ndp, grad_attended, grad_middle, tokens, first_gain, second_part, attended,
        qkv, probs_low, probs_high, first_all, whole, layer_parts, feed_grads,
    )
    outs = finish(ndp, bucket_index, base, outs, down_in[0] if down_in else None, feed_grads)
    if not down_in:
        sums = lax.psum_scatter(feed_grads, "dp", scatter_dimension=1, tiled=True).astype(jnp.float32)
        outs = (*outs, sums[0], sums[1], sums[2])
    return (*outs[:7], outs[7].T, *outs[8:])


def solution(mesh):
    return jax.shard_map(
        per_device,
        mesh=mesh,
        in_specs=(
            P(("dp", "tensor"), None),
            P(),
            P(None, "tensor"),
            P(None, "tensor"),
            P(None, "tensor"),
            P(None, "tensor"),
            P(None, "tensor"),
            P(),
            P(None, "tensor"),
            P(None, "tensor"),
            P(None, "tensor"),
            P("dp", None),
            P(),
            P(("dp", "tensor"), None),
        ),
        out_specs=(
            P(("dp", "tensor"), None),
            P(("dp", "tensor"), None),
            P(),
            P("dp", "tensor"),
            P("dp", "tensor"),
            P("dp", "tensor"),
            P("dp", "tensor"),
            P(None, "tensor"),
            P(),
            P("dp", "tensor"),
            P("dp", "tensor"),
            P("dp", "tensor"),
        ),
        check_vma=False,
    )
```

```python
import functools

import jax
import jax.numpy as jnp
from jax import lax
from jax.experimental import pallas as pl
from jax.experimental.pallas import tpu as pltpu
from jax.sharding import PartitionSpec as P

NB = 32
LEN = 1024
QB = 256
PIECE = 256
NPIECE = 2
HALF = LEN // NPIECE
SPAN = 5 * QB
DIST = 2 * LEN

EPSILON = 1e-06
MASKED = -1000000000.0
HIGHEST = lax.Precision.HIGHEST
VMEM_LIMIT = 60 * 1024 * 1024
MESH = pl.DeviceIdType.MESH


def normed(row_block, gain_vec):
    inv_rms = lax.rsqrt(jnp.mean(row_block * row_block, axis=-1, keepdims=True) + EPSILON)
    return row_block * inv_rms * gain_vec


def dot(a, b, dims):
    return lax.dot_general(a, b, (dims, ((), ())), preferred_element_type=jnp.float32)


def key_count(block):
    return HALF if (block + 1) * QB <= HALF else LEN


def toeplitz(bucket_ref, table_ref, head):
    bucket_row = jnp.concatenate([row_of(bucket_ref), jnp.zeros((1, 1), jnp.int32)], axis=1)
    row = jnp.zeros(bucket_row.shape, jnp.float32)
    for bucket in range(NB):
        row = jnp.where(bucket_row == bucket, table_ref[head, bucket], row)
    rows = jnp.broadcast_to(row, (QB, DIST))
    return pltpu.roll(rows, DIST - (QB - 1), 1, stride=1, stride_axis=0)[:, :SPAN]


def row_of(ref):
    return ref[...].reshape(1, ref.shape[0])


def label_of(position, starts):
    label = jnp.zeros(position.shape, jnp.int32)
    for piece, start in enumerate(starts):
        inside = (position >= start) & (position < start + PIECE)
        label = jnp.where(inside, piece + 1, label)
    return label


def allowed_block(block, starts):
    keys = key_count(block)
    query = block * QB + lax.broadcasted_iota(jnp.int32, (QB, 1), 0)
    key = lax.broadcasted_iota(jnp.int32, (1, keys), 1)
    query_label = label_of(query, starts)
    key_label = label_of(key, starts)
    return (key <= query) | ((query_label == key_label) & (query_label > 0))


def attend_block(block, head_dim, allowed, qkv_ref, bias_ref, low_ref, high_ref):
    keys = key_count(block)
    first = LEN - QB - block * QB
    rows = pl.ds(block * QB, QB)
    outs = []
    for head in range(bias_ref.shape[0]):
        cols = pl.ds(head * head_dim, head_dim)
        raw = dot(qkv_ref[0, rows, cols], qkv_ref[1, pl.ds(0, keys), cols], ((1,), (1,)))
        scores = jnp.where(allowed, raw + bias_ref[head, :, pl.ds(first, keys)], MASKED)
        peak = jnp.max(scores, axis=-1, keepdims=True)
        powered = jnp.exp(scores - peak)
        total = jnp.sum(powered, axis=-1, keepdims=True)
        probs = (powered * (1.0 / total)).astype(jnp.bfloat16)
        if keys == HALF:
            low_ref[head, rows, :] = probs
        else:
            high_ref[head, pl.ds(block * QB - HALF, QB), :] = probs
        outs.append(dot(probs, qkv_ref[2, pl.ds(0, keys), cols], ((1,), (0,))))
    return jnp.concatenate(outs, axis=1).astype(jnp.bfloat16)


def pack(rows):
    half = rows.shape[0] // 2
    return jnp.concatenate([rows[:half], rows[half:]], axis=1)


def unpack(packed, start, width):
    half = packed.shape[1] // 2
    return jnp.concatenate(
        [packed[:, start : start + width], packed[:, half + start : half + start + width]], axis=0
    )


def greet(t, nt):
    barrier = pltpu.get_barrier_semaphore()
    for k in range(1, nt):
        pl.semaphore_signal(
            barrier, inc=1, device_id={"tensor": lax.rem(t + k, nt)}, device_id_type=MESH
        )
    return barrier


def line_copy(t, nt, way, step, buf, piece, pieces, send_sem, recv_sem):
    sign = 1 if way == 0 else -1
    origin = jnp.clip(t - sign * step, 0, nt - 1)
    rows = buf.shape[1] // pieces
    part = buf.at[origin, pl.ds(piece * rows, rows)]
    return pltpu.make_async_remote_copy(
        src_ref=part,
        dst_ref=part,
        send_sem=send_sem,
        recv_sem=recv_sem,
        device_id={"tensor": jnp.clip(t + sign, 0, nt - 1)},
        device_id_type=MESH,
    )


def gather_attend_kernel(
    nt, ndp, pieces, heads, head_dim, exchange,
    x_ref, cot_ref, gain_ref, gain2_ref, bucket_ref, table_ref, start_ref, *rest,
):
    weight_refs, rest = rest[: 4 if exchange else 1], rest[4 if exchange else 1 :]
    (
        first_out, cot_out, qkv_out, low_out, high_out, own_out, whole_out, middle_out, second_out,
        first, qkv, low, high, bias, att, own, whole,
        send_sem, recv_sem, swap_send, swap_recv, line_send, line_recv, chip_send, chip_recv, core_send, core_recv,
        local_sem,
    ) = rest
    t = lax.axis_index("tensor")
    d = lax.axis_index("dp")
    core = lax.rem(d, 2)
    chip = d // 2
    chips = ndp // 2
    barrier = greet(t, nt)
    greeted = nt - 1
    if exchange:
        for k in range(chips):
            peer = 2 * lax.rem(chip + k, chips) + core if k else d + 1 - 2 * core
            pl.semaphore_signal(barrier, inc=1, device_id={"dp": peer}, device_id_type=MESH)
        greeted += chips
    inner = heads * head_dim
    share = whole.shape[1] // ndp
    own_cot = pltpu.make_async_copy(cot_ref, cot_out.at[t], local_sem.at[0])
    own_cot.start()
    if exchange:
        loads = [
            pltpu.make_async_copy(weight, whole.at[t, pl.ds(i * inner, inner)], local_sem.at[1 + i])
            for i, weight in enumerate(weight_refs)
        ]
    else:
        loads = [pltpu.make_async_copy(weight_refs[0], whole, local_sem.at[1])]
    for one in loads:
        one.start()

    def slices(index, plane):
        return whole.at[plane, pl.ds(pl.multiple_of(index * share, share), share)]

    def remote(src, dst, send, recv, **target):
        return pltpu.make_async_remote_copy(
            src_ref=src, dst_ref=dst, send_sem=send, recv_sem=recv, device_id=target, device_id_type=MESH
        )

    def plane_at(q):
        return lax.rem(t + q, nt)

    def to_plane(q):
        return remote(slices(d, t), slices(d, t), line_send.at[q - 1], line_recv.at[t], tensor=plane_at(q))

    def from_plane(q):
        p = plane_at(q)
        return remote(slices(d, p), slices(d, p), line_send.at[q - 1], line_recv.at[p], tensor=p)

    def to_chip(k, q):
        part = slices(d, plane_at(q))
        return remote(
            part, part, chip_send.at[k - 1, q - 1], chip_recv.at[k - 1, q - 1], dp=2 * lax.rem(chip + k, chips) + core
        )

    def from_chip(k, q):
        peer = 2 * lax.rem(chip - k + chips, chips) + core
        part = slices(peer, plane_at(q))
        return remote(part, part, chip_send.at[k - 1, q - 1], chip_recv.at[k - 1, q - 1], dp=peer)

    def to_core(k, q):
        part = slices(2 * lax.rem(chip - k + chips, chips) + core, plane_at(q))
        return remote(part, part, core_send.at[k, q - 1], core_recv.at[k, q - 1], dp=d + 1 - 2 * core)

    def from_core(k, q):
        part = slices(2 * lax.rem(chip - k + chips, chips) + 1 - core, plane_at(q))
        return remote(part, part, core_send.at[k, q - 1], core_recv.at[k, q - 1], dp=d + 1 - 2 * core)

    for one in loads:
        one.wait()
    pl.semaphore_wait(barrier, greeted)
    if exchange:
        for q in range(1, nt):
            to_plane(q).start()
    first[t] = normed(x_ref[...].astype(jnp.float32), row_of(gain_ref)).astype(jnp.bfloat16)

    def copy(way, stage, step, piece):
        buf = first if stage == 0 else cot_out
        return line_copy(
            t, nt, way, step, buf, piece, pieces,
            send_sem.at[way, stage, step, piece], recv_sem.at[way, stage, step, piece],
        )

    def landed(way, stage, step, piece):
        sign = 1 if way == 0 else -1
        buf = first if stage == 0 else cot_out
        rows = buf.shape[1] // pieces
        part = buf.at[jnp.clip(t - sign * step, 0, nt - 1), pl.ds(piece * rows, rows)]
        remote(
            part, part, send_sem.at[way, stage, step - 1, piece], recv_sem.at[way, stage, step - 1, piece],
            tensor=jnp.clip(t + sign, 0, nt - 1),
        ).wait_recv()

    ways = ((0, t, t < nt - 1), (1, nt - 1 - t, t > 0))

    def tick(k):
        for piece in range(pieces):
            for way, last, onward in ways:
                if k < nt:
                    @pl.when(k <= last)
                    def _():
                        if k > 0:
                            landed(way, 0, k, piece)

                        @pl.when(onward)
                        def _():
                            copy(way, 0, k, piece).start()

                if k > 0:
                    step = k - last - 1

                    @pl.when((step >= 1) & (step <= last))
                    def _():
                        landed(way, 1, step, piece)

                        @pl.when(onward)
                        def _():
                            copy(way, 1, step, piece).start()

                    @pl.when((step == 0) & onward)
                    def _():
                        copy(way, 0, last, piece).wait_send()
                        copy(way, 1, 0, piece).start()

    def project(origin):
        rows = pl.ds(pl.multiple_of(origin * QB, QB), QB)
        for place in range(3):
            weight = whole[t, pl.ds(place * inner, inner), :]
            qkv[place, rows, :] = dot(first[origin], weight, ((1,), (1,))).astype(jnp.bfloat16)

    tick(0)
    project(t)
    for head in range(heads):
        bias[head] = toeplitz(bucket_ref, table_ref, head)
    own_cot.wait()
    for k in range(1, nt):
        tick(k)

        @pl.when(t - k >= 0)
        def _():
            project(t - k)

        @pl.when(t + k < nt)
        def _():
            project(t + k)

        if exchange and k == 2:
            for q in range(1, nt):
                from_plane(q).wait_recv()
                for j in range(1, chips):
                    to_chip(j, q).start()
                to_core(0, q).start()

    starts = [start_ref[0, piece] for piece in range(NPIECE)]
    keep = [
        pltpu.make_async_copy(first, first_out, local_sem.at[5]),
        pltpu.make_async_copy(qkv, qkv_out, local_sem.at[6]),
    ]
    for one in keep:
        one.start()

    def swap(block):
        return remote(att.at[block], own.at[t], swap_send.at[block], swap_recv.at[t], tensor=block)

    for block in range(LEN // QB):
        att[block] = pack(attend_block(block, head_dim, allowed_block(block, starts), qkv, bias, low, high))

        @pl.when(t != block)
        def _():
            swap(block).start()

        @pl.when(t == block)
        def _():
            own[t] = att[block]

    late = [
        pltpu.make_async_copy(low, low_out, local_sem.at[7]),
        pltpu.make_async_copy(high, high_out, local_sem.at[8]),
    ]
    for one in late:
        one.start()
    tick(nt)
    if exchange:
        for k in range(1, chips):
            for q in range(1, nt):
                from_chip(k, q).wait_recv()
                to_core(k, q).start()
    tick(nt + 1)
    for block in range(nt):
        @pl.when(t != block)
        def _():
            remote(att.at[block], own.at[block], swap_send.at[block], swap_recv.at[block], tensor=block).wait_recv()

    if exchange:
        for k in range(chips):
            for q in range(1, nt):
                from_core(k, q).wait_recv()
    late += [
        pltpu.make_async_copy(own, own_out, local_sem.at[9]),
        pltpu.make_async_copy(whole, whole_out, local_sem.at[10]),
    ]
    for one in late[2:]:
        one.start()
    total = x_ref[...].astype(jnp.float32)
    for j in range(nt):
        total = total + dot(unpack(own[j], 0, inner), whole[j, pl.ds(3 * inner, inner), :], ((1,), (0,)))
    middle_out[...] = total
    second_out[...] = normed(total, row_of(gain2_ref)).astype(jnp.bfloat16)
    for k in range(nt + 2, 2 * nt):
        tick(k)
    for block in range(nt):
        @pl.when(t != block)
        def _():
            swap(block).wait_send()

    for one in keep + late:
        one.wait()
    if exchange:
        for q in range(1, nt):
            to_plane(q).wait_send()
            for k in range(1, chips):
                to_chip(k, q).wait_send()
            for k in range(chips):
                to_core(k, q).wait_send()
    for piece in range(pieces):
        for way, last, onward in ways:
            for stage in range(2):
                for step in range(nt):
                    @pl.when(onward & ((step < last) if stage == 0 else (step <= last)))
                    def _():
                        copy(way, stage, step, piece).wait_send()


def gather_attend(nt, ndp, tokens, cotangent, gain, gain2, weights, buckets, table, starts):
    heads = table.shape[0]
    rows, width = tokens.shape
    inner = weights[0].shape[0]
    low, full = jnp.bfloat16, jnp.float32
    pieces = 2
    exchange = (4 * inner // ndp) % 16 == 0
    if not exchange:
        joined = jnp.concatenate(weights, axis=0)
        part = joined.shape[0] // ndp
        mine = lax.dynamic_slice_in_dim(joined, lax.axis_index("dp") * part, part, 0)
        weights = (lax.all_gather(mine, ("tensor", "dp"), axis=0, tiled=True).reshape(nt, *joined.shape),)
    chips = ndp // 2
    smem = pl.BlockSpec(memory_space=pltpu.SMEM)
    hbm = pl.BlockSpec(memory_space=pl.ANY)
    vmem = pl.BlockSpec(memory_space=pltpu.VMEM)
    shapes = (
        (nt, rows, width), (nt, rows, width), (3, LEN, inner), (heads, HALF, HALF), (heads, HALF, LEN),
        (nt, rows // 2, 2 * inner), (nt, 4 * inner, width),
    )
    dma = pltpu.SemaphoreType.DMA
    return pl.pallas_call(
        functools.partial(gather_attend_kernel, nt, ndp, pieces, heads, inner // heads, exchange),
        out_shape=tuple(jax.ShapeDtypeStruct(shape, low) for shape in shapes)
        + (jax.ShapeDtypeStruct((rows, width), full), jax.ShapeDtypeStruct((rows, width), low)),
        in_specs=[vmem, hbm, vmem, vmem, vmem, smem, smem] + [hbm] * len(weights),
        out_specs=(hbm,) * 7 + (vmem, vmem),
        scratch_shapes=[
            pltpu.VMEM((nt, rows, width), low),
            pltpu.VMEM((3, LEN, inner), low),
            pltpu.VMEM((heads, HALF, HALF), low),
            pltpu.VMEM((heads, HALF, LEN), low),
            pltpu.VMEM((heads, QB, SPAN), full),
            pltpu.VMEM((nt, rows // 2, 2 * inner), low),
            pltpu.VMEM((nt, rows // 2, 2 * inner), low),
            pltpu.VMEM((nt, 4 * inner, width), low),
            dma((2, 2, nt, pieces)), dma((2, 2, nt, pieces)), dma((nt,)), dma((nt,)),
            dma((nt - 1,)), dma((nt,)), dma((chips - 1, nt - 1)), dma((chips - 1, nt - 1)),
            dma((chips, nt - 1)), dma((chips, nt - 1)), dma((11,)),
        ],
        compiler_params=pltpu.CompilerParams(
            vmem_limit_bytes=VMEM_LIMIT, collective_id=0, has_side_effects=True
        ),
        name="gather_attend",
    )(tokens, cotangent, gain, gain2, buckets, table, starts, *weights)


def fold_diagonals(grid):
    rows = QB // 2
    width = grid.shape[1]
    while rows >= 1:
        grid = grid[:rows] + pltpu.roll(grid[rows : 2 * rows], width - rows, 1)
        rows //= 2
    return grid


def gelu_parts(v):
    root, cubic = 0.7978845608028654, 0.044715
    square = v * v
    bend = jnp.tanh(root * v * (1.0 + cubic * square))
    half = 0.5 * (1.0 + bend)
    slope = half + 0.5 * v * (1.0 - bend * bend) * root * (1.0 + 3.0 * cubic * square)
    return v * half, slope


def feed_kernel(
    nt, ndp, pieces, halves, fused,
    gain_ref, middle_hbm, second_hbm, cot_own_hbm, whole_hbm, cot_hbm, wg_hbm, wu_hbm, wd_hbm,
    base_out, gm_out, gain_out, ga_out, lo_out, lo_in, grads_out, *rest,
):
    if fused:
        down_out, *rest = rest
    (
        middle, cot_own_ref, buf, cot, wg, wu, wd, hid, gg, gu, gs, lo, wo, mate_in, acc_in, far_in, grads, *rest,
    ) = rest
    *rest, send_sem, recv_sem, rs_send, rs_recv, lo_send, lo_recv, local_sem = rest
    t = lax.axis_index("tensor")
    d = lax.axis_index("dp")
    core = lax.rem(d, 2)
    chips = ndp // 2
    barrier = greet(t, nt)
    own_load = pltpu.make_async_copy(second_hbm, buf.at[t], local_sem.at[11])
    own_load.start()
    if fused:
        sums, pair_send, pair_recv, chip_send, chip_recv = rest
        chip = d // 2
        for k in range(chips):
            peer = 2 * lax.rem(chip + k, chips) + core if k else d + 1 - 2 * core
            pl.semaphore_signal(barrier, inc=1, device_id={"dp": peer}, device_id_type=MESH)
    loads = [
        pltpu.make_async_copy(a, b, local_sem.at[i])
        for i, (a, b) in enumerate(((wg_hbm, wg), (wu_hbm, wu), (wd_hbm, wd), (cot_hbm, cot)))
    ]
    for one in loads:
        one.start()
    row_count = middle.shape[0]
    size = row_count // pieces
    inner = wo.shape[1]
    wo_load = pltpu.make_async_copy(whole_hbm.at[:, pl.ds(3 * inner, inner)], wo, local_sem.at[4])
    wo_load.start()
    late_loads = [
        pltpu.make_async_copy(middle_hbm, middle, local_sem.at[9]),
        pltpu.make_async_copy(cot_own_hbm, cot_own_ref, local_sem.at[10]),
    ]
    for one in late_loads:
        one.start()
    keep = []
    own_load.wait()
    pl.semaphore_wait(barrier, nt - 1 + chips * fused)
    mate = t + 1 - 2 * lax.rem(t, 2)
    is_end = (t == 0) | (t == nt - 1)
    ways = ((0, t, t < nt - 1), (1, nt - 1 - t, t > 0))

    def copy(way, step, piece):
        return line_copy(
            t, nt, way, step, buf, piece, pieces,
            send_sem.at[way, step, piece], recv_sem.at[way, step, piece],
        )

    def landed(way, step, piece):
        sign = 1 if way == 0 else -1
        part = buf.at[jnp.clip(t - sign * step, 0, nt - 1), pl.ds(piece * size, size)]
        pltpu.make_async_remote_copy(
            src_ref=part, dst_ref=part,
            send_sem=send_sem.at[way, step - 1, piece], recv_sem=recv_sem.at[way, step - 1, piece],
            device_id={"tensor": jnp.clip(t + sign, 0, nt - 1)}, device_id_type=MESH,
        ).wait_recv()

    def remote(src, dst, target, send, recv):
        return pltpu.make_async_remote_copy(
            src_ref=src, dst_ref=dst, send_sem=send, recv_sem=recv,
            device_id={"tensor": target}, device_id_type=MESH,
        )

    wide = buf.shape[2] // halves

    def to_mate(piece, half):
        part = (pl.ds(piece * size, size), pl.ds(half * wide, wide))
        return remote(
            gs.at[(mate, *part)], mate_in.at[part], mate, rs_send.at[0, piece, half], rs_recv.at[0, piece, half]
        )

    def to_acc(origin, piece, half):
        part = (pl.ds(piece * size, size), pl.ds(half * wide, wide))
        j = lax.rem(origin, 2)
        return remote(
            gs.at[(origin, *part)], acc_in.at[(j, *part)], mate,
            rs_send.at[1 + j, piece, half], rs_recv.at[1 + j, piece, half],
        )

    def to_far(origin, piece, half):
        part = (pl.ds(piece * size, size), pl.ds(half * wide, wide))
        j = lax.rem(origin, 2)
        return remote(
            gs.at[(origin, *part)], far_in.at[part], origin, rs_send.at[3 + j, piece, half], rs_recv.at[3, piece, half]
        )

    def feed(origin, piece):
        rows = pl.ds(pl.multiple_of(piece * size, size), size)
        flat = pl.ds(pl.multiple_of(origin * row_count + piece * size, size), size)
        normal = buf[origin, rows]
        gate = dot(normal, wg[...], ((1,), (1,)))
        up = dot(normal, wu[...], ((1,), (1,)))
        grad_hidden = dot(cot[origin, rows], wd[...], ((1,), (1,)))
        act, slope = gelu_parts(gate)
        hidden = (act * up).astype(jnp.bfloat16)
        hid[flat, :] = hidden
        grad_gate = (grad_hidden * up * slope).astype(jnp.bfloat16)
        grad_up = (grad_hidden * act).astype(jnp.bfloat16)
        gg[flat, :] = grad_gate
        gu[flat, :] = grad_up
        for half in range(halves):
            cols = pl.ds(half * wide, wide)
            gs[origin, rows, cols] = (
                dot(grad_gate, wg[:, cols], ((1,), (0,))) + dot(grad_up, wu[:, cols], ((1,), (0,)))
            ).astype(jnp.bfloat16)

            @pl.when(origin == mate)
            def _():
                to_mate(piece, half).start()

            @pl.when((origin != mate) & (origin != t) & is_end)
            def _():
                to_acc(origin, piece, half).start()

        lo[origin, rows] = dot(hidden, wd[...], ((1,), (0,))).astype(jnp.bfloat16)

    span = 256
    flat_rows = nt * row_count
    spans = buf.shape[2] // span
    head = jnp.where(t < nt // 2, 0, 1)
    last_one = jnp.where(t < nt // 2, nt - 1, 0)
    head_rows = pl.ds(pl.multiple_of(head * row_count, row_count), flat_rows - row_count)
    last_rows = pl.ds(pl.multiple_of(last_one * row_count, row_count), row_count)

    def columns(ref, i):
        cols = pl.ds(pl.multiple_of(i * span, span), span)
        return ref[pl.ds(head, nt - 1), :, cols].reshape(flat_rows - row_count, span)

    def grad_head(which, left, right, rows):
        grads[which, rows, :] = dot(left, right[head_rows, :], ((0,), (0,))).astype(jnp.bfloat16)

    def grad_last(which, left, right, rows):
        grads[which, rows, :] = (
            grads[which, rows, :].astype(jnp.float32) + dot(left, right[last_rows, :], ((0,), (0,)))
        ).astype(jnp.bfloat16)

    def down_head(i, carry):
        rows = pl.ds(pl.multiple_of(i * span, span), span)
        grad_head(2, columns(cot, i), hid, rows)
        return carry

    def gate_up_head(i, carry):
        rows = pl.ds(pl.multiple_of(i * span, span), span)
        left = columns(buf, i)
        grad_head(0, left, gg, rows)
        grad_head(1, left, gu, rows)
        return carry

    def down_last(i, carry):
        rows = pl.ds(pl.multiple_of(i * span, span), span)
        grad_last(2, cot[last_one, :, rows], hid, rows)
        return carry

    def gate_up_last(i, carry):
        rows = pl.ds(pl.multiple_of(i * span, span), span)
        left = buf[last_one, :, rows]
        grad_last(0, left, gg, rows)
        grad_last(1, left, gu, rows)
        return carry

    for piece in range(pieces):
        for way, last, onward in ways:
            @pl.when(onward)
            def _():
                copy(way, 0, piece).start()

    for one in loads:
        one.wait()

    def unit(u, carry):
        step = u // pieces
        piece = lax.rem(u, pieces)

        @pl.when(step > 0)
        def _():
            for way, last, onward in ways:
                @pl.when(step <= last)
                def _():
                    landed(way, step, piece)

                    @pl.when(onward)
                    def _():
                        copy(way, step, piece).start()

        def side(way, carry):
            origin = t - (1 - 2 * way) * step
            there = (origin >= 0) & (origin < nt) & ((step > 0) | (way == 0))

            @pl.when(there)
            def _():
                feed(origin, piece)

            return carry

        lax.fori_loop(0, 2, side, carry)

        @pl.when(u == (nt - 1) * pieces - 1)
        def _():
            lax.fori_loop(0, spans, down_head, 0)

        @pl.when(u == (nt - 1) * pieces)
        def _():
            lax.fori_loop(0, spans, gate_up_head, 0)

        return carry

    lax.fori_loop(0, nt * pieces, unit, 0)

    near = jnp.where(t < nt // 2, nt // 2, nt // 2 - 1)
    far = jnp.where(t < nt // 2, nt - 1, 0)

    def pass_on(origin, piece):
        @pl.when(jnp.logical_not(is_end))
        def _():
            rows = pl.ds(piece * size, size)
            j = lax.rem(origin, 2)
            for half in range(halves):
                to_acc(origin, piece, half).wait_recv()
                cols = pl.ds(half * wide, wide)
                gs[origin, rows, cols] = (
                    gs[origin, rows, cols].astype(jnp.float32) + acc_in[j, rows, cols].astype(jnp.float32)
                ).astype(jnp.bfloat16)
                to_far(origin, piece, half).start()

    share = buf.shape[2] // ndp

    def block_rows(index):
        return pl.ds(pl.multiple_of(index * share, share), share)

    def pair(which, c):
        return pltpu.make_async_remote_copy(
            src_ref=grads.at[which, block_rows(2 * c + 1 - core)], dst_ref=sums.at[which, c],
            send_sem=pair_send.at[which, c], recv_sem=pair_recv.at[which, c],
            device_id={"dp": d + 1 - 2 * core}, device_id_type=MESH,
        )

    def down_copy(k):
        to = lax.rem(chip + k, chips)
        return pltpu.make_async_remote_copy(
            src_ref=sums.at[2, to], dst_ref=down_out.at[k - 1],
            send_sem=chip_send.at[k - 1], recv_sem=chip_recv.at[k - 1],
            device_id={"dp": 2 * to + core}, device_id_type=MESH,
        )

    def pair_start(*which):
        if fused:
            for w in which:
                for c in range(chips):
                    pair(w, c).start()

    def pair_sum(which):
        if fused:
            for c in range(chips):
                pair(which, c).wait_recv()
                sums[which, c] = (
                    grads[which, block_rows(2 * c + core)].astype(jnp.float32) + sums[which, c].astype(jnp.float32)
                ).astype(jnp.bfloat16)
            if which == 2:
                for k in range(1, chips):
                    down_copy(k).start()
                one = pltpu.make_async_copy(sums.at[2, chip], down_out.at[chips - 1], local_sem.at[8])
            else:
                one = pltpu.make_async_copy(sums.at[which], grads_out.at[which], local_sem.at[6 + which])
        else:
            one = pltpu.make_async_copy(grads.at[which], grads_out.at[which], local_sem.at[6 + which])
        one.start()
        keep.append(one)

    def lo_acc(piece):
        rows = pl.ds(piece * size, size)
        return remote(lo.at[far, rows], lo_in.at[rows], mate, lo_send.at[piece], lo_recv.at[piece])

    @pl.when(is_end)
    def _():
        for piece in range(pieces):
            lo_acc(piece).start()

    keep.append(pltpu.make_async_copy(lo, lo_out, local_sem.at[5]))
    keep[-1].start()
    pass_on(near, 0)
    lax.fori_loop(0, spans, down_last, 0)
    pair_start(2)
    pass_on(near, 1)
    lax.fori_loop(0, spans, gate_up_last, 0)
    pair_start(0, 1)
    pair_sum(2)
    pass_on(far, 0)
    pass_on(far, 1)
    for one in late_loads:
        one.wait()

    wo_load.wait()
    for piece in range(pieces):
        rows = pl.ds(piece * size, size)
        for half in range(halves):
            to_mate(piece, half).wait_recv()
            part = (rows, pl.ds(half * wide, wide))
            remote(
                gs.at[(t, *part)], far_in.at[part], mate, rs_send.at[3, piece, half], rs_recv.at[3, piece, half]
            ).wait_recv()
        grad_second = (
            gs[t, rows].astype(jnp.float32)
            + mate_in[rows].astype(jnp.float32)
            + far_in[rows].astype(jnp.float32)
        )
        mid = middle[rows]
        inv = lax.rsqrt(jnp.mean(mid * mid, axis=-1, keepdims=True) + EPSILON)
        scaled = row_of(gain_ref) * grad_second
        along = jnp.mean(scaled * mid, axis=-1, keepdims=True)
        grad_middle = cot_own_ref[rows].astype(jnp.float32) + inv * scaled - mid * (inv * inv * inv * along)
        gm_out[rows] = grad_middle
        part = jnp.sum(grad_second * mid * inv, axis=0, keepdims=True)
        if piece == 0:
            gain_out[...] = part
        else:
            gain_out[...] += part
        grad_low = grad_middle.astype(jnp.bfloat16)
        for j in range(nt):
            ga_out[j, :, pl.ds(piece * inner, inner)] = dot(grad_low, wo[j], ((1,), (1,))).astype(jnp.bfloat16)

    pair_sum(0)
    pair_sum(1)
    base_out[...] = middle[...] + lo[t].astype(jnp.float32)

    @pl.when(jnp.logical_not(is_end))
    def _():
        for piece in range(pieces):
            lo_acc(piece).wait_recv()

    for one in keep:
        one.wait()
    for piece in range(pieces):
        for way, last, onward in ways:
            for step in range(nt):
                @pl.when(onward & (step <= last))
                def _():
                    copy(way, step, piece).wait_send()

        @pl.when(is_end)
        def _():
            lo_acc(piece).wait_send()

        for half in range(halves):
            to_mate(piece, half).wait_send()
            for origin in (near, far):
                @pl.when(is_end)
                def _():
                    to_acc(origin, piece, half).wait_send()

                @pl.when(jnp.logical_not(is_end))
                def _():
                    to_far(origin, piece, half).wait_send()

    if fused:
        for which in range(3):
            for c in range(chips):
                pair(which, c).wait_send()
        for k in range(1, chips):
            down_copy(k).wait()


def feed(nt, ndp, middle, second, gain, cotangent, whole, cot_all, gate_weight, up_weight, down_weight):
    rows, width = middle.shape
    hidden = gate_weight.shape[0]
    low, full = jnp.bfloat16, jnp.float32
    pieces, halves = 2, 2
    hbm = pl.BlockSpec(memory_space=pl.ANY)
    vmem = pl.BlockSpec(memory_space=pltpu.VMEM)
    inner = whole.shape[1] // 4
    dma = pltpu.SemaphoreType.DMA
    shape = jax.ShapeDtypeStruct
    share, chips = width // ndp, ndp // 2
    fused = share % 16 == 0
    sums = (3, chips, share, hidden)
    pairs = [
        pltpu.VMEM(sums, low), dma((3, chips)), dma((3, chips)), dma((chips - 1,)), dma((chips - 1,))
    ] if fused else []
    return pl.pallas_call(
        functools.partial(feed_kernel, nt, ndp, pieces, halves, fused),
        out_shape=(
            shape((rows, width), full), shape((rows, width), full), shape((1, width), full),
            shape((nt, rows // 2, 2 * inner), low), shape((nt, rows, width), low), shape((rows, width), low),
            shape((2, *sums[1:]) if fused else (3, width, hidden), low),
        ) + (shape((chips, share, hidden), low),) * fused,
        in_specs=[vmem] + [hbm] * 8,
        out_specs=(vmem, vmem, vmem, vmem, hbm, hbm, hbm) + (hbm,) * fused,
        scratch_shapes=[
            pltpu.VMEM((rows, width), full), pltpu.VMEM((rows, width), low),
            pltpu.VMEM((nt, rows, width), low), pltpu.VMEM((nt, rows, width), low),
            pltpu.VMEM((hidden, width), low), pltpu.VMEM((hidden, width), low), pltpu.VMEM((hidden, width), low),
            pltpu.VMEM((nt * rows, hidden), low), pltpu.VMEM((nt * rows, hidden), low), pltpu.VMEM((nt * rows, hidden), low),
            pltpu.VMEM((nt, rows, width), low), pltpu.VMEM((nt, rows, width), low),
            pltpu.VMEM((nt, inner, width), low),
            pltpu.VMEM((rows, width), low), pltpu.VMEM((2, rows, width), low), pltpu.VMEM((rows, width), low),
            pltpu.VMEM((3, width, hidden), low), *pairs,
            dma((2, nt, pieces)), dma((2, nt, pieces)), dma((5, pieces, halves)), dma((4, pieces, halves)),
            dma((pieces,)), dma((pieces,)),
            dma((12,)),
        ],
        compiler_params=pltpu.CompilerParams(
            vmem_limit_bytes=VMEM_LIMIT, collective_id=1, has_side_effects=True
        ),
        name="feed",
    )(gain, middle, second, cotangent, whole, cot_all, gate_weight, up_weight, down_weight)


def back_kernel(
    nt, ndp, pieces, heads, head_dim, grad_type, fused,
    ga_ref, gain_ref, gain2_ref, gm_hbm, x_hbm, own_hbm,
    qkv_hbm, low_hbm, high_hbm, first_hbm, weight_hbm, lo_hbm, lo_part_hbm, *rest,
):
    if fused:
        feed_hbm, *rest = rest
    input_out, q_out, k_out, v_out, o_out, gains_in, dist_in, far_in, mate_in, *rest = rest
    if fused:
        feed_in, *rest = rest
    (
        gm_ref, x_ref, own_ref,
        ga_in, qkv, low, high, first, weight, lo, acc_in, lo_part,
        gq, gq_send, gq_in, diag, dk_acc, dv_acc,
        og, og_sum, og_chip, og_line, og_line_in, pg, pg_sum, pg_chip,
        gains_line, gains_own, dist_own,
        swap_send, swap_recv, back_send, back_recv, lo_send, lo_recv,
        pair_send, pair_recv, chip_send, chip_recv, line_send, line_recv,
        gl_send, gl_recv, gd_send, gd_recv, dist_send, dist_recv, local_sem, *rest,
    ) = rest
    if fused:
        feed_send, feed_recv = rest
    t = lax.axis_index("tensor")
    d = lax.axis_index("dp")
    core = lax.rem(d, 2)
    chip = d // 2
    chips = ndp // 2
    barrier = greet(t, nt)
    for k in range(1, ndp):
        pl.semaphore_signal(
            barrier, inc=1, device_id={"dp": lax.rem(d + k, ndp)}, device_id_type=MESH
        )
    mate = t + 1 - 2 * lax.rem(t, 2)
    is_end = (t == 0) | (t == nt - 1)
    near = jnp.where(t < nt // 2, nt // 2, nt // 2 - 1)
    far = jnp.where(t < nt // 2, nt - 1, 0)
    loads = [
        pltpu.make_async_copy(a, b, local_sem.at[i])
        for i, (a, b) in enumerate(
            ((qkv_hbm, qkv), (low_hbm, low), (high_hbm, high), (first_hbm, first),
             (weight_hbm.at[:, pl.ds(0, weight.shape[1])], weight),
             (lo_hbm.at[near], lo.at[0]), (lo_hbm.at[far], lo.at[1]), (lo_hbm.at[mate], lo.at[2]),
             (gm_hbm, gm_ref), (x_hbm, x_ref), (own_hbm, own_ref), (lo_part_hbm, lo_part))
        )
    ]
    for one in loads:
        one.start()
    others = (far, near, mate)
    row_count, width = x_ref.shape
    inner = heads * head_dim
    size = row_count // pieces
    share = width // ndp
    full = jnp.float32

    def remote(src, dst, send, recv, **target):
        return pltpu.make_async_remote_copy(
            src_ref=src, dst_ref=dst, send_sem=send, recv_sem=recv,
            device_id=target, device_id_type=MESH,
        )

    def swap(peer):
        return remote(ga_ref.at[peer], ga_in.at[t], swap_send.at[peer], swap_recv.at[t], tensor=peer)

    def swap_in(peer):
        return remote(ga_ref.at[peer], ga_in.at[peer], swap_send.at[peer], swap_recv.at[peer], tensor=peer)

    def lo_acc(piece):
        rows = pl.ds(piece * size, size)
        return remote(lo.at[0, rows], acc_in.at[rows], lo_send.at[0, piece], lo_recv.at[0, piece], tensor=mate)

    def lo_final(place, origin, piece):
        rows = pl.ds(piece * size, size)
        return remote(
            lo.at[place, rows], far_in.at[rows], lo_send.at[place, piece], lo_recv.at[1, piece], tensor=origin
        )

    def lo_mate(piece):
        rows = pl.ds(piece * size, size)
        return remote(lo.at[2, rows], mate_in.at[rows], lo_send.at[2, piece], lo_recv.at[2, piece], tensor=mate)

    pl.semaphore_wait(barrier, nt - 1 + ndp - 1)
    for peer in others:
        swap(peer).start()
    ga_in[t] = ga_ref[t]
    if fused:
        def feed_copy(which, k):
            to = lax.rem(chip + k, chips)
            return remote(
                feed_hbm.at[which, to], feed_in.at[k - 1, which],
                feed_send.at[k - 1, which], feed_recv.at[k - 1, which], dp=2 * to + core,
            )

        own_feed = pltpu.make_async_copy(feed_hbm.at[:, chip], feed_in.at[chips - 1], local_sem.at[13])
        own_feed.start()
        for which in range(2):
            for k in range(1, chips):
                feed_copy(which, k).start()

    def block_rows(index):
        return pl.ds(pl.multiple_of(index * share, share), share)

    def pair(kind, c):
        grads, landing = ((og, og_sum), (pg, pg_sum))[kind]
        return remote(
            grads.at[block_rows(2 * c + 1 - core)], landing.at[c],
            pair_send.at[kind, c], pair_recv.at[kind, c], dp=d + 1 - 2 * core,
        )

    def chip_copy(kind, k):
        sums, landing = ((og_sum, og_chip), (pg_sum, pg_chip))[kind]
        to = lax.rem(chip + k, chips)
        return remote(
            sums.at[to], landing.at[k - 1], chip_send.at[kind, k - 1], chip_recv.at[kind, k - 1], dp=2 * to + core
        )

    def pair_sum(kind):
        grads, sums = ((og, og_sum), (pg, pg_sum))[kind]
        for c in range(chips):
            pair(kind, c).wait_recv()
            sums[c] = (grads[block_rows(2 * c + core)].astype(full) + sums[c].astype(full)).astype(grad_type)
        for k in range(1, chips):
            chip_copy(kind, k).start()

    def chip_sum(kind):
        sums, landing = ((og_sum, og_chip), (pg_sum, pg_chip))[kind]
        total = sums[chip].astype(full)
        for k in range(1, chips):
            chip_copy(kind, k).wait_recv()
            total = total + landing[k - 1].astype(full)
        return total

    for one in loads[5:]:
        one.wait()
    span = 256
    spans = width // span
    own = jnp.concatenate([unpack(own_ref[j], 0, inner) for j in range(nt)], axis=1)
    for i in range(spans):
        left = gm_ref[:, pl.ds(i * span, span)].astype(jnp.bfloat16)
        og[pl.ds(i * span, span), :] = dot(left, own, ((0,), (0,))).astype(grad_type)
    for c in range(chips):
        pair(0, c).start()

    for i in range(3):
        loads[i].wait()
    blocks = LEN // QB
    diag[...] = jnp.zeros_like(diag)
    for block in reversed(range(blocks)):
        keys = key_count(block)
        rows = pl.ds(block * QB, QB)
        first_col = LEN - block * QB

        for waited in (1, 0) if block == 1 else () if block == 0 else (block,):
            @pl.when(t != waited)
            def _():
                swap_in(waited).wait_recv()

        if block == 1:
            for piece in range(pieces):
                @pl.when(is_end)
                def _():
                    lo_acc(piece).start()

                @pl.when(jnp.logical_not(is_end))
                def _():
                    rows_lo = pl.ds(piece * size, size)
                    lo[1, rows_lo] = (lo[1, rows_lo].astype(full) + lo_part[rows_lo].astype(full)).astype(jnp.bfloat16)
                    lo_final(1, far, piece).start()

        parts = []
        for head in range(heads):
            cols = pl.ds(head * head_dim, head_dim)
            if keys == HALF:
                probs_low = low[head, rows, :]
            else:
                probs_low = high[head, pl.ds(block * QB - HALF, QB), :]
            probs = probs_low.astype(full)
            do = unpack(ga_in[block], head * head_dim, head_dim)
            grad_probs = dot(do, qkv[2, pl.ds(0, keys), cols], ((1,), (1,)))
            weighted = jnp.sum(probs * grad_probs, axis=-1, keepdims=True)
            grad_low = (probs * (grad_probs - weighted)).astype(jnp.bfloat16)
            reach = pl.ds(first_col, keys)
            diag[head, :, reach] = diag[head, :, reach] + grad_low.astype(full)
            parts.append(dot(grad_low, qkv[1, pl.ds(0, keys), cols], ((1,), (0,))))
            key_part = dot(grad_low, qkv[0, rows, cols], ((0,), (0,)))
            value_part = dot(probs_low, do, ((0,), (0,)))
            if block == blocks - 1:
                dk_acc[head] = key_part
                dv_acc[head] = value_part
            else:
                dk_acc[head, pl.ds(0, keys), :] += key_part
                dv_acc[head, pl.ds(0, keys), :] += value_part
        gq[rows, pl.ds(0, inner)] = jnp.concatenate(parts, axis=1).astype(jnp.bfloat16)
        if block == 1:
            pair_sum(0)
    for block in range(blocks):
        rows = pl.ds(block * QB, QB)
        sides = [acc[head, rows, :] for acc in (dk_acc, dv_acc) for head in range(heads)]
        gq[rows, pl.ds(inner, 2 * inner)] = jnp.concatenate(sides, axis=1).astype(jnp.bfloat16)

    for block in range(blocks):
        gq_send[block] = pack(gq[pl.ds(block * QB, QB), :])

    def token_rows(peer):
        return pl.ds(pl.multiple_of(peer * row_count, row_count), row_count)

    def give(peer):
        return remote(
            gq_send.at[peer], gq_in.at[t], back_send.at[peer], back_recv.at[t], tensor=peer
        )

    def taken(peer):
        return remote(
            gq_send.at[peer], gq_in.at[peer], back_send.at[peer], back_recv.at[peer], tensor=peer
        )

    for peer in others:
        give(peer).start()
    for head in range(heads):
        dist_own[pl.ds(head, 1), :] = fold_diagonals(diag[head])
    dist_keep = pltpu.make_async_copy(dist_own, dist_in.at[d], local_sem.at[12])
    dist_keep.start()

    def dist_copy(k):
        return remote(
            dist_own, dist_in.at[d], dist_send.at[k - 1], dist_recv.at[d], dp=lax.rem(d + k, ndp)
        )

    for k in range(1, ndp):
        dist_copy(k).start()
    loads[3].wait()
    for i in range(spans):
        cols = pl.ds(i * span, span)
        left = first[:, :, cols].reshape(nt * row_count, span)
        pg[cols, :] = dot(left, gq[...], ((0,), (0,))).astype(grad_type)
    for c in range(chips):
        pair(1, c).start()
    total = chip_sum(0)
    for j in range(nt):
        og_line[j] = total[:, j * inner : (j + 1) * inner].astype(grad_type)

    def line_copy_out(peer):
        return remote(og_line.at[peer], og_line_in.at[t], line_send.at[peer], line_recv.at[t], tensor=peer)

    def line_in(peer):
        return remote(og_line.at[peer], og_line_in.at[peer], line_send.at[peer], line_recv.at[peer], tensor=peer)

    for peer in others:
        line_copy_out(peer).start()
    pair_sum(1)

    @pl.when(jnp.logical_not(is_end))
    def _():
        for piece in range(pieces):
            lo_acc(piece).wait_recv()
        lo[0] = (lo[0].astype(full) + acc_in[...].astype(full)).astype(jnp.bfloat16)

    loads[4].wait()
    inputs = x_ref[...].astype(full)
    inv = lax.rsqrt(jnp.mean(inputs * inputs, axis=-1, keepdims=True) + EPSILON)
    grad_first = dot(gq[token_rows(t)], weight[t], ((1,), (0,)))
    for peer in (mate, near, far):
        taken(peer).wait_recv()
        grad_first = grad_first + dot(unpack(gq_in[peer], 0, 3 * inner), weight[peer], ((1,), (0,)))
    scaled = row_of(gain_ref) * grad_first
    along = jnp.mean(scaled * inputs, axis=-1, keepdims=True)
    gains_line[t, pl.ds(0, 1), :] = jnp.sum(grad_first * inputs * inv, axis=0, keepdims=True)
    gains_line[t, pl.ds(1, 1), :] = gain2_ref[...]

    def gain_copy(peer):
        return remote(gains_line.at[t], gains_line.at[t], gl_send.at[peer], gl_recv.at[t], tensor=peer)

    def gain_landed(peer):
        return remote(gains_line.at[peer], gains_line.at[peer], gl_send.at[peer], gl_recv.at[peer], tensor=peer)

    for peer in others:
        gain_copy(peer).start()
    for piece in range(pieces):
        lo_mate(piece).start()

        @pl.when(jnp.logical_not(is_end))
        def _():
            lo_final(0, near, piece).start()

    input_out[...] = (gm_ref[...] + inv * scaled - inputs * (inv * inv * inv * along)).astype(jnp.bfloat16)
    for peer in others:
        gain_landed(peer).wait_recv()
    gains_own[...] = gains_line[0] + gains_line[1] + gains_line[2] + gains_line[3]
    gains_keep = pltpu.make_async_copy(gains_own, gains_in.at[d], local_sem.at[14])
    gains_keep.start()

    def gains_copy(k):
        return remote(
            gains_own, gains_in.at[d], gd_send.at[k - 1], gd_recv.at[d], dp=lax.rem(d + k, ndp)
        )

    for k in range(1, ndp):
        gains_copy(k).start()
    total = chip_sum(1)
    q_out[...] = total[:, :inner]
    k_out[...] = total[:, inner : 2 * inner]
    v_out[...] = total[:, 2 * inner :]
    total = og_line[t].astype(full)
    for peer in others:
        line_in(peer).wait_recv()
        total = total + og_line_in[peer].astype(full)
    o_out[...] = total

    def others_of(landing, send, recv):
        for k in range(1, ndp):
            peer = lax.rem(d + k, ndp)
            remote(landing.at[peer], landing.at[peer], send.at[k - 1], recv.at[peer], dp=peer).wait_recv()

    others_of(dist_in, dist_send, dist_recv)
    if fused:
        own_feed.wait()
        for which in range(2):
            for k in range(1, chips):
                feed_copy(which, k).wait_recv()
    for piece in range(pieces):
        lo_final(0, near, piece).wait_recv()
        lo_mate(piece).wait_recv()
    others_of(gains_in, gd_send, gd_recv)
    dist_keep.wait()
    gains_keep.wait()

    for peer in others:
        swap(peer).wait_send()
        give(peer).wait_send()
        line_copy_out(peer).wait_send()
        gain_copy(peer).wait_send()
    for piece in range(pieces):
        lo_mate(piece).wait_send()

        @pl.when(is_end)
        def _():
            lo_acc(piece).wait_send()

        @pl.when(jnp.logical_not(is_end))
        def _():
            lo_final(0, near, piece).wait_send()
            lo_final(1, far, piece).wait_send()

    if fused:
        for which in range(2):
            for k in range(1, chips):
                feed_copy(which, k).wait_send()
    for kind in range(2):
        for c in range(chips):
            pair(kind, c).wait_send()
        for k in range(1, chips):
            chip_copy(kind, k).wait_send()
    for k in range(1, ndp):
        dist_copy(k).wait_send()
        gains_copy(k).wait_send()


def back(nt, ndp, grad_attended, grad_middle, tokens, gain, gain2_part, attended, qkv, probs_low, probs_high, first_all, weights, layer_parts, layer_far, feed_grads):
    rows, width = tokens.shape
    heads = probs_low.shape[0]
    inner = qkv.shape[2]
    head_dim = inner // heads
    low, full = jnp.bfloat16, jnp.float32
    pieces = 2
    share, chips = width // ndp, ndp // 2
    grad_type = low if share % 16 == 0 else full
    hbm = pl.BlockSpec(memory_space=pl.ANY)
    vmem = pl.BlockSpec(memory_space=pltpu.VMEM)
    dma = pltpu.SemaphoreType.DMA
    shape = jax.ShapeDtypeStruct
    reach = SPAN + QB
    scratch = lambda *dims, kind=low: pltpu.VMEM(dims, kind)
    part = shape((share, inner), full)
    fused = feed_grads.ndim == 4
    hidden = feed_grads.shape[-1]
    feeds = [dma((chips - 1, 2)), dma((chips - 1, 2))] if fused else []
    return pl.pallas_call(
        functools.partial(back_kernel, nt, ndp, pieces, heads, head_dim, grad_type, fused),
        out_shape=(
            shape((rows, width), low), part, part, part, part,
            shape((ndp, 2, width), full), shape((ndp, heads, reach), full),
            shape((rows, width), low), shape((rows, width), low),
        ) + (shape((chips, 2, share, hidden), low),) * fused,
        in_specs=[vmem] * 3 + [hbm] * (10 + fused),
        out_specs=(vmem,) * 5 + (hbm,) * (4 + fused),
        scratch_shapes=[
            scratch(rows, width, kind=full), scratch(rows, width), scratch(nt, rows // 2, 2 * inner),
            scratch(nt, rows // 2, 2 * inner), scratch(3, LEN, inner), scratch(heads, HALF, HALF), scratch(heads, HALF, LEN),
            scratch(nt, rows, width), scratch(nt, 3 * inner, width), scratch(3, rows, width), scratch(rows, width), scratch(rows, width),
            scratch(nt * rows, 3 * inner), scratch(nt, rows // 2, 6 * inner), scratch(nt, rows // 2, 6 * inner), scratch(heads, QB, reach, kind=full),
            scratch(heads, LEN, head_dim, kind=full), scratch(heads, LEN, head_dim, kind=full),
            scratch(width, nt * inner, kind=grad_type), scratch(chips, share, nt * inner, kind=grad_type),
            scratch(chips - 1, share, nt * inner, kind=grad_type),
            scratch(nt, share, inner, kind=grad_type), scratch(nt, share, inner, kind=grad_type),
            scratch(width, 3 * inner, kind=grad_type), scratch(chips, share, 3 * inner, kind=grad_type),
            scratch(chips - 1, share, 3 * inner, kind=grad_type),
            scratch(nt, 2, width, kind=full), scratch(2, width, kind=full), scratch(heads, reach, kind=full),
            dma((nt,)), dma((nt,)), dma((nt,)), dma((nt,)), dma((3, pieces)), dma((3, pieces)),
            dma((2, chips)), dma((2, chips)), dma((2, chips - 1)), dma((2, chips - 1)), dma((nt,)), dma((nt,)),
            dma((nt,)), dma((nt,)), dma((ndp - 1,)), dma((ndp,)), dma((ndp - 1,)), dma((ndp,)), dma((15,)), *feeds,
        ],
        compiler_params=pltpu.CompilerParams(
            vmem_limit_bytes=VMEM_LIMIT, collective_id=2, has_side_effects=True
        ),
        cost_estimate=pl.CostEstimate(flops=60 * 10**9, bytes_accessed=200 * 10**6, transcendentals=0),
        name="back",
    )(
        grad_attended, gain, gain2_part, grad_middle, tokens, attended,
        qkv, probs_low, probs_high, first_all, weights, layer_parts, layer_far, *((feed_grads,) if fused else ()),
    )


def finish_kernel(
    fused, bucket_ref, base_ref, far_ref, mate_ref, input_ref, q_ref, k_ref, v_ref, o_ref, gains_ref, dist_ref, *rest,
):
    if fused:
        feed_ref, down_ref, *rest = rest
    layer_out, input_out, gain_out, q_out, k_out, v_out, o_out, table_out, gain2_out, *feed_outs = rest
    full = jnp.float32
    layer_out[...] = (base_ref[...] + far_ref[...].astype(full) + mate_ref[...].astype(full)).astype(jnp.bfloat16)
    input_out[...] = input_ref[...]
    for a, b in ((q_ref, q_out), (k_ref, k_out), (v_ref, v_out), (o_ref, o_out)):
        b[...] = a[...]

    @pl.when(pl.program_id(0) == 0)
    def _():
        gains, dist = gains_ref[0], dist_ref[0]
        for k in range(1, gains_ref.shape[0]):
            gains = gains + gains_ref[k]
            dist = dist + dist_ref[k]
        gain_out[...] = gains[0:1].reshape(gain_out.shape)
        gain2_out[...] = gains[1:2].reshape(gain2_out.shape)
        reach = dist.shape[1]
        shifted = jnp.concatenate([jnp.zeros((1, 1), jnp.int32), row_of(bucket_ref)], axis=1)[:, :reach]
        hot = (lax.broadcasted_iota(jnp.int32, (NB, reach), 0) == shifted).astype(full)
        table_out[...] = lax.dot_general(
            dist, hot, (((1,), (1,)), ((), ())), precision=HIGHEST, preferred_element_type=full
        )

    for which in range(len(feed_outs)):
        parts = [down_ref[k] if which == 2 else feed_ref[k, which] for k in range(feed_ref.shape[0])]
        total = parts[0].astype(full)
        for part in parts[1:]:
            total = total + part.astype(full)
        feed_outs[which][...] = total


def finish(buckets, base, outs):
    fused = len(outs) > 9
    input_grad, query_grad, key_grad, value_grad, out_grad, gains, dist, far_in, mate_in = outs[:9]
    rows, width = base.shape
    share, inner = query_grad.shape
    low, full = jnp.bfloat16, jnp.float32
    shape = jax.ShapeDtypeStruct
    steps = 4 if share % 64 == 0 and rows % 64 == 0 else 1
    vmem = pl.BlockSpec(memory_space=pltpu.VMEM)
    wide = pl.BlockSpec((rows // steps, width), lambda i: (i, 0))
    small = pl.BlockSpec((share // steps, inner), lambda i: (i, 0))
    part = shape(query_grad.shape, full)
    ins, feeds, blocks = [], (), ()
    if fused:
        chips, kinds, _, hidden = outs[9].shape
        ins = [
            pl.BlockSpec((chips, kinds, share // steps, hidden), lambda i: (0, 0, i, 0)),
            pl.BlockSpec((chips, share // steps, hidden), lambda i: (0, i, 0)),
        ]
        feeds = (shape((share, hidden), full),) * (kinds + 1)
        blocks = (pl.BlockSpec((share // steps, hidden), lambda i: (i, 0)),) * (kinds + 1)
    return pl.pallas_call(
        functools.partial(finish_kernel, fused),
        grid=(steps,),
        out_shape=(
            shape((rows, width), low), shape((rows, width), low), shape((width,), full), part, part, part, part,
            shape((dist.shape[1], NB), full), shape((width,), full),
        ) + feeds,
        in_specs=[vmem] + [wide] * 4 + [small] * 4 + [vmem] * 2 + ins,
        out_specs=(wide, wide, vmem) + (small,) * 4 + (vmem, vmem) + blocks,
        compiler_params=pltpu.CompilerParams(vmem_limit_bytes=VMEM_LIMIT),
        name="finish",
    )(
        buckets, base, far_in, mate_in, input_grad, query_grad, key_grad, value_grad, out_grad, gains, dist,
        *outs[9:],
    )


def per_device(
    tokens,
    first_gain,
    query_weight,
    key_weight,
    value_weight,
    out_weight,
    bucket_table,
    second_gain,
    gate_weight,
    up_weight,
    down_weight,
    piece_start,
    bucket_index,
    cotangent,
):
    nt, ndp = lax.axis_size("tensor"), lax.axis_size("dp")
    weights = (query_weight.T, key_weight.T, value_weight.T, out_weight.T)
    first_all, cot_all, qkv, probs_low, probs_high, attended, whole, middle, second = gather_attend(
        nt, ndp, tokens, cotangent, first_gain, second_gain, weights, bucket_index, bucket_table.T, piece_start
    )
    base, grad_middle, second_part, grad_attended, layer_parts, layer_far, feed_grads, *down_in = feed(
        nt, ndp, middle, second, second_gain, cotangent, whole, cot_all, gate_weight.T, up_weight.T, down_weight.T
    )
    outs = back(
        nt, ndp, grad_attended, grad_middle, tokens, first_gain, second_part, attended,
        qkv, probs_low, probs_high, first_all, whole, layer_parts, layer_far, feed_grads,
    )
    outs = finish(bucket_index, base, (*outs, *down_in))
    if feed_grads.ndim == 3:
        sums = lax.psum_scatter(feed_grads, "dp", scatter_dimension=1, tiled=True).astype(jnp.float32)
        outs = (*outs, sums[0], sums[1], sums[2])
    return (*outs[:7], outs[7].T, *outs[8:])


def solution(mesh):
    return jax.shard_map(
        per_device,
        mesh=mesh,
        in_specs=(
            P(("dp", "tensor"), None),
            P(),
            P(None, "tensor"),
            P(None, "tensor"),
            P(None, "tensor"),
            P(None, "tensor"),
            P(None, "tensor"),
            P(),
            P(None, "tensor"),
            P(None, "tensor"),
            P(None, "tensor"),
            P("dp", None),
            P(),
            P(("dp", "tensor"), None),
        ),
        out_specs=(
            P(("dp", "tensor"), None),
            P(("dp", "tensor"), None),
            P(),
            P("dp", "tensor"),
            P("dp", "tensor"),
            P("dp", "tensor"),
            P("dp", "tensor"),
            P(None, "tensor"),
            P(),
            P("dp", "tensor"),
            P("dp", "tensor"),
            P("dp", "tensor"),
        ),
        check_vma=False,
    )
```

```python
import functools

import jax
import jax.numpy as jnp
from jax import lax
from jax.experimental import pallas as pl
from jax.experimental.pallas import tpu as pltpu
from jax.sharding import PartitionSpec as P

NB = 32
LEN = 1024
QB = 256
PIECE = 256
NPIECE = 2
HALF = LEN // NPIECE
SPAN = 5 * QB
DIST = 2 * LEN

EPSILON = 1e-06
MASKED = -1000000000.0
HIGHEST = lax.Precision.HIGHEST
VMEM_LIMIT = 60 * 1024 * 1024
MESH = pl.DeviceIdType.MESH


def normed(row_block, gain_vec):
    inv_rms = lax.rsqrt(jnp.mean(row_block * row_block, axis=-1, keepdims=True) + EPSILON)
    return row_block * inv_rms * gain_vec


def dot(a, b, dims):
    return lax.dot_general(a, b, (dims, ((), ())), preferred_element_type=jnp.float32)


def key_count(block):
    return HALF if (block + 1) * QB <= HALF else LEN


def toeplitz(bucket_ref, table_ref, head):
    bucket_row = jnp.concatenate([row_of(bucket_ref), jnp.zeros((1, 1), jnp.int32)], axis=1)
    row = jnp.zeros(bucket_row.shape, jnp.float32)
    for bucket in range(NB):
        row = jnp.where(bucket_row == bucket, table_ref[head, bucket], row)
    rows = jnp.broadcast_to(row, (QB, DIST))
    return pltpu.roll(rows, DIST - (QB - 1), 1, stride=1, stride_axis=0)[:, :SPAN]


def row_of(ref):
    return ref[...].reshape(1, ref.shape[0])


def label_of(position, starts):
    label = jnp.zeros(position.shape, jnp.int32)
    for piece, start in enumerate(starts):
        inside = (position >= start) & (position < start + PIECE)
        label = jnp.where(inside, piece + 1, label)
    return label


def allowed_block(block, starts):
    keys = key_count(block)
    query = block * QB + lax.broadcasted_iota(jnp.int32, (QB, 1), 0)
    key = lax.broadcasted_iota(jnp.int32, (1, keys), 1)
    query_label = label_of(query, starts)
    key_label = label_of(key, starts)
    return (key <= query) | ((query_label == key_label) & (query_label > 0))


def attend_block(block, head_dim, allowed, qkv_ref, bias_ref, low_ref, high_ref):
    keys = key_count(block)
    first = LEN - QB - block * QB
    rows = pl.ds(block * QB, QB)
    outs = []
    for head in range(bias_ref.shape[0]):
        cols = pl.ds(head * head_dim, head_dim)
        raw = dot(qkv_ref[0, rows, cols], qkv_ref[1, pl.ds(0, keys), cols], ((1,), (1,)))
        scores = jnp.where(allowed, raw + bias_ref[head, :, pl.ds(first, keys)], MASKED)
        peak = jnp.max(scores, axis=-1, keepdims=True)
        powered = jnp.exp(scores - peak)
        total = jnp.sum(powered, axis=-1, keepdims=True)
        probs = (powered * (1.0 / total)).astype(jnp.bfloat16)
        if keys == HALF:
            low_ref[head, rows, :] = probs
        else:
            high_ref[head, pl.ds(block * QB - HALF, QB), :] = probs
        outs.append(dot(probs, qkv_ref[2, pl.ds(0, keys), cols], ((1,), (0,))))
    return jnp.concatenate(outs, axis=1).astype(jnp.bfloat16)


def pack(rows):
    half = rows.shape[0] // 2
    return jnp.concatenate([rows[:half], rows[half:]], axis=1)


def unpack(packed, start, width):
    half = packed.shape[1] // 2
    return jnp.concatenate(
        [packed[:, start : start + width], packed[:, half + start : half + start + width]], axis=0
    )


def greet(t, nt):
    barrier = pltpu.get_barrier_semaphore()
    for k in range(1, nt):
        pl.semaphore_signal(
            barrier, inc=1, device_id={"tensor": lax.rem(t + k, nt)}, device_id_type=MESH
        )
    return barrier


def line_copy(t, nt, way, step, buf, piece, pieces, send_sem, recv_sem):
    sign = 1 if way == 0 else -1
    origin = jnp.clip(t - sign * step, 0, nt - 1)
    rows = buf.shape[1] // pieces
    part = buf.at[origin, pl.ds(piece * rows, rows)]
    return pltpu.make_async_remote_copy(
        src_ref=part,
        dst_ref=part,
        send_sem=send_sem,
        recv_sem=recv_sem,
        device_id={"tensor": jnp.clip(t + sign, 0, nt - 1)},
        device_id_type=MESH,
    )


def gather_attend_kernel(
    nt, ndp, pieces, heads, head_dim, exchange,
    x_ref, cot_ref, gain_ref, gain2_ref, bucket_ref, table_ref, start_ref, *rest,
):
    weight_refs, rest = rest[: 4 if exchange else 1], rest[4 if exchange else 1 :]
    (
        first_out, cot_out, qkv_out, low_out, high_out, own_out, whole_out, middle_out, second_out,
        first, qkv, low, high, bias, att, own, whole,
        send_sem, recv_sem, swap_send, swap_recv, line_send, line_recv, chip_send, chip_recv, core_send, core_recv,
        local_sem,
    ) = rest
    t = lax.axis_index("tensor")
    d = lax.axis_index("dp")
    core = lax.rem(d, 2)
    chip = d // 2
    chips = ndp // 2
    barrier = greet(t, nt)
    greeted = nt - 1
    if exchange:
        for k in range(chips):
            peer = 2 * lax.rem(chip + k, chips) + core if k else d + 1 - 2 * core
            pl.semaphore_signal(barrier, inc=1, device_id={"dp": peer}, device_id_type=MESH)
        greeted += chips
    inner = heads * head_dim
    share = whole.shape[1] // ndp
    own_cot = pltpu.make_async_copy(cot_ref, cot_out.at[t], local_sem.at[0])
    own_cot.start()
    if exchange:
        loads = [
            pltpu.make_async_copy(weight, whole.at[t, pl.ds(i * inner, inner)], local_sem.at[1 + i])
            for i, weight in enumerate(weight_refs)
        ]
    else:
        loads = [pltpu.make_async_copy(weight_refs[0], whole, local_sem.at[1])]
    for one in loads:
        one.start()

    def slices(index, plane):
        return whole.at[plane, pl.ds(pl.multiple_of(index * share, share), share)]

    def remote(src, dst, send, recv, **target):
        return pltpu.make_async_remote_copy(
            src_ref=src, dst_ref=dst, send_sem=send, recv_sem=recv, device_id=target, device_id_type=MESH
        )

    def plane_at(q):
        return lax.rem(t + q, nt)

    def to_plane(q):
        return remote(slices(d, t), slices(d, t), line_send.at[q - 1], line_recv.at[t], tensor=plane_at(q))

    def from_plane(q):
        p = plane_at(q)
        return remote(slices(d, p), slices(d, p), line_send.at[q - 1], line_recv.at[p], tensor=p)

    def to_chip(k, q):
        part = slices(d, plane_at(q))
        return remote(
            part, part, chip_send.at[k - 1, q - 1], chip_recv.at[k - 1, q - 1], dp=2 * lax.rem(chip + k, chips) + core
        )

    def from_chip(k, q):
        peer = 2 * lax.rem(chip - k + chips, chips) + core
        part = slices(peer, plane_at(q))
        return remote(part, part, chip_send.at[k - 1, q - 1], chip_recv.at[k - 1, q - 1], dp=peer)

    def to_core(k, q):
        part = slices(2 * lax.rem(chip - k + chips, chips) + core, plane_at(q))
        return remote(part, part, core_send.at[k, q - 1], core_recv.at[k, q - 1], dp=d + 1 - 2 * core)

    def from_core(k, q):
        part = slices(2 * lax.rem(chip - k + chips, chips) + 1 - core, plane_at(q))
        return remote(part, part, core_send.at[k, q - 1], core_recv.at[k, q - 1], dp=d + 1 - 2 * core)

    for one in loads:
        one.wait()
    pl.semaphore_wait(barrier, greeted)
    if exchange:
        for q in range(1, nt):
            to_plane(q).start()
    first[t] = normed(x_ref[...].astype(jnp.float32), row_of(gain_ref)).astype(jnp.bfloat16)

    def copy(way, stage, step, piece):
        buf = first if stage == 0 else cot_out
        return line_copy(
            t, nt, way, step, buf, piece, pieces,
            send_sem.at[way, stage, step, piece], recv_sem.at[way, stage, step, piece],
        )

    def landed(way, stage, step, piece):
        sign = 1 if way == 0 else -1
        buf = first if stage == 0 else cot_out
        rows = buf.shape[1] // pieces
        part = buf.at[jnp.clip(t - sign * step, 0, nt - 1), pl.ds(piece * rows, rows)]
        remote(
            part, part, send_sem.at[way, stage, step - 1, piece], recv_sem.at[way, stage, step - 1, piece],
            tensor=jnp.clip(t + sign, 0, nt - 1),
        ).wait_recv()

    ways = ((0, t, t < nt - 1), (1, nt - 1 - t, t > 0))

    def tick(k):
        for piece in range(pieces):
            for way, last, onward in ways:
                if k < nt:
                    @pl.when(k <= last)
                    def _():
                        if k > 0:
                            landed(way, 0, k, piece)

                        @pl.when(onward)
                        def _():
                            copy(way, 0, k, piece).start()

                if k > 0:
                    step = k - last - 1

                    @pl.when((step >= 1) & (step <= last))
                    def _():
                        landed(way, 1, step, piece)

                        @pl.when(onward)
                        def _():
                            copy(way, 1, step, piece).start()

                    @pl.when((step == 0) & onward)
                    def _():
                        copy(way, 0, last, piece).wait_send()
                        copy(way, 1, 0, piece).start()

    def project(origin):
        rows = pl.ds(pl.multiple_of(origin * QB, QB), QB)
        for place in range(3):
            weight = whole[t, pl.ds(place * inner, inner), :]
            qkv[place, rows, :] = dot(first[origin], weight, ((1,), (1,))).astype(jnp.bfloat16)

    tick(0)
    project(t)
    for head in range(heads):
        bias[head] = toeplitz(bucket_ref, table_ref, head)
    own_cot.wait()
    for k in range(1, nt):
        tick(k)

        @pl.when(t - k >= 0)
        def _():
            project(t - k)

        @pl.when(t + k < nt)
        def _():
            project(t + k)

        if exchange and k == 2:
            for q in range(1, nt):
                from_plane(q).wait_recv()
                for j in range(1, chips):
                    to_chip(j, q).start()
                to_core(0, q).start()

    starts = [start_ref[0, piece] for piece in range(NPIECE)]
    keep = [
        pltpu.make_async_copy(first, first_out, local_sem.at[5]),
        pltpu.make_async_copy(qkv, qkv_out, local_sem.at[6]),
    ]
    for one in keep:
        one.start()

    def swap(block):
        return remote(att.at[block], own.at[t], swap_send.at[block], swap_recv.at[t], tensor=block)

    for block in range(LEN // QB):
        att[block] = pack(attend_block(block, head_dim, allowed_block(block, starts), qkv, bias, low, high))

        @pl.when(t != block)
        def _():
            swap(block).start()

        @pl.when(t == block)
        def _():
            own[t] = att[block]

    late = [
        pltpu.make_async_copy(low, low_out, local_sem.at[7]),
        pltpu.make_async_copy(high, high_out, local_sem.at[8]),
    ]
    for one in late:
        one.start()
    tick(nt)
    if exchange:
        for k in range(1, chips):
            for q in range(1, nt):
                from_chip(k, q).wait_recv()
                to_core(k, q).start()
    tick(nt + 1)
    for block in range(nt):
        @pl.when(t != block)
        def _():
            remote(att.at[block], own.at[block], swap_send.at[block], swap_recv.at[block], tensor=block).wait_recv()

    if exchange:
        for k in range(chips):
            for q in range(1, nt):
                from_core(k, q).wait_recv()
    late += [
        pltpu.make_async_copy(own, own_out, local_sem.at[9]),
        pltpu.make_async_copy(whole, whole_out, local_sem.at[10]),
    ]
    for one in late[2:]:
        one.start()
    total = x_ref[...].astype(jnp.float32)
    for j in range(nt):
        total = total + dot(unpack(own[j], 0, inner), whole[j, pl.ds(3 * inner, inner), :], ((1,), (0,)))
    middle_out[...] = total
    second_out[...] = normed(total, row_of(gain2_ref)).astype(jnp.bfloat16)
    for k in range(nt + 2, 2 * nt):
        tick(k)
    for block in range(nt):
        @pl.when(t != block)
        def _():
            swap(block).wait_send()

    for one in keep + late:
        one.wait()
    if exchange:
        for q in range(1, nt):
            to_plane(q).wait_send()
            for k in range(1, chips):
                to_chip(k, q).wait_send()
            for k in range(chips):
                to_core(k, q).wait_send()
    for piece in range(pieces):
        for way, last, onward in ways:
            for stage in range(2):
                for step in range(nt):
                    @pl.when(onward & ((step < last) if stage == 0 else (step <= last)))
                    def _():
                        copy(way, stage, step, piece).wait_send()


def gather_attend(nt, ndp, tokens, cotangent, gain, gain2, weights, buckets, table, starts):
    heads = table.shape[0]
    rows, width = tokens.shape
    inner = weights[0].shape[0]
    low, full = jnp.bfloat16, jnp.float32
    pieces = 2
    exchange = (4 * inner // ndp) % 16 == 0
    if not exchange:
        joined = jnp.concatenate(weights, axis=0)
        part = joined.shape[0] // ndp
        mine = lax.dynamic_slice_in_dim(joined, lax.axis_index("dp") * part, part, 0)
        weights = (lax.all_gather(mine, ("tensor", "dp"), axis=0, tiled=True).reshape(nt, *joined.shape),)
    chips = ndp // 2
    smem = pl.BlockSpec(memory_space=pltpu.SMEM)
    hbm = pl.BlockSpec(memory_space=pl.ANY)
    vmem = pl.BlockSpec(memory_space=pltpu.VMEM)
    shapes = (
        (nt, rows, width), (nt, rows, width), (3, LEN, inner), (heads, HALF, HALF), (heads, HALF, LEN),
        (nt, rows // 2, 2 * inner), (nt, 4 * inner, width),
    )
    dma = pltpu.SemaphoreType.DMA
    return pl.pallas_call(
        functools.partial(gather_attend_kernel, nt, ndp, pieces, heads, inner // heads, exchange),
        out_shape=tuple(jax.ShapeDtypeStruct(shape, low) for shape in shapes)
        + (jax.ShapeDtypeStruct((rows, width), full), jax.ShapeDtypeStruct((rows, width), low)),
        in_specs=[vmem, hbm, vmem, vmem, vmem, smem, smem] + [hbm] * len(weights),
        out_specs=(hbm,) * 7 + (vmem, vmem),
        scratch_shapes=[
            pltpu.VMEM((nt, rows, width), low),
            pltpu.VMEM((3, LEN, inner), low),
            pltpu.VMEM((heads, HALF, HALF), low),
            pltpu.VMEM((heads, HALF, LEN), low),
            pltpu.VMEM((heads, QB, SPAN), full),
            pltpu.VMEM((nt, rows // 2, 2 * inner), low),
            pltpu.VMEM((nt, rows // 2, 2 * inner), low),
            pltpu.VMEM((nt, 4 * inner, width), low),
            dma((2, 2, nt, pieces)), dma((2, 2, nt, pieces)), dma((nt,)), dma((nt,)),
            dma((nt - 1,)), dma((nt,)), dma((chips - 1, nt - 1)), dma((chips - 1, nt - 1)),
            dma((chips, nt - 1)), dma((chips, nt - 1)), dma((11,)),
        ],
        compiler_params=pltpu.CompilerParams(
            vmem_limit_bytes=VMEM_LIMIT, collective_id=0, has_side_effects=True
        ),
        name="gather_attend",
    )(tokens, cotangent, gain, gain2, buckets, table, starts, *weights)


def fold_diagonals(grid):
    rows = QB // 2
    width = grid.shape[1]
    while rows >= 1:
        grid = grid[:rows] + pltpu.roll(grid[rows : 2 * rows], width - rows, 1)
        rows //= 2
    return grid


def gelu_parts(v):
    root, cubic = 0.7978845608028654, 0.044715
    square = v * v
    bend = jnp.tanh(root * v * (1.0 + cubic * square))
    half = 0.5 * (1.0 + bend)
    slope = half + 0.5 * v * (1.0 - bend * bend) * root * (1.0 + 3.0 * cubic * square)
    return v * half, slope


def feed_kernel(
    nt, ndp, pieces, halves, fused,
    gain_ref, middle_hbm, second_hbm, cot_own_hbm, whole_hbm, cot_hbm, wg_hbm, wu_hbm, wd_hbm,
    base_out, gm_out, gain_out, ga_out, lo_out, lo_in, grads_out, *rest,
):
    if fused:
        down_out, *rest = rest
    (
        middle, cot_own_ref, buf, cot, wg, wu, wd, hid, gg, gu, gs, lo, wo, mate_in, acc_in, far_in, grads, *rest,
    ) = rest
    *rest, send_sem, recv_sem, rs_send, rs_recv, lo_send, lo_recv, local_sem = rest
    t = lax.axis_index("tensor")
    d = lax.axis_index("dp")
    core = lax.rem(d, 2)
    chips = ndp // 2
    barrier = greet(t, nt)
    own_load = pltpu.make_async_copy(second_hbm, buf.at[t], local_sem.at[11])
    own_load.start()
    if fused:
        sums, pair_send, pair_recv, chip_send, chip_recv = rest
        chip = d // 2
        for k in range(chips):
            peer = 2 * lax.rem(chip + k, chips) + core if k else d + 1 - 2 * core
            pl.semaphore_signal(barrier, inc=1, device_id={"dp": peer}, device_id_type=MESH)
    loads = [
        pltpu.make_async_copy(a, b, local_sem.at[i])
        for i, (a, b) in enumerate(((wg_hbm, wg), (wu_hbm, wu), (wd_hbm, wd), (cot_hbm, cot)))
    ]
    for one in loads:
        one.start()
    row_count = middle.shape[0]
    size = row_count // pieces
    inner = wo.shape[1]
    wo_load = pltpu.make_async_copy(whole_hbm.at[:, pl.ds(3 * inner, inner)], wo, local_sem.at[4])
    wo_load.start()
    late_loads = [
        pltpu.make_async_copy(middle_hbm, middle, local_sem.at[9]),
        pltpu.make_async_copy(cot_own_hbm, cot_own_ref, local_sem.at[10]),
    ]
    for one in late_loads:
        one.start()
    keep = []
    own_load.wait()
    pl.semaphore_wait(barrier, nt - 1 + chips * fused)
    mate = t + 1 - 2 * lax.rem(t, 2)
    is_end = (t == 0) | (t == nt - 1)
    ways = ((0, t, t < nt - 1), (1, nt - 1 - t, t > 0))

    def copy(way, step, piece):
        return line_copy(
            t, nt, way, step, buf, piece, pieces,
            send_sem.at[way, step, piece], recv_sem.at[way, step, piece],
        )

    def landed(way, step, piece):
        sign = 1 if way == 0 else -1
        part = buf.at[jnp.clip(t - sign * step, 0, nt - 1), pl.ds(piece * size, size)]
        pltpu.make_async_remote_copy(
            src_ref=part, dst_ref=part,
            send_sem=send_sem.at[way, step - 1, piece], recv_sem=recv_sem.at[way, step - 1, piece],
            device_id={"tensor": jnp.clip(t + sign, 0, nt - 1)}, device_id_type=MESH,
        ).wait_recv()

    def remote(src, dst, target, send, recv):
        return pltpu.make_async_remote_copy(
            src_ref=src, dst_ref=dst, send_sem=send, recv_sem=recv,
            device_id={"tensor": target}, device_id_type=MESH,
        )

    wide = buf.shape[2] // halves

    def to_mate(piece, half):
        part = (pl.ds(piece * size, size), pl.ds(half * wide, wide))
        return remote(
            gs.at[(mate, *part)], mate_in.at[part], mate, rs_send.at[0, piece, half], rs_recv.at[0, piece, half]
        )

    def to_acc(origin, piece, half):
        part = (pl.ds(piece * size, size), pl.ds(half * wide, wide))
        j = lax.rem(origin, 2)
        return remote(
            gs.at[(origin, *part)], acc_in.at[(j, *part)], mate,
            rs_send.at[1 + j, piece, half], rs_recv.at[1 + j, piece, half],
        )

    def to_far(origin, piece, half):
        part = (pl.ds(piece * size, size), pl.ds(half * wide, wide))
        j = lax.rem(origin, 2)
        return remote(
            gs.at[(origin, *part)], far_in.at[part], origin, rs_send.at[3 + j, piece, half], rs_recv.at[3, piece, half]
        )

    def feed(origin, piece):
        rows = pl.ds(pl.multiple_of(piece * size, size), size)
        flat = pl.ds(pl.multiple_of(origin * row_count + piece * size, size), size)
        normal = buf[origin, rows]
        gate = dot(normal, wg[...], ((1,), (1,)))
        up = dot(normal, wu[...], ((1,), (1,)))
        grad_hidden = dot(cot[origin, rows], wd[...], ((1,), (1,)))
        act, slope = gelu_parts(gate)
        hidden = (act * up).astype(jnp.bfloat16)
        hid[flat, :] = hidden
        grad_gate = (grad_hidden * up * slope).astype(jnp.bfloat16)
        grad_up = (grad_hidden * act).astype(jnp.bfloat16)
        gg[flat, :] = grad_gate
        gu[flat, :] = grad_up
        for half in range(halves):
            cols = pl.ds(half * wide, wide)
            gs[origin, rows, cols] = (
                dot(grad_gate, wg[:, cols], ((1,), (0,))) + dot(grad_up, wu[:, cols], ((1,), (0,)))
            ).astype(jnp.bfloat16)

            @pl.when(origin == mate)
            def _():
                to_mate(piece, half).start()

            @pl.when((origin != mate) & (origin != t) & is_end)
            def _():
                to_acc(origin, piece, half).start()

        lo[origin, rows] = dot(hidden, wd[...], ((1,), (0,))).astype(jnp.bfloat16)

    span = 256
    flat_rows = nt * row_count
    spans = buf.shape[2] // span
    head = jnp.where(t < nt // 2, 0, 1)
    last_one = jnp.where(t < nt // 2, nt - 1, 0)
    head_rows = pl.ds(pl.multiple_of(head * row_count, row_count), flat_rows - row_count)
    last_rows = pl.ds(pl.multiple_of(last_one * row_count, row_count), row_count)

    def columns(ref, i):
        cols = pl.ds(pl.multiple_of(i * span, span), span)
        return ref[pl.ds(head, nt - 1), :, cols].reshape(flat_rows - row_count, span)

    def grad_head(which, left, right, rows):
        grads[which, rows, :] = dot(left, right[head_rows, :], ((0,), (0,))).astype(jnp.bfloat16)

    def grad_last(which, left, right, rows):
        grads[which, rows, :] = (
            grads[which, rows, :].astype(jnp.float32) + dot(left, right[last_rows, :], ((0,), (0,)))
        ).astype(jnp.bfloat16)

    def down_head(i, carry):
        rows = pl.ds(pl.multiple_of(i * span, span), span)
        grad_head(2, columns(cot, i), hid, rows)
        return carry

    def gate_up_head(i, carry):
        rows = pl.ds(pl.multiple_of(i * span, span), span)
        left = columns(buf, i)
        grad_head(0, left, gg, rows)
        grad_head(1, left, gu, rows)
        return carry

    def down_last(i, carry):
        rows = pl.ds(pl.multiple_of(i * span, span), span)
        grad_last(2, cot[last_one, :, rows], hid, rows)
        return carry

    def gate_up_last(i, carry):
        rows = pl.ds(pl.multiple_of(i * span, span), span)
        left = buf[last_one, :, rows]
        grad_last(0, left, gg, rows)
        grad_last(1, left, gu, rows)
        return carry

    for piece in range(pieces):
        for way, last, onward in ways:
            @pl.when(onward)
            def _():
                copy(way, 0, piece).start()

    for one in loads:
        one.wait()

    def unit(u, carry):
        step = u // pieces
        piece = lax.rem(u, pieces)

        @pl.when(step > 0)
        def _():
            for way, last, onward in ways:
                @pl.when(step <= last)
                def _():
                    landed(way, step, piece)

                    @pl.when(onward)
                    def _():
                        copy(way, step, piece).start()

        def side(way, carry):
            origin = t - (1 - 2 * way) * step
            there = (origin >= 0) & (origin < nt) & ((step > 0) | (way == 0))

            @pl.when(there)
            def _():
                feed(origin, piece)

            return carry

        lax.fori_loop(0, 2, side, carry)

        @pl.when(u == (nt - 1) * pieces - 1)
        def _():
            lax.fori_loop(0, spans, down_head, 0)

        @pl.when(u == (nt - 1) * pieces)
        def _():
            lax.fori_loop(0, spans, gate_up_head, 0)

        return carry

    lax.fori_loop(0, nt * pieces, unit, 0)

    near = jnp.where(t < nt // 2, nt // 2, nt // 2 - 1)
    far = jnp.where(t < nt // 2, nt - 1, 0)

    def pass_on(origin, piece):
        @pl.when(jnp.logical_not(is_end))
        def _():
            rows = pl.ds(piece * size, size)
            j = lax.rem(origin, 2)
            for half in range(halves):
                to_acc(origin, piece, half).wait_recv()
                cols = pl.ds(half * wide, wide)
                gs[origin, rows, cols] = (
                    gs[origin, rows, cols].astype(jnp.float32) + acc_in[j, rows, cols].astype(jnp.float32)
                ).astype(jnp.bfloat16)
                to_far(origin, piece, half).start()

    share = buf.shape[2] // ndp

    def block_rows(index):
        return pl.ds(pl.multiple_of(index * share, share), share)

    def pair(which, c):
        return pltpu.make_async_remote_copy(
            src_ref=grads.at[which, block_rows(2 * c + 1 - core)], dst_ref=sums.at[which, c],
            send_sem=pair_send.at[which, c], recv_sem=pair_recv.at[which, c],
            device_id={"dp": d + 1 - 2 * core}, device_id_type=MESH,
        )

    def down_copy(k):
        to = lax.rem(chip + k, chips)
        return pltpu.make_async_remote_copy(
            src_ref=sums.at[2, to], dst_ref=down_out.at[k - 1],
            send_sem=chip_send.at[k - 1], recv_sem=chip_recv.at[k - 1],
            device_id={"dp": 2 * to + core}, device_id_type=MESH,
        )

    def pair_start(*which):
        if fused:
            for w in which:
                for c in range(chips):
                    pair(w, c).start()

    def pair_sum(which):
        if fused:
            for c in range(chips):
                pair(which, c).wait_recv()
                sums[which, c] = (
                    grads[which, block_rows(2 * c + core)].astype(jnp.float32) + sums[which, c].astype(jnp.float32)
                ).astype(jnp.bfloat16)
            if which == 2:
                for k in range(1, chips):
                    down_copy(k).start()
                one = pltpu.make_async_copy(sums.at[2, chip], down_out.at[chips - 1], local_sem.at[8])
            else:
                one = pltpu.make_async_copy(sums.at[which], grads_out.at[which], local_sem.at[6 + which])
        else:
            one = pltpu.make_async_copy(grads.at[which], grads_out.at[which], local_sem.at[6 + which])
        one.start()
        keep.append(one)

    def lo_acc(piece):
        rows = pl.ds(piece * size, size)
        return remote(lo.at[far, rows], lo_in.at[rows], mate, lo_send.at[piece], lo_recv.at[piece])

    @pl.when(is_end)
    def _():
        for piece in range(pieces):
            lo_acc(piece).start()

    keep.append(pltpu.make_async_copy(lo, lo_out, local_sem.at[5]))
    keep[-1].start()
    pass_on(near, 0)
    lax.fori_loop(0, spans, down_last, 0)
    pair_start(2)
    pass_on(near, 1)
    lax.fori_loop(0, spans, gate_up_last, 0)
    pair_start(0, 1)
    pair_sum(2)
    pass_on(far, 0)
    pass_on(far, 1)
    for one in late_loads:
        one.wait()

    wo_load.wait()
    for piece in range(pieces):
        rows = pl.ds(piece * size, size)
        for half in range(halves):
            to_mate(piece, half).wait_recv()
            part = (rows, pl.ds(half * wide, wide))
            remote(
                gs.at[(t, *part)], far_in.at[part], mate, rs_send.at[3, piece, half], rs_recv.at[3, piece, half]
            ).wait_recv()
        grad_second = (
            gs[t, rows].astype(jnp.float32)
            + mate_in[rows].astype(jnp.float32)
            + far_in[rows].astype(jnp.float32)
        )
        mid = middle[rows]
        inv = lax.rsqrt(jnp.mean(mid * mid, axis=-1, keepdims=True) + EPSILON)
        scaled = row_of(gain_ref) * grad_second
        along = jnp.mean(scaled * mid, axis=-1, keepdims=True)
        grad_middle = cot_own_ref[rows].astype(jnp.float32) + inv * scaled - mid * (inv * inv * inv * along)
        gm_out[rows] = grad_middle
        part = jnp.sum(grad_second * mid * inv, axis=0, keepdims=True)
        if piece == 0:
            gain_out[...] = part
        else:
            gain_out[...] += part
        grad_low = grad_middle.astype(jnp.bfloat16)
        for j in range(nt):
            ga_out[j, :, pl.ds(piece * inner, inner)] = dot(grad_low, wo[j], ((1,), (1,))).astype(jnp.bfloat16)

    pair_sum(0)
    pair_sum(1)
    base_out[...] = middle[...] + lo[t].astype(jnp.float32)

    @pl.when(jnp.logical_not(is_end))
    def _():
        for piece in range(pieces):
            lo_acc(piece).wait_recv()

    for one in keep:
        one.wait()
    for piece in range(pieces):
        for way, last, onward in ways:
            for step in range(nt):
                @pl.when(onward & (step <= last))
                def _():
                    copy(way, step, piece).wait_send()

        @pl.when(is_end)
        def _():
            lo_acc(piece).wait_send()

        for half in range(halves):
            to_mate(piece, half).wait_send()
            for origin in (near, far):
                @pl.when(is_end)
                def _():
                    to_acc(origin, piece, half).wait_send()

                @pl.when(jnp.logical_not(is_end))
                def _():
                    to_far(origin, piece, half).wait_send()

    if fused:
        for which in range(3):
            for c in range(chips):
                pair(which, c).wait_send()
        for k in range(1, chips):
            down_copy(k).wait()


def feed(nt, ndp, middle, second, gain, cotangent, whole, cot_all, gate_weight, up_weight, down_weight):
    rows, width = middle.shape
    hidden = gate_weight.shape[0]
    low, full = jnp.bfloat16, jnp.float32
    pieces, halves = 2, 1
    hbm = pl.BlockSpec(memory_space=pl.ANY)
    vmem = pl.BlockSpec(memory_space=pltpu.VMEM)
    inner = whole.shape[1] // 4
    dma = pltpu.SemaphoreType.DMA
    shape = jax.ShapeDtypeStruct
    share, chips = width // ndp, ndp // 2
    fused = share % 16 == 0
    sums = (3, chips, share, hidden)
    pairs = [
        pltpu.VMEM(sums, low), dma((3, chips)), dma((3, chips)), dma((chips - 1,)), dma((chips - 1,))
    ] if fused else []
    return pl.pallas_call(
        functools.partial(feed_kernel, nt, ndp, pieces, halves, fused),
        out_shape=(
            shape((rows, width), full), shape((rows, width), full), shape((1, width), full),
            shape((nt, rows // 2, 2 * inner), low), shape((nt, rows, width), low), shape((rows, width), low),
            shape((2, *sums[1:]) if fused else (3, width, hidden), low),
        ) + (shape((chips, share, hidden), low),) * fused,
        in_specs=[vmem] + [hbm] * 8,
        out_specs=(vmem, vmem, vmem, vmem, hbm, hbm, hbm) + (hbm,) * fused,
        scratch_shapes=[
            pltpu.VMEM((rows, width), full), pltpu.VMEM((rows, width), low),
            pltpu.VMEM((nt, rows, width), low), pltpu.VMEM((nt, rows, width), low),
            pltpu.VMEM((hidden, width), low), pltpu.VMEM((hidden, width), low), pltpu.VMEM((hidden, width), low),
            pltpu.VMEM((nt * rows, hidden), low), pltpu.VMEM((nt * rows, hidden), low), pltpu.VMEM((nt * rows, hidden), low),
            pltpu.VMEM((nt, rows, width), low), pltpu.VMEM((nt, rows, width), low),
            pltpu.VMEM((nt, inner, width), low),
            pltpu.VMEM((rows, width), low), pltpu.VMEM((2, rows, width), low), pltpu.VMEM((rows, width), low),
            pltpu.VMEM((3, width, hidden), low), *pairs,
            dma((2, nt, pieces)), dma((2, nt, pieces)), dma((5, pieces, halves)), dma((4, pieces, halves)),
            dma((pieces,)), dma((pieces,)),
            dma((12,)),
        ],
        compiler_params=pltpu.CompilerParams(
            vmem_limit_bytes=VMEM_LIMIT, collective_id=1, has_side_effects=True
        ),
        name="feed",
    )(gain, middle, second, cotangent, whole, cot_all, gate_weight, up_weight, down_weight)


def back_kernel(
    nt, ndp, pieces, heads, head_dim, grad_type, fused,
    ga_ref, gain_ref, gain2_ref, gm_hbm, x_hbm, own_hbm,
    qkv_hbm, low_hbm, high_hbm, first_hbm, weight_hbm, lo_hbm, lo_part_hbm, *rest,
):
    if fused:
        feed_hbm, *rest = rest
    input_out, q_out, k_out, v_out, o_out, gains_in, dist_in, far_in, mate_in, *rest = rest
    if fused:
        feed_in, *rest = rest
    (
        gm_ref, x_ref, own_ref,
        ga_in, qkv, low, high, first, weight, lo, acc_in, lo_part,
        gq, dq_send, dq_in, dkv_send, dkv_in, diag, dk_acc, dv_acc,
        og, og_sum, og_chip, og_line, og_line_in, pg, pg_sum, pg_chip,
        gains_line, gains_own, dist_own,
        swap_send, swap_recv, dq_done, dq_here, dkv_done, dkv_here, lo_send, lo_recv,
        pair_send, pair_recv, chip_send, chip_recv, line_send, line_recv,
        gl_send, gl_recv, gd_send, gd_recv, dist_send, dist_recv, local_sem, *rest,
    ) = rest
    if fused:
        feed_send, feed_recv = rest
    t = lax.axis_index("tensor")
    d = lax.axis_index("dp")
    core = lax.rem(d, 2)
    chip = d // 2
    chips = ndp // 2
    barrier = greet(t, nt)
    for k in range(1, ndp):
        pl.semaphore_signal(
            barrier, inc=1, device_id={"dp": lax.rem(d + k, ndp)}, device_id_type=MESH
        )
    mate = t + 1 - 2 * lax.rem(t, 2)
    is_end = (t == 0) | (t == nt - 1)
    near = jnp.where(t < nt // 2, nt // 2, nt // 2 - 1)
    far = jnp.where(t < nt // 2, nt - 1, 0)
    loads = [
        pltpu.make_async_copy(a, b, local_sem.at[i])
        for i, (a, b) in enumerate(
            ((qkv_hbm, qkv), (low_hbm, low), (high_hbm, high), (first_hbm, first),
             (weight_hbm.at[:, pl.ds(0, weight.shape[1])], weight),
             (lo_hbm.at[near], lo.at[0]), (lo_hbm.at[far], lo.at[1]), (lo_hbm.at[mate], lo.at[2]),
             (gm_hbm, gm_ref), (x_hbm, x_ref), (own_hbm, own_ref), (lo_part_hbm, lo_part))
        )
    ]
    for one in loads:
        one.start()
    others = (far, near, mate)
    row_count, width = x_ref.shape
    inner = heads * head_dim
    size = row_count // pieces
    share = width // ndp
    full = jnp.float32

    def remote(src, dst, send, recv, **target):
        return pltpu.make_async_remote_copy(
            src_ref=src, dst_ref=dst, send_sem=send, recv_sem=recv,
            device_id=target, device_id_type=MESH,
        )

    def swap(peer):
        return remote(ga_ref.at[peer], ga_in.at[t], swap_send.at[peer], swap_recv.at[t], tensor=peer)

    def swap_in(peer):
        return remote(ga_ref.at[peer], ga_in.at[peer], swap_send.at[peer], swap_recv.at[peer], tensor=peer)

    def lo_acc(piece):
        rows = pl.ds(piece * size, size)
        return remote(lo.at[0, rows], acc_in.at[rows], lo_send.at[0, piece], lo_recv.at[0, piece], tensor=mate)

    def lo_final(place, origin, piece):
        rows = pl.ds(piece * size, size)
        return remote(
            lo.at[place, rows], far_in.at[rows], lo_send.at[place, piece], lo_recv.at[1, piece], tensor=origin
        )

    def lo_mate(piece):
        rows = pl.ds(piece * size, size)
        return remote(lo.at[2, rows], mate_in.at[rows], lo_send.at[2, piece], lo_recv.at[2, piece], tensor=mate)

    pl.semaphore_wait(barrier, nt - 1 + ndp - 1)
    for peer in others:
        swap(peer).start()
    ga_in[t] = ga_ref[t]
    if fused:
        def feed_copy(which, k):
            to = lax.rem(chip + k, chips)
            return remote(
                feed_hbm.at[which, to], feed_in.at[k - 1, which],
                feed_send.at[k - 1, which], feed_recv.at[k - 1, which], dp=2 * to + core,
            )

        own_feed = pltpu.make_async_copy(feed_hbm.at[:, chip], feed_in.at[chips - 1], local_sem.at[13])
        own_feed.start()
        for which in range(2):
            for k in range(1, chips):
                feed_copy(which, k).start()

    def block_rows(index):
        return pl.ds(pl.multiple_of(index * share, share), share)

    def pair(kind, c):
        grads, landing = ((og, og_sum), (pg, pg_sum))[kind]
        return remote(
            grads.at[block_rows(2 * c + 1 - core)], landing.at[c],
            pair_send.at[kind, c], pair_recv.at[kind, c], dp=d + 1 - 2 * core,
        )

    def chip_copy(kind, k):
        sums, landing = ((og_sum, og_chip), (pg_sum, pg_chip))[kind]
        to = lax.rem(chip + k, chips)
        return remote(
            sums.at[to], landing.at[k - 1], chip_send.at[kind, k - 1], chip_recv.at[kind, k - 1], dp=2 * to + core
        )

    def pair_sum(kind):
        grads, sums = ((og, og_sum), (pg, pg_sum))[kind]
        for c in range(chips):
            pair(kind, c).wait_recv()
            sums[c] = (grads[block_rows(2 * c + core)].astype(full) + sums[c].astype(full)).astype(grad_type)
        for k in range(1, chips):
            chip_copy(kind, k).start()

    def chip_sum(kind):
        sums, landing = ((og_sum, og_chip), (pg_sum, pg_chip))[kind]
        total = sums[chip].astype(full)
        for k in range(1, chips):
            chip_copy(kind, k).wait_recv()
            total = total + landing[k - 1].astype(full)
        return total

    for one in loads[5:]:
        one.wait()
    for piece in range(pieces):
        @pl.when(is_end)
        def _():
            lo_acc(piece).start()

        @pl.when(jnp.logical_not(is_end))
        def _():
            rows_lo = pl.ds(piece * size, size)
            lo[1, rows_lo] = (lo[1, rows_lo].astype(full) + lo_part[rows_lo].astype(full)).astype(jnp.bfloat16)
            lo_final(1, far, piece).start()

    span = 256
    spans = width // span
    own = jnp.concatenate([unpack(own_ref[j], 0, inner) for j in range(nt)], axis=1)
    for i in range(spans):
        left = gm_ref[:, pl.ds(i * span, span)].astype(jnp.bfloat16)
        og[pl.ds(i * span, span), :] = dot(left, own, ((0,), (0,))).astype(grad_type)
    for c in range(chips):
        pair(0, c).start()

    for i in range(3):
        loads[i].wait()
    def give(peer):
        return (
            remote(dq_send.at[peer], dq_in.at[t], dq_done.at[peer], dq_here.at[t], tensor=peer),
            remote(dkv_send.at[peer], dkv_in.at[t], dkv_done.at[peer], dkv_here.at[t], tensor=peer),
        )

    def taken(peer):
        return (
            remote(dq_send.at[peer], dq_in.at[peer], dq_done.at[peer], dq_here.at[peer], tensor=peer),
            remote(dkv_send.at[peer], dkv_in.at[peer], dkv_done.at[peer], dkv_here.at[peer], tensor=peer),
        )

    def give_keys(block):
        rows = pl.ds(block * QB, QB)
        sides = [acc[head, rows, :] for acc in (dk_acc, dv_acc) for head in range(heads)]
        side = jnp.concatenate(sides, axis=1).astype(jnp.bfloat16)
        gq[rows, pl.ds(inner, 2 * inner)] = side
        dkv_send[block] = side

        @pl.when(t != block)
        def _():
            give(block)[1].start()

    blocks = LEN // QB
    diag[...] = jnp.zeros_like(diag)
    for block in reversed(range(blocks)):
        keys = key_count(block)
        rows = pl.ds(block * QB, QB)
        first_col = LEN - block * QB

        for waited in (1, 0) if block == 1 else () if block == 0 else (block,):
            @pl.when(t != waited)
            def _():
                swap_in(waited).wait_recv()

        parts = []
        for head in range(heads):
            cols = pl.ds(head * head_dim, head_dim)
            if keys == HALF:
                probs_low = low[head, rows, :]
            else:
                probs_low = high[head, pl.ds(block * QB - HALF, QB), :]
            probs = probs_low.astype(full)
            do = unpack(ga_in[block], head * head_dim, head_dim)
            grad_probs = dot(do, qkv[2, pl.ds(0, keys), cols], ((1,), (1,)))
            weighted = jnp.sum(probs * grad_probs, axis=-1, keepdims=True)
            grad_low = (probs * (grad_probs - weighted)).astype(jnp.bfloat16)
            reach = pl.ds(first_col, keys)
            diag[head, :, reach] = diag[head, :, reach] + grad_low.astype(full)
            parts.append(dot(grad_low, qkv[1, pl.ds(0, keys), cols], ((1,), (0,))))
            key_part = dot(grad_low, qkv[0, rows, cols], ((0,), (0,)))
            value_part = dot(probs_low, do, ((0,), (0,)))
            if block == blocks - 1:
                dk_acc[head] = key_part
                dv_acc[head] = value_part
            else:
                dk_acc[head, pl.ds(0, keys), :] += key_part
                dv_acc[head, pl.ds(0, keys), :] += value_part
        side = jnp.concatenate(parts, axis=1).astype(jnp.bfloat16)
        gq[rows, pl.ds(0, inner)] = side
        dq_send[block] = pack(side)

        @pl.when(t != block)
        def _():
            give(block)[0].start()

        if block * QB == HALF:
            for done in range(block, blocks):
                give_keys(done)
        if block == 1:
            pair_sum(0)
    for block in range(HALF // QB):
        give_keys(block)

    def token_rows(peer):
        return pl.ds(pl.multiple_of(peer * row_count, row_count), row_count)

    for head in range(heads):
        dist_own[pl.ds(head, 1), :] = fold_diagonals(diag[head])
    dist_keep = pltpu.make_async_copy(dist_own, dist_in.at[d], local_sem.at[12])
    dist_keep.start()

    def dist_copy(k):
        return remote(
            dist_own, dist_in.at[d], dist_send.at[k - 1], dist_recv.at[d], dp=lax.rem(d + k, ndp)
        )

    for k in range(1, ndp):
        dist_copy(k).start()
    loads[3].wait()
    for i in range(spans):
        cols = pl.ds(i * span, span)
        left = first[:, :, cols].reshape(nt * row_count, span)
        pg[cols, :] = dot(left, gq[...], ((0,), (0,))).astype(grad_type)
    for c in range(chips):
        pair(1, c).start()
    total = chip_sum(0)
    for j in range(nt):
        og_line[j] = total[:, j * inner : (j + 1) * inner].astype(grad_type)

    def line_copy_out(peer):
        return remote(og_line.at[peer], og_line_in.at[t], line_send.at[peer], line_recv.at[t], tensor=peer)

    def line_in(peer):
        return remote(og_line.at[peer], og_line_in.at[peer], line_send.at[peer], line_recv.at[peer], tensor=peer)

    for peer in others:
        line_copy_out(peer).start()
    pair_sum(1)

    @pl.when(jnp.logical_not(is_end))
    def _():
        for piece in range(pieces):
            lo_acc(piece).wait_recv()
        lo[0] = (lo[0].astype(full) + acc_in[...].astype(full)).astype(jnp.bfloat16)

    loads[4].wait()
    inputs = x_ref[...].astype(full)
    inv = lax.rsqrt(jnp.mean(inputs * inputs, axis=-1, keepdims=True) + EPSILON)
    grad_first = dot(gq[token_rows(t)], weight[t], ((1,), (0,)))
    for peer in (mate, near, far):
        for one in taken(peer):
            one.wait_recv()
        grad_first = (
            grad_first
            + dot(unpack(dq_in[peer], 0, inner), weight[peer, pl.ds(0, inner), :], ((1,), (0,)))
            + dot(dkv_in[peer], weight[peer, pl.ds(inner, 2 * inner), :], ((1,), (0,)))
        )
    scaled = row_of(gain_ref) * grad_first
    along = jnp.mean(scaled * inputs, axis=-1, keepdims=True)
    gains_line[t, pl.ds(0, 1), :] = jnp.sum(grad_first * inputs * inv, axis=0, keepdims=True)
    gains_line[t, pl.ds(1, 1), :] = gain2_ref[...]

    def gain_copy(peer):
        return remote(gains_line.at[t], gains_line.at[t], gl_send.at[peer], gl_recv.at[t], tensor=peer)

    def gain_landed(peer):
        return remote(gains_line.at[peer], gains_line.at[peer], gl_send.at[peer], gl_recv.at[peer], tensor=peer)

    for peer in others:
        gain_copy(peer).start()
    for piece in range(pieces):
        lo_mate(piece).start()

        @pl.when(jnp.logical_not(is_end))
        def _():
            lo_final(0, near, piece).start()

    input_out[...] = (gm_ref[...] + inv * scaled - inputs * (inv * inv * inv * along)).astype(jnp.bfloat16)
    for peer in others:
        gain_landed(peer).wait_recv()
    gains_own[...] = gains_line[0] + gains_line[1] + gains_line[2] + gains_line[3]
    gains_keep = pltpu.make_async_copy(gains_own, gains_in.at[d], local_sem.at[14])
    gains_keep.start()

    def gains_copy(k):
        return remote(
            gains_own, gains_in.at[d], gd_send.at[k - 1], gd_recv.at[d], dp=lax.rem(d + k, ndp)
        )

    for k in range(1, ndp):
        gains_copy(k).start()
    total = chip_sum(1)
    q_out[...] = total[:, :inner]
    k_out[...] = total[:, inner : 2 * inner]
    v_out[...] = total[:, 2 * inner :]
    total = og_line[t].astype(full)
    for peer in others:
        line_in(peer).wait_recv()
        total = total + og_line_in[peer].astype(full)
    o_out[...] = total

    def others_of(landing, send, recv):
        for k in range(1, ndp):
            peer = lax.rem(d + k, ndp)
            remote(landing.at[peer], landing.at[peer], send.at[k - 1], recv.at[peer], dp=peer).wait_recv()

    others_of(dist_in, dist_send, dist_recv)
    if fused:
        own_feed.wait()
        for which in range(2):
            for k in range(1, chips):
                feed_copy(which, k).wait_recv()
    for piece in range(pieces):
        lo_final(0, near, piece).wait_recv()
        lo_mate(piece).wait_recv()
    others_of(gains_in, gd_send, gd_recv)
    dist_keep.wait()
    gains_keep.wait()

    for peer in others:
        swap(peer).wait_send()
        for one in give(peer):
            one.wait_send()
        line_copy_out(peer).wait_send()
        gain_copy(peer).wait_send()
    for piece in range(pieces):
        lo_mate(piece).wait_send()

        @pl.when(is_end)
        def _():
            lo_acc(piece).wait_send()

        @pl.when(jnp.logical_not(is_end))
        def _():
            lo_final(0, near, piece).wait_send()
            lo_final(1, far, piece).wait_send()

    if fused:
        for which in range(2):
            for k in range(1, chips):
                feed_copy(which, k).wait_send()
    for kind in range(2):
        for c in range(chips):
            pair(kind, c).wait_send()
        for k in range(1, chips):
            chip_copy(kind, k).wait_send()
    for k in range(1, ndp):
        dist_copy(k).wait_send()
        gains_copy(k).wait_send()


def back(nt, ndp, grad_attended, grad_middle, tokens, gain, gain2_part, attended, qkv, probs_low, probs_high, first_all, weights, layer_parts, layer_far, feed_grads):
    rows, width = tokens.shape
    heads = probs_low.shape[0]
    inner = qkv.shape[2]
    head_dim = inner // heads
    low, full = jnp.bfloat16, jnp.float32
    pieces = 2
    share, chips = width // ndp, ndp // 2
    grad_type = low if share % 16 == 0 else full
    hbm = pl.BlockSpec(memory_space=pl.ANY)
    vmem = pl.BlockSpec(memory_space=pltpu.VMEM)
    dma = pltpu.SemaphoreType.DMA
    shape = jax.ShapeDtypeStruct
    reach = SPAN + QB
    scratch = lambda *dims, kind=low: pltpu.VMEM(dims, kind)
    part = shape((share, inner), full)
    fused = feed_grads.ndim == 4
    hidden = feed_grads.shape[-1]
    feeds = [dma((chips - 1, 2)), dma((chips - 1, 2))] if fused else []
    return pl.pallas_call(
        functools.partial(back_kernel, nt, ndp, pieces, heads, head_dim, grad_type, fused),
        out_shape=(
            shape((rows, width), low), part, part, part, part,
            shape((ndp, 2, width), full), shape((ndp, heads, reach), full),
            shape((rows, width), low), shape((rows, width), low),
        ) + (shape((chips, 2, share, hidden), low),) * fused,
        in_specs=[vmem] * 3 + [hbm] * (10 + fused),
        out_specs=(vmem,) * 5 + (hbm,) * (4 + fused),
        scratch_shapes=[
            scratch(rows, width, kind=full), scratch(rows, width), scratch(nt, rows // 2, 2 * inner),
            scratch(nt, rows // 2, 2 * inner), scratch(3, LEN, inner), scratch(heads, HALF, HALF), scratch(heads, HALF, LEN),
            scratch(nt, rows, width), scratch(nt, 3 * inner, width), scratch(3, rows, width), scratch(rows, width), scratch(rows, width),
            scratch(nt * rows, 3 * inner), scratch(nt, rows // 2, 2 * inner), scratch(nt, rows // 2, 2 * inner),
            scratch(nt, rows, 2 * inner), scratch(nt, rows, 2 * inner), scratch(heads, QB, reach, kind=full),
            scratch(heads, LEN, head_dim, kind=full), scratch(heads, LEN, head_dim, kind=full),
            scratch(width, nt * inner, kind=grad_type), scratch(chips, share, nt * inner, kind=grad_type),
            scratch(chips - 1, share, nt * inner, kind=grad_type),
            scratch(nt, share, inner, kind=grad_type), scratch(nt, share, inner, kind=grad_type),
            scratch(width, 3 * inner, kind=grad_type), scratch(chips, share, 3 * inner, kind=grad_type),
            scratch(chips - 1, share, 3 * inner, kind=grad_type),
            scratch(nt, 2, width, kind=full), scratch(2, width, kind=full), scratch(heads, reach, kind=full),
            dma((nt,)), dma((nt,)), dma((nt,)), dma((nt,)), dma((nt,)), dma((nt,)), dma((3, pieces)), dma((3, pieces)),
            dma((2, chips)), dma((2, chips)), dma((2, chips - 1)), dma((2, chips - 1)), dma((nt,)), dma((nt,)),
            dma((nt,)), dma((nt,)), dma((ndp - 1,)), dma((ndp,)), dma((ndp - 1,)), dma((ndp,)), dma((15,)), *feeds,
        ],
        compiler_params=pltpu.CompilerParams(
            vmem_limit_bytes=VMEM_LIMIT, collective_id=2, has_side_effects=True
        ),
        cost_estimate=pl.CostEstimate(flops=60 * 10**9, bytes_accessed=200 * 10**6, transcendentals=0),
        name="back",
    )(
        grad_attended, gain, gain2_part, grad_middle, tokens, attended,
        qkv, probs_low, probs_high, first_all, weights, layer_parts, layer_far, *((feed_grads,) if fused else ()),
    )


def finish_kernel(
    fused, bucket_ref, base_ref, far_ref, mate_ref, input_ref, q_ref, k_ref, v_ref, o_ref, gains_ref, dist_ref, *rest,
):
    if fused:
        feed_ref, down_ref, *rest = rest
    layer_out, input_out, gain_out, q_out, k_out, v_out, o_out, table_out, gain2_out, *feed_outs = rest
    full = jnp.float32
    layer_out[...] = (base_ref[...] + far_ref[...].astype(full) + mate_ref[...].astype(full)).astype(jnp.bfloat16)
    input_out[...] = input_ref[...]
    for a, b in ((q_ref, q_out), (k_ref, k_out), (v_ref, v_out), (o_ref, o_out)):
        b[...] = a[...]

    @pl.when(pl.program_id(0) == 0)
    def _():
        gains, dist = gains_ref[0], dist_ref[0]
        for k in range(1, gains_ref.shape[0]):
            gains = gains + gains_ref[k]
            dist = dist + dist_ref[k]
        gain_out[...] = gains[0:1].reshape(gain_out.shape)
        gain2_out[...] = gains[1:2].reshape(gain2_out.shape)
        reach = dist.shape[1]
        shifted = jnp.concatenate([jnp.zeros((1, 1), jnp.int32), row_of(bucket_ref)], axis=1)[:, :reach]
        hot = (lax.broadcasted_iota(jnp.int32, (NB, reach), 0) == shifted).astype(full)
        table_out[...] = lax.dot_general(
            dist, hot, (((1,), (1,)), ((), ())), precision=HIGHEST, preferred_element_type=full
        )

    for which in range(len(feed_outs)):
        parts = [down_ref[k] if which == 2 else feed_ref[k, which] for k in range(feed_ref.shape[0])]
        total = parts[0].astype(full)
        for part in parts[1:]:
            total = total + part.astype(full)
        feed_outs[which][...] = total


def finish(buckets, base, outs):
    fused = len(outs) > 9
    input_grad, query_grad, key_grad, value_grad, out_grad, gains, dist, far_in, mate_in = outs[:9]
    rows, width = base.shape
    share, inner = query_grad.shape
    low, full = jnp.bfloat16, jnp.float32
    shape = jax.ShapeDtypeStruct
    steps = 4 if share % 64 == 0 and rows % 64 == 0 else 1
    vmem = pl.BlockSpec(memory_space=pltpu.VMEM)
    wide = pl.BlockSpec((rows // steps, width), lambda i: (i, 0))
    small = pl.BlockSpec((share // steps, inner), lambda i: (i, 0))
    part = shape(query_grad.shape, full)
    ins, feeds, blocks = [], (), ()
    if fused:
        chips, kinds, _, hidden = outs[9].shape
        ins = [
            pl.BlockSpec((chips, kinds, share // steps, hidden), lambda i: (0, 0, i, 0)),
            pl.BlockSpec((chips, share // steps, hidden), lambda i: (0, i, 0)),
        ]
        feeds = (shape((share, hidden), full),) * (kinds + 1)
        blocks = (pl.BlockSpec((share // steps, hidden), lambda i: (i, 0)),) * (kinds + 1)
    return pl.pallas_call(
        functools.partial(finish_kernel, fused),
        grid=(steps,),
        out_shape=(
            shape((rows, width), low), shape((rows, width), low), shape((width,), full), part, part, part, part,
            shape((dist.shape[1], NB), full), shape((width,), full),
        ) + feeds,
        in_specs=[vmem] + [wide] * 4 + [small] * 4 + [vmem] * 2 + ins,
        out_specs=(wide, wide, vmem) + (small,) * 4 + (vmem, vmem) + blocks,
        compiler_params=pltpu.CompilerParams(vmem_limit_bytes=VMEM_LIMIT),
        name="finish",
    )(
        buckets, base, far_in, mate_in, input_grad, query_grad, key_grad, value_grad, out_grad, gains, dist,
        *outs[9:],
    )


def per_device(
    tokens,
    first_gain,
    query_weight,
    key_weight,
    value_weight,
    out_weight,
    bucket_table,
    second_gain,
    gate_weight,
    up_weight,
    down_weight,
    piece_start,
    bucket_index,
    cotangent,
):
    nt, ndp = lax.axis_size("tensor"), lax.axis_size("dp")
    weights = (query_weight.T, key_weight.T, value_weight.T, out_weight.T)
    first_all, cot_all, qkv, probs_low, probs_high, attended, whole, middle, second = gather_attend(
        nt, ndp, tokens, cotangent, first_gain, second_gain, weights, bucket_index, bucket_table.T, piece_start
    )
    base, grad_middle, second_part, grad_attended, layer_parts, layer_far, feed_grads, *down_in = feed(
        nt, ndp, middle, second, second_gain, cotangent, whole, cot_all, gate_weight.T, up_weight.T, down_weight.T
    )
    outs = back(
        nt, ndp, grad_attended, grad_middle, tokens, first_gain, second_part, attended,
        qkv, probs_low, probs_high, first_all, whole, layer_parts, layer_far, feed_grads,
    )
    outs = finish(bucket_index, base, (*outs, *down_in))
    if feed_grads.ndim == 3:
        sums = lax.psum_scatter(feed_grads, "dp", scatter_dimension=1, tiled=True).astype(jnp.float32)
        outs = (*outs, sums[0], sums[1], sums[2])
    return (*outs[:7], outs[7].T, *outs[8:])


def solution(mesh):
    return jax.shard_map(
        per_device,
        mesh=mesh,
        in_specs=(
            P(("dp", "tensor"), None),
            P(),
            P(None, "tensor"),
            P(None, "tensor"),
            P(None, "tensor"),
            P(None, "tensor"),
            P(None, "tensor"),
            P(),
            P(None, "tensor"),
            P(None, "tensor"),
            P(None, "tensor"),
            P("dp", None),
            P(),
            P(("dp", "tensor"), None),
        ),
        out_specs=(
            P(("dp", "tensor"), None),
            P(("dp", "tensor"), None),
            P(),
            P("dp", "tensor"),
            P("dp", "tensor"),
            P("dp", "tensor"),
            P("dp", "tensor"),
            P(None, "tensor"),
            P(),
            P("dp", "tensor"),
            P("dp", "tensor"),
            P("dp", "tensor"),
        ),
        check_vma=False,
    )
```

```python
import functools

import jax
import jax.numpy as jnp
from jax import lax
from jax.experimental import pallas as pl
from jax.experimental.pallas import tpu as pltpu
from jax.sharding import PartitionSpec as P

NB = 32
LEN = 1024
QB = 256
PIECE = 256
NPIECE = 2
HALF = LEN // NPIECE
SPAN = 5 * QB
DIST = 2 * LEN

EPSILON = 1e-06
MASKED = -1000000000.0
HIGHEST = lax.Precision.HIGHEST
VMEM_LIMIT = 60 * 1024 * 1024
MESH = pl.DeviceIdType.MESH


def normed(row_block, gain_vec):
    inv_rms = lax.rsqrt(jnp.mean(row_block * row_block, axis=-1, keepdims=True) + EPSILON)
    return row_block * inv_rms * gain_vec


def dot(a, b, dims):
    return lax.dot_general(a, b, (dims, ((), ())), preferred_element_type=jnp.float32)


def key_count(block):
    return HALF if (block + 1) * QB <= HALF else LEN


def toeplitz(bucket_ref, table_ref, head):
    bucket_row = jnp.concatenate([row_of(bucket_ref), jnp.zeros((1, 1), jnp.int32)], axis=1)
    row = jnp.zeros(bucket_row.shape, jnp.float32)
    for bucket in range(NB):
        row = jnp.where(bucket_row == bucket, table_ref[head, bucket], row)
    rows = jnp.broadcast_to(row, (QB, DIST))
    return pltpu.roll(rows, DIST - (QB - 1), 1, stride=1, stride_axis=0)[:, :SPAN]


def row_of(ref):
    return ref[...].reshape(1, ref.shape[0])


def label_of(position, starts):
    label = jnp.zeros(position.shape, jnp.int32)
    for piece, start in enumerate(starts):
        inside = (position >= start) & (position < start + PIECE)
        label = jnp.where(inside, piece + 1, label)
    return label


def allowed_block(block, starts):
    keys = key_count(block)
    query = block * QB + lax.broadcasted_iota(jnp.int32, (QB, 1), 0)
    key = lax.broadcasted_iota(jnp.int32, (1, keys), 1)
    query_label = label_of(query, starts)
    key_label = label_of(key, starts)
    return (key <= query) | ((query_label == key_label) & (query_label > 0))


def attend_block(block, head_dim, allowed, qkv_ref, bias_ref, low_ref, high_ref):
    keys = key_count(block)
    first = LEN - QB - block * QB
    rows = pl.ds(block * QB, QB)
    outs = []
    for head in range(bias_ref.shape[0]):
        cols = pl.ds(head * head_dim, head_dim)
        raw = dot(qkv_ref[0, rows, cols], qkv_ref[1, pl.ds(0, keys), cols], ((1,), (1,)))
        scores = jnp.where(allowed, raw + bias_ref[head, :, pl.ds(first, keys)], MASKED)
        peak = jnp.max(scores, axis=-1, keepdims=True)
        powered = jnp.exp(scores - peak)
        total = jnp.sum(powered, axis=-1, keepdims=True)
        probs = (powered * (1.0 / total)).astype(jnp.bfloat16)
        if keys == HALF:
            low_ref[head, rows, :] = probs
        else:
            high_ref[head, pl.ds(block * QB - HALF, QB), :] = probs
        outs.append(dot(probs, qkv_ref[2, pl.ds(0, keys), cols], ((1,), (0,))))
    return jnp.concatenate(outs, axis=1).astype(jnp.bfloat16)


def pack(rows):
    half = rows.shape[0] // 2
    return jnp.concatenate([rows[:half], rows[half:]], axis=1)


def unpack(packed, start, width):
    half = packed.shape[1] // 2
    return jnp.concatenate(
        [packed[:, start : start + width], packed[:, half + start : half + start + width]], axis=0
    )


def greet(t, nt):
    barrier = pltpu.get_barrier_semaphore()
    for k in range(1, nt):
        pl.semaphore_signal(
            barrier, inc=1, device_id={"tensor": lax.rem(t + k, nt)}, device_id_type=MESH
        )
    return barrier


def line_copy(t, nt, way, step, buf, piece, pieces, send_sem, recv_sem):
    sign = 1 if way == 0 else -1
    origin = jnp.clip(t - sign * step, 0, nt - 1)
    rows = buf.shape[1] // pieces
    part = buf.at[origin, pl.ds(piece * rows, rows)]
    return pltpu.make_async_remote_copy(
        src_ref=part,
        dst_ref=part,
        send_sem=send_sem,
        recv_sem=recv_sem,
        device_id={"tensor": jnp.clip(t + sign, 0, nt - 1)},
        device_id_type=MESH,
    )


def gather_attend_kernel(
    nt, ndp, pieces, heads, head_dim, exchange,
    x_ref, cot_ref, gain_ref, gain2_ref, bucket_ref, table_ref, start_ref, *rest,
):
    weight_refs, rest = rest[: 4 if exchange else 1], rest[4 if exchange else 1 :]
    (
        first_out, cot_out, qkv_out, low_out, high_out, own_out, whole_out, middle_out, second_out,
        first, qkv, low, high, bias, att, own, whole,
        send_sem, recv_sem, swap_send, swap_recv, line_send, line_recv, chip_send, chip_recv, core_send, core_recv,
        local_sem,
    ) = rest
    t = lax.axis_index("tensor")
    d = lax.axis_index("dp")
    core = lax.rem(d, 2)
    chip = d // 2
    chips = ndp // 2
    barrier = greet(t, nt)
    greeted = nt - 1
    if exchange:
        for k in range(chips):
            peer = 2 * lax.rem(chip + k, chips) + core if k else d + 1 - 2 * core
            pl.semaphore_signal(barrier, inc=1, device_id={"dp": peer}, device_id_type=MESH)
        greeted += chips
    inner = heads * head_dim
    share = whole.shape[1] // ndp
    own_cot = pltpu.make_async_copy(cot_ref, cot_out.at[t], local_sem.at[0])
    own_cot.start()
    if exchange:
        loads = [
            pltpu.make_async_copy(weight, whole.at[t, pl.ds(i * inner, inner)], local_sem.at[1 + i])
            for i, weight in enumerate(weight_refs)
        ]
    else:
        loads = [pltpu.make_async_copy(weight_refs[0], whole, local_sem.at[1])]
    for one in loads:
        one.start()

    def slices(index, plane):
        return whole.at[plane, pl.ds(pl.multiple_of(index * share, share), share)]

    def remote(src, dst, send, recv, **target):
        return pltpu.make_async_remote_copy(
            src_ref=src, dst_ref=dst, send_sem=send, recv_sem=recv, device_id=target, device_id_type=MESH
        )

    def plane_at(q):
        return lax.rem(t + q, nt)

    def to_plane(q):
        return remote(slices(d, t), slices(d, t), line_send.at[q - 1], line_recv.at[t], tensor=plane_at(q))

    def from_plane(q):
        p = plane_at(q)
        return remote(slices(d, p), slices(d, p), line_send.at[q - 1], line_recv.at[p], tensor=p)

    def to_chip(k, q):
        part = slices(d, plane_at(q))
        return remote(
            part, part, chip_send.at[k - 1, q - 1], chip_recv.at[k - 1, q - 1], dp=2 * lax.rem(chip + k, chips) + core
        )

    def from_chip(k, q):
        peer = 2 * lax.rem(chip - k + chips, chips) + core
        part = slices(peer, plane_at(q))
        return remote(part, part, chip_send.at[k - 1, q - 1], chip_recv.at[k - 1, q - 1], dp=peer)

    def to_core(k, q):
        part = slices(2 * lax.rem(chip - k + chips, chips) + core, plane_at(q))
        return remote(part, part, core_send.at[k, q - 1], core_recv.at[k, q - 1], dp=d + 1 - 2 * core)

    def from_core(k, q):
        part = slices(2 * lax.rem(chip - k + chips, chips) + 1 - core, plane_at(q))
        return remote(part, part, core_send.at[k, q - 1], core_recv.at[k, q - 1], dp=d + 1 - 2 * core)

    for one in loads:
        one.wait()
    pl.semaphore_wait(barrier, greeted)
    if exchange:
        for q in range(1, nt):
            to_plane(q).start()
    first[t] = normed(x_ref[...].astype(jnp.float32), row_of(gain_ref)).astype(jnp.bfloat16)

    def copy(way, stage, step, piece):
        buf = first if stage == 0 else cot_out
        return line_copy(
            t, nt, way, step, buf, piece, pieces,
            send_sem.at[way, stage, step, piece], recv_sem.at[way, stage, step, piece],
        )

    def landed(way, stage, step, piece):
        sign = 1 if way == 0 else -1
        buf = first if stage == 0 else cot_out
        rows = buf.shape[1] // pieces
        part = buf.at[jnp.clip(t - sign * step, 0, nt - 1), pl.ds(piece * rows, rows)]
        remote(
            part, part, send_sem.at[way, stage, step - 1, piece], recv_sem.at[way, stage, step - 1, piece],
            tensor=jnp.clip(t + sign, 0, nt - 1),
        ).wait_recv()

    ways = ((0, t, t < nt - 1), (1, nt - 1 - t, t > 0))

    def tick(k):
        for piece in range(pieces):
            for way, last, onward in ways:
                if k < nt:
                    @pl.when(k <= last)
                    def _():
                        if k > 0:
                            landed(way, 0, k, piece)

                        @pl.when(onward)
                        def _():
                            copy(way, 0, k, piece).start()

                if k > 0:
                    step = k - last - 1

                    @pl.when((step >= 1) & (step <= last))
                    def _():
                        landed(way, 1, step, piece)

                        @pl.when(onward)
                        def _():
                            copy(way, 1, step, piece).start()

                    @pl.when((step == 0) & onward)
                    def _():
                        copy(way, 0, last, piece).wait_send()
                        copy(way, 1, 0, piece).start()

    def project(origin):
        rows = pl.ds(pl.multiple_of(origin * QB, QB), QB)
        for place in range(3):
            weight = whole[t, pl.ds(place * inner, inner), :]
            qkv[place, rows, :] = dot(first[origin], weight, ((1,), (1,))).astype(jnp.bfloat16)

    tick(0)
    project(t)
    for head in range(heads):
        bias[head] = toeplitz(bucket_ref, table_ref, head)
    own_cot.wait()
    for k in range(1, nt):
        tick(k)

        @pl.when(t - k >= 0)
        def _():
            project(t - k)

        @pl.when(t + k < nt)
        def _():
            project(t + k)

        if exchange and k == 2:
            for q in range(1, nt):
                from_plane(q).wait_recv()
                for j in range(1, chips):
                    to_chip(j, q).start()
                to_core(0, q).start()

    starts = [start_ref[0, piece] for piece in range(NPIECE)]
    keep = [
        pltpu.make_async_copy(first, first_out, local_sem.at[5]),
        pltpu.make_async_copy(qkv, qkv_out, local_sem.at[6]),
    ]
    for one in keep:
        one.start()

    def swap(block):
        return remote(att.at[block], own.at[t], swap_send.at[block], swap_recv.at[t], tensor=block)

    for block in range(LEN // QB):
        att[block] = pack(attend_block(block, head_dim, allowed_block(block, starts), qkv, bias, low, high))

        @pl.when(t != block)
        def _():
            swap(block).start()

        @pl.when(t == block)
        def _():
            own[t] = att[block]

    late = [
        pltpu.make_async_copy(low, low_out, local_sem.at[7]),
        pltpu.make_async_copy(high, high_out, local_sem.at[8]),
    ]
    for one in late:
        one.start()
    tick(nt)
    if exchange:
        for k in range(1, chips):
            for q in range(1, nt):
                from_chip(k, q).wait_recv()
                to_core(k, q).start()
    tick(nt + 1)
    for block in range(nt):
        @pl.when(t != block)
        def _():
            remote(att.at[block], own.at[block], swap_send.at[block], swap_recv.at[block], tensor=block).wait_recv()

    if exchange:
        for k in range(chips):
            for q in range(1, nt):
                from_core(k, q).wait_recv()
    late += [
        pltpu.make_async_copy(own, own_out, local_sem.at[9]),
        pltpu.make_async_copy(whole, whole_out, local_sem.at[10]),
    ]
    for one in late[2:]:
        one.start()
    total = x_ref[...].astype(jnp.float32)
    for j in range(nt):
        total = total + dot(unpack(own[j], 0, inner), whole[j, pl.ds(3 * inner, inner), :], ((1,), (0,)))
    middle_out[...] = total
    second_out[...] = normed(total, row_of(gain2_ref)).astype(jnp.bfloat16)
    for k in range(nt + 2, 2 * nt):
        tick(k)
    for block in range(nt):
        @pl.when(t != block)
        def _():
            swap(block).wait_send()

    for one in keep + late:
        one.wait()
    if exchange:
        for q in range(1, nt):
            to_plane(q).wait_send()
            for k in range(1, chips):
                to_chip(k, q).wait_send()
            for k in range(chips):
                to_core(k, q).wait_send()
    for piece in range(pieces):
        for way, last, onward in ways:
            for stage in range(2):
                for step in range(nt):
                    @pl.when(onward & ((step < last) if stage == 0 else (step <= last)))
                    def _():
                        copy(way, stage, step, piece).wait_send()


def gather_attend(nt, ndp, tokens, cotangent, gain, gain2, weights, buckets, table, starts):
    heads = table.shape[0]
    rows, width = tokens.shape
    inner = weights[0].shape[0]
    low, full = jnp.bfloat16, jnp.float32
    pieces = 2
    exchange = (4 * inner // ndp) % 16 == 0
    if not exchange:
        joined = jnp.concatenate(weights, axis=0)
        part = joined.shape[0] // ndp
        mine = lax.dynamic_slice_in_dim(joined, lax.axis_index("dp") * part, part, 0)
        weights = (lax.all_gather(mine, ("tensor", "dp"), axis=0, tiled=True).reshape(nt, *joined.shape),)
    chips = ndp // 2
    smem = pl.BlockSpec(memory_space=pltpu.SMEM)
    hbm = pl.BlockSpec(memory_space=pl.ANY)
    vmem = pl.BlockSpec(memory_space=pltpu.VMEM)
    shapes = (
        (nt, rows, width), (nt, rows, width), (3, LEN, inner), (heads, HALF, HALF), (heads, HALF, LEN),
        (nt, rows // 2, 2 * inner), (nt, 4 * inner, width),
    )
    dma = pltpu.SemaphoreType.DMA
    return pl.pallas_call(
        functools.partial(gather_attend_kernel, nt, ndp, pieces, heads, inner // heads, exchange),
        out_shape=tuple(jax.ShapeDtypeStruct(shape, low) for shape in shapes)
        + (jax.ShapeDtypeStruct((rows, width), full), jax.ShapeDtypeStruct((rows, width), low)),
        in_specs=[vmem, hbm, vmem, vmem, vmem, smem, smem] + [hbm] * len(weights),
        out_specs=(hbm,) * 7 + (vmem, vmem),
        scratch_shapes=[
            pltpu.VMEM((nt, rows, width), low),
            pltpu.VMEM((3, LEN, inner), low),
            pltpu.VMEM((heads, HALF, HALF), low),
            pltpu.VMEM((heads, HALF, LEN), low),
            pltpu.VMEM((heads, QB, SPAN), full),
            pltpu.VMEM((nt, rows // 2, 2 * inner), low),
            pltpu.VMEM((nt, rows // 2, 2 * inner), low),
            pltpu.VMEM((nt, 4 * inner, width), low),
            dma((2, 2, nt, pieces)), dma((2, 2, nt, pieces)), dma((nt,)), dma((nt,)),
            dma((nt - 1,)), dma((nt,)), dma((chips - 1, nt - 1)), dma((chips - 1, nt - 1)),
            dma((chips, nt - 1)), dma((chips, nt - 1)), dma((11,)),
        ],
        compiler_params=pltpu.CompilerParams(
            vmem_limit_bytes=VMEM_LIMIT, collective_id=0, has_side_effects=True
        ),
        name="gather_attend",
    )(tokens, cotangent, gain, gain2, buckets, table, starts, *weights)


def fold_diagonals(grid):
    rows = QB // 2
    width = grid.shape[1]
    while rows >= 1:
        grid = grid[:rows] + pltpu.roll(grid[rows : 2 * rows], width - rows, 1)
        rows //= 2
    return grid


def gelu_parts(v):
    root, cubic = 0.7978845608028654, 0.044715
    square = v * v
    bend = jnp.tanh(root * v * (1.0 + cubic * square))
    half = 0.5 * (1.0 + bend)
    slope = half + 0.5 * v * (1.0 - bend * bend) * root * (1.0 + 3.0 * cubic * square)
    return v * half, slope


def feed_kernel(
    nt, ndp, pieces, halves, fused,
    gain_ref, middle_hbm, second_hbm, cot_own_hbm, whole_hbm, cot_hbm, wg_hbm, wu_hbm, wd_hbm,
    base_out, gm_out, gain_out, ga_out, lo_out, lo_in, grads_out, *rest,
):
    if fused:
        down_out, *rest = rest
    (
        middle, cot_own_ref, buf, cot, wg, wu, wd, hid, gg, gu, gs, lo, wo, mate_in, acc_in, far_in, grads, *rest,
    ) = rest
    *rest, send_sem, recv_sem, rs_send, rs_recv, lo_send, lo_recv, local_sem = rest
    t = lax.axis_index("tensor")
    d = lax.axis_index("dp")
    core = lax.rem(d, 2)
    chips = ndp // 2
    barrier = greet(t, nt)
    own_load = pltpu.make_async_copy(second_hbm, buf.at[t], local_sem.at[11])
    own_load.start()
    if fused:
        sums, pair_send, pair_recv, chip_send, chip_recv = rest
        chip = d // 2
        for k in range(chips):
            peer = 2 * lax.rem(chip + k, chips) + core if k else d + 1 - 2 * core
            pl.semaphore_signal(barrier, inc=1, device_id={"dp": peer}, device_id_type=MESH)
    loads = [
        pltpu.make_async_copy(a, b, local_sem.at[i])
        for i, (a, b) in enumerate(((wg_hbm, wg), (wu_hbm, wu), (wd_hbm, wd), (cot_hbm, cot)))
    ]
    for one in loads:
        one.start()
    row_count = middle.shape[0]
    size = row_count // pieces
    inner = wo.shape[1]
    wo_load = pltpu.make_async_copy(whole_hbm.at[:, pl.ds(3 * inner, inner)], wo, local_sem.at[4])
    wo_load.start()
    late_loads = [
        pltpu.make_async_copy(middle_hbm, middle, local_sem.at[9]),
        pltpu.make_async_copy(cot_own_hbm, cot_own_ref, local_sem.at[10]),
    ]
    for one in late_loads:
        one.start()
    keep = []
    own_load.wait()
    pl.semaphore_wait(barrier, nt - 1 + chips * fused)
    mate = t + 1 - 2 * lax.rem(t, 2)
    is_end = (t == 0) | (t == nt - 1)
    ways = ((0, t, t < nt - 1), (1, nt - 1 - t, t > 0))

    def copy(way, step, piece):
        return line_copy(
            t, nt, way, step, buf, piece, pieces,
            send_sem.at[way, step, piece], recv_sem.at[way, step, piece],
        )

    def landed(way, step, piece):
        sign = 1 if way == 0 else -1
        part = buf.at[jnp.clip(t - sign * step, 0, nt - 1), pl.ds(piece * size, size)]
        pltpu.make_async_remote_copy(
            src_ref=part, dst_ref=part,
            send_sem=send_sem.at[way, step - 1, piece], recv_sem=recv_sem.at[way, step - 1, piece],
            device_id={"tensor": jnp.clip(t + sign, 0, nt - 1)}, device_id_type=MESH,
        ).wait_recv()

    def remote(src, dst, target, send, recv):
        return pltpu.make_async_remote_copy(
            src_ref=src, dst_ref=dst, send_sem=send, recv_sem=recv,
            device_id={"tensor": target}, device_id_type=MESH,
        )

    wide = buf.shape[2] // halves

    def to_mate(piece, half):
        part = (pl.ds(piece * size, size), pl.ds(half * wide, wide))
        return remote(
            gs.at[(mate, *part)], mate_in.at[part], mate, rs_send.at[0, piece, half], rs_recv.at[0, piece, half]
        )

    def to_acc(origin, piece, half):
        part = (pl.ds(piece * size, size), pl.ds(half * wide, wide))
        j = lax.rem(origin, 2)
        return remote(
            gs.at[(origin, *part)], acc_in.at[(j, *part)], mate,
            rs_send.at[1 + j, piece, half], rs_recv.at[1 + j, piece, half],
        )

    def to_far(origin, piece, half):
        part = (pl.ds(piece * size, size), pl.ds(half * wide, wide))
        j = lax.rem(origin, 2)
        return remote(
            gs.at[(origin, *part)], far_in.at[part], origin, rs_send.at[3 + j, piece, half], rs_recv.at[3, piece, half]
        )

    def feed(origin, piece):
        rows = pl.ds(pl.multiple_of(piece * size, size), size)
        flat = pl.ds(pl.multiple_of(origin * row_count + piece * size, size), size)
        normal = buf[origin, rows]
        gate = dot(normal, wg[...], ((1,), (1,)))
        up = dot(normal, wu[...], ((1,), (1,)))
        grad_hidden = dot(cot[origin, rows], wd[...], ((1,), (1,)))
        act, slope = gelu_parts(gate)
        hidden = (act * up).astype(jnp.bfloat16)
        hid[flat, :] = hidden
        grad_gate = (grad_hidden * up * slope).astype(jnp.bfloat16)
        grad_up = (grad_hidden * act).astype(jnp.bfloat16)
        gg[flat, :] = grad_gate
        gu[flat, :] = grad_up
        for half in range(halves):
            cols = pl.ds(half * wide, wide)
            gs[origin, rows, cols] = (
                dot(grad_gate, wg[:, cols], ((1,), (0,))) + dot(grad_up, wu[:, cols], ((1,), (0,)))
            ).astype(jnp.bfloat16)

            @pl.when(origin == mate)
            def _():
                to_mate(piece, half).start()

            @pl.when((origin != mate) & (origin != t) & is_end)
            def _():
                to_acc(origin, piece, half).start()

        lo[origin, rows] = dot(hidden, wd[...], ((1,), (0,))).astype(jnp.bfloat16)

    span = 256
    flat_rows = nt * row_count
    spans = buf.shape[2] // span
    head = jnp.where(t < nt // 2, 0, 1)
    last_one = jnp.where(t < nt // 2, nt - 1, 0)
    head_rows = pl.ds(pl.multiple_of(head * row_count, row_count), flat_rows - row_count)
    last_rows = pl.ds(pl.multiple_of(last_one * row_count, row_count), row_count)

    def columns(ref, i):
        cols = pl.ds(pl.multiple_of(i * span, span), span)
        return ref[pl.ds(head, nt - 1), :, cols].reshape(flat_rows - row_count, span)

    def grad_head(which, left, right, rows):
        grads[which, rows, :] = dot(left, right[head_rows, :], ((0,), (0,))).astype(jnp.bfloat16)

    def grad_last(which, left, right, rows):
        grads[which, rows, :] = (
            grads[which, rows, :].astype(jnp.float32) + dot(left, right[last_rows, :], ((0,), (0,)))
        ).astype(jnp.bfloat16)

    def down_head(i, carry):
        rows = pl.ds(pl.multiple_of(i * span, span), span)
        grad_head(2, columns(cot, i), hid, rows)
        return carry

    def gate_up_head(i, carry):
        rows = pl.ds(pl.multiple_of(i * span, span), span)
        left = columns(buf, i)
        grad_head(0, left, gg, rows)
        grad_head(1, left, gu, rows)
        return carry

    def down_last(i, carry):
        rows = pl.ds(pl.multiple_of(i * span, span), span)
        grad_last(2, cot[last_one, :, rows], hid, rows)
        return carry

    def gate_up_last(i, carry):
        rows = pl.ds(pl.multiple_of(i * span, span), span)
        left = buf[last_one, :, rows]
        grad_last(0, left, gg, rows)
        grad_last(1, left, gu, rows)
        return carry

    for piece in range(pieces):
        for way, last, onward in ways:
            @pl.when(onward)
            def _():
                copy(way, 0, piece).start()

    for one in loads:
        one.wait()

    def unit(u, carry):
        step = u // pieces
        piece = lax.rem(u, pieces)

        @pl.when(step > 0)
        def _():
            for way, last, onward in ways:
                @pl.when(step <= last)
                def _():
                    landed(way, step, piece)

                    @pl.when(onward)
                    def _():
                        copy(way, step, piece).start()

        def side(way, carry):
            origin = t - (1 - 2 * way) * step
            there = (origin >= 0) & (origin < nt) & ((step > 0) | (way == 0))

            @pl.when(there)
            def _():
                feed(origin, piece)

            return carry

        lax.fori_loop(0, 2, side, carry)

        @pl.when(u == (nt - 1) * pieces - 1)
        def _():
            lax.fori_loop(0, spans, down_head, 0)

        @pl.when((u == (nt - 1) * pieces) & jnp.logical_not(is_end))
        def _():
            lax.fori_loop(0, spans, gate_up_head, 0)

        return carry

    lax.fori_loop(0, nt * pieces, unit, 0)

    near = jnp.where(t < nt // 2, nt // 2, nt // 2 - 1)
    far = jnp.where(t < nt // 2, nt - 1, 0)

    def pass_on(origin, piece):
        @pl.when(jnp.logical_not(is_end))
        def _():
            rows = pl.ds(piece * size, size)
            j = lax.rem(origin, 2)
            for half in range(halves):
                to_acc(origin, piece, half).wait_recv()
                cols = pl.ds(half * wide, wide)
                gs[origin, rows, cols] = (
                    gs[origin, rows, cols].astype(jnp.float32) + acc_in[j, rows, cols].astype(jnp.float32)
                ).astype(jnp.bfloat16)
                to_far(origin, piece, half).start()

    share = buf.shape[2] // ndp

    def block_rows(index):
        return pl.ds(pl.multiple_of(index * share, share), share)

    def pair(which, c):
        return pltpu.make_async_remote_copy(
            src_ref=grads.at[which, block_rows(2 * c + 1 - core)], dst_ref=sums.at[which, c],
            send_sem=pair_send.at[which, c], recv_sem=pair_recv.at[which, c],
            device_id={"dp": d + 1 - 2 * core}, device_id_type=MESH,
        )

    def down_copy(k):
        to = lax.rem(chip + k, chips)
        return pltpu.make_async_remote_copy(
            src_ref=sums.at[2, to], dst_ref=down_out.at[k - 1],
            send_sem=chip_send.at[k - 1], recv_sem=chip_recv.at[k - 1],
            device_id={"dp": 2 * to + core}, device_id_type=MESH,
        )

    def pair_start(*which):
        if fused:
            for w in which:
                for c in range(chips):
                    pair(w, c).start()

    def pair_sum(which):
        if fused:
            for c in range(chips):
                pair(which, c).wait_recv()
                sums[which, c] = (
                    grads[which, block_rows(2 * c + core)].astype(jnp.float32) + sums[which, c].astype(jnp.float32)
                ).astype(jnp.bfloat16)
            if which == 2:
                for k in range(1, chips):
                    down_copy(k).start()
                one = pltpu.make_async_copy(sums.at[2, chip], down_out.at[chips - 1], local_sem.at[8])
            else:
                one = pltpu.make_async_copy(sums.at[which], grads_out.at[which], local_sem.at[6 + which])
        else:
            one = pltpu.make_async_copy(grads.at[which], grads_out.at[which], local_sem.at[6 + which])
        one.start()
        keep.append(one)

    def lo_acc(piece):
        rows = pl.ds(piece * size, size)
        return remote(lo.at[far, rows], lo_in.at[rows], mate, lo_send.at[piece], lo_recv.at[piece])

    @pl.when(is_end)
    def _():
        for piece in range(pieces):
            lo_acc(piece).start()

    keep.append(pltpu.make_async_copy(lo, lo_out, local_sem.at[5]))
    keep[-1].start()
    pass_on(near, 0)
    lax.fori_loop(0, spans, down_last, 0)
    pair_start(2)
    pass_on(near, 1)

    @pl.when(is_end)
    def _():
        lax.fori_loop(0, spans, gate_up_head, 0)

    pair_sum(2)
    lax.fori_loop(0, spans, gate_up_last, 0)
    pair_start(0, 1)
    pass_on(far, 0)
    pass_on(far, 1)
    for one in late_loads:
        one.wait()

    wo_load.wait()
    for piece in range(pieces):
        rows = pl.ds(piece * size, size)
        for half in range(halves):
            to_mate(piece, half).wait_recv()
            part = (rows, pl.ds(half * wide, wide))
            remote(
                gs.at[(t, *part)], far_in.at[part], mate, rs_send.at[3, piece, half], rs_recv.at[3, piece, half]
            ).wait_recv()
        grad_second = (
            gs[t, rows].astype(jnp.float32)
            + mate_in[rows].astype(jnp.float32)
            + far_in[rows].astype(jnp.float32)
        )
        mid = middle[rows]
        inv = lax.rsqrt(jnp.mean(mid * mid, axis=-1, keepdims=True) + EPSILON)
        scaled = row_of(gain_ref) * grad_second
        along = jnp.mean(scaled * mid, axis=-1, keepdims=True)
        grad_middle = cot_own_ref[rows].astype(jnp.float32) + inv * scaled - mid * (inv * inv * inv * along)
        gm_out[rows] = grad_middle
        part = jnp.sum(grad_second * mid * inv, axis=0, keepdims=True)
        if piece == 0:
            gain_out[...] = part
        else:
            gain_out[...] += part
        grad_low = grad_middle.astype(jnp.bfloat16)
        for j in range(nt):
            ga_out[j, :, pl.ds(piece * inner, inner)] = dot(grad_low, wo[j], ((1,), (1,))).astype(jnp.bfloat16)

    pair_sum(0)
    pair_sum(1)
    base_out[...] = middle[...] + lo[t].astype(jnp.float32)

    @pl.when(jnp.logical_not(is_end))
    def _():
        for piece in range(pieces):
            lo_acc(piece).wait_recv()

    for one in keep:
        one.wait()
    for piece in range(pieces):
        for way, last, onward in ways:
            for step in range(nt):
                @pl.when(onward & (step <= last))
                def _():
                    copy(way, step, piece).wait_send()

        @pl.when(is_end)
        def _():
            lo_acc(piece).wait_send()

        for half in range(halves):
            to_mate(piece, half).wait_send()
            for origin in (near, far):
                @pl.when(is_end)
                def _():
                    to_acc(origin, piece, half).wait_send()

                @pl.when(jnp.logical_not(is_end))
                def _():
                    to_far(origin, piece, half).wait_send()

    if fused:
        for which in range(3):
            for c in range(chips):
                pair(which, c).wait_send()
        for k in range(1, chips):
            down_copy(k).wait()


def feed(nt, ndp, middle, second, gain, cotangent, whole, cot_all, gate_weight, up_weight, down_weight):
    rows, width = middle.shape
    hidden = gate_weight.shape[0]
    low, full = jnp.bfloat16, jnp.float32
    pieces, halves = 2, 1
    hbm = pl.BlockSpec(memory_space=pl.ANY)
    vmem = pl.BlockSpec(memory_space=pltpu.VMEM)
    inner = whole.shape[1] // 4
    dma = pltpu.SemaphoreType.DMA
    shape = jax.ShapeDtypeStruct
    share, chips = width // ndp, ndp // 2
    fused = share % 16 == 0
    sums = (3, chips, share, hidden)
    pairs = [
        pltpu.VMEM(sums, low), dma((3, chips)), dma((3, chips)), dma((chips - 1,)), dma((chips - 1,))
    ] if fused else []
    return pl.pallas_call(
        functools.partial(feed_kernel, nt, ndp, pieces, halves, fused),
        out_shape=(
            shape((rows, width), full), shape((rows, width), full), shape((1, width), full),
            shape((nt, rows // 2, 2 * inner), low), shape((nt, rows, width), low), shape((rows, width), low),
            shape((2, *sums[1:]) if fused else (3, width, hidden), low),
        ) + (shape((chips, share, hidden), low),) * fused,
        in_specs=[vmem] + [hbm] * 8,
        out_specs=(vmem, vmem, vmem, vmem, hbm, hbm, hbm) + (hbm,) * fused,
        scratch_shapes=[
            pltpu.VMEM((rows, width), full), pltpu.VMEM((rows, width), low),
            pltpu.VMEM((nt, rows, width), low), pltpu.VMEM((nt, rows, width), low),
            pltpu.VMEM((hidden, width), low), pltpu.VMEM((hidden, width), low), pltpu.VMEM((hidden, width), low),
            pltpu.VMEM((nt * rows, hidden), low), pltpu.VMEM((nt * rows, hidden), low), pltpu.VMEM((nt * rows, hidden), low),
            pltpu.VMEM((nt, rows, width), low), pltpu.VMEM((nt, rows, width), low),
            pltpu.VMEM((nt, inner, width), low),
            pltpu.VMEM((rows, width), low), pltpu.VMEM((2, rows, width), low), pltpu.VMEM((rows, width), low),
            pltpu.VMEM((3, width, hidden), low), *pairs,
            dma((2, nt, pieces)), dma((2, nt, pieces)), dma((5, pieces, halves)), dma((4, pieces, halves)),
            dma((pieces,)), dma((pieces,)),
            dma((12,)),
        ],
        compiler_params=pltpu.CompilerParams(
            vmem_limit_bytes=VMEM_LIMIT, collective_id=1, has_side_effects=True
        ),
        name="feed",
    )(gain, middle, second, cotangent, whole, cot_all, gate_weight, up_weight, down_weight)


def back_kernel(
    nt, ndp, pieces, heads, head_dim, grad_type, fused,
    ga_ref, gain_ref, gain2_ref, gm_hbm, x_hbm, own_hbm,
    qkv_hbm, low_hbm, high_hbm, first_hbm, weight_hbm, lo_hbm, lo_part_hbm, *rest,
):
    if fused:
        feed_hbm, *rest = rest
    input_out, q_out, k_out, v_out, o_out, gains_in, dist_in, far_in, mate_in, *rest = rest
    if fused:
        feed_in, *rest = rest
    (
        gm_ref, x_ref, own_ref,
        ga_in, qkv, low, high, first, weight, lo, acc_in, lo_part,
        gq, dq_send, dq_in, dkv_send, dkv_in, diag, dk_acc, dv_acc,
        og, og_sum, og_chip, og_line, og_line_in, pg, pg_sum, pg_chip,
        gains_line, gains_own, dist_own,
        swap_send, swap_recv, dq_done, dq_here, dkv_done, dkv_here, lo_send, lo_recv,
        pair_send, pair_recv, chip_send, chip_recv, line_send, line_recv,
        gl_send, gl_recv, gd_send, gd_recv, dist_send, dist_recv, local_sem, *rest,
    ) = rest
    if fused:
        feed_send, feed_recv = rest
    t = lax.axis_index("tensor")
    d = lax.axis_index("dp")
    core = lax.rem(d, 2)
    chip = d // 2
    chips = ndp // 2
    barrier = greet(t, nt)
    for k in range(1, ndp):
        pl.semaphore_signal(
            barrier, inc=1, device_id={"dp": lax.rem(d + k, ndp)}, device_id_type=MESH
        )
    mate = t + 1 - 2 * lax.rem(t, 2)
    is_end = (t == 0) | (t == nt - 1)
    near = jnp.where(t < nt // 2, nt // 2, nt // 2 - 1)
    far = jnp.where(t < nt // 2, nt - 1, 0)
    loads = [
        pltpu.make_async_copy(a, b, local_sem.at[i])
        for i, (a, b) in enumerate(
            ((qkv_hbm, qkv), (low_hbm, low), (high_hbm, high), (first_hbm, first),
             (weight_hbm.at[:, pl.ds(0, weight.shape[1])], weight),
             (lo_hbm.at[near], lo.at[0]), (lo_hbm.at[far], lo.at[1]), (lo_hbm.at[mate], lo.at[2]),
             (gm_hbm, gm_ref), (x_hbm, x_ref), (own_hbm, own_ref), (lo_part_hbm, lo_part))
        )
    ]
    for one in loads:
        one.start()
    others = (far, near, mate)
    row_count, width = x_ref.shape
    inner = heads * head_dim
    size = row_count // pieces
    share = width // ndp
    full = jnp.float32

    def remote(src, dst, send, recv, **target):
        return pltpu.make_async_remote_copy(
            src_ref=src, dst_ref=dst, send_sem=send, recv_sem=recv,
            device_id=target, device_id_type=MESH,
        )

    def swap(peer):
        return remote(ga_ref.at[peer], ga_in.at[t], swap_send.at[peer], swap_recv.at[t], tensor=peer)

    def swap_in(peer):
        return remote(ga_ref.at[peer], ga_in.at[peer], swap_send.at[peer], swap_recv.at[peer], tensor=peer)

    def lo_acc(piece):
        rows = pl.ds(piece * size, size)
        return remote(lo.at[0, rows], acc_in.at[rows], lo_send.at[0, piece], lo_recv.at[0, piece], tensor=mate)

    def lo_final(place, origin, piece):
        rows = pl.ds(piece * size, size)
        return remote(
            lo.at[place, rows], far_in.at[rows], lo_send.at[place, piece], lo_recv.at[1, piece], tensor=origin
        )

    def lo_mate(piece):
        rows = pl.ds(piece * size, size)
        return remote(lo.at[2, rows], mate_in.at[rows], lo_send.at[2, piece], lo_recv.at[2, piece], tensor=mate)

    pl.semaphore_wait(barrier, nt - 1 + ndp - 1)
    for peer in others:
        swap(peer).start()
    ga_in[t] = ga_ref[t]
    if fused:
        def feed_copy(which, k):
            to = lax.rem(chip + k, chips)
            return remote(
                feed_hbm.at[which, to], feed_in.at[k - 1, which],
                feed_send.at[k - 1, which], feed_recv.at[k - 1, which], dp=2 * to + core,
            )

        own_feed = pltpu.make_async_copy(feed_hbm.at[:, chip], feed_in.at[chips - 1], local_sem.at[13])
        own_feed.start()
        for which in range(2):
            for k in range(1, chips):
                feed_copy(which, k).start()

    def block_rows(index):
        return pl.ds(pl.multiple_of(index * share, share), share)

    def pair(kind, c):
        grads, landing = ((og, og_sum), (pg, pg_sum))[kind]
        return remote(
            grads.at[block_rows(2 * c + 1 - core)], landing.at[c],
            pair_send.at[kind, c], pair_recv.at[kind, c], dp=d + 1 - 2 * core,
        )

    def chip_copy(kind, k):
        sums, landing = ((og_sum, og_chip), (pg_sum, pg_chip))[kind]
        to = lax.rem(chip + k, chips)
        return remote(
            sums.at[to], landing.at[k - 1], chip_send.at[kind, k - 1], chip_recv.at[kind, k - 1], dp=2 * to + core
        )

    def pair_sum(kind):
        grads, sums = ((og, og_sum), (pg, pg_sum))[kind]
        for c in range(chips):
            pair(kind, c).wait_recv()
            sums[c] = (grads[block_rows(2 * c + core)].astype(full) + sums[c].astype(full)).astype(grad_type)
        for k in range(1, chips):
            chip_copy(kind, k).start()

    def chip_sum(kind):
        sums, landing = ((og_sum, og_chip), (pg_sum, pg_chip))[kind]
        total = sums[chip].astype(full)
        for k in range(1, chips):
            chip_copy(kind, k).wait_recv()
            total = total + landing[k - 1].astype(full)
        return total

    for one in loads[5:]:
        one.wait()
    for piece in range(pieces):
        @pl.when(is_end)
        def _():
            lo_acc(piece).start()

        @pl.when(jnp.logical_not(is_end))
        def _():
            rows_lo = pl.ds(piece * size, size)
            lo[1, rows_lo] = (lo[1, rows_lo].astype(full) + lo_part[rows_lo].astype(full)).astype(jnp.bfloat16)
            lo_final(1, far, piece).start()

    span = 256
    spans = width // span
    own = jnp.concatenate([unpack(own_ref[j], 0, inner) for j in range(nt)], axis=1)
    for i in range(spans):
        left = gm_ref[:, pl.ds(i * span, span)].astype(jnp.bfloat16)
        og[pl.ds(i * span, span), :] = dot(left, own, ((0,), (0,))).astype(grad_type)
    for c in range(chips):
        pair(0, c).start()

    for i in range(3):
        loads[i].wait()
    def give(peer):
        return (
            remote(dq_send.at[peer], dq_in.at[t], dq_done.at[peer], dq_here.at[t], tensor=peer),
            remote(dkv_send.at[peer], dkv_in.at[t], dkv_done.at[peer], dkv_here.at[t], tensor=peer),
        )

    def taken(peer):
        return (
            remote(dq_send.at[peer], dq_in.at[peer], dq_done.at[peer], dq_here.at[peer], tensor=peer),
            remote(dkv_send.at[peer], dkv_in.at[peer], dkv_done.at[peer], dkv_here.at[peer], tensor=peer),
        )

    def give_keys(block):
        rows = pl.ds(block * QB, QB)
        sides = [acc[head, rows, :] for acc in (dk_acc, dv_acc) for head in range(heads)]
        side = jnp.concatenate(sides, axis=1).astype(jnp.bfloat16)
        gq[rows, pl.ds(inner, 2 * inner)] = side
        dkv_send[block] = side

        @pl.when(t != block)
        def _():
            give(block)[1].start()

    blocks = LEN // QB
    diag[...] = jnp.zeros_like(diag)
    for block in reversed(range(blocks)):
        keys = key_count(block)
        rows = pl.ds(block * QB, QB)
        first_col = LEN - block * QB

        for waited in (1, 0) if block == 1 else () if block == 0 else (block,):
            @pl.when(t != waited)
            def _():
                swap_in(waited).wait_recv()

        parts = []
        for head in range(heads):
            cols = pl.ds(head * head_dim, head_dim)
            if keys == HALF:
                probs_low = low[head, rows, :]
            else:
                probs_low = high[head, pl.ds(block * QB - HALF, QB), :]
            probs = probs_low.astype(full)
            do = unpack(ga_in[block], head * head_dim, head_dim)
            grad_probs = dot(do, qkv[2, pl.ds(0, keys), cols], ((1,), (1,)))
            weighted = jnp.sum(probs * grad_probs, axis=-1, keepdims=True)
            grad_low = (probs * (grad_probs - weighted)).astype(jnp.bfloat16)
            reach = pl.ds(first_col, keys)
            diag[head, :, reach] = diag[head, :, reach] + grad_low.astype(full)
            parts.append(dot(grad_low, qkv[1, pl.ds(0, keys), cols], ((1,), (0,))))
            key_part = dot(grad_low, qkv[0, rows, cols], ((0,), (0,)))
            value_part = dot(probs_low, do, ((0,), (0,)))
            if block == blocks - 1:
                dk_acc[head] = key_part
                dv_acc[head] = value_part
            else:
                dk_acc[head, pl.ds(0, keys), :] += key_part
                dv_acc[head, pl.ds(0, keys), :] += value_part
        side = jnp.concatenate(parts, axis=1).astype(jnp.bfloat16)
        gq[rows, pl.ds(0, inner)] = side
        dq_send[block] = pack(side)

        @pl.when(t != block)
        def _():
            give(block)[0].start()

        if block * QB == HALF:
            for done in range(block, blocks):
                give_keys(done)
        if block == 1:
            pair_sum(0)
    for block in range(HALF // QB):
        give_keys(block)

    def token_rows(peer):
        return pl.ds(pl.multiple_of(peer * row_count, row_count), row_count)

    for head in range(heads):
        dist_own[pl.ds(head, 1), :] = fold_diagonals(diag[head])
    dist_keep = pltpu.make_async_copy(dist_own, dist_in.at[d], local_sem.at[12])
    dist_keep.start()

    def dist_copy(k):
        return remote(
            dist_own, dist_in.at[d], dist_send.at[k - 1], dist_recv.at[d], dp=lax.rem(d + k, ndp)
        )

    for k in range(1, ndp):
        dist_copy(k).start()
    loads[3].wait()
    for i in range(spans):
        cols = pl.ds(i * span, span)
        left = first[:, :, cols].reshape(nt * row_count, span)
        pg[cols, :] = dot(left, gq[...], ((0,), (0,))).astype(grad_type)
    for c in range(chips):
        pair(1, c).start()
    total = chip_sum(0)
    for j in range(nt):
        og_line[j] = total[:, j * inner : (j + 1) * inner].astype(grad_type)

    def line_copy_out(peer):
        return remote(og_line.at[peer], og_line_in.at[t], line_send.at[peer], line_recv.at[t], tensor=peer)

    def line_in(peer):
        return remote(og_line.at[peer], og_line_in.at[peer], line_send.at[peer], line_recv.at[peer], tensor=peer)

    for peer in others:
        line_copy_out(peer).start()
    pair_sum(1)

    @pl.when(jnp.logical_not(is_end))
    def _():
        for piece in range(pieces):
            lo_acc(piece).wait_recv()
        lo[0] = (lo[0].astype(full) + acc_in[...].astype(full)).astype(jnp.bfloat16)

    loads[4].wait()
    inputs = x_ref[...].astype(full)
    inv = lax.rsqrt(jnp.mean(inputs * inputs, axis=-1, keepdims=True) + EPSILON)
    grad_first = dot(gq[token_rows(t)], weight[t], ((1,), (0,)))
    for peer in (mate, near, far):
        for one in taken(peer):
            one.wait_recv()
        grad_first = (
            grad_first
            + dot(unpack(dq_in[peer], 0, inner), weight[peer, pl.ds(0, inner), :], ((1,), (0,)))
            + dot(dkv_in[peer], weight[peer, pl.ds(inner, 2 * inner), :], ((1,), (0,)))
        )
    scaled = row_of(gain_ref) * grad_first
    along = jnp.mean(scaled * inputs, axis=-1, keepdims=True)
    gains_line[t, pl.ds(0, 1), :] = jnp.sum(grad_first * inputs * inv, axis=0, keepdims=True)
    gains_line[t, pl.ds(1, 1), :] = gain2_ref[...]

    def gain_copy(peer):
        return remote(gains_line.at[t], gains_line.at[t], gl_send.at[peer], gl_recv.at[t], tensor=peer)

    def gain_landed(peer):
        return remote(gains_line.at[peer], gains_line.at[peer], gl_send.at[peer], gl_recv.at[peer], tensor=peer)

    for peer in others:
        gain_copy(peer).start()
    for piece in range(pieces):
        lo_mate(piece).start()

        @pl.when(jnp.logical_not(is_end))
        def _():
            lo_final(0, near, piece).start()

    input_out[...] = (gm_ref[...] + inv * scaled - inputs * (inv * inv * inv * along)).astype(jnp.bfloat16)
    for peer in others:
        gain_landed(peer).wait_recv()
    gains_own[...] = gains_line[0] + gains_line[1] + gains_line[2] + gains_line[3]
    gains_keep = pltpu.make_async_copy(gains_own, gains_in.at[d], local_sem.at[14])
    gains_keep.start()

    def gains_copy(k):
        return remote(
            gains_own, gains_in.at[d], gd_send.at[k - 1], gd_recv.at[d], dp=lax.rem(d + k, ndp)
        )

    for k in range(1, ndp):
        gains_copy(k).start()
    total = chip_sum(1)
    q_out[...] = total[:, :inner]
    k_out[...] = total[:, inner : 2 * inner]
    v_out[...] = total[:, 2 * inner :]
    total = og_line[t].astype(full)
    for peer in others:
        line_in(peer).wait_recv()
        total = total + og_line_in[peer].astype(full)
    o_out[...] = total

    def others_of(landing, send, recv):
        for k in range(1, ndp):
            peer = lax.rem(d + k, ndp)
            remote(landing.at[peer], landing.at[peer], send.at[k - 1], recv.at[peer], dp=peer).wait_recv()

    others_of(dist_in, dist_send, dist_recv)
    if fused:
        own_feed.wait()
        for which in range(2):
            for k in range(1, chips):
                feed_copy(which, k).wait_recv()
    for piece in range(pieces):
        lo_final(0, near, piece).wait_recv()
        lo_mate(piece).wait_recv()
    others_of(gains_in, gd_send, gd_recv)
    dist_keep.wait()
    gains_keep.wait()

    for peer in others:
        swap(peer).wait_send()
        for one in give(peer):
            one.wait_send()
        line_copy_out(peer).wait_send()
        gain_copy(peer).wait_send()
    for piece in range(pieces):
        lo_mate(piece).wait_send()

        @pl.when(is_end)
        def _():
            lo_acc(piece).wait_send()

        @pl.when(jnp.logical_not(is_end))
        def _():
            lo_final(0, near, piece).wait_send()
            lo_final(1, far, piece).wait_send()

    if fused:
        for which in range(2):
            for k in range(1, chips):
                feed_copy(which, k).wait_send()
    for kind in range(2):
        for c in range(chips):
            pair(kind, c).wait_send()
        for k in range(1, chips):
            chip_copy(kind, k).wait_send()
    for k in range(1, ndp):
        dist_copy(k).wait_send()
        gains_copy(k).wait_send()


def back(nt, ndp, grad_attended, grad_middle, tokens, gain, gain2_part, attended, qkv, probs_low, probs_high, first_all, weights, layer_parts, layer_far, feed_grads):
    rows, width = tokens.shape
    heads = probs_low.shape[0]
    inner = qkv.shape[2]
    head_dim = inner // heads
    low, full = jnp.bfloat16, jnp.float32
    pieces = 2
    share, chips = width // ndp, ndp // 2
    grad_type = low if share % 16 == 0 else full
    hbm = pl.BlockSpec(memory_space=pl.ANY)
    vmem = pl.BlockSpec(memory_space=pltpu.VMEM)
    dma = pltpu.SemaphoreType.DMA
    shape = jax.ShapeDtypeStruct
    reach = SPAN + QB
    scratch = lambda *dims, kind=low: pltpu.VMEM(dims, kind)
    part = shape((share, inner), full)
    fused = feed_grads.ndim == 4
    hidden = feed_grads.shape[-1]
    feeds = [dma((chips - 1, 2)), dma((chips - 1, 2))] if fused else []
    return pl.pallas_call(
        functools.partial(back_kernel, nt, ndp, pieces, heads, head_dim, grad_type, fused),
        out_shape=(
            shape((rows, width), low), part, part, part, part,
            shape((ndp, 2, width), full), shape((ndp, heads, reach), full),
            shape((rows, width), low), shape((rows, width), low),
        ) + (shape((chips, 2, share, hidden), low),) * fused,
        in_specs=[vmem] * 3 + [hbm] * (10 + fused),
        out_specs=(vmem,) * 5 + (hbm,) * (4 + fused),
        scratch_shapes=[
            scratch(rows, width, kind=full), scratch(rows, width), scratch(nt, rows // 2, 2 * inner),
            scratch(nt, rows // 2, 2 * inner), scratch(3, LEN, inner), scratch(heads, HALF, HALF), scratch(heads, HALF, LEN),
            scratch(nt, rows, width), scratch(nt, 3 * inner, width), scratch(3, rows, width), scratch(rows, width), scratch(rows, width),
            scratch(nt * rows, 3 * inner), scratch(nt, rows // 2, 2 * inner), scratch(nt, rows // 2, 2 * inner),
            scratch(nt, rows, 2 * inner), scratch(nt, rows, 2 * inner), scratch(heads, QB, reach, kind=full),
            scratch(heads, LEN, head_dim, kind=full), scratch(heads, LEN, head_dim, kind=full),
            scratch(width, nt * inner, kind=grad_type), scratch(chips, share, nt * inner, kind=grad_type),
            scratch(chips - 1, share, nt * inner, kind=grad_type),
            scratch(nt, share, inner, kind=grad_type), scratch(nt, share, inner, kind=grad_type),
            scratch(width, 3 * inner, kind=grad_type), scratch(chips, share, 3 * inner, kind=grad_type),
            scratch(chips - 1, share, 3 * inner, kind=grad_type),
            scratch(nt, 2, width, kind=full), scratch(2, width, kind=full), scratch(heads, reach, kind=full),
            dma((nt,)), dma((nt,)), dma((nt,)), dma((nt,)), dma((nt,)), dma((nt,)), dma((3, pieces)), dma((3, pieces)),
            dma((2, chips)), dma((2, chips)), dma((2, chips - 1)), dma((2, chips - 1)), dma((nt,)), dma((nt,)),
            dma((nt,)), dma((nt,)), dma((ndp - 1,)), dma((ndp,)), dma((ndp - 1,)), dma((ndp,)), dma((15,)), *feeds,
        ],
        compiler_params=pltpu.CompilerParams(
            vmem_limit_bytes=VMEM_LIMIT, collective_id=2, has_side_effects=True
        ),
        cost_estimate=pl.CostEstimate(flops=60 * 10**9, bytes_accessed=200 * 10**6, transcendentals=0),
        name="back",
    )(
        grad_attended, gain, gain2_part, grad_middle, tokens, attended,
        qkv, probs_low, probs_high, first_all, weights, layer_parts, layer_far, *((feed_grads,) if fused else ()),
    )


def finish_kernel(
    fused, bucket_ref, base_ref, far_ref, mate_ref, input_ref, q_ref, k_ref, v_ref, o_ref, gains_ref, dist_ref, *rest,
):
    if fused:
        feed_ref, down_ref, *rest = rest
    layer_out, input_out, gain_out, q_out, k_out, v_out, o_out, table_out, gain2_out, *feed_outs = rest
    full = jnp.float32
    layer_out[...] = (base_ref[...] + far_ref[...].astype(full) + mate_ref[...].astype(full)).astype(jnp.bfloat16)
    input_out[...] = input_ref[...]
    for a, b in ((q_ref, q_out), (k_ref, k_out), (v_ref, v_out), (o_ref, o_out)):
        b[...] = a[...]

    @pl.when(pl.program_id(0) == 0)
    def _():
        gains, dist = gains_ref[0], dist_ref[0]
        for k in range(1, gains_ref.shape[0]):
            gains = gains + gains_ref[k]
            dist = dist + dist_ref[k]
        gain_out[...] = gains[0:1].reshape(gain_out.shape)
        gain2_out[...] = gains[1:2].reshape(gain2_out.shape)
        reach = dist.shape[1]
        shifted = jnp.concatenate([jnp.zeros((1, 1), jnp.int32), row_of(bucket_ref)], axis=1)[:, :reach]
        hot = (lax.broadcasted_iota(jnp.int32, (NB, reach), 0) == shifted).astype(full)
        table_out[...] = lax.dot_general(
            dist, hot, (((1,), (1,)), ((), ())), precision=HIGHEST, preferred_element_type=full
        )

    for which in range(len(feed_outs)):
        parts = [down_ref[k] if which == 2 else feed_ref[k, which] for k in range(feed_ref.shape[0])]
        total = parts[0].astype(full)
        for part in parts[1:]:
            total = total + part.astype(full)
        feed_outs[which][...] = total


def finish(buckets, base, outs):
    fused = len(outs) > 9
    input_grad, query_grad, key_grad, value_grad, out_grad, gains, dist, far_in, mate_in = outs[:9]
    rows, width = base.shape
    share, inner = query_grad.shape
    low, full = jnp.bfloat16, jnp.float32
    shape = jax.ShapeDtypeStruct
    steps = 2 if share % 32 == 0 and rows % 32 == 0 else 1
    vmem = pl.BlockSpec(memory_space=pltpu.VMEM)
    wide = pl.BlockSpec((rows // steps, width), lambda i: (i, 0))
    small = pl.BlockSpec((share // steps, inner), lambda i: (i, 0))
    part = shape(query_grad.shape, full)
    ins, feeds, blocks = [], (), ()
    if fused:
        chips, kinds, _, hidden = outs[9].shape
        ins = [
            pl.BlockSpec((chips, kinds, share // steps, hidden), lambda i: (0, 0, i, 0)),
            pl.BlockSpec((chips, share // steps, hidden), lambda i: (0, i, 0)),
        ]
        feeds = (shape((share, hidden), full),) * (kinds + 1)
        blocks = (pl.BlockSpec((share // steps, hidden), lambda i: (i, 0)),) * (kinds + 1)
    return pl.pallas_call(
        functools.partial(finish_kernel, fused),
        grid=(steps,),
        out_shape=(
            shape((rows, width), low), shape((rows, width), low), shape((width,), full), part, part, part, part,
            shape((dist.shape[1], NB), full), shape((width,), full),
        ) + feeds,
        in_specs=[vmem] + [wide] * 4 + [small] * 4 + [vmem] * 2 + ins,
        out_specs=(wide, wide, vmem) + (small,) * 4 + (vmem, vmem) + blocks,
        compiler_params=pltpu.CompilerParams(vmem_limit_bytes=VMEM_LIMIT),
        name="finish",
    )(
        buckets, base, far_in, mate_in, input_grad, query_grad, key_grad, value_grad, out_grad, gains, dist,
        *outs[9:],
    )


def per_device(
    tokens,
    first_gain,
    query_weight,
    key_weight,
    value_weight,
    out_weight,
    bucket_table,
    second_gain,
    gate_weight,
    up_weight,
    down_weight,
    piece_start,
    bucket_index,
    cotangent,
):
    nt, ndp = lax.axis_size("tensor"), lax.axis_size("dp")
    weights = (query_weight.T, key_weight.T, value_weight.T, out_weight.T)
    first_all, cot_all, qkv, probs_low, probs_high, attended, whole, middle, second = gather_attend(
        nt, ndp, tokens, cotangent, first_gain, second_gain, weights, bucket_index, bucket_table.T, piece_start
    )
    base, grad_middle, second_part, grad_attended, layer_parts, layer_far, feed_grads, *down_in = feed(
        nt, ndp, middle, second, second_gain, cotangent, whole, cot_all, gate_weight.T, up_weight.T, down_weight.T
    )
    outs = back(
        nt, ndp, grad_attended, grad_middle, tokens, first_gain, second_part, attended,
        qkv, probs_low, probs_high, first_all, whole, layer_parts, layer_far, feed_grads,
    )
    outs = finish(bucket_index, base, (*outs, *down_in))
    if feed_grads.ndim == 3:
        sums = lax.psum_scatter(feed_grads, "dp", scatter_dimension=1, tiled=True).astype(jnp.float32)
        outs = (*outs, sums[0], sums[1], sums[2])
    return (*outs[:7], outs[7].T, *outs[8:])


def solution(mesh):
    return jax.shard_map(
        per_device,
        mesh=mesh,
        in_specs=(
            P(("dp", "tensor"), None),
            P(),
            P(None, "tensor"),
            P(None, "tensor"),
            P(None, "tensor"),
            P(None, "tensor"),
            P(None, "tensor"),
            P(),
            P(None, "tensor"),
            P(None, "tensor"),
            P(None, "tensor"),
            P("dp", None),
            P(),
            P(("dp", "tensor"), None),
        ),
        out_specs=(
            P(("dp", "tensor"), None),
            P(("dp", "tensor"), None),
            P(),
            P("dp", "tensor"),
            P("dp", "tensor"),
            P("dp", "tensor"),
            P("dp", "tensor"),
            P(None, "tensor"),
            P(),
            P("dp", "tensor"),
            P("dp", "tensor"),
            P("dp", "tensor"),
        ),
        check_vma=False,
    )
```

```python
import functools

import jax
import jax.numpy as jnp
from jax import lax
from jax.experimental import pallas as pl
from jax.experimental.pallas import tpu as pltpu
from jax.sharding import PartitionSpec as P

NB = 32
LEN = 1024
QB = 256
PIECE = 256
NPIECE = 2
HALF = LEN // NPIECE
SPAN = 5 * QB
DIST = 2 * LEN

EPSILON = 1e-06
MASKED = -1000000000.0
HIGHEST = lax.Precision.HIGHEST
VMEM_LIMIT = 60 * 1024 * 1024
MESH = pl.DeviceIdType.MESH


def normed(row_block, gain_vec):
    inv_rms = lax.rsqrt(jnp.mean(row_block * row_block, axis=-1, keepdims=True) + EPSILON)
    return row_block * inv_rms * gain_vec


def dot(a, b, dims):
    return lax.dot_general(a, b, (dims, ((), ())), preferred_element_type=jnp.float32)


def key_count(block):
    return HALF if (block + 1) * QB <= HALF else LEN


def toeplitz(bucket_ref, table_ref, head):
    bucket_row = jnp.concatenate([row_of(bucket_ref), jnp.zeros((1, 1), jnp.int32)], axis=1)
    row = jnp.zeros(bucket_row.shape, jnp.float32)
    for bucket in range(NB):
        row = jnp.where(bucket_row == bucket, table_ref[head, bucket], row)
    rows = jnp.broadcast_to(row, (QB, DIST))
    return pltpu.roll(rows, DIST - (QB - 1), 1, stride=1, stride_axis=0)[:, :SPAN]


def row_of(ref):
    return ref[...].reshape(1, ref.shape[0])


def label_of(position, starts):
    label = jnp.zeros(position.shape, jnp.int32)
    for piece, start in enumerate(starts):
        inside = (position >= start) & (position < start + PIECE)
        label = jnp.where(inside, piece + 1, label)
    return label


def allowed_block(block, starts):
    keys = key_count(block)
    query = block * QB + lax.broadcasted_iota(jnp.int32, (QB, 1), 0)
    key = lax.broadcasted_iota(jnp.int32, (1, keys), 1)
    query_label = label_of(query, starts)
    key_label = label_of(key, starts)
    return (key <= query) | ((query_label == key_label) & (query_label > 0))


def attend_block(block, head_dim, allowed, qkv_ref, bias_ref, low_ref, high_ref):
    keys = key_count(block)
    first = LEN - QB - block * QB
    rows = pl.ds(block * QB, QB)
    outs = []
    for head in range(bias_ref.shape[0]):
        cols = pl.ds(head * head_dim, head_dim)
        raw = dot(qkv_ref[0, rows, cols], qkv_ref[1, pl.ds(0, keys), cols], ((1,), (1,)))
        scores = jnp.where(allowed, raw + bias_ref[head, :, pl.ds(first, keys)], MASKED)
        peak = jnp.max(scores, axis=-1, keepdims=True)
        powered = jnp.exp(scores - peak)
        total = jnp.sum(powered, axis=-1, keepdims=True)
        probs = (powered * (1.0 / total)).astype(jnp.bfloat16)
        if keys == HALF:
            low_ref[head, rows, :] = probs
        else:
            high_ref[head, pl.ds(block * QB - HALF, QB), :] = probs
        outs.append(dot(probs, qkv_ref[2, pl.ds(0, keys), cols], ((1,), (0,))))
    return jnp.concatenate(outs, axis=1).astype(jnp.bfloat16)


def pack(rows):
    half = rows.shape[0] // 2
    return jnp.concatenate([rows[:half], rows[half:]], axis=1)


def unpack(packed, start, width):
    half = packed.shape[1] // 2
    return jnp.concatenate(
        [packed[:, start : start + width], packed[:, half + start : half + start + width]], axis=0
    )


def greet(t, nt):
    barrier = pltpu.get_barrier_semaphore()
    for k in range(1, nt):
        pl.semaphore_signal(
            barrier, inc=1, device_id={"tensor": lax.rem(t + k, nt)}, device_id_type=MESH
        )
    return barrier


def line_copy(t, nt, way, step, buf, piece, pieces, send_sem, recv_sem):
    sign = 1 if way == 0 else -1
    origin = jnp.clip(t - sign * step, 0, nt - 1)
    rows = buf.shape[1] // pieces
    part = buf.at[origin, pl.ds(piece * rows, rows)]
    return pltpu.make_async_remote_copy(
        src_ref=part,
        dst_ref=part,
        send_sem=send_sem,
        recv_sem=recv_sem,
        device_id={"tensor": jnp.clip(t + sign, 0, nt - 1)},
        device_id_type=MESH,
    )


def gather_attend_kernel(
    nt, ndp, pieces, heads, head_dim, exchange,
    x_ref, cot_ref, gain_ref, gain2_ref, bucket_ref, table_ref, start_ref, *rest,
):
    weight_refs, rest = rest[: 4 if exchange else 1], rest[4 if exchange else 1 :]
    (
        first_out, cot_out, qkv_out, low_out, high_out, own_out, whole_out, middle_out, second_out,
        first, qkv, low, high, bias, att, own, whole,
        send_sem, recv_sem, swap_send, swap_recv, line_send, line_recv, chip_send, chip_recv, core_send, core_recv,
        local_sem,
    ) = rest
    t = lax.axis_index("tensor")
    d = lax.axis_index("dp")
    core = lax.rem(d, 2)
    chip = d // 2
    chips = ndp // 2
    barrier = greet(t, nt)
    greeted = nt - 1
    if exchange:
        for k in range(chips):
            peer = 2 * lax.rem(chip + k, chips) + core if k else d + 1 - 2 * core
            pl.semaphore_signal(barrier, inc=1, device_id={"dp": peer}, device_id_type=MESH)
        greeted += chips
    inner = heads * head_dim
    share = whole.shape[1] // ndp
    own_cot = pltpu.make_async_copy(cot_ref, cot_out.at[t], local_sem.at[0])
    own_cot.start()
    if exchange:
        loads = [
            pltpu.make_async_copy(weight, whole.at[t, pl.ds(i * inner, inner)], local_sem.at[1 + i])
            for i, weight in enumerate(weight_refs)
        ]
    else:
        loads = [pltpu.make_async_copy(weight_refs[0], whole, local_sem.at[1])]
    for one in loads:
        one.start()

    def slices(index, plane):
        return whole.at[plane, pl.ds(pl.multiple_of(index * share, share), share)]

    def remote(src, dst, send, recv, **target):
        return pltpu.make_async_remote_copy(
            src_ref=src, dst_ref=dst, send_sem=send, recv_sem=recv, device_id=target, device_id_type=MESH
        )

    def plane_at(q):
        return lax.rem(t + q, nt)

    def to_plane(q):
        return remote(slices(d, t), slices(d, t), line_send.at[q - 1], line_recv.at[t], tensor=plane_at(q))

    def from_plane(q):
        p = plane_at(q)
        return remote(slices(d, p), slices(d, p), line_send.at[q - 1], line_recv.at[p], tensor=p)

    def to_chip(k, q):
        part = slices(d, plane_at(q))
        return remote(
            part, part, chip_send.at[k - 1, q - 1], chip_recv.at[k - 1, q - 1], dp=2 * lax.rem(chip + k, chips) + core
        )

    def from_chip(k, q):
        peer = 2 * lax.rem(chip - k + chips, chips) + core
        part = slices(peer, plane_at(q))
        return remote(part, part, chip_send.at[k - 1, q - 1], chip_recv.at[k - 1, q - 1], dp=peer)

    def to_core(k, q):
        part = slices(2 * lax.rem(chip - k + chips, chips) + core, plane_at(q))
        return remote(part, part, core_send.at[k, q - 1], core_recv.at[k, q - 1], dp=d + 1 - 2 * core)

    def from_core(k, q):
        part = slices(2 * lax.rem(chip - k + chips, chips) + 1 - core, plane_at(q))
        return remote(part, part, core_send.at[k, q - 1], core_recv.at[k, q - 1], dp=d + 1 - 2 * core)

    for one in loads:
        one.wait()
    pl.semaphore_wait(barrier, greeted)
    if exchange:
        for q in range(1, nt):
            to_plane(q).start()
    first[t] = normed(x_ref[...].astype(jnp.float32), row_of(gain_ref)).astype(jnp.bfloat16)

    def copy(way, stage, step, piece):
        buf = first if stage == 0 else cot_out
        return line_copy(
            t, nt, way, step, buf, piece, pieces,
            send_sem.at[way, stage, step, piece], recv_sem.at[way, stage, step, piece],
        )

    def landed(way, stage, step, piece):
        sign = 1 if way == 0 else -1
        buf = first if stage == 0 else cot_out
        rows = buf.shape[1] // pieces
        part = buf.at[jnp.clip(t - sign * step, 0, nt - 1), pl.ds(piece * rows, rows)]
        remote(
            part, part, send_sem.at[way, stage, step - 1, piece], recv_sem.at[way, stage, step - 1, piece],
            tensor=jnp.clip(t + sign, 0, nt - 1),
        ).wait_recv()

    ways = ((0, t, t < nt - 1), (1, nt - 1 - t, t > 0))

    def tick(k):
        for piece in range(pieces):
            for way, last, onward in ways:
                if k < nt:
                    @pl.when(k <= last)
                    def _():
                        if k > 0:
                            landed(way, 0, k, piece)

                        @pl.when(onward)
                        def _():
                            copy(way, 0, k, piece).start()

                if k > 0:
                    step = k - last - 1

                    @pl.when((step >= 1) & (step <= last))
                    def _():
                        landed(way, 1, step, piece)

                        @pl.when(onward)
                        def _():
                            copy(way, 1, step, piece).start()

                    @pl.when((step == 0) & onward)
                    def _():
                        copy(way, 0, last, piece).wait_send()
                        copy(way, 1, 0, piece).start()

    def project(origin):
        rows = pl.ds(pl.multiple_of(origin * QB, QB), QB)
        for place in range(3):
            weight = whole[t, pl.ds(place * inner, inner), :]
            qkv[place, rows, :] = dot(first[origin], weight, ((1,), (1,))).astype(jnp.bfloat16)

    tick(0)
    project(t)
    for head in range(heads):
        bias[head] = toeplitz(bucket_ref, table_ref, head)
    own_cot.wait()
    for k in range(1, nt):
        tick(k)

        @pl.when(t - k >= 0)
        def _():
            project(t - k)

        @pl.when(t + k < nt)
        def _():
            project(t + k)

        if exchange and k == 2:
            for q in range(1, nt):
                from_plane(q).wait_recv()
                for j in range(1, chips):
                    to_chip(j, q).start()
                to_core(0, q).start()

    starts = [start_ref[0, piece] for piece in range(NPIECE)]
    keep = [
        pltpu.make_async_copy(first, first_out, local_sem.at[5]),
        pltpu.make_async_copy(qkv, qkv_out, local_sem.at[6]),
    ]
    for one in keep:
        one.start()

    def swap(block):
        return remote(att.at[block], own.at[t], swap_send.at[block], swap_recv.at[t], tensor=block)

    for block in range(LEN // QB):
        att[block] = pack(attend_block(block, head_dim, allowed_block(block, starts), qkv, bias, low, high))

        @pl.when(t != block)
        def _():
            swap(block).start()

        @pl.when(t == block)
        def _():
            own[t] = att[block]

    late = [
        pltpu.make_async_copy(low, low_out, local_sem.at[7]),
        pltpu.make_async_copy(high, high_out, local_sem.at[8]),
    ]
    for one in late:
        one.start()
    tick(nt)
    if exchange:
        for k in range(1, chips):
            for q in range(1, nt):
                from_chip(k, q).wait_recv()
                to_core(k, q).start()
    tick(nt + 1)
    for block in range(nt):
        @pl.when(t != block)
        def _():
            remote(att.at[block], own.at[block], swap_send.at[block], swap_recv.at[block], tensor=block).wait_recv()

    if exchange:
        for k in range(chips):
            for q in range(1, nt):
                from_core(k, q).wait_recv()
    late += [
        pltpu.make_async_copy(own, own_out, local_sem.at[9]),
        pltpu.make_async_copy(whole, whole_out, local_sem.at[10]),
    ]
    for one in late[2:]:
        one.start()
    total = x_ref[...].astype(jnp.float32)
    for j in range(nt):
        total = total + dot(unpack(own[j], 0, inner), whole[j, pl.ds(3 * inner, inner), :], ((1,), (0,)))
    middle_out[...] = total
    second_out[...] = normed(total, row_of(gain2_ref)).astype(jnp.bfloat16)
    for k in range(nt + 2, 2 * nt):
        tick(k)
    for block in range(nt):
        @pl.when(t != block)
        def _():
            swap(block).wait_send()

    for one in keep + late:
        one.wait()
    if exchange:
        for q in range(1, nt):
            to_plane(q).wait_send()
            for k in range(1, chips):
                to_chip(k, q).wait_send()
            for k in range(chips):
                to_core(k, q).wait_send()
    for piece in range(pieces):
        for way, last, onward in ways:
            for stage in range(2):
                for step in range(nt):
                    @pl.when(onward & ((step < last) if stage == 0 else (step <= last)))
                    def _():
                        copy(way, stage, step, piece).wait_send()


def gather_attend(nt, ndp, tokens, cotangent, gain, gain2, weights, buckets, table, starts):
    heads = table.shape[0]
    rows, width = tokens.shape
    inner = weights[0].shape[0]
    low, full = jnp.bfloat16, jnp.float32
    pieces = 2
    exchange = (4 * inner // ndp) % 16 == 0
    if not exchange:
        joined = jnp.concatenate(weights, axis=0)
        part = joined.shape[0] // ndp
        mine = lax.dynamic_slice_in_dim(joined, lax.axis_index("dp") * part, part, 0)
        weights = (lax.all_gather(mine, ("tensor", "dp"), axis=0, tiled=True).reshape(nt, *joined.shape),)
    chips = ndp // 2
    smem = pl.BlockSpec(memory_space=pltpu.SMEM)
    hbm = pl.BlockSpec(memory_space=pl.ANY)
    vmem = pl.BlockSpec(memory_space=pltpu.VMEM)
    shapes = (
        (nt, rows, width), (nt, rows, width), (3, LEN, inner), (heads, HALF, HALF), (heads, HALF, LEN),
        (nt, rows // 2, 2 * inner), (nt, 4 * inner, width),
    )
    dma = pltpu.SemaphoreType.DMA
    return pl.pallas_call(
        functools.partial(gather_attend_kernel, nt, ndp, pieces, heads, inner // heads, exchange),
        out_shape=tuple(jax.ShapeDtypeStruct(shape, low) for shape in shapes)
        + (jax.ShapeDtypeStruct((rows, width), full), jax.ShapeDtypeStruct((rows, width), low)),
        in_specs=[vmem, hbm, vmem, vmem, vmem, smem, smem] + [hbm] * len(weights),
        out_specs=(hbm,) * 7 + (vmem, vmem),
        scratch_shapes=[
            pltpu.VMEM((nt, rows, width), low),
            pltpu.VMEM((3, LEN, inner), low),
            pltpu.VMEM((heads, HALF, HALF), low),
            pltpu.VMEM((heads, HALF, LEN), low),
            pltpu.VMEM((heads, QB, SPAN), full),
            pltpu.VMEM((nt, rows // 2, 2 * inner), low),
            pltpu.VMEM((nt, rows // 2, 2 * inner), low),
            pltpu.VMEM((nt, 4 * inner, width), low),
            dma((2, 2, nt, pieces)), dma((2, 2, nt, pieces)), dma((nt,)), dma((nt,)),
            dma((nt - 1,)), dma((nt,)), dma((chips - 1, nt - 1)), dma((chips - 1, nt - 1)),
            dma((chips, nt - 1)), dma((chips, nt - 1)), dma((11,)),
        ],
        compiler_params=pltpu.CompilerParams(
            vmem_limit_bytes=VMEM_LIMIT, collective_id=0, has_side_effects=True
        ),
        name="gather_attend",
    )(tokens, cotangent, gain, gain2, buckets, table, starts, *weights)


def fold_diagonals(grid):
    rows = QB // 2
    width = grid.shape[1]
    while rows >= 1:
        grid = grid[:rows] + pltpu.roll(grid[rows : 2 * rows], width - rows, 1)
        rows //= 2
    return grid


def gelu_parts(v):
    root, cubic = 0.7978845608028654, 0.044715
    square = v * v
    bend = jnp.tanh(root * v * (1.0 + cubic * square))
    half = 0.5 * (1.0 + bend)
    slope = half + 0.5 * v * (1.0 - bend * bend) * root * (1.0 + 3.0 * cubic * square)
    return v * half, slope


def feed_kernel(
    nt, ndp, pieces, halves, fused,
    gain_ref, middle_hbm, second_hbm, cot_own_hbm, whole_hbm, cot_hbm, wg_hbm, wu_hbm, wd_hbm,
    base_out, gm_out, gain_out, ga_out, lo_out, lo_in, grads_out, *rest,
):
    if fused:
        down_out, *rest = rest
    (
        middle, cot_own_ref, buf, cot, wg, wu, wd, hid, gg, gu, gs, lo, wo, mate_in, acc_in, far_in, grads, *rest,
    ) = rest
    *rest, send_sem, recv_sem, rs_send, rs_recv, lo_send, lo_recv, local_sem = rest
    t = lax.axis_index("tensor")
    d = lax.axis_index("dp")
    core = lax.rem(d, 2)
    chips = ndp // 2
    barrier = greet(t, nt)
    own_load = pltpu.make_async_copy(second_hbm, buf.at[t], local_sem.at[11])
    own_load.start()
    if fused:
        sums, pair_send, pair_recv, chip_send, chip_recv = rest
        chip = d // 2
        for k in range(chips):
            peer = 2 * lax.rem(chip + k, chips) + core if k else d + 1 - 2 * core
            pl.semaphore_signal(barrier, inc=1, device_id={"dp": peer}, device_id_type=MESH)
    loads = [
        pltpu.make_async_copy(a, b, local_sem.at[i])
        for i, (a, b) in enumerate(((wg_hbm, wg), (wu_hbm, wu), (wd_hbm, wd), (cot_hbm, cot)))
    ]
    for one in loads:
        one.start()
    row_count = middle.shape[0]
    size = row_count // pieces
    inner = wo.shape[1]
    wo_load = pltpu.make_async_copy(whole_hbm.at[:, pl.ds(3 * inner, inner)], wo, local_sem.at[4])
    wo_load.start()
    late_loads = [
        pltpu.make_async_copy(middle_hbm, middle, local_sem.at[9]),
        pltpu.make_async_copy(cot_own_hbm, cot_own_ref, local_sem.at[10]),
    ]
    for one in late_loads:
        one.start()
    keep = []
    own_load.wait()
    pl.semaphore_wait(barrier, nt - 1 + chips * fused)
    mate = t + 1 - 2 * lax.rem(t, 2)
    is_end = (t == 0) | (t == nt - 1)
    ways = ((0, t, t < nt - 1), (1, nt - 1 - t, t > 0))

    def copy(way, step, piece):
        return line_copy(
            t, nt, way, step, buf, piece, pieces,
            send_sem.at[way, step, piece], recv_sem.at[way, step, piece],
        )

    def landed(way, step, piece):
        sign = 1 if way == 0 else -1
        part = buf.at[jnp.clip(t - sign * step, 0, nt - 1), pl.ds(piece * size, size)]
        pltpu.make_async_remote_copy(
            src_ref=part, dst_ref=part,
            send_sem=send_sem.at[way, step - 1, piece], recv_sem=recv_sem.at[way, step - 1, piece],
            device_id={"tensor": jnp.clip(t + sign, 0, nt - 1)}, device_id_type=MESH,
        ).wait_recv()

    def remote(src, dst, target, send, recv):
        return pltpu.make_async_remote_copy(
            src_ref=src, dst_ref=dst, send_sem=send, recv_sem=recv,
            device_id={"tensor": target}, device_id_type=MESH,
        )

    wide = buf.shape[2] // halves

    def to_mate(piece, half):
        part = (pl.ds(piece * size, size), pl.ds(half * wide, wide))
        return remote(
            gs.at[(mate, *part)], mate_in.at[part], mate, rs_send.at[0, piece, half], rs_recv.at[0, piece, half]
        )

    def to_acc(origin, piece, half):
        part = (pl.ds(piece * size, size), pl.ds(half * wide, wide))
        j = lax.rem(origin, 2)
        return remote(
            gs.at[(origin, *part)], acc_in.at[(j, *part)], mate,
            rs_send.at[1 + j, piece, half], rs_recv.at[1 + j, piece, half],
        )

    def to_far(origin, piece, half):
        part = (pl.ds(piece * size, size), pl.ds(half * wide, wide))
        j = lax.rem(origin, 2)
        return remote(
            gs.at[(origin, *part)], far_in.at[part], origin, rs_send.at[3 + j, piece, half], rs_recv.at[3, piece, half]
        )

    def feed(origin, piece):
        rows = pl.ds(pl.multiple_of(piece * size, size), size)
        flat = pl.ds(pl.multiple_of(origin * row_count + piece * size, size), size)
        normal = buf[origin, rows]
        gate = dot(normal, wg[...], ((1,), (1,)))
        up = dot(normal, wu[...], ((1,), (1,)))
        grad_hidden = dot(cot[origin, rows], wd[...], ((1,), (1,)))
        act, slope = gelu_parts(gate)
        hidden = (act * up).astype(jnp.bfloat16)
        hid[flat, :] = hidden
        grad_gate = (grad_hidden * up * slope).astype(jnp.bfloat16)
        grad_up = (grad_hidden * act).astype(jnp.bfloat16)
        gg[flat, :] = grad_gate
        gu[flat, :] = grad_up
        for half in range(halves):
            cols = pl.ds(half * wide, wide)
            gs[origin, rows, cols] = (
                dot(grad_gate, wg[:, cols], ((1,), (0,))) + dot(grad_up, wu[:, cols], ((1,), (0,)))
            ).astype(jnp.bfloat16)

            @pl.when(origin == mate)
            def _():
                to_mate(piece, half).start()

            @pl.when((origin != mate) & (origin != t) & is_end)
            def _():
                to_acc(origin, piece, half).start()

        lo[origin, rows] = dot(hidden, wd[...], ((1,), (0,))).astype(jnp.bfloat16)

    span = 256
    flat_rows = nt * row_count
    spans = buf.shape[2] // span
    head = jnp.where(t < nt // 2, 0, 1)
    last_one = jnp.where(t < nt // 2, nt - 1, 0)
    head_rows = pl.ds(pl.multiple_of(head * row_count, row_count), flat_rows - row_count)
    last_rows = pl.ds(pl.multiple_of(last_one * row_count, row_count), row_count)

    def columns(ref, i):
        cols = pl.ds(pl.multiple_of(i * span, span), span)
        return ref[pl.ds(head, nt - 1), :, cols].reshape(flat_rows - row_count, span)

    def grad_head(which, left, right, rows):
        grads[which, rows, :] = dot(left, right[head_rows, :], ((0,), (0,))).astype(jnp.bfloat16)

    def grad_last(which, left, right, rows):
        grads[which, rows, :] = (
            grads[which, rows, :].astype(jnp.float32) + dot(left, right[last_rows, :], ((0,), (0,)))
        ).astype(jnp.bfloat16)

    def down_head(i, carry):
        rows = pl.ds(pl.multiple_of(i * span, span), span)
        grad_head(2, columns(cot, i), hid, rows)
        return carry

    def gate_up_head(i, carry):
        rows = pl.ds(pl.multiple_of(i * span, span), span)
        left = columns(buf, i)
        grad_head(0, left, gg, rows)
        grad_head(1, left, gu, rows)
        return carry

    def down_last(i, carry):
        rows = pl.ds(pl.multiple_of(i * span, span), span)
        grad_last(2, cot[last_one, :, rows], hid, rows)
        return carry

    def gate_up_last(i, carry):
        rows = pl.ds(pl.multiple_of(i * span, span), span)
        left = buf[last_one, :, rows]
        grad_last(0, left, gg, rows)
        grad_last(1, left, gu, rows)
        return carry

    for piece in range(pieces):
        for way, last, onward in ways:
            @pl.when(onward)
            def _():
                copy(way, 0, piece).start()

    for one in loads:
        one.wait()

    def unit(u, carry):
        step = u // pieces
        piece = lax.rem(u, pieces)

        @pl.when(step > 0)
        def _():
            for way, last, onward in ways:
                @pl.when(step <= last)
                def _():
                    landed(way, step, piece)

                    @pl.when(onward)
                    def _():
                        copy(way, step, piece).start()

        def side(way, carry):
            origin = t - (1 - 2 * way) * step
            there = (origin >= 0) & (origin < nt) & ((step > 0) | (way == 0))

            @pl.when(there)
            def _():
                feed(origin, piece)

            return carry

        lax.fori_loop(0, 2, side, carry)

        @pl.when(u == (nt - 1) * pieces - 1)
        def _():
            lax.fori_loop(0, spans, down_head, 0)

        @pl.when((u == (nt - 1) * pieces) & jnp.logical_not(is_end))
        def _():
            lax.fori_loop(0, spans, gate_up_head, 0)

        return carry

    lax.fori_loop(0, nt * pieces, unit, 0)

    near = jnp.where(t < nt // 2, nt // 2, nt // 2 - 1)
    far = jnp.where(t < nt // 2, nt - 1, 0)

    def pass_on(origin, piece):
        @pl.when(jnp.logical_not(is_end))
        def _():
            rows = pl.ds(piece * size, size)
            j = lax.rem(origin, 2)
            for half in range(halves):
                to_acc(origin, piece, half).wait_recv()
                cols = pl.ds(half * wide, wide)
                gs[origin, rows, cols] = (
                    gs[origin, rows, cols].astype(jnp.float32) + acc_in[j, rows, cols].astype(jnp.float32)
                ).astype(jnp.bfloat16)
                to_far(origin, piece, half).start()

    share = buf.shape[2] // ndp

    def block_rows(index):
        return pl.ds(pl.multiple_of(index * share, share), share)

    def pair(which, c):
        return pltpu.make_async_remote_copy(
            src_ref=grads.at[which, block_rows(2 * c + 1 - core)], dst_ref=sums.at[which, c],
            send_sem=pair_send.at[which, c], recv_sem=pair_recv.at[which, c],
            device_id={"dp": d + 1 - 2 * core}, device_id_type=MESH,
        )

    def down_copy(k):
        to = lax.rem(chip + k, chips)
        return pltpu.make_async_remote_copy(
            src_ref=sums.at[2, to], dst_ref=down_out.at[k - 1],
            send_sem=chip_send.at[k - 1], recv_sem=chip_recv.at[k - 1],
            device_id={"dp": 2 * to + core}, device_id_type=MESH,
        )

    def pair_start(*which):
        if fused:
            for w in which:
                for c in range(chips):
                    pair(w, c).start()

    def pair_sum(which):
        if fused:
            for c in range(chips):
                pair(which, c).wait_recv()
                sums[which, c] = (
                    grads[which, block_rows(2 * c + core)].astype(jnp.float32) + sums[which, c].astype(jnp.float32)
                ).astype(jnp.bfloat16)
            if which == 2:
                for k in range(1, chips):
                    down_copy(k).start()
                one = pltpu.make_async_copy(sums.at[2, chip], down_out.at[chips - 1], local_sem.at[8])
            else:
                one = pltpu.make_async_copy(sums.at[which], grads_out.at[which], local_sem.at[6 + which])
        else:
            one = pltpu.make_async_copy(grads.at[which], grads_out.at[which], local_sem.at[6 + which])
        one.start()
        keep.append(one)

    def lo_acc(piece):
        rows = pl.ds(piece * size, size)
        return remote(lo.at[far, rows], lo_in.at[rows], mate, lo_send.at[piece], lo_recv.at[piece])

    @pl.when(is_end)
    def _():
        for piece in range(pieces):
            lo_acc(piece).start()

    keep.append(pltpu.make_async_copy(lo, lo_out, local_sem.at[5]))
    keep[-1].start()
    pass_on(near, 0)
    lax.fori_loop(0, spans, down_last, 0)
    pair_start(2)
    pass_on(near, 1)

    @pl.when(is_end)
    def _():
        lax.fori_loop(0, spans, gate_up_head, 0)

    pair_sum(2)
    lax.fori_loop(0, spans, gate_up_last, 0)
    pair_start(0, 1)
    pass_on(far, 0)
    pass_on(far, 1)
    for one in late_loads:
        one.wait()
    pair_sum(0)
    pair_sum(1)
    wo_load.wait()
    for piece in range(pieces):
        rows = pl.ds(piece * size, size)
        for half in range(halves):
            to_mate(piece, half).wait_recv()
            part = (rows, pl.ds(half * wide, wide))
            remote(
                gs.at[(t, *part)], far_in.at[part], mate, rs_send.at[3, piece, half], rs_recv.at[3, piece, half]
            ).wait_recv()
        grad_second = (
            gs[t, rows].astype(jnp.float32)
            + mate_in[rows].astype(jnp.float32)
            + far_in[rows].astype(jnp.float32)
        )
        mid = middle[rows]
        inv = lax.rsqrt(jnp.mean(mid * mid, axis=-1, keepdims=True) + EPSILON)
        scaled = row_of(gain_ref) * grad_second
        along = jnp.mean(scaled * mid, axis=-1, keepdims=True)
        grad_middle = cot_own_ref[rows].astype(jnp.float32) + inv * scaled - mid * (inv * inv * inv * along)
        gm_out[rows] = grad_middle
        part = jnp.sum(grad_second * mid * inv, axis=0, keepdims=True)
        if piece == 0:
            gain_out[...] = part
        else:
            gain_out[...] += part
        grad_low = grad_middle.astype(jnp.bfloat16)
        for j in range(nt):
            ga_out[j, :, pl.ds(piece * inner, inner)] = dot(grad_low, wo[j], ((1,), (1,))).astype(jnp.bfloat16)

    base_out[...] = middle[...] + lo[t].astype(jnp.float32)

    @pl.when(jnp.logical_not(is_end))
    def _():
        for piece in range(pieces):
            lo_acc(piece).wait_recv()

    for one in keep:
        one.wait()
    for piece in range(pieces):
        for way, last, onward in ways:
            for step in range(nt):
                @pl.when(onward & (step <= last))
                def _():
                    copy(way, step, piece).wait_send()

        @pl.when(is_end)
        def _():
            lo_acc(piece).wait_send()

        for half in range(halves):
            to_mate(piece, half).wait_send()
            for origin in (near, far):
                @pl.when(is_end)
                def _():
                    to_acc(origin, piece, half).wait_send()

                @pl.when(jnp.logical_not(is_end))
                def _():
                    to_far(origin, piece, half).wait_send()

    if fused:
        for which in range(3):
            for c in range(chips):
                pair(which, c).wait_send()
        for k in range(1, chips):
            down_copy(k).wait()


def feed(nt, ndp, middle, second, gain, cotangent, whole, cot_all, gate_weight, up_weight, down_weight):
    rows, width = middle.shape
    hidden = gate_weight.shape[0]
    low, full = jnp.bfloat16, jnp.float32
    pieces, halves = 2, 2
    hbm = pl.BlockSpec(memory_space=pl.ANY)
    vmem = pl.BlockSpec(memory_space=pltpu.VMEM)
    inner = whole.shape[1] // 4
    dma = pltpu.SemaphoreType.DMA
    shape = jax.ShapeDtypeStruct
    share, chips = width // ndp, ndp // 2
    fused = share % 16 == 0
    sums = (3, chips, share, hidden)
    pairs = [
        pltpu.VMEM(sums, low), dma((3, chips)), dma((3, chips)), dma((chips - 1,)), dma((chips - 1,))
    ] if fused else []
    return pl.pallas_call(
        functools.partial(feed_kernel, nt, ndp, pieces, halves, fused),
        out_shape=(
            shape((rows, width), full), shape((rows, width), full), shape((1, width), full),
            shape((nt, rows // 2, 2 * inner), low), shape((nt, rows, width), low), shape((rows, width), low),
            shape((2, *sums[1:]) if fused else (3, width, hidden), low),
        ) + (shape((chips, share, hidden), low),) * fused,
        in_specs=[vmem] + [hbm] * 8,
        out_specs=(vmem, vmem, vmem, vmem, hbm, hbm, hbm) + (hbm,) * fused,
        scratch_shapes=[
            pltpu.VMEM((rows, width), full), pltpu.VMEM((rows, width), low),
            pltpu.VMEM((nt, rows, width), low), pltpu.VMEM((nt, rows, width), low),
            pltpu.VMEM((hidden, width), low), pltpu.VMEM((hidden, width), low), pltpu.VMEM((hidden, width), low),
            pltpu.VMEM((nt * rows, hidden), low), pltpu.VMEM((nt * rows, hidden), low), pltpu.VMEM((nt * rows, hidden), low),
            pltpu.VMEM((nt, rows, width), low), pltpu.VMEM((nt, rows, width), low),
            pltpu.VMEM((nt, inner, width), low),
            pltpu.VMEM((rows, width), low), pltpu.VMEM((2, rows, width), low), pltpu.VMEM((rows, width), low),
            pltpu.VMEM((3, width, hidden), low), *pairs,
            dma((2, nt, pieces)), dma((2, nt, pieces)), dma((5, pieces, halves)), dma((4, pieces, halves)),
            dma((pieces,)), dma((pieces,)),
            dma((12,)),
        ],
        compiler_params=pltpu.CompilerParams(
            vmem_limit_bytes=VMEM_LIMIT, collective_id=1, has_side_effects=True
        ),
        name="feed",
    )(gain, middle, second, cotangent, whole, cot_all, gate_weight, up_weight, down_weight)


def back_kernel(
    nt, ndp, pieces, heads, head_dim, grad_type, fused,
    ga_ref, gain_ref, gain2_ref, gm_hbm, x_hbm, own_hbm,
    qkv_hbm, low_hbm, high_hbm, first_hbm, weight_hbm, lo_hbm, lo_part_hbm, *rest,
):
    if fused:
        feed_hbm, *rest = rest
    input_out, q_out, k_out, v_out, o_out, gains_in, dist_in, far_in, mate_in, *rest = rest
    if fused:
        feed_in, *rest = rest
    (
        gm_ref, x_ref, own_ref,
        ga_in, qkv, low, high, first, weight, lo, acc_in, lo_part,
        gq, dq_send, dq_in, dkv_send, dkv_in, diag, dk_acc, dv_acc,
        og, og_sum, og_chip, og_line, og_line_in, pg, pg_sum, pg_chip,
        gains_line, gains_own, dist_own,
        swap_send, swap_recv, dq_done, dq_here, dkv_done, dkv_here, lo_send, lo_recv,
        pair_send, pair_recv, chip_send, chip_recv, line_send, line_recv,
        gl_send, gl_recv, gd_send, gd_recv, dist_send, dist_recv, local_sem, *rest,
    ) = rest
    if fused:
        feed_send, feed_recv = rest
    t = lax.axis_index("tensor")
    d = lax.axis_index("dp")
    core = lax.rem(d, 2)
    chip = d // 2
    chips = ndp // 2
    barrier = greet(t, nt)
    for k in range(1, ndp):
        pl.semaphore_signal(
            barrier, inc=1, device_id={"dp": lax.rem(d + k, ndp)}, device_id_type=MESH
        )
    mate = t + 1 - 2 * lax.rem(t, 2)
    is_end = (t == 0) | (t == nt - 1)
    near = jnp.where(t < nt // 2, nt // 2, nt // 2 - 1)
    far = jnp.where(t < nt // 2, nt - 1, 0)
    loads = [
        pltpu.make_async_copy(a, b, local_sem.at[i])
        for i, (a, b) in enumerate(
            ((qkv_hbm, qkv), (low_hbm, low), (high_hbm, high), (first_hbm, first),
             (weight_hbm.at[:, pl.ds(0, weight.shape[1])], weight),
             (lo_hbm.at[near], lo.at[0]), (lo_hbm.at[far], lo.at[1]), (lo_hbm.at[mate], lo.at[2]),
             (gm_hbm, gm_ref), (x_hbm, x_ref), (own_hbm, own_ref), (lo_part_hbm, lo_part))
        )
    ]
    for one in loads:
        one.start()
    others = (far, near, mate)
    row_count, width = x_ref.shape
    inner = heads * head_dim
    size = row_count // pieces
    share = width // ndp
    full = jnp.float32

    def remote(src, dst, send, recv, **target):
        return pltpu.make_async_remote_copy(
            src_ref=src, dst_ref=dst, send_sem=send, recv_sem=recv,
            device_id=target, device_id_type=MESH,
        )

    def swap(peer):
        return remote(ga_ref.at[peer], ga_in.at[t], swap_send.at[peer], swap_recv.at[t], tensor=peer)

    def swap_in(peer):
        return remote(ga_ref.at[peer], ga_in.at[peer], swap_send.at[peer], swap_recv.at[peer], tensor=peer)

    def lo_acc(piece):
        rows = pl.ds(piece * size, size)
        return remote(lo.at[0, rows], acc_in.at[rows], lo_send.at[0, piece], lo_recv.at[0, piece], tensor=mate)

    def lo_final(place, origin, piece):
        rows = pl.ds(piece * size, size)
        return remote(
            lo.at[place, rows], far_in.at[rows], lo_send.at[place, piece], lo_recv.at[1, piece], tensor=origin
        )

    def lo_mate(piece):
        rows = pl.ds(piece * size, size)
        return remote(lo.at[2, rows], mate_in.at[rows], lo_send.at[2, piece], lo_recv.at[2, piece], tensor=mate)

    diag[...] = jnp.zeros_like(diag)
    pl.semaphore_wait(barrier, nt - 1 + ndp - 1)
    for peer in others:
        swap(peer).start()
    ga_in[t] = ga_ref[t]
    if fused:
        def feed_copy(which, k):
            to = lax.rem(chip + k, chips)
            return remote(
                feed_hbm.at[which, to], feed_in.at[k - 1, which],
                feed_send.at[k - 1, which], feed_recv.at[k - 1, which], dp=2 * to + core,
            )

        own_feed = pltpu.make_async_copy(feed_hbm.at[:, chip], feed_in.at[chips - 1], local_sem.at[13])
        own_feed.start()
        for which in range(2):
            for k in range(1, chips):
                feed_copy(which, k).start()

    def block_rows(index):
        return pl.ds(pl.multiple_of(index * share, share), share)

    def pair(kind, c):
        grads, landing = ((og, og_sum), (pg, pg_sum))[kind]
        return remote(
            grads.at[block_rows(2 * c + 1 - core)], landing.at[c],
            pair_send.at[kind, c], pair_recv.at[kind, c], dp=d + 1 - 2 * core,
        )

    def chip_copy(kind, k):
        sums, landing = ((og_sum, og_chip), (pg_sum, pg_chip))[kind]
        to = lax.rem(chip + k, chips)
        return remote(
            sums.at[to], landing.at[k - 1], chip_send.at[kind, k - 1], chip_recv.at[kind, k - 1], dp=2 * to + core
        )

    def pair_sum(kind):
        grads, sums = ((og, og_sum), (pg, pg_sum))[kind]
        for c in range(chips):
            pair(kind, c).wait_recv()
            sums[c] = (grads[block_rows(2 * c + core)].astype(full) + sums[c].astype(full)).astype(grad_type)
        for k in range(1, chips):
            chip_copy(kind, k).start()

    def chip_sum(kind):
        sums, landing = ((og_sum, og_chip), (pg_sum, pg_chip))[kind]
        total = sums[chip].astype(full)
        for k in range(1, chips):
            chip_copy(kind, k).wait_recv()
            total = total + landing[k - 1].astype(full)
        return total

    for one in loads[5:]:
        one.wait()
    for piece in range(pieces):
        @pl.when(is_end)
        def _():
            lo_acc(piece).start()

        @pl.when(jnp.logical_not(is_end))
        def _():
            rows_lo = pl.ds(piece * size, size)
            lo[1, rows_lo] = (lo[1, rows_lo].astype(full) + lo_part[rows_lo].astype(full)).astype(jnp.bfloat16)
            lo_final(1, far, piece).start()

    span = 256
    spans = width // span
    own = jnp.concatenate([unpack(own_ref[j], 0, inner) for j in range(nt)], axis=1)
    for i in range(spans):
        left = gm_ref[:, pl.ds(i * span, span)].astype(jnp.bfloat16)
        og[pl.ds(i * span, span), :] = dot(left, own, ((0,), (0,))).astype(grad_type)
    for c in range(chips):
        pair(0, c).start()

    for i in range(3):
        loads[i].wait()
    def give(peer):
        return (
            remote(dq_send.at[peer], dq_in.at[t], dq_done.at[peer], dq_here.at[t], tensor=peer),
            remote(dkv_send.at[peer], dkv_in.at[t], dkv_done.at[peer], dkv_here.at[t], tensor=peer),
        )

    def taken(peer):
        return (
            remote(dq_send.at[peer], dq_in.at[peer], dq_done.at[peer], dq_here.at[peer], tensor=peer),
            remote(dkv_send.at[peer], dkv_in.at[peer], dkv_done.at[peer], dkv_here.at[peer], tensor=peer),
        )

    def give_keys(block):
        rows = pl.ds(block * QB, QB)
        sides = [acc[head, rows, :] for acc in (dk_acc, dv_acc) for head in range(heads)]
        side = jnp.concatenate(sides, axis=1).astype(jnp.bfloat16)
        gq[rows, pl.ds(inner, 2 * inner)] = side
        dkv_send[block] = side

        @pl.when(t != block)
        def _():
            give(block)[1].start()

    blocks = LEN // QB
    for block in reversed(range(blocks)):
        keys = key_count(block)
        rows = pl.ds(block * QB, QB)
        first_col = LEN - block * QB

        for waited in (1, 0) if block == 1 else () if block == 0 else (block,):
            @pl.when(t != waited)
            def _():
                swap_in(waited).wait_recv()

        parts = []
        for head in range(heads):
            cols = pl.ds(head * head_dim, head_dim)
            if keys == HALF:
                probs_low = low[head, rows, :]
            else:
                probs_low = high[head, pl.ds(block * QB - HALF, QB), :]
            probs = probs_low.astype(full)
            do = unpack(ga_in[block], head * head_dim, head_dim)
            grad_probs = dot(do, qkv[2, pl.ds(0, keys), cols], ((1,), (1,)))
            weighted = jnp.sum(probs * grad_probs, axis=-1, keepdims=True)
            grad_low = (probs * (grad_probs - weighted)).astype(jnp.bfloat16)
            reach = pl.ds(first_col, keys)
            diag[head, :, reach] = diag[head, :, reach] + grad_low.astype(full)
            parts.append(dot(grad_low, qkv[1, pl.ds(0, keys), cols], ((1,), (0,))))
            key_part = dot(grad_low, qkv[0, rows, cols], ((0,), (0,)))
            value_part = dot(probs_low, do, ((0,), (0,)))
            if block == blocks - 1:
                dk_acc[head] = key_part
                dv_acc[head] = value_part
            else:
                dk_acc[head, pl.ds(0, keys), :] += key_part
                dv_acc[head, pl.ds(0, keys), :] += value_part
        side = jnp.concatenate(parts, axis=1).astype(jnp.bfloat16)
        gq[rows, pl.ds(0, inner)] = side
        dq_send[block] = pack(side)

        @pl.when(t != block)
        def _():
            give(block)[0].start()

        if block * QB == HALF:
            for done in range(block, blocks):
                give_keys(done)
        if block == 1:
            pair_sum(0)
    for block in range(HALF // QB):
        give_keys(block)

    def token_rows(peer):
        return pl.ds(pl.multiple_of(peer * row_count, row_count), row_count)

    for head in range(heads):
        dist_own[pl.ds(head, 1), :] = fold_diagonals(diag[head])
    dist_keep = pltpu.make_async_copy(dist_own, dist_in.at[d], local_sem.at[12])
    dist_keep.start()

    def dist_copy(k):
        return remote(
            dist_own, dist_in.at[d], dist_send.at[k - 1], dist_recv.at[d], dp=lax.rem(d + k, ndp)
        )

    for k in range(1, ndp):
        dist_copy(k).start()
    loads[3].wait()
    for i in range(spans):
        cols = pl.ds(i * span, span)
        left = first[:, :, cols].reshape(nt * row_count, span)
        pg[cols, :] = dot(left, gq[...], ((0,), (0,))).astype(grad_type)
    for c in range(chips):
        pair(1, c).start()
    total = chip_sum(0)
    for j in range(nt):
        og_line[j] = total[:, j * inner : (j + 1) * inner].astype(grad_type)

    def line_copy_out(peer):
        return remote(og_line.at[peer], og_line_in.at[t], line_send.at[peer], line_recv.at[t], tensor=peer)

    def line_in(peer):
        return remote(og_line.at[peer], og_line_in.at[peer], line_send.at[peer], line_recv.at[peer], tensor=peer)

    for peer in others:
        line_copy_out(peer).start()
    pair_sum(1)

    @pl.when(jnp.logical_not(is_end))
    def _():
        for piece in range(pieces):
            lo_acc(piece).wait_recv()
        lo[0] = (lo[0].astype(full) + acc_in[...].astype(full)).astype(jnp.bfloat16)

    loads[4].wait()
    inputs = x_ref[...].astype(full)
    inv = lax.rsqrt(jnp.mean(inputs * inputs, axis=-1, keepdims=True) + EPSILON)
    grad_first = dot(gq[token_rows(t)], weight[t], ((1,), (0,)))
    for peer in (mate, near, far):
        for one in taken(peer):
            one.wait_recv()
        grad_first = (
            grad_first
            + dot(unpack(dq_in[peer], 0, inner), weight[peer, pl.ds(0, inner), :], ((1,), (0,)))
            + dot(dkv_in[peer], weight[peer, pl.ds(inner, 2 * inner), :], ((1,), (0,)))
        )
    scaled = row_of(gain_ref) * grad_first
    along = jnp.mean(scaled * inputs, axis=-1, keepdims=True)
    gains_line[t, pl.ds(0, 1), :] = jnp.sum(grad_first * inputs * inv, axis=0, keepdims=True)
    gains_line[t, pl.ds(1, 1), :] = gain2_ref[...]

    def gain_copy(peer):
        return remote(gains_line.at[t], gains_line.at[t], gl_send.at[peer], gl_recv.at[t], tensor=peer)

    def gain_landed(peer):
        return remote(gains_line.at[peer], gains_line.at[peer], gl_send.at[peer], gl_recv.at[peer], tensor=peer)

    for peer in others:
        gain_copy(peer).start()
    for piece in range(pieces):
        lo_mate(piece).start()

        @pl.when(jnp.logical_not(is_end))
        def _():
            lo_final(0, near, piece).start()

    input_out[...] = (gm_ref[...] + inv * scaled - inputs * (inv * inv * inv * along)).astype(jnp.bfloat16)
    for peer in others:
        gain_landed(peer).wait_recv()
    gains_own[...] = gains_line[0] + gains_line[1] + gains_line[2] + gains_line[3]
    gains_keep = pltpu.make_async_copy(gains_own, gains_in.at[d], local_sem.at[14])
    gains_keep.start()

    def gains_copy(k):
        return remote(
            gains_own, gains_in.at[d], gd_send.at[k - 1], gd_recv.at[d], dp=lax.rem(d + k, ndp)
        )

    for k in range(1, ndp):
        gains_copy(k).start()
    total = chip_sum(1)
    q_out[...] = total[:, :inner]
    k_out[...] = total[:, inner : 2 * inner]
    v_out[...] = total[:, 2 * inner :]
    total = og_line[t].astype(full)
    for peer in others:
        line_in(peer).wait_recv()
        total = total + og_line_in[peer].astype(full)
    o_out[...] = total

    def others_of(landing, send, recv):
        for k in range(1, ndp):
            peer = lax.rem(d + k, ndp)
            remote(landing.at[peer], landing.at[peer], send.at[k - 1], recv.at[peer], dp=peer).wait_recv()

    others_of(dist_in, dist_send, dist_recv)
    if fused:
        own_feed.wait()
        for which in range(2):
            for k in range(1, chips):
                feed_copy(which, k).wait_recv()
    for piece in range(pieces):
        lo_final(0, near, piece).wait_recv()
        lo_mate(piece).wait_recv()
    others_of(gains_in, gd_send, gd_recv)
    dist_keep.wait()
    gains_keep.wait()

    for peer in others:
        swap(peer).wait_send()
        for one in give(peer):
            one.wait_send()
        line_copy_out(peer).wait_send()
        gain_copy(peer).wait_send()
    for piece in range(pieces):
        lo_mate(piece).wait_send()

        @pl.when(is_end)
        def _():
            lo_acc(piece).wait_send()

        @pl.when(jnp.logical_not(is_end))
        def _():
            lo_final(0, near, piece).wait_send()
            lo_final(1, far, piece).wait_send()

    if fused:
        for which in range(2):
            for k in range(1, chips):
                feed_copy(which, k).wait_send()
    for kind in range(2):
        for c in range(chips):
            pair(kind, c).wait_send()
        for k in range(1, chips):
            chip_copy(kind, k).wait_send()
    for k in range(1, ndp):
        dist_copy(k).wait_send()
        gains_copy(k).wait_send()


def back(nt, ndp, grad_attended, grad_middle, tokens, gain, gain2_part, attended, qkv, probs_low, probs_high, first_all, weights, layer_parts, layer_far, feed_grads):
    rows, width = tokens.shape
    heads = probs_low.shape[0]
    inner = qkv.shape[2]
    head_dim = inner // heads
    low, full = jnp.bfloat16, jnp.float32
    pieces = 2
    share, chips = width // ndp, ndp // 2
    grad_type = low if share % 16 == 0 else full
    hbm = pl.BlockSpec(memory_space=pl.ANY)
    vmem = pl.BlockSpec(memory_space=pltpu.VMEM)
    dma = pltpu.SemaphoreType.DMA
    shape = jax.ShapeDtypeStruct
    reach = SPAN + QB
    scratch = lambda *dims, kind=low: pltpu.VMEM(dims, kind)
    part = shape((share, inner), full)
    fused = feed_grads.ndim == 4
    hidden = feed_grads.shape[-1]
    feeds = [dma((chips - 1, 2)), dma((chips - 1, 2))] if fused else []
    return pl.pallas_call(
        functools.partial(back_kernel, nt, ndp, pieces, heads, head_dim, grad_type, fused),
        out_shape=(
            shape((rows, width), low), part, part, part, part,
            shape((ndp, 2, width), full), shape((ndp, heads, reach), full),
            shape((rows, width), low), shape((rows, width), low),
        ) + (shape((chips, 2, share, hidden), low),) * fused,
        in_specs=[vmem] * 3 + [hbm] * (10 + fused),
        out_specs=(vmem,) * 5 + (hbm,) * (4 + fused),
        scratch_shapes=[
            scratch(rows, width, kind=full), scratch(rows, width), scratch(nt, rows // 2, 2 * inner),
            scratch(nt, rows // 2, 2 * inner), scratch(3, LEN, inner), scratch(heads, HALF, HALF), scratch(heads, HALF, LEN),
            scratch(nt, rows, width), scratch(nt, 3 * inner, width), scratch(3, rows, width), scratch(rows, width), scratch(rows, width),
            scratch(nt * rows, 3 * inner), scratch(nt, rows // 2, 2 * inner), scratch(nt, rows // 2, 2 * inner),
            scratch(nt, rows, 2 * inner), scratch(nt, rows, 2 * inner), scratch(heads, QB, reach, kind=full),
            scratch(heads, LEN, head_dim, kind=full), scratch(heads, LEN, head_dim, kind=full),
            scratch(width, nt * inner, kind=grad_type), scratch(chips, share, nt * inner, kind=grad_type),
            scratch(chips - 1, share, nt * inner, kind=grad_type),
            scratch(nt, share, inner, kind=grad_type), scratch(nt, share, inner, kind=grad_type),
            scratch(width, 3 * inner, kind=grad_type), scratch(chips, share, 3 * inner, kind=grad_type),
            scratch(chips - 1, share, 3 * inner, kind=grad_type),
            scratch(nt, 2, width, kind=full), scratch(2, width, kind=full), scratch(heads, reach, kind=full),
            dma((nt,)), dma((nt,)), dma((nt,)), dma((nt,)), dma((nt,)), dma((nt,)), dma((3, pieces)), dma((3, pieces)),
            dma((2, chips)), dma((2, chips)), dma((2, chips - 1)), dma((2, chips - 1)), dma((nt,)), dma((nt,)),
            dma((nt,)), dma((nt,)), dma((ndp - 1,)), dma((ndp,)), dma((ndp - 1,)), dma((ndp,)), dma((15,)), *feeds,
        ],
        compiler_params=pltpu.CompilerParams(
            vmem_limit_bytes=VMEM_LIMIT, collective_id=2, has_side_effects=True
        ),
        cost_estimate=pl.CostEstimate(flops=60 * 10**9, bytes_accessed=200 * 10**6, transcendentals=0),
        name="back",
    )(
        grad_attended, gain, gain2_part, grad_middle, tokens, attended,
        qkv, probs_low, probs_high, first_all, weights, layer_parts, layer_far, *((feed_grads,) if fused else ()),
    )


def finish_kernel(
    fused, bucket_ref, base_ref, far_ref, mate_ref, input_ref, q_ref, k_ref, v_ref, o_ref, gains_ref, dist_ref, *rest,
):
    if fused:
        feed_ref, down_ref, *rest = rest
    layer_out, input_out, gain_out, q_out, k_out, v_out, o_out, table_out, gain2_out, *feed_outs = rest
    full = jnp.float32
    layer_out[...] = (base_ref[...] + far_ref[...].astype(full) + mate_ref[...].astype(full)).astype(jnp.bfloat16)
    input_out[...] = input_ref[...]
    for a, b in ((q_ref, q_out), (k_ref, k_out), (v_ref, v_out), (o_ref, o_out)):
        b[...] = a[...]

    @pl.when(pl.program_id(0) == 0)
    def _():
        gains, dist = gains_ref[0], dist_ref[0]
        for k in range(1, gains_ref.shape[0]):
            gains = gains + gains_ref[k]
            dist = dist + dist_ref[k]
        gain_out[...] = gains[0:1].reshape(gain_out.shape)
        gain2_out[...] = gains[1:2].reshape(gain2_out.shape)
        reach = dist.shape[1]
        shifted = jnp.concatenate([jnp.zeros((1, 1), jnp.int32), row_of(bucket_ref)], axis=1)[:, :reach]
        hot = (lax.broadcasted_iota(jnp.int32, (NB, reach), 0) == shifted).astype(full)
        table_out[...] = lax.dot_general(
            dist, hot, (((1,), (1,)), ((), ())), precision=HIGHEST, preferred_element_type=full
        )

    for which in range(len(feed_outs)):
        parts = [down_ref[k] if which == 2 else feed_ref[k, which] for k in range(feed_ref.shape[0])]
        total = parts[0].astype(full)
        for part in parts[1:]:
            total = total + part.astype(full)
        feed_outs[which][...] = total


def finish(buckets, base, outs):
    fused = len(outs) > 9
    input_grad, query_grad, key_grad, value_grad, out_grad, gains, dist, far_in, mate_in = outs[:9]
    rows, width = base.shape
    share, inner = query_grad.shape
    low, full = jnp.bfloat16, jnp.float32
    shape = jax.ShapeDtypeStruct
    steps = 2 if share % 32 == 0 and rows % 32 == 0 else 1
    vmem = pl.BlockSpec(memory_space=pltpu.VMEM)
    wide = pl.BlockSpec((rows // steps, width), lambda i: (i, 0))
    small = pl.BlockSpec((share // steps, inner), lambda i: (i, 0))
    part = shape(query_grad.shape, full)
    ins, feeds, blocks = [], (), ()
    if fused:
        chips, kinds, _, hidden = outs[9].shape
        ins = [
            pl.BlockSpec((chips, kinds, share // steps, hidden), lambda i: (0, 0, i, 0)),
            pl.BlockSpec((chips, share // steps, hidden), lambda i: (0, i, 0)),
        ]
        feeds = (shape((share, hidden), full),) * (kinds + 1)
        blocks = (pl.BlockSpec((share // steps, hidden), lambda i: (i, 0)),) * (kinds + 1)
    return pl.pallas_call(
        functools.partial(finish_kernel, fused),
        grid=(steps,),
        out_shape=(
            shape((rows, width), low), shape((rows, width), low), shape((width,), full), part, part, part, part,
            shape((dist.shape[1], NB), full), shape((width,), full),
        ) + feeds,
        in_specs=[vmem] + [wide] * 4 + [small] * 4 + [vmem] * 2 + ins,
        out_specs=(wide, wide, vmem) + (small,) * 4 + (vmem, vmem) + blocks,
        compiler_params=pltpu.CompilerParams(vmem_limit_bytes=VMEM_LIMIT),
        name="finish",
    )(
        buckets, base, far_in, mate_in, input_grad, query_grad, key_grad, value_grad, out_grad, gains, dist,
        *outs[9:],
    )


def per_device(
    tokens,
    first_gain,
    query_weight,
    key_weight,
    value_weight,
    out_weight,
    bucket_table,
    second_gain,
    gate_weight,
    up_weight,
    down_weight,
    piece_start,
    bucket_index,
    cotangent,
):
    nt, ndp = lax.axis_size("tensor"), lax.axis_size("dp")
    weights = (query_weight.T, key_weight.T, value_weight.T, out_weight.T)
    first_all, cot_all, qkv, probs_low, probs_high, attended, whole, middle, second = gather_attend(
        nt, ndp, tokens, cotangent, first_gain, second_gain, weights, bucket_index, bucket_table.T, piece_start
    )
    base, grad_middle, second_part, grad_attended, layer_parts, layer_far, feed_grads, *down_in = feed(
        nt, ndp, middle, second, second_gain, cotangent, whole, cot_all, gate_weight.T, up_weight.T, down_weight.T
    )
    outs = back(
        nt, ndp, grad_attended, grad_middle, tokens, first_gain, second_part, attended,
        qkv, probs_low, probs_high, first_all, whole, layer_parts, layer_far, feed_grads,
    )
    outs = finish(bucket_index, base, (*outs, *down_in))
    if feed_grads.ndim == 3:
        sums = lax.psum_scatter(feed_grads, "dp", scatter_dimension=1, tiled=True).astype(jnp.float32)
        outs = (*outs, sums[0], sums[1], sums[2])
    return (*outs[:7], outs[7].T, *outs[8:])


def solution(mesh):
    return jax.shard_map(
        per_device,
        mesh=mesh,
        in_specs=(
            P(("dp", "tensor"), None),
            P(),
            P(None, "tensor"),
            P(None, "tensor"),
            P(None, "tensor"),
            P(None, "tensor"),
            P(None, "tensor"),
            P(),
            P(None, "tensor"),
            P(None, "tensor"),
            P(None, "tensor"),
            P("dp", None),
            P(),
            P(("dp", "tensor"), None),
        ),
        out_specs=(
            P(("dp", "tensor"), None),
            P(("dp", "tensor"), None),
            P(),
            P("dp", "tensor"),
            P("dp", "tensor"),
            P("dp", "tensor"),
            P("dp", "tensor"),
            P(None, "tensor"),
            P(),
            P("dp", "tensor"),
            P("dp", "tensor"),
            P("dp", "tensor"),
        ),
        check_vma=False,
    )
```
